32 devices in a mesh: dp: 4 (over z), row: 4 (over y, x), col: 2 (over core).
Axes of the slice: x: 2, y: 2, z: 4, core: 2. Of those that a mesh axis runs over, the one named last changes fastest.
Arguments:
- inputs: bfloat16 [4096, 2560], P(('dp', 'col'), 'row'), may hold values from -6 to 6
- positions: int32 [4096], P(('dp', 'row')), may hold values from 0 to 767, as said below
- branch_matrix: float32 [2560, 2560], P(('row', 'dp'), 'col'), may hold values from -0.125 to 0.125
- gelu_matrix: float32 [2560, 2560], P(('row', 'dp'), 'col'), may hold values from -0.125 to 0.125
- output_matrix: float32 [2560, 2560], P(('col', 'dp'), 'row'), may hold values from -0.5 to 0.5
- gate_matrix: float32 [2560, 7680], P(('row', 'dp'), 'col'), may hold values from -0.125 to 0.125
- up_matrix: float32 [2560, 7680], P(('row', 'dp'), 'col'), may hold values from -0.125 to 0.125
- down_matrix: float32 [7680, 2560], P(('col', 'dp'), 'row'), may hold values from -0.09375 to 0.09375
- input_blocks: float32 [10, 256, 256], P('col', 'dp'), may hold values from -0.375 to 0.375
- decay_blocks: float32 [10, 256, 256], P('col', 'dp'), may hold values from -0.375 to 0.375
- conv_taps: float32 [4, 2560], P(None, ('col', 'dp')), may hold values from -3 to 3
- conv_bias: float32 [2560], P(('col', 'dp')), may hold values from -3 to 3
- branch_bias: float32 [2560], P(('col', 'dp')), may hold values from -3 to 3
- gelu_bias: float32 [2560], P(('col', 'dp')), may hold values from -3 to 3
- input_bias: float32 [2560], P(('col', 'dp')), may hold values from -3 to 3
- decay_bias: float32 [2560], P(('col', 'dp')), may hold values from -3 to 3
- decay_param: float32 [2560], P(('col', 'dp')), may hold values from -11 to -2.5
- output_bias: float32 [2560], P(('row', 'dp')), may hold values from -3 to 3
- gate_bias: float32 [7680], P(('col', 'dp')), may hold values from -3 to 3
- up_bias: float32 [7680], P(('col', 'dp')), may hold values from -3 to 3
- down_bias: float32 [2560], P(('row', 'dp')), may hold values from -3 to 3
- norm_first: float32 [2560], P(('row', 'dp')), may hold values from -3 to 3
- norm_second: float32 [2560], P(('row', 'dp')), may hold values from -3 to 3
- cotangent: bfloat16 [4096, 2560], P(('dp', 'col'), 'row'), may hold values from -6 to 6
Outputs:
- layer_out: bfloat16 [4096, 2560], P(('dp', 'col'), 'row')
- input_grad: float32 [4096, 2560], P(('dp', 'col'), 'row')
- branch_matrix_grad: float32 [2560, 2560], P(('row', 'dp'), 'col')
- gelu_matrix_grad: float32 [2560, 2560], P(('row', 'dp'), 'col')
- output_matrix_grad: float32 [2560, 2560], P(('col', 'dp'), 'row')
- gate_matrix_grad: float32 [2560, 7680], P(('row', 'dp'), 'col')
- up_matrix_grad: float32 [2560, 7680], P(('row', 'dp'), 'col')
- down_matrix_grad: float32 [7680, 2560], P(('col', 'dp'), 'row')
- input_blocks_grad: float32 [10, 256, 256], P('col', 'dp')
- decay_blocks_grad: float32 [10, 256, 256], P('col', 'dp')
- conv_taps_grad: float32 [4, 2560], P(None, ('col', 'dp'))
- conv_bias_grad: float32 [2560], P(('col', 'dp'))
- branch_bias_grad: float32 [2560], P(('col', 'dp'))
- gelu_bias_grad: float32 [2560], P(('col', 'dp'))
- input_bias_grad: float32 [2560], P(('col', 'dp'))
- decay_bias_grad: float32 [2560], P(('col', 'dp'))
- decay_param_grad: float32 [2560], P(('col', 'dp'))
- output_bias_grad: float32 [2560], P(('row', 'dp'))
- gate_bias_grad: float32 [7680], P(('col', 'dp'))
- up_bias_grad: float32 [7680], P(('col', 'dp'))
- down_bias_grad: float32 [2560], P(('row', 'dp'))
- norm_first_grad: float32 [2560], P(('row', 'dp'))
- norm_second_grad: float32 [2560], P(('row', 'dp'))
The draws below stay inside these ranges and needn't reach their ends.
Inputs may be any that keep to these rules, and one draw needn't show every extreme that they name: `positions`: within each aligned block of 1024 tokens of one index of dp the first position is 0, and each next one is the previous plus one or 0, where a sequence starts; each such block of 1024 tokens holds three sequences, the second of them 1024 - 256 tokens long.
All inputs are finite; a program needn't handle non-finite values.
Results may differ from the reference program's by a relative error of at most 0.0075.
The reference program's roundings to bfloat16 on the way count: a program that leaves them out, or rounds other values in their place, can miss the bound.
Values may be sent and summed in bfloat16 or wider, within the bound.
A program may use at most 256 MiB of HBM per device.

```python
import jax
import jax.numpy as jnp
from jax import lax

D = 2560
R = 2560
FF = 7680
HEADS = 10
BLK = 256
CONV = 4
GROUP_TOK = 1024
ROW_TOK = 256
TOKENS = 4096


def draw_positions(key, part):
    key = jax.random.fold_in(key, 7)
    groups = TOKENS // GROUP_TOK
    opening = jax.random.randint(key, (groups, 1), 1, ROW_TOK)
    closing = opening + (GROUP_TOK - ROW_TOK)
    places = jnp.arange(GROUP_TOK, dtype=jnp.int32)[None, :]
    starts = jnp.where(places < opening, 0, jnp.where(places < closing, opening, closing))
    return (places - starts).reshape(TOKENS).astype(jnp.int32)


def draw_decay_param(key, part):
    key = jax.random.fold_in(key, 11)
    pick_key, slow_key, fast_key = jax.random.split(key, 3)
    keep_share = 0.5
    slow_logs = jax.random.uniform(slow_key, (R,), jnp.float32, jnp.log(3e-05), jnp.log(0.0002))
    fast_logs = jax.random.uniform(fast_key, (R,), jnp.float32, jnp.log(0.005), jnp.log(0.05))
    chosen = jnp.where(jax.random.uniform(pick_key, (R,), jnp.float32) < keep_share, slow_logs, fast_logs)
    rate_values = jnp.exp(chosen)
    return jnp.log(jnp.expm1(rate_values)).astype(jnp.float32)


def block_scale(own_key, extent, cuts, least, top_value):
    loudness = 1.0
    for axis_at, shards_of in cuts:
        heights = jax.random.uniform(jax.random.fold_in(jax.random.fold_in(own_key, 6), axis_at), (shards_of,), jnp.float32, least / len(cuts), top_value / len(cuts))
        loudness = loudness * jnp.repeat(jnp.exp(heights), extent[axis_at] // shards_of).reshape((-1,) + (1,) * (len(extent) - 1 - axis_at))
    return loudness


def normal_values(rng, shape, deviation, bound, cuts=(), kind=jnp.bfloat16):
    level = block_scale(rng, shape, cuts, -0.22, 0.18) if cuts else 1.0
    entries = jax.random.normal(rng, shape, jnp.float32) * deviation * level
    return jnp.minimum(jnp.maximum(entries, -bound), bound).astype(kind)


def setup_inputs(seed: int = 0) -> dict:
    streams_of = jax.random.split(jax.random.key(seed), 25)
    inputs = normal_values(streams_of[0], (TOKENS, D), 1.0, 6.0, ((0, 8), (1, 4)))
    positions = draw_positions(jax.random.fold_in(streams_of[24], 71), 0)
    branch_matrix = normal_values(streams_of[2], (D, R), D ** -0.5, 0.125, ((0, 16), (1, 2)), jnp.float32)
    gelu_matrix = normal_values(streams_of[3], (D, R), D ** -0.5, 0.125, ((0, 16), (1, 2)), jnp.float32)
    output_matrix = normal_values(streams_of[4], (R, D), (R // 16) ** -0.5, 0.5, ((0, 8), (1, 4)), jnp.float32)
    gate_matrix = normal_values(streams_of[5], (D, FF), D ** -0.5, 0.125, ((0, 16), (1, 2)), jnp.float32)
    up_matrix = normal_values(streams_of[6], (D, FF), D ** -0.5, 0.125, ((0, 16), (1, 2)), jnp.float32)
    down_matrix = normal_values(streams_of[7], (FF, D), (FF // 2) ** -0.5, 0.09375, ((0, 8), (1, 4)), jnp.float32)
    input_blocks = normal_values(streams_of[8], (HEADS, BLK, BLK), BLK ** -0.5, 0.375, ((0, 2), (1, 4)), jnp.float32)
    decay_blocks = normal_values(streams_of[9], (HEADS, BLK, BLK), BLK ** -0.5, 0.375, ((0, 2), (1, 4)), jnp.float32)
    conv_taps = normal_values(streams_of[10], (CONV, R), 0.5, 3.0, ((1, 8),), jnp.float32)
    conv_bias = normal_values(streams_of[11], (R,), 0.3, 3.0, ((0, 8),), jnp.float32)
    branch_bias = normal_values(streams_of[12], (R,), 0.3, 3.0, ((0, 8),), jnp.float32)
    gelu_bias = normal_values(streams_of[13], (R,), 0.3, 3.0, ((0, 8),), jnp.float32)
    input_bias = normal_values(streams_of[14], (R,), 0.3, 3.0, ((0, 8),), jnp.float32)
    decay_bias = normal_values(streams_of[15], (R,), 0.3, 3.0, ((0, 8),), jnp.float32)
    decay_param = draw_decay_param(jax.random.fold_in(streams_of[24], 71), 0)
    output_bias = normal_values(streams_of[17], (D,), 0.3, 3.0, ((0, 16),), jnp.float32)
    gate_bias = normal_values(streams_of[18], (FF,), 0.3, 3.0, ((0, 8),), jnp.float32)
    up_bias = normal_values(streams_of[19], (FF,), 0.3, 3.0, ((0, 8),), jnp.float32)
    down_bias = normal_values(streams_of[20], (D,), 0.3, 3.0, ((0, 16),), jnp.float32)
    norm_first = normal_values(streams_of[21], (D,), 0.3, 3.0, ((0, 16),), jnp.float32)
    norm_second = normal_values(streams_of[22], (D,), 0.3, 3.0, ((0, 16),), jnp.float32)
    cotangent = normal_values(streams_of[23], (TOKENS, D), 1.0, 6.0, ((0, 8), (1, 4)))
    return dict(inputs=inputs, positions=positions, branch_matrix=branch_matrix, gelu_matrix=gelu_matrix, output_matrix=output_matrix, gate_matrix=gate_matrix, up_matrix=up_matrix, down_matrix=down_matrix, input_blocks=input_blocks, decay_blocks=decay_blocks, conv_taps=conv_taps, conv_bias=conv_bias, branch_bias=branch_bias, gelu_bias=gelu_bias, input_bias=input_bias, decay_bias=decay_bias, decay_param=decay_param, output_bias=output_bias, gate_bias=gate_bias, up_bias=up_bias, down_bias=down_bias, norm_first=norm_first, norm_second=norm_second, cotangent=cotangent)


epsilon = 1e-06
highest = lax.Precision.HIGHEST

@jax.custom_vjp
def low(v):
    return lax.optimization_barrier(v.astype(jnp.bfloat16)).astype(jnp.float32)

@jax.custom_vjp
def low_back(v):
    return v

def low_keep(v):
    return (low(v), None)

def low_pass(kept, grad):
    return (grad,)

def back_keep(v):
    return (v, None)

def back_low(kept, grad):
    return (low(grad),)
low.defvjp(low_keep, low_pass)
low_back.defvjp(back_keep, back_low)

def product(left, right):
    return jnp.dot(left, right, precision=highest, preferred_element_type=jnp.float32)

def rms_scale(values, gain):
    mean_square = lax.optimization_barrier(jnp.mean(values * values, axis=-1, keepdims=True))
    return values * lax.rsqrt(mean_square + epsilon) * (1.0 + gain)

def combine(earlier, later):
    return (earlier[0] * later[0], later[0] * earlier[1] + later[1])

def gate_math(conv, logit_in, logit_decay, input_bias, decay_bias, decay_param, starting):
    input_gate = jax.nn.sigmoid(logit_in + input_bias)
    decay_gate = jax.nn.sigmoid(logit_decay + decay_bias)
    log_decay = -8.0 * decay_gate * jax.nn.softplus(decay_param)
    decay = jnp.where(starting, 0.0, jnp.exp(log_decay))
    multiplier = jnp.where(starting, 1.0, jnp.sqrt(-jnp.expm1(2.0 * log_decay)))
    return (decay, multiplier * input_gate * conv)

def group_forward(params, rows, spots):
    rounded = [low(value) for value in params]
    branch_matrix, gelu_matrix, output_matrix, gate_matrix, up_matrix, down_matrix, input_blocks, decay_blocks, conv_taps, conv_bias, branch_bias, gelu_bias, input_bias, decay_bias, decay_param, output_bias, gate_bias, up_bias, down_bias, norm_first, norm_second = rounded
    length = rows.shape[0]
    normed_first = low(rms_scale(rows, norm_first))
    branch = low_back(product(normed_first, branch_matrix)) + branch_bias
    gelu_in = low_back(product(normed_first, gelu_matrix)) + gelu_bias
    side = jax.nn.gelu(gelu_in)
    conv = conv_bias + sum((conv_taps[k] * jnp.pad(branch, ((k, 0), (0, 0)))[:length] * (spots >= k).astype(jnp.float32) for k in range(CONV)))
    conv_low = low(conv).reshape(length, HEADS, BLK)
    logit_in = low_back(jnp.einsum('thi,hij->thj', conv_low, input_blocks, precision=highest)).reshape(length, R)
    logit_decay = low_back(jnp.einsum('thi,hij->thj', conv_low, decay_blocks, precision=highest)).reshape(length, R)
    starting = spots == 0
    decay, pushed = gate_math(conv, logit_in, logit_decay, input_bias, decay_bias, decay_param, starting)
    state = lax.associative_scan(combine, (decay, pushed), axis=0)[1]
    mixed = low(state * side)
    middle = rows + low_back(product(mixed, output_matrix)) + output_bias
    normed_second = low(rms_scale(middle, norm_second))
    gate_value = low_back(product(normed_second, gate_matrix)) + gate_bias
    up_value = low_back(product(normed_second, up_matrix)) + up_bias
    hidden = low(jax.nn.gelu(gate_value) * up_value)
    return middle + low_back(product(hidden, down_matrix)) + down_bias

def reference(inputs, positions, branch_matrix, gelu_matrix, output_matrix, gate_matrix, up_matrix, down_matrix, input_blocks, decay_blocks, conv_taps, conv_bias, branch_bias, gelu_bias, input_bias, decay_bias, decay_param, output_bias, gate_bias, up_bias, down_bias, norm_first, norm_second, cotangent):
    params = (branch_matrix, gelu_matrix, output_matrix, gate_matrix, up_matrix, down_matrix, input_blocks, decay_blocks, conv_taps, conv_bias, branch_bias, gelu_bias, input_bias, decay_bias, decay_param, output_bias, gate_bias, up_bias, down_bias, norm_first, norm_second)
    groups = TOKENS // GROUP_TOK
    rows_all = inputs.astype(jnp.float32).reshape(groups, GROUP_TOK, D)
    cot_all = cotangent.astype(jnp.float32).reshape(groups, GROUP_TOK, D)
    spot_all = positions.reshape(groups, GROUP_TOK, 1)

    def step(totals, pieces):
        rows, cot, spots = pieces

        def forward(weights, values):
            return group_forward(weights, values, spots)
        result, pull = jax.vjp(forward, params, rows)
        weight_grads, row_grad = pull(cot)
        totals = jax.tree.map(lambda total, grad: total + grad, totals, weight_grads)
        return (totals, (result, row_grad))
    initial = jax.tree.map(jnp.zeros_like, params)
    totals, (results, row_grads) = lax.scan(step, initial, (rows_all, cot_all, spot_all))
    layer_out = results.reshape(TOKENS, D).astype(jnp.bfloat16)
    input_grad = row_grads.reshape(TOKENS, D)
    return (layer_out, input_grad, totals[0], totals[1], totals[2], totals[3], totals[4], totals[5], totals[6], totals[7], totals[8], totals[9], totals[10], totals[11], totals[12], totals[13], totals[14], totals[15], totals[16], totals[17], totals[18], totals[19], totals[20])
```

```python
import functools

import jax
import jax.numpy as jnp
from jax import lax
from jax.experimental import pallas as pl
from jax.experimental.pallas import tpu as pltpu
from jax.sharding import PartitionSpec as P

D = 2560
epsilon = 1e-06
LOW = jnp.bfloat16
WIDE = jnp.float32


def flip(values, offset):
    count = lax.axis_size("row")
    return lax.ppermute(values, "row", [(i, i ^ offset) for i in range(count)])


def swap(values):
    return lax.ppermute(values, "col", [(0, 1), (1, 0)])


def gather_rows(block):
    half = block.shape[0] // 2
    first, second = block[:half], block[half:]
    first_1 = flip(first, 1)
    second_2 = flip(second, 2)
    second_1 = flip(second, 1)
    first_2 = flip(first, 2)
    first_3 = flip(first_1, 2)
    second_3 = flip(second_2, 1)
    return [
        block,
        jnp.concatenate((first_1, second_1), axis=0),
        jnp.concatenate((first_2, second_2), axis=0),
        jnp.concatenate((first_3, second_3), axis=0),
    ]


def scatter_rows(blocks):
    half = blocks[0].shape[0] // 2
    first = [block[:half] for block in blocks]
    second = [block[half:] for block in blocks]
    first_2 = flip(first[2].astype(LOW), 2)
    first_3 = flip(first[3].astype(LOW), 2)
    second_1 = flip(second[1].astype(LOW), 1)
    second_3 = flip(second[3].astype(LOW), 1)
    first_far = flip((first[1] + first_3.astype(WIDE)).astype(LOW), 1)
    second_far = flip((second[2] + second_3.astype(WIDE)).astype(LOW), 2)
    return jnp.concatenate(
        (
            first[0] + first_2.astype(WIDE) + first_far.astype(WIDE),
            second[0] + second_1.astype(WIDE) + second_far.astype(WIDE),
        ),
        axis=0,
    )


def exchange_rows(blocks):
    return [blocks[0]] + [flip(blocks[k], k) for k in range(1, len(blocks))]


def step_up(values, first, last):
    count = lax.axis_size("dp")
    return lax.ppermute(values, "dp", [(i, i + 1) for i in range(count - 1) if first <= i <= last])


def step_down(values, first, last):
    count = lax.axis_size("dp")
    pairs = [(count - 1 - i, count - 2 - i) for i in range(count - 1) if first <= i <= last]
    return lax.ppermute(values, "dp", pairs)


def gather_line(block):
    count, place = lax.axis_size("dp"), lax.axis_index("dp")
    up, down = [block], [block]
    for step in range(1, count):
        up.append(step_up(up[-1], step - 1, count))
        down.append(step_down(down[-1], step - 1, count))
    return [block] + [jnp.where(place >= s, up[s], down[count - s]) for s in range(1, count)]


def scatter_line(blocks):
    count = lax.axis_size("dp")
    up, down = None, None
    for step in range(1, count):
        rising, falling = blocks[step], blocks[count - step]
        if up is not None:
            rising, falling = rising + up.astype(WIDE), falling + down.astype(WIDE)
        up = step_up(rising.astype(LOW), 0, step - 1)
        down = step_down(falling.astype(LOW), 0, step - 1)
    return blocks[0] + up.astype(WIDE) + down.astype(WIDE)


def turned(step):
    count = lax.axis_size("dp")
    return lax.rem(lax.axis_index("dp") + count - step, count)


def in_order(blocks, axis):
    size = blocks[0].shape[axis]
    shape = list(blocks[0].shape)
    shape[axis] = size * len(blocks)
    whole = jnp.zeros(shape, blocks[0].dtype)
    for s, block in enumerate(blocks):
        whole = lax.dynamic_update_slice_in_dim(whole, block, turned(s) * size, axis)
    return whole


def cut(whole, axis):
    count = lax.axis_size("dp")
    size = whole.shape[axis] // count
    return [lax.dynamic_slice_in_dim(whole, turned(s) * size, size, axis) for s in range(count)]


def exchange_line(blocks):
    count = lax.axis_size("dp")
    arrived = [blocks[0]] + [None] * (count - 1)
    for s in range(1, count):
        moved = lax.ppermute(blocks[s], "dp", [(i, (i + count - s) % count) for i in range(count)])
        arrived[count - s] = moved
    return arrived


def rows_in_order(blocks, axis):
    place = lax.axis_index("row")
    size = blocks[0].shape[axis]
    shape = list(blocks[0].shape)
    shape[axis] = size * len(blocks)
    whole = jnp.zeros(shape, blocks[0].dtype)
    for k, block in enumerate(blocks):
        whole = lax.dynamic_update_slice_in_dim(whole, block, (place ^ k) * size, axis)
    return whole


def rows_cut(whole, axis):
    count, place = lax.axis_size("row"), lax.axis_index("row")
    size = whole.shape[axis] // count
    return [
        lax.dynamic_slice_in_dim(whole, (place ^ k) * size, size, axis) for k in range(count)
    ]


def gather_cols(block):
    other = swap(block)
    first = lax.axis_index("col") == 0
    return jnp.concatenate(
        (jnp.where(first, block, other), jnp.where(first, other, block)), axis=0
    )


def scatter_cols(whole, kind):
    half = whole.shape[0] // 2
    place = lax.axis_index("col")
    mine = lax.dynamic_slice_in_dim(whole, place * half, half, 0)
    theirs = lax.dynamic_slice_in_dim(whole, (1 - place) * half, half, 0)
    return mine + swap(theirs.astype(kind)).astype(WIDE)


def shifted(shard, axis, by):
    count = lax.axis_size(axis)
    pairs = [(i, i + by) for i in range(count) if 0 <= i + by < count]
    return lax.ppermute(shard, axis, pairs)


def entering(shard, combine, identity, reverse):
    count, place = lax.axis_size("row"), lax.axis_index("row")
    decay, value = shard
    packed = jnp.stack((decay, value))
    everything = [packed] + [flip(packed, k) for k in range(1, count)]
    table = jnp.stack(everything)
    before = identity
    for k in range(count):
        at = count - 1 - k if reverse else k
        reached = at > place if reverse else at < place
        entry = lax.dynamic_index_in_dim(table, place ^ at, 0, keepdims=False)
        new = combine(before, (entry[0], entry[1]))
        before = tuple(jnp.where(reached, a, b) for a, b in zip(new, before))
    return before


def combine(earlier, later):
    return (earlier[0] * later[0], later[0] * earlier[1] + later[1])


def scan_rows(decay, value, reverse):
    count = decay.shape[0]
    rows = lax.broadcasted_iota(jnp.int32, decay.shape, 0)
    reach = 1
    while reach < count:
        turn = count - reach if reverse else reach
        inside = rows < count - reach if reverse else rows >= reach
        decay_far = jnp.where(inside, pltpu.roll(decay, turn, 0), 1.0)
        value_far = jnp.where(inside, pltpu.roll(value, turn, 0), 0.0)
        value = decay * value_far + value
        decay = decay * decay_far
        reach *= 2
    return decay, value


def minus_expm1(v):
    series = 1.0 + v / 9.0
    for k in range(8, 1, -1):
        series = 1.0 + (v / k) * series
    return jnp.where(v > -0.5, -v * series, 1.0 - jnp.exp(v))


def recurrence_forward(
    taps_count, proj, halo, spots, vectors, input_full, decay_full, conv_out, in_out, dec_out,
    running_out, local_out, padded,
):
    count = proj.shape[0]
    conv_shift, branch_shift, _, input_shift, decay_shift, rate = (
        vectors[taps_count + i : taps_count + i + 1, :] for i in range(6)
    )
    padded[8 - halo.shape[0] : 8, :] = halo[...] + branch_shift
    padded[8 : 8 + count, :] = proj[...] + branch_shift
    spot = spots[...]
    conv = conv_shift + vectors[0:1, :] * padded[8 : 8 + count, :]
    for k in range(1, taps_count):
        earlier = padded[8 - k : 8 - k + count, :]
        conv = conv + vectors[k : k + 1, :] * jnp.where(spot >= k, earlier, 0.0)
    conv_out[...] = conv
    low = conv.astype(LOW)
    input_gate = jax.nn.sigmoid(
        jnp.dot(low, input_full[0], preferred_element_type=WIDE) + input_shift
    )
    decay_gate = jax.nn.sigmoid(
        jnp.dot(low, decay_full[0], preferred_element_type=WIDE) + decay_shift
    )
    in_out[...] = input_gate
    dec_out[...] = decay_gate
    log_decay = rate * decay_gate
    starting = spot == 0
    decay = jnp.where(starting, 0.0, jnp.exp(log_decay))
    multiplier = jnp.where(starting, 1.0, jnp.sqrt(minus_expm1(2.0 * log_decay)))
    running, local = scan_rows(decay, multiplier * input_gate * conv, False)
    running_out[...] = running
    local_out[...] = local


def recurrence_turn(dec_gate, spots, rate, grad_direct, reach_out, local_out, first_out, padded):
    count = dec_gate.shape[0]
    decay = jnp.where(spots[...] == 0, 0.0, jnp.exp(rate[...] * dec_gate[...]))
    padded[0:count, :] = decay
    padded[count : count + 8, :] = jnp.ones((8, decay.shape[1]), WIDE)
    following = padded[1 : count + 1, :]
    reach, local = scan_rows(following, grad_direct[...], True)
    reach_out[...] = reach
    local_out[...] = local
    first_out[0:1, :] = decay[0:1, :] * reach[0:1, :]
    first_out[1:2, :] = decay[0:1, :] * local[0:1, :]


def recurrence_backward(
    taps_count, proj, halo, spots, vectors, input_full, decay_full, conv_in, in_gate, dec_gate,
    running, local, state_in, reach, local_grad, carry, branch_out, head_out, sums_out, in_grad_out,
    dec_grad_out, padded, spread,
):
    count, width = proj.shape
    branch_shift, rate = vectors[taps_count + 1 : taps_count + 2, :], vectors[taps_count + 5 :, :]
    spot = spots[...]
    entering_state = state_in[...]
    grad_state = local_grad[...] + reach[...] * carry[...]
    state = local[...] + running[...] * entering_state
    padded[8:, :] = state
    padded[7:8, :] = entering_state
    grad_decay = grad_state * padded[7 : 7 + count, :]
    input_gate, decay_gate, conv = in_gate[...], dec_gate[...], conv_in[...]
    starting = spot == 0
    log_decay = rate * decay_gate
    decay = jnp.exp(log_decay)
    multiplier = jnp.where(starting, 1.0, jnp.sqrt(minus_expm1(2.0 * log_decay)))
    grad_gated = grad_state * conv
    grad_log = jnp.where(
        starting, 0.0, decay * (grad_decay - grad_gated * input_gate * (decay / multiplier))
    )
    grad_in = grad_gated * multiplier * (input_gate * (1.0 - input_gate))
    grad_gate = grad_log * decay_gate
    grad_dec = grad_gate * rate * (1.0 - decay_gate)
    low = conv.astype(LOW)
    low_in, low_dec = grad_in.astype(LOW), grad_dec.astype(LOW)
    across = (((1,), (1,)), ((), ()))
    along = (((0,), (0,)), ((), ()))
    grad_conv = (
        grad_state * multiplier * input_gate
        + lax.dot_general(low_in, input_full[0], across, preferred_element_type=WIDE)
        + lax.dot_general(low_dec, decay_full[0], across, preferred_element_type=WIDE)
    )
    in_grad_out[0] = lax.dot_general(low, low_in, along, preferred_element_type=WIDE)
    dec_grad_out[0] = lax.dot_general(low, low_dec, along, preferred_element_type=WIDE)
    padded[8 - halo.shape[0] : 8, :] = halo[...] + branch_shift
    padded[8:, :] = proj[...] + branch_shift
    spread[0:8, :] = jnp.zeros((8, width), WIDE)
    spread[8:, :] = vectors[0:1, :] * grad_conv
    sums_out[0:1, :] = jnp.sum(grad_conv * padded[8:, :], axis=0, keepdims=True)
    for k in range(1, taps_count):
        kept = jnp.where(spot >= k, grad_conv, 0.0)
        sums_out[k : k + 1, :] = jnp.sum(
            kept * padded[8 - k : 8 - k + count, :], axis=0, keepdims=True
        )
        spread[8 - k : 8 - k + count, :] += vectors[k : k + 1, :] * kept
    branch = spread[8:, :]
    branch_out[...] = branch
    head = spread[0:8, :]
    head_out[...] = head
    sums_out[taps_count : taps_count + 1, :] = jnp.sum(grad_conv, axis=0, keepdims=True)
    sums_out[taps_count + 1 : taps_count + 2, :] = jnp.sum(
        branch, axis=0, keepdims=True
    ) + jnp.sum(head, axis=0, keepdims=True)
    sums_out[taps_count + 2 : taps_count + 3, :] = jnp.sum(grad_in, axis=0, keepdims=True)
    sums_out[taps_count + 3 : taps_count + 4, :] = jnp.sum(grad_dec, axis=0, keepdims=True)
    sums_out[taps_count + 4 : taps_count + 5, :] = jnp.sum(grad_gate, axis=0, keepdims=True)


def by_head(rows, width):
    return pl.BlockSpec((rows, width), lambda h: (0, h))


def by_block(width):
    return pl.BlockSpec((1, width, width), lambda h: (h, 0, 0))


def whole_column(rows):
    return pl.BlockSpec((rows, 1), lambda h: (0, 0))


def wide_shape(*shape):
    return jax.ShapeDtypeStruct(shape, WIDE)


kernel_params = pltpu.CompilerParams(vmem_limit_bytes=40 * 1024 * 1024)


def times(piece, matrix):
    return jnp.dot(piece, matrix, preferred_element_type=WIDE)


def times_flipped(piece, matrix):
    return lax.dot_general(piece, matrix, (((1,), (1,)), ((), ())), preferred_element_type=WIDE)


def left_product(left, right):
    return lax.dot_general(left, right, (((0,), (0,)), ((), ())), preferred_element_type=WIDE)


def shards(
    inputs,
    positions,
    branch_matrix,
    gelu_matrix,
    output_matrix,
    gate_matrix,
    up_matrix,
    down_matrix,
    input_blocks,
    decay_blocks,
    conv_taps,
    conv_bias,
    branch_bias,
    gelu_bias,
    input_bias,
    decay_bias,
    decay_param,
    output_bias,
    gate_bias,
    up_bias,
    down_bias,
    norm_first,
    norm_second,
    cotangent,
):
    count_dp, count_row = lax.axis_size("dp"), lax.axis_size("row")
    place_dp, place_row = lax.axis_index("dp"), lax.axis_index("row")
    width = branch_matrix.shape[1]
    hidden_part = down_matrix.shape[0]
    block_width = input_blocks.shape[2]
    heads_here = input_blocks.shape[0]
    conv_width = conv_taps.shape[0]

    channel_pack = jnp.concatenate(
        (
            conv_taps,
            jnp.stack((conv_bias, branch_bias, gelu_bias, input_bias, decay_bias, decay_param)),
        ),
        axis=0,
    ).astype(LOW)
    channel_vectors = (
        lax.all_gather(channel_pack, "dp", axis=0)
        .transpose(1, 0, 2)
        .reshape(channel_pack.shape[0], width)
        .astype(WIDE)
    )
    gelu_shift, decay_raw = channel_vectors[conv_width + 2], channel_vectors[-1]
    width_pack = jnp.stack((norm_first, output_bias, down_bias, norm_second)).astype(LOW)
    width_here = (
        lax.all_gather(width_pack, "dp", axis=0)
        .transpose(1, 0, 2)
        .reshape(width_pack.shape[0], width_pack.shape[1] * count_dp)
    )
    width_all = jnp.concatenate(
        [width_here] + [flip(width_here, k) for k in range(1, count_row)], axis=1
    ).astype(WIDE)
    gain_first = width_here[0].astype(WIDE)
    output_shift, down_shift, gain_second = width_all[1], width_all[2], width_all[3]

    resid = inputs.astype(WIDE)
    total_first = lax.psum(jnp.sum(resid * resid, axis=1), "row")
    inverse_first = lax.rsqrt(total_first / D + epsilon)[:, None]
    normed_first = (resid * inverse_first * (1.0 + gain_first)).astype(LOW)
    normed_first_all = gather_cols(normed_first)

    branch_full = in_order(gather_line(branch_matrix.astype(LOW)), 0)
    gelu_full = in_order(gather_line(gelu_matrix.astype(LOW)), 0)
    branch = scatter_rows(rows_cut(times(normed_first_all, branch_full), 0))
    gelu_in = scatter_rows(rows_cut(times(normed_first_all, gelu_full), 0)) + gelu_shift
    side, gelu_pull = jax.vjp(jax.nn.gelu, gelu_in)

    block_pack = jnp.concatenate((input_blocks, decay_blocks), axis=0).astype(LOW)
    block_count, block_part = block_pack.shape[0], block_pack.shape[1]
    share = block_part // count_row
    own_share = lax.dynamic_slice_in_dim(block_pack, place_row * share, share, 1)
    line_shares = jnp.concatenate(
        gather_line(own_share.reshape(block_count * share, block_width)), axis=0
    )
    blocks_full = jnp.zeros((block_count, block_width, block_width), LOW)
    for k, arrived in enumerate(gather_rows(line_shares)):
        for s in range(count_dp):
            piece = arrived[s * block_count * share : (s + 1) * block_count * share]
            blocks_full = lax.dynamic_update_slice_in_dim(
                blocks_full,
                piece.reshape(block_count, share, block_width),
                turned(s) * block_part + (place_row ^ k) * share,
                1,
            )
    input_full, decay_full = blocks_full[:heads_here], blocks_full[heads_here:]

    def hidden_columns(matrix):
        part = in_order(exchange_line(cut(matrix.astype(LOW), 1)), 0)
        return jnp.concatenate(gather_rows(part), axis=0)

    gate_full = hidden_columns(gate_matrix)
    up_full = hidden_columns(up_matrix)
    down_full = jnp.concatenate(gather_rows(down_matrix.astype(LOW)), axis=1)
    output_full = in_order(gather_line(output_matrix.astype(LOW)), 0)

    cot_own = jnp.concatenate(exchange_rows(rows_cut(cotangent, 0)), axis=1)
    cot_line = gather_line(cot_own)

    def both_cores(line):
        stacked = jnp.concatenate(line, axis=0)
        return gather_cols(stacked)

    cot_all = both_cores(cot_line)

    steps_count = branch.shape[0]
    spots = positions[:, None]
    lower = shifted(branch[steps_count - conv_width + 1 :], "row", 1)
    rate = -8.0 * jax.nn.softplus(decay_raw)
    vectors = jnp.concatenate((channel_vectors[:-1], rate[None, :]), axis=0)
    grid = (heads_here,)
    head_rows = by_head(steps_count, block_width)
    vector_rows = by_head(vectors.shape[0], block_width)
    halo_rows = by_head(conv_width - 1, block_width)
    one_row = by_head(1, block_width)
    tokens_shape = wide_shape(steps_count, width)
    conv, input_gate, decay_gate, running, local_state = pl.pallas_call(
        functools.partial(recurrence_forward, conv_width),
        grid=grid,
        in_specs=[
            head_rows, halo_rows, whole_column(steps_count), vector_rows, by_block(block_width),
            by_block(block_width),
        ],
        out_specs=[head_rows] * 5,
        out_shape=[tokens_shape] * 5,
        scratch_shapes=[pltpu.VMEM((8 + steps_count, block_width), WIDE)],
        compiler_params=kernel_params,
        name="recurrence_forward",
    )(branch, lower, spots, vectors, input_full, decay_full)
    ones_row = jnp.ones((width,), WIDE)
    zeros_row = jnp.zeros((width,), WIDE)
    carried = entering((running[-1], local_state[-1]), combine, (ones_row, zeros_row), False)
    state_in = carried[1][None, :]
    state = local_state + running * state_in
    mixed = (state * side).astype(LOW)
    mixed_all = rows_in_order(gather_rows(mixed), 0)

    delta = scatter_cols(times(mixed_all, output_full), WIDE)
    middle = jnp.concatenate(exchange_rows(rows_cut(resid + delta, 0)), axis=1) + output_shift
    inverse_second = lax.rsqrt(jnp.mean(middle * middle, axis=1, keepdims=True) + epsilon)
    normed_second = (middle * inverse_second * (1.0 + gain_second)).astype(LOW)
    normed_second_all = both_cores(gather_line(normed_second))

    def feed(gate_value, up_value):
        return jax.nn.gelu(gate_value) * up_value

    hidden_value, feed_pull = jax.vjp(
        feed,
        times(normed_second_all, gate_full) + gate_bias.astype(LOW).astype(WIDE),
        times(normed_second_all, up_full) + up_bias.astype(LOW).astype(WIDE),
    )
    hidden = hidden_value.astype(LOW)
    grad_hidden = times_flipped(cot_all, down_full)
    grad_gate, grad_up = feed_pull(grad_hidden)
    grad_gate_low, grad_up_low = grad_gate.astype(LOW), grad_up.astype(LOW)

    def to_owner(partial):
        own = scatter_cols(partial, LOW)
        size = own.shape[0] // count_dp
        return scatter_line([own[s * size : (s + 1) * size] for s in range(count_dp)])

    grad_normed_second = to_owner(
        times_flipped(grad_gate_low, gate_full) + times_flipped(grad_up_low, up_full)
    )
    forward_sum = to_owner(times(hidden, down_full))
    layer_low = (middle + forward_sum + down_shift).astype(LOW)
    size = layer_low.shape[1] // count_row
    layer_out = rows_in_order(
        exchange_rows([layer_low[:, k * size : (k + 1) * size] for k in range(count_row)]), 0
    )

    def row_blocks(partial):
        size = partial.shape[0] // count_row
        return [partial[k * size : (k + 1) * size] for k in range(count_row)]

    down_partial = left_product(hidden, cot_all)
    down_grad = scatter_rows(
        [down_partial[:, k * size : (k + 1) * size] for k in range(count_row)]
    )

    def to_columns(partial):
        own = scatter_rows(row_blocks(partial)).astype(LOW)
        return in_order(exchange_line(cut(own, 0)), 1).astype(WIDE)

    gate_grad = to_columns(left_product(normed_second_all, grad_gate_low))
    up_grad = to_columns(left_product(normed_second_all, grad_up_low))
    hidden_sums = lax.psum(jnp.stack((jnp.sum(grad_gate, axis=0), jnp.sum(grad_up, axis=0))), "row")

    scaled = grad_normed_second * (1.0 + gain_second)
    inner = jnp.sum(scaled * middle, axis=1, keepdims=True)
    back_second = inverse_second * scaled - middle * inverse_second**3 * inner / D
    norm_second_sum = jnp.sum(grad_normed_second * middle * inverse_second, axis=0)
    grad_middle = cot_own.astype(WIDE) + back_second
    output_bias_sum = jnp.sum(grad_middle, axis=0)
    grad_middle_here = rows_in_order(
        exchange_rows([grad_middle[:, k * size : (k + 1) * size] for k in range(count_row)]), 0
    )
    grad_middle_all = gather_cols(grad_middle_here.astype(LOW))
    output_grad = scatter_line(cut(left_product(mixed_all, grad_middle_all), 0))
    grad_mixed = scatter_rows(rows_cut(times_flipped(grad_middle_all, output_full), 0))

    grad_direct = grad_mixed * side
    grad_side = grad_mixed * state
    reach, local_grad, first_row = pl.pallas_call(
        recurrence_turn,
        grid=grid,
        in_specs=[head_rows, whole_column(steps_count), one_row, head_rows],
        out_specs=[head_rows, head_rows, by_head(2, block_width)],
        out_shape=[tokens_shape, tokens_shape, wide_shape(2, width)],
        scratch_shapes=[pltpu.VMEM((steps_count + 8, block_width), WIDE)],
        compiler_params=kernel_params,
        name="recurrence_turn",
    )(decay_gate, spots, rate[None, :], grad_direct)
    later_carry = entering((first_row[0], first_row[1]), combine, (ones_row, zeros_row), True)
    grad_branch, head_rows_out, channel_part, input_blocks_grad, decay_blocks_grad = pl.pallas_call(
        functools.partial(recurrence_backward, conv_width),
        grid=grid,
        in_specs=[
            head_rows, halo_rows, whole_column(steps_count), vector_rows, by_block(block_width),
            by_block(block_width), head_rows, head_rows, head_rows, head_rows, head_rows, one_row,
            head_rows, head_rows, one_row,
        ],
        out_specs=[
            head_rows, by_head(8, block_width), by_head(conv_width + 5, block_width),
            by_block(block_width), by_block(block_width),
        ],
        out_shape=[
            tokens_shape, wide_shape(8, width), wide_shape(conv_width + 5, width),
            wide_shape(heads_here, block_width, block_width),
            wide_shape(heads_here, block_width, block_width),
        ],
        scratch_shapes=[pltpu.VMEM((8 + steps_count, block_width), WIDE)] * 2,
        compiler_params=kernel_params,
        name="recurrence_backward",
    )(
        branch, lower, spots, vectors, input_full, decay_full, conv, input_gate, decay_gate,
        running, local_state, state_in, reach, local_grad, later_carry[1][None, :],
    )
    upper = shifted(head_rows_out[8 - conv_width + 1 :], "row", -1)
    grad_branch = grad_branch + jnp.concatenate(
        (jnp.zeros((steps_count - conv_width + 1, width), WIDE), upper), axis=0
    )
    grad_gelu_in = lax.optimization_barrier(gelu_pull(grad_side)[0])
    gelu_bias_grad = jnp.sum(grad_gelu_in, axis=0)

    grad_gelu_all = rows_in_order(gather_rows(grad_gelu_in.astype(LOW)), 0)
    gelu_grad = scatter_line(cut(left_product(normed_first_all, grad_gelu_all), 0))
    grad_branch_all = rows_in_order(gather_rows(grad_branch.astype(LOW)), 0)
    branch_grad = scatter_line(cut(left_product(normed_first_all, grad_branch_all), 0))

    block_sums = jnp.concatenate((input_blocks_grad, decay_blocks_grad), axis=0)

    def share_sums(s, k):
        at = turned(s) * block_part + (place_row ^ k) * share
        piece = lax.dynamic_slice_in_dim(block_sums, at, share, 1)
        return piece.reshape(block_count * share, block_width)

    share_total = scatter_rows(
        [
            jnp.concatenate([share_sums(s, k) for s in range(count_dp)], axis=0)
            for k in range(count_row)
        ]
    )
    length = block_count * share
    share_total = scatter_line(
        [share_total[s * length : (s + 1) * length] for s in range(count_dp)]
    )
    block_grads = rows_in_order(
        [
            piece.reshape(block_count, share, block_width)
            for piece in gather_rows(share_total.astype(LOW))
        ],
        1,
    ).astype(WIDE)

    grad_normed_first = scatter_cols(
        times_flipped(grad_branch_all, branch_full) + times_flipped(grad_gelu_all, gelu_full), WIDE
    )
    scaled = grad_normed_first * (1.0 + gain_first)
    inner = lax.psum(jnp.sum(scaled * resid, axis=1), "row")[:, None]
    back_first = inverse_first * scaled - resid * inverse_first**3 * inner / D
    norm_first_sum = jnp.sum(grad_normed_first * resid * inverse_first, axis=0)
    input_grad = grad_middle_here + back_first

    conv_bias_grad, branch_bias_grad, input_bias_grad, decay_bias_grad, rate_grad = channel_part[
        conv_width:
    ]
    decay_param_grad = -8.0 * rate_grad * jax.nn.sigmoid(decay_raw)
    channel_sums = lax.psum(
        jnp.concatenate(
            (
                channel_part[:conv_width],
                jnp.stack(
                    (
                        conv_bias_grad,
                        branch_bias_grad,
                        gelu_bias_grad,
                        input_bias_grad,
                        decay_bias_grad,
                        decay_param_grad,
                    )
                ),
            ),
            axis=0,
        ),
        ("row", "dp"),
    )
    channel_size = width // count_dp
    channel_sums = lax.dynamic_slice_in_dim(channel_sums, place_dp * channel_size, channel_size, 1)
    wide_sums = jnp.stack((output_bias_sum, norm_second_sum))
    wide_parts = exchange_rows([wide_sums[:, k * size : (k + 1) * size] for k in range(count_row)])
    width_sums = lax.psum(
        jnp.concatenate(
            (
                sum(wide_parts),
                jnp.stack((jnp.sum(cotangent.astype(WIDE), axis=0), norm_first_sum)),
            ),
            axis=0,
        ),
        ("dp", "col"),
    )
    width_size = width_sums.shape[1] // count_dp
    width_sums = lax.dynamic_slice_in_dim(width_sums, place_dp * width_size, width_size, 1)

    return (
        layer_out,
        input_grad,
        branch_grad,
        gelu_grad,
        output_grad,
        gate_grad,
        up_grad,
        down_grad,
        block_grads[:heads_here],
        block_grads[heads_here:],
        channel_sums[:conv_width],
        channel_sums[conv_width],
        channel_sums[conv_width + 1],
        channel_sums[conv_width + 2],
        channel_sums[conv_width + 3],
        channel_sums[conv_width + 4],
        channel_sums[conv_width + 5],
        width_sums[0],
        hidden_sums[0],
        hidden_sums[1],
        width_sums[2],
        width_sums[3],
        width_sums[1],
    )


def solution(mesh):
    in_specs = (
        P(("dp", "col"), "row"),
        P(("dp", "row")),
        P(("row", "dp"), "col"),
        P(("row", "dp"), "col"),
        P(("col", "dp"), "row"),
        P(("row", "dp"), "col"),
        P(("row", "dp"), "col"),
        P(("col", "dp"), "row"),
        P("col", "dp", None),
        P("col", "dp", None),
        P(None, ("col", "dp")),
        P(("col", "dp")),
        P(("col", "dp")),
        P(("col", "dp")),
        P(("col", "dp")),
        P(("col", "dp")),
        P(("col", "dp")),
        P(("row", "dp")),
        P(("col", "dp")),
        P(("col", "dp")),
        P(("row", "dp")),
        P(("row", "dp")),
        P(("row", "dp")),
        P(("dp", "col"), "row"),
    )
    out_specs = (
        P(("dp", "col"), "row"),
        P(("dp", "col"), "row"),
        P(("row", "dp"), "col"),
        P(("row", "dp"), "col"),
        P(("col", "dp"), "row"),
        P(("row", "dp"), "col"),
        P(("row", "dp"), "col"),
        P(("col", "dp"), "row"),
        P("col", "dp", None),
        P("col", "dp", None),
        P(None, ("col", "dp")),
        P(("col", "dp")),
        P(("col", "dp")),
        P(("col", "dp")),
        P(("col", "dp")),
        P(("col", "dp")),
        P(("col", "dp")),
        P(("row", "dp")),
        P(("col", "dp")),
        P(("col", "dp")),
        P(("row", "dp")),
        P(("row", "dp")),
        P(("row", "dp")),
    )
    return jax.shard_map(shards, mesh=mesh, in_specs=in_specs, out_specs=out_specs, check_vma=False)
```

```python
import functools

import jax
import jax.numpy as jnp
from jax import lax
from jax.experimental import pallas as pl
from jax.experimental.pallas import tpu as pltpu
from jax.sharding import PartitionSpec as P

epsilon = 1e-06
LOW = jnp.bfloat16
WIDE = jnp.float32
MESH = pl.DeviceIdType.MESH
VMEM = pl.BlockSpec(memory_space=pltpu.VMEM)
ANY = pl.BlockSpec(memory_space=pl.ANY)


class Links:
    def __init__(self, send, recv, local):
        self.send, self.recv, self.local = send, recv, local
        self.sent = self.kept = 0

    def copy(self, src, dst, **where):
        k, self.sent = self.sent, self.sent + 1
        return pltpu.make_async_remote_copy(
            src_ref=src,
            dst_ref=dst,
            send_sem=self.send.at[k],
            recv_sem=self.recv.at[k],
            device_id=where,
            device_id_type=MESH,
        )

    def keep(self, src, dst):
        k, self.kept = self.kept, self.kept + 1
        copy = pltpu.make_async_copy(src, dst, self.local.at[k])
        copy.start()
        return copy


class Place:
    def __init__(self, count_dp):
        self.row, self.dp, self.col = (lax.axis_index(name) for name in ("row", "dp", "col"))
        self.count = count_dp
        first, second = lax.rem(self.row, 2), lax.div(self.row, 2)
        self.near = [self.row, self.row + 1 - 2 * first, self.row + 2 - 4 * second, 3 - self.row]
        self.other = 1 - self.col

    def turn(self, index):
        return lax.rem(index + self.count, self.count)


def greet(place, rows=False, line=False, cores=False):
    barrier = pltpu.get_barrier_semaphore()
    partners = []
    if rows:
        partners += [{"row": place.near[k]} for k in range(1, 4)]
    if line:
        partners += [{"dp": place.turn(place.dp + k)} for k in range(1, place.count)]
    if cores:
        partners += [{"col": place.other}]
    for where in partners:
        pl.semaphore_signal(barrier, inc=1, device_id=where, device_id_type=MESH)
    pl.semaphore_wait(barrier, len(partners))


def run(tasks):
    live = list(tasks)
    while live:
        live = [task for task in live if next(task, None) is not None]


def chain(*tasks):
    for task in tasks:
        yield from task


def when(condition, action):
    pl.when(condition)(lambda: action() and None)


def halves(size):
    first = -(-size // 32) * 16
    return (pl.ds(0, first), pl.ds(first, size - first))


def by_rows(count, body):
    step = 16 if count % 16 == 0 else count

    def lap(i, carry):
        body(pl.ds(pl.multiple_of(i * step, step), step))
        return carry

    lax.fori_loop(0, count // step, lap, 0)


def by_pieces(pieces, height, body):
    def lap(i, carry):
        by_rows(height, lambda rows: body(i, rows))
        return carry

    if pieces == 1:
        by_rows(height, lambda rows: body(0, rows))
    else:
        lax.fori_loop(0, pieces, lap, 0)


def gather_rows(links, place, own, piece):
    row, near, side, _ = place.near
    out = [
        links.copy(own(0), piece(row, 0), row=near),
        links.copy(own(1), piece(row, 1), row=side),
        links.copy(own(1), piece(row, 1), row=near),
        links.copy(own(0), piece(row, 0), row=side),
    ]
    for copy in out:
        copy.start()
    yield 1
    out[0].wait_recv()
    out.append(links.copy(piece(near, 0), piece(near, 0), row=side))
    out[4].start()
    out[1].wait_recv()
    out.append(links.copy(piece(side, 1), piece(side, 1), row=near))
    out[5].start()
    yield 1
    for copy in out[2:]:
        copy.wait_recv()
    for copy in out:
        copy.wait_send()


def exchange_rows(links, place, source, target):
    out = [
        links.copy(source(place.near[k]), target(place.row), row=place.near[k])
        for k in range(1, 4)
    ]
    for copy in out:
        copy.start()
    yield 1
    for copy in out:
        copy.wait_recv()
    for copy in out:
        copy.wait_send()


def exchange_line(links, place, source, target):
    out = []
    for k in range(1, place.count):
        far = place.turn(place.dp + k)
        out.append(links.copy(source(far), target(place.dp), dp=far))
    for copy in out:
        copy.start()
    yield 1
    for copy in out:
        copy.wait_recv()
    for copy in out:
        copy.wait_send()


def gather_line(links, place, own, piece, share=False):
    z, count, turn = place.dp, place.count, place.turn
    ups, downs, shared = [], [], []

    def pass_on(block, valid):
        copy = links.copy(piece(block), piece(block), col=place.other)
        when(valid, copy.start)
        shared.append((copy, valid))

    if share:
        copy = links.copy(own, piece(z), col=place.other)
        copy.start()
        shared.append((copy, z >= 0))
    for step in range(1, count + 1):
        if step > 1:
            yield 1
            below, above = z >= step - 1, z <= count - step
            when(below, ups[-1].wait_recv)
            when(above, downs[-1].wait_recv)
        if step < count:
            low, high = turn(z - step + 1), turn(z + step - 1)
            ups.append(
                links.copy(own if step == 1 else piece(low), piece(low), dp=turn(z + 1))
            )
            downs.append(
                links.copy(own if step == 1 else piece(high), piece(high), dp=turn(z - 1))
            )
            when((z >= step - 1) & (z < count - 1), ups[-1].start)
            when((z <= count - step) & (z > 0), downs[-1].start)
        if step > 1 and share:
            pass_on(turn(z - step + 1), below)
            pass_on(turn(z + step - 1), above)
    yield 1
    for copy, valid in shared:
        when(valid, copy.wait_recv)
    for step in range(1, count):
        when((z >= step - 1) & (z < count - 1), ups[step - 1].wait_send)
        when((z <= count - step) & (z > 0), downs[step - 1].wait_send)
    for copy, valid in shared:
        when(valid, copy.wait_send)


def scatter_rows(links, place, part, buffers, result):
    row, near, side, far = place.near
    heights = [part(row, h).shape[0] for h in range(2)]

    def buffer(i, h):
        return buffers.at[i, pl.ds(0, heights[h])]

    out = [
        links.copy(part(far, 0), buffer(5, 0), row=side),
        links.copy(part(far, 1), buffer(7, 1), row=near),
        links.copy(part(side, 0), buffer(4, 0), row=side),
        links.copy(part(near, 1), buffer(6, 1), row=near),
    ]
    for copy in out:
        copy.start()
    loads = [
        links.keep(part(near, 0), buffer(0, 0)),
        links.keep(part(side, 1), buffer(1, 1)),
        links.keep(part(row, 0), buffer(2, 0)),
        links.keep(part(row, 1), buffer(3, 1)),
    ]
    yield 1
    for h, target in ((0, near), (1, side)):
        loads[h].wait()
        out[h].wait_recv()

        def add(rows, h=h):
            total = buffers[h, rows].astype(WIDE) + buffers[5 + 2 * h, rows].astype(WIDE)
            buffers[h, rows] = total.astype(LOW)

        by_rows(heights[h], add)
        out.append(links.copy(buffer(h, h), buffer(8 + h, h), row=target))
        out[-1].start()
        yield 1
    for h in range(2):
        loads[2 + h].wait()
        out[2 + h].wait_recv()
        out[4 + h].wait_recv()

        def finish(rows, h=h):
            result(
                h,
                rows,
                buffers[2 + h, rows].astype(WIDE)
                + buffers[4 + 2 * h, rows].astype(WIDE)
                + buffers[8 + h, rows].astype(WIDE),
            )

        by_rows(heights[h], finish)
    for copy in out:
        copy.wait_send()


def row_buffers(size, width):
    return pltpu.VMEM((10, halves(size)[0].size, width), LOW)


def scatter_line(links, place, ready, term, ups_in, downs_in, staging, result):
    z, count, turn = place.dp, place.count, place.turn
    pieces, height = ups_in.shape[1:3]
    ups, downs = [None], [None]

    def sends_up(t):
        return (z <= t - 1) & (z < count - 1)

    def sends_down(t):
        return (z >= count - t) & (z > 0)

    def fill(slot, block, arrived):
        def body(i, rows):
            value = term(block, i, rows)
            if arrived is not None:
                value = value + arrived[i, rows].astype(WIDE)
            staging[slot, i, rows] = value.astype(LOW)

        by_pieces(pieces, height, body)

    for t in range(1, count):
        ready(t)
        ready(count - t)
        for which in range(2):
            copies, into = ((ups, ups_in), (downs, downs_in))[which]
            sends = (sends_up, sends_down)[which]
            first = (z == 0, z == count - 1)[which]
            block = (turn(z - t), turn(z + t))[which]
            target = (turn(z + 1), turn(z - 1))[which]
            slot = 2 * which + t % 2
            if t > 2:
                when(sends(t - 2), copies[t - 2].wait_send)
            copy = links.copy(staging.at[slot], into.at[t - 1], dp=target)
            copies.append(copy)

            def begin(copy=copy, slot=slot, block=block):
                fill(slot, block, None)
                copy.start()

            when(sends(t) & first, begin)
            if t > 1:

                def go_on(copy=copy, slot=slot, block=block, before=copies[t - 1], into=into, t=t):
                    before.wait_recv()
                    fill(slot, block, into.at[t - 2])
                    copy.start()

                when(sends(t) & jnp.logical_not(first), go_on)
        yield 1
    ready(0)
    last = count - 1
    from_below, from_above = ups_in.at[last - 1], downs_in.at[last - 1]
    when(z > 0, ups[last].wait_recv)
    when(z < last, downs[last].wait_recv)

    def finish(below, above):
        def body(i, rows):
            value = term(z, i, rows)
            if below:
                value = value + from_below[i, rows].astype(WIDE)
            if above:
                value = value + from_above[i, rows].astype(WIDE)
            result(i, rows, value)

        by_pieces(pieces, height, body)

    when(z == 0, lambda: finish(False, True))
    when((z > 0) & (z < last), lambda: finish(True, True))
    when(z == last, lambda: finish(True, False))
    for t in range(max(1, count - 2), count):
        when(sends_up(t), ups[t].wait_send)
        when(sends_down(t), downs[t].wait_send)


def line_buffers(count, pieces, height, width):
    return [pltpu.VMEM((slots, pieces, height, width), LOW) for slots in (count - 1, count - 1, 4)]


def token_scatter(links, place, partial, ours, theirs, buffers, result):
    out, loads = [], []
    for s in list(range(1, place.count)) + [0]:
        block = place.turn(place.dp - s)
        out.append(
            links.copy(partial.at[place.other, block], theirs.at[block], col=place.other)
        )
        out[-1].start()
        loads.append(links.keep(partial.at[place.col, block], ours.at[block]))
    waited = set()

    def ready(s):
        if s not in waited:
            waited.add(s)
            at = s - 1 if s else place.count - 1
            out[at].wait_recv()
            loads[at].wait()

    def term(block, i, rows):
        return ours[block, rows].astype(WIDE) + theirs[block, rows].astype(WIDE)

    yield 1
    yield from scatter_line(
        links, place, ready, term, *buffers, lambda i, rows, value: result(rows, value)
    )
    for copy in out:
        copy.wait_send()


def call(kernel, name, number, ins, outs, scratch, remote, local):
    return pl.pallas_call(
        kernel,
        in_specs=[VMEM if inside else ANY for _, inside in ins],
        out_specs=[VMEM if inside else ANY for _, _, inside in outs],
        out_shape=[jax.ShapeDtypeStruct(shape, kind) for shape, kind, _ in outs],
        scratch_shapes=list(scratch)
        + [
            pltpu.SemaphoreType.DMA((remote,)),
            pltpu.SemaphoreType.DMA((remote,)),
            pltpu.SemaphoreType.DMA((local,)),
        ],
        compiler_params=pltpu.CompilerParams(
            collective_id=number, has_side_effects=True, vmem_limit_bytes=58 * 1024 * 1024
        ),
        name=name,
    )(*[array for array, _ in ins])


def lanes(index, width):
    return pl.ds(pl.multiple_of(index * width, 128), width)


def strip(index, height, step=16):
    return pl.ds(pl.multiple_of(index * height, step), height)


def gather_inputs(
    count, x, cot, wxy, wout, wgate, wup, wdown, blk, cvec, wvec, x_all, cot_all, wxy_all, wout_all,
    gate_all, up_all, down_all, blk_all, cvec_all, wvec_all, send, recv, local,
):
    place = Place(count)
    links = Links(send, recv, local)
    row, z, col = place.row, place.dp, place.col
    greet(place, rows=True, line=True, cores=True)
    tall, wide = x.shape
    half, quarter = tall // 2, tall // 4
    down_halves = halves(wdown.shape[0])
    kept = []

    def keep(src, dst):
        kept.append(links.keep(src, dst))
        return kept[-1]

    def projections():
        mine = links.keep(wxy.at[row], wxy_all.at[row, z])
        yield from exchange_rows(
            links, place, lambda q: wxy.at[q], lambda q: wxy_all.at[q, z]
        )
        mine.wait()
        yield from gather_line(links, place, wxy_all.at[:, z], lambda b: wxy_all.at[:, b])

    def inputs():
        def at(q, core):
            return x_all.at[strip(core, tall), lanes(q, wide)]

        keep(x, at(row, col))
        shared = [links.copy(x, at(row, col), col=place.other)]
        shared[0].start()
        yield from gather_rows(
            links,
            place,
            lambda h: x.at[pl.ds(half * h, half)],
            lambda q, h: x_all.at[strip(2 * col + h, half), lanes(q, wide)],
        )
        for k in range(1, 4):
            q = place.near[k]
            shared.append(links.copy(at(q, col), at(q, col), col=place.other))
            shared[-1].start()
        yield 1
        for copy in shared:
            copy.wait_recv()
        for copy in shared:
            copy.wait_send()

    def channel_vectors():
        keep(cvec, cvec_all.at[z])
        yield from exchange_line(links, place, lambda b: cvec, lambda b: cvec_all.at[b])

    def width_vectors():
        mine = links.keep(wvec, wvec_all.at[row, z])
        yield from exchange_line(links, place, lambda b: wvec, lambda b: wvec_all.at[row, b])
        mine.wait()
        yield from exchange_rows(
            links, place, lambda q: wvec_all.at[row], lambda q: wvec_all.at[q]
        )

    def gate_blocks():
        mine = links.keep(blk, blk_all.at[z, row])
        yield from exchange_line(links, place, lambda b: blk, lambda b: blk_all.at[b, row])
        mine.wait()
        middle = count // 2
        yield from gather_rows(
            links,
            place,
            lambda h: blk_all.at[pl.ds(middle * h, middle), row],
            lambda q, h: blk_all.at[pl.ds(middle * h, middle), q],
        )

    def hidden_columns(matrix, whole):
        mine = links.keep(matrix.at[z], whole.at[row, z])
        yield from exchange_line(
            links, place, lambda b: matrix.at[b], lambda b: whole.at[row, b]
        )
        mine.wait()
        middle = count // 2
        yield from gather_rows(
            links,
            place,
            lambda h: whole.at[row, pl.ds(middle * h, middle)],
            lambda q, h: whole.at[q, pl.ds(middle * h, middle)],
        )

    def hidden_rows():
        keep(wdown, down_all.at[:, lanes(row, wide)])
        yield from gather_rows(
            links,
            place,
            lambda h: wdown.at[down_halves[h]],
            lambda q, h: down_all.at[down_halves[h], lanes(q, wide)],
        )

    def cotangents():
        def block(b):
            return cot_all.at[strip(col * count + b, quarter)]

        def spot(q):
            return cot_all.at[strip(col * count + z, quarter), lanes(q, wide)]

        mine = links.keep(cot.at[strip(row, quarter)], spot(row))
        yield from exchange_rows(links, place, lambda q: cot.at[strip(q, quarter)], spot)
        mine.wait()
        yield from gather_line(links, place, block(z), block, share=True)

    def output_rows():
        keep(wout, wout_all.at[z])
        yield from gather_line(links, place, wout, lambda b: wout_all.at[b])

    run(
        [
            projections(),
            inputs(),
            channel_vectors(),
            width_vectors(),
            gate_blocks(),
            hidden_columns(wgate, gate_all),
            hidden_columns(wup, up_all),
            cotangents(),
            hidden_rows(),
            output_rows(),
        ]
    )
    for copy in kept:
        copy.wait()


def spread_projected(count, proj, out, send, recv, local):
    place = Place(count)
    links = Links(send, recv, local)
    greet(place, rows=True)
    tall = out.shape[1]
    tokens = tall - 8

    def source(q):
        return proj.at[pl.ds(pl.multiple_of(q * tokens, 8), tall)]

    mine = links.keep(source(place.row), out.at[place.row])
    run([exchange_rows(links, place, source, lambda q: out.at[q])])
    mine.wait()


def combine(earlier, later):
    return (earlier[0] * later[0], later[0] * earlier[1] + later[1])


def scan_rows(decay, value, reverse):
    count = decay.shape[0]
    rows = lax.broadcasted_iota(jnp.int32, decay.shape, 0)
    reach = 1
    while reach < count:
        turn = count - reach if reverse else reach
        inside = rows < count - reach if reverse else rows >= reach
        decay_far = jnp.where(inside, pltpu.roll(decay, turn, 0), 1.0)
        value_far = jnp.where(inside, pltpu.roll(value, turn, 0), 0.0)
        value = decay * value_far + value
        decay = decay * decay_far
        reach *= 2
    return decay, value


def minus_expm1(v):
    series = 1.0 + v / 9.0
    for k in range(8, 1, -1):
        series = 1.0 + (v / k) * series
    return jnp.where(v > -0.5, -v * series, 1.0 - jnp.exp(v))


def each_head(heads, width, body):
    def lap(h, carry):
        body(h, pl.ds(pl.multiple_of(h * width, 128), width))
        return carry

    lax.fori_loop(0, heads, lap, 0)


def carry_over(links, place, ends, table, reverse):
    run([exchange_rows(links, place, lambda q: ends, lambda q: table.at[q])])
    row = place.row
    state = jnp.zeros((1, ends.shape[1]), WIDE)
    for k in range(4):
        q = 3 - k if reverse else k

        def entry(i):
            return table[q, i : i + 1, :]

        reached = q > row if reverse else q < row
        state = jnp.where(reached, entry(0) * state + entry(1), state)
    return state


def recurrence_forward(
    count, taps, proj, side, spots, vectors, blocks, conv_out, in_out, dec_out, state_out,
    entering_out, mixed_all, running, local_state, ends, table, mixed, send, recv, local,
):
    place = Place(count)
    links = Links(send, recv, local)
    greet(place, rows=True)
    tokens, width = side.shape
    heads, block = blocks.shape[0] // 2, blocks.shape[1]
    spot = spots[...]
    ends[...] = jnp.zeros(ends.shape, WIDE)
    entering_out[...] = jnp.zeros(ends.shape, WIDE)

    def one_head(h, at):
        def vector(i):
            return vectors[i : i + 1, at]

        conv = vector(taps) + vector(0) * (proj[8:, at] + vector(taps + 1))
        for k in range(1, taps):
            earlier = proj[8 - k : 8 - k + tokens, at] + vector(taps + 1)
            conv = conv + vector(k) * jnp.where(spot >= k, earlier, 0.0)
        conv_out[:, at] = conv
        low = conv.astype(LOW)
        input_gate = jax.nn.sigmoid(
            jnp.dot(low, blocks[h], preferred_element_type=WIDE) + vector(taps + 3)
        )
        decay_gate = jax.nn.sigmoid(
            jnp.dot(low, blocks[heads + h], preferred_element_type=WIDE) + vector(taps + 4)
        )
        in_out[:, at] = input_gate
        dec_out[:, at] = decay_gate
        log_decay = vector(taps + 5) * decay_gate
        starting = spot == 0
        decay = jnp.where(starting, 0.0, jnp.exp(log_decay))
        multiplier = jnp.where(starting, 1.0, jnp.sqrt(minus_expm1(2.0 * log_decay)))
        reach, state = scan_rows(decay, multiplier * input_gate * conv, False)
        running[:, at] = reach
        local_state[:, at] = state
        ends[0:1, at] = reach[tokens - 1 :, :]
        ends[1:2, at] = state[tokens - 1 :, :]

    each_head(heads, block, one_head)
    own = links.keep(ends, table.at[place.row])
    own.wait()
    entering_out[0:1, :] = carry_over(links, place, ends, table, False)

    def finish(h, at):
        state = local_state[:, at] + running[:, at] * entering_out[0:1, at]
        state_out[:, at] = state
        mixed[:, at] = (state * side[:, at]).astype(LOW)

    each_head(heads, block, finish)
    half = tokens // 2
    mine = links.keep(mixed, mixed_all.at[strip(place.row, tokens)])
    run(
        [
            gather_rows(
                links,
                place,
                lambda h: mixed.at[pl.ds(half * h, half)],
                lambda q, h: mixed_all.at[strip(2 * q + h, half)],
            )
        ]
    )
    mine.wait()


def recurrence_backward(
    count, taps, proj, side, spots, vectors, blocks, conv_in, in_gate, dec_gate, state_in, entering,
    grad_mixed, branch_out, sums_out, blocks_out, reach, local_grad, branch, ends, table, heads_in,
    heads_here, padded, spread, send, recv, local,
):
    place = Place(count)
    links = Links(send, recv, local)
    greet(place, rows=True)
    tokens, width = side.shape
    heads, block = blocks.shape[0] // 2, blocks.shape[1]
    spot = spots[...]
    starting = spot == 0
    ends[...] = jnp.zeros(ends.shape, WIDE)

    def backwards(h, at):
        rate = vectors[taps + 5 : taps + 6, at]
        decay = jnp.where(starting, 0.0, jnp.exp(rate * dec_gate[:, at]))
        padded[0:tokens, :] = decay
        padded[tokens:, :] = jnp.ones((8, block), WIDE)
        far, grad = scan_rows(padded[1 : tokens + 1, :], grad_mixed[:, at] * side[:, at], True)
        reach[:, at] = far
        local_grad[:, at] = grad
        ends[0:1, at] = decay[0:1, :] * far[0:1, :]
        ends[1:2, at] = decay[0:1, :] * grad[0:1, :]

    each_head(heads, block, backwards)
    own = links.keep(ends, table.at[place.row])
    own.wait()
    heads_here[0:1, :] = carry_over(links, place, ends, table, True)

    def one_head(h, at):
        def vector(i):
            return vectors[i : i + 1, at]

        grad_state = local_grad[:, at] + reach[:, at] * heads_here[0:1, at]
        padded[8:, :] = state_in[:, at]
        padded[7:8, :] = entering[0:1, at]
        grad_decay = grad_state * padded[7 : 7 + tokens, :]
        input_gate, decay_gate, conv = in_gate[:, at], dec_gate[:, at], conv_in[:, at]
        rate = vector(taps + 5)
        log_decay = rate * decay_gate
        decay = jnp.exp(log_decay)
        multiplier = jnp.where(starting, 1.0, jnp.sqrt(minus_expm1(2.0 * log_decay)))
        grad_gated = grad_state * conv
        grad_log = jnp.where(
            starting, 0.0, decay * (grad_decay - grad_gated * input_gate * (decay / multiplier))
        )
        grad_in = grad_gated * multiplier * (input_gate * (1.0 - input_gate))
        grad_gate = grad_log * decay_gate
        grad_dec = grad_gate * rate * (1.0 - decay_gate)
        low = conv.astype(LOW)
        low_in, low_dec = grad_in.astype(LOW), grad_dec.astype(LOW)
        across = (((1,), (1,)), ((), ()))
        along = (((0,), (0,)), ((), ()))
        grad_conv = (
            grad_state * multiplier * input_gate
            + lax.dot_general(low_in, blocks[h], across, preferred_element_type=WIDE)
            + lax.dot_general(low_dec, blocks[heads + h], across, preferred_element_type=WIDE)
        )
        blocks_out[h] = lax.dot_general(low, low_in, along, preferred_element_type=WIDE)
        blocks_out[heads + h] = lax.dot_general(low, low_dec, along, preferred_element_type=WIDE)
        spread[0:8, :] = jnp.zeros((8, block), WIDE)
        spread[8:, :] = vector(0) * grad_conv
        shift = vector(taps + 1)

        def total(values):
            return jnp.sum(values, axis=0, keepdims=True)

        sums_out[0:1, at] = total(grad_conv * (proj[8:, at] + shift))
        for k in range(1, taps):
            kept = jnp.where(spot >= k, grad_conv, 0.0)
            sums_out[k : k + 1, at] = total(kept * (proj[8 - k : 8 - k + tokens, at] + shift))
            spread[8 - k : 8 - k + tokens, :] += vector(k) * kept
        branch[:, at] = spread[8:, :]
        heads_in[0, :, at] = spread[0:8, :]
        sums_out[taps : taps + 1, at] = total(grad_conv)
        sums_out[taps + 1 : taps + 2, at] = total(spread[...])
        sums_out[taps + 2 : taps + 3, at] = total(grad_in)
        sums_out[taps + 3 : taps + 4, at] = total(grad_dec)
        sums_out[taps + 4 : taps + 5, at] = total(grad_gate)
        sums_out[taps + 5 :, at] = jnp.zeros((sums_out.shape[0] - taps - 5, block), WIDE)

    each_head(heads, block, one_head)
    row = place.row
    before = lax.rem(row + 3, 4)
    owed = links.copy(heads_in.at[0], heads_in.at[1], row=before)
    owed.start()
    owed.wait_recv()
    owed.wait_send()

    def finish(h, at):
        last = jnp.where(row < 3, heads_in[1, :, at], 0.0)
        branch[tokens - 8 :, at] += last
        branch_out[:, at] = branch[:, at].astype(LOW)

    each_head(heads, block, finish)


def output_and_norm(
    count, partial, x, vectors, middle_out, normed_all, mine, theirs, here, wide, normed, send,
    recv, local,
):
    place = Place(count)
    links = Links(send, recv, local)
    greet(place, rows=True, line=True, cores=True)
    row, z, col = place.row, place.dp, place.col
    tall, narrow = x.shape
    quarter = tall // 4
    other = links.copy(partial.at[strip(place.other, tall, 8)], theirs, col=place.other)
    other.start()
    load = links.keep(partial.at[strip(col, tall, 8)], mine)
    load.wait()
    other.wait_recv()

    def add(rows):
        here[rows] = mine[rows] + theirs[rows] + x[rows].astype(WIDE)

    by_rows(tall, add)

    def source(q):
        return here.at[strip(q, quarter)]

    own = links.keep(source(row), wide.at[:, lanes(row, narrow)])
    run([exchange_rows(links, place, source, lambda q: wide.at[:, lanes(q, narrow)])])
    own.wait()
    other.wait_send()
    shift, gain = vectors[1:2, :], vectors[3:4, :]
    full = wide.shape[1]

    def norm(rows):
        middle = wide[rows] + shift
        middle_out[rows] = middle
        mean = jnp.sum(middle * middle, axis=1, keepdims=True) / full
        normed[rows] = (middle * lax.rsqrt(mean + epsilon) * (1.0 + gain)).astype(LOW)

    by_rows(quarter, norm)

    def block(b):
        return normed_all.at[strip(col * count + b, quarter)]

    keep = links.keep(normed, block(z))
    run([gather_line(links, place, normed, block, share=True)])
    keep.wait()


def norm_rule(rows, grad, value, gain, sums, at):
    full = value.shape[1]
    inverse = lax.rsqrt(jnp.sum(value * value, axis=1, keepdims=True) / full + epsilon)
    scaled = grad * (1.0 + gain)
    inner = jnp.sum(scaled * value, axis=1, keepdims=True)
    sums[at : at + 1, :] += jnp.sum(grad * value * inverse, axis=0, keepdims=True)
    return inverse * scaled - value * (inverse * inverse * inverse) * (inner / full)


def second_norm_back(
    count, grad_partial, cot_all, middle, vectors, down_partial, grad_middle, grad_all, sums, down_out,
    ours, theirs, ups, downs, staging, cot, low, buffers, send, recv, local,
):
    place = Place(count)
    links = Links(send, recv, local)
    greet(place, rows=True, line=True, cores=True)
    row, z, col = place.row, place.dp, place.col
    quarter, full = middle.shape
    narrow = full // 4
    tall = 4 * quarter
    down_halves = halves(down_partial.shape[0])
    sums[...] = jnp.zeros(sums.shape, WIDE)
    gain = vectors[3:4, :]
    load = links.keep(cot_all.at[strip(col * count + z, quarter)], cot)

    def back(rows, grad):
        own = cot[rows].astype(WIDE)
        total = own + norm_rule(rows, grad, middle[rows], gain, sums, 0)
        sums[1:2, :] += jnp.sum(total, axis=0, keepdims=True)
        sums[2:3, :] += jnp.sum(own, axis=0, keepdims=True)
        grad_middle[rows] = total
        low[rows] = total.astype(LOW)

    def tokens():
        load.wait()
        yield from token_scatter(
            links, place, grad_partial, ours, theirs, (ups, downs, staging), back
        )

        def block(q):
            return grad_all.at[strip(4 * col + q, quarter)]

        mine = links.keep(low.at[:, lanes(row, narrow)], block(row))
        yield from exchange_rows(
            links, place, lambda q: low.at[:, lanes(q, narrow)], block
        )
        mine.wait()
        both = grad_all.at[strip(col, tall)]
        share = links.copy(both, both, col=place.other)
        share.start()
        yield 1
        share.wait_recv()
        share.wait_send()

    def keep_down(h, rows, value):
        down_out[pl.ds(pl.multiple_of(down_halves[h].start + rows.start, 16), rows.size)] = value

    run(
        [
            tokens(),
            scatter_rows(
                links,
                place,
                lambda q, h: down_partial.at[down_halves[h], lanes(q, narrow)],
                buffers,
                keep_down,
            ),
        ]
    )


def mixed_and_output(
    count, mixed_partial, out_partial, middle, vectors, gate_partial, mixed_out, layer_out, gate_out,
    mixed_buffers, ours, theirs, ups, downs, staging, low, gate_buffers, send, recv, local,
):
    place = Place(count)
    links = Links(send, recv, local)
    greet(place, rows=True, line=True, cores=True)
    row = place.row
    quarter, full = middle.shape
    narrow = full // 4
    shift = vectors[2:3, :]
    half = mixed_partial.shape[0] // 8
    gate_half = gate_partial.shape[0] // 8

    def keep_mixed(h, rows, value):
        mixed_out[h, rows] = value

    def keep_gate(h, rows, value):
        gate_out[h, rows] = value.astype(LOW)

    def finish(rows, value):
        low[rows] = (middle[rows] + value + shift).astype(LOW)

    def tokens():
        yield from token_scatter(
            links, place, out_partial, ours, theirs, (ups, downs, staging), finish
        )
        mine = links.keep(low.at[:, lanes(row, narrow)], layer_out.at[row])
        yield from exchange_rows(
            links, place, lambda q: low.at[:, lanes(q, narrow)], lambda q: layer_out.at[q]
        )
        mine.wait()

    run(
        [
            scatter_rows(
                links,
                place,
                lambda q, h: mixed_partial.at[strip(2 * q + h, half)],
                mixed_buffers,
                keep_mixed,
            ),
            tokens(),
            scatter_rows(
                links,
                place,
                lambda q, h: gate_partial.at[strip(2 * q + h, gate_half)],
                gate_buffers,
                keep_gate,
            ),
        ]
    )


def spread_gradients(
    count, blocks, up_partial, output_partial, gate_own, all_out, up_out, output_out, gate_out,
    up_buffers, ups, downs, staging, own, send, recv, local,
):
    place = Place(count)
    links = Links(send, recv, local)
    greet(place, rows=True, line=True)
    row, z = place.row, place.dp
    half = up_partial.shape[0] // 8
    mine = links.keep(blocks.at[row], all_out.at[row])
    kept = links.keep(gate_own.at[z], gate_out.at[z])
    load = links.keep(output_partial, own)

    def keep_up(h, rows, value):
        up_out[h, rows] = value.astype(LOW)

    def keep_output(i, rows, value):
        output_out[rows] = value

    def outputs():
        load.wait()
        yield from scatter_line(
            links,
            place,
            lambda s: None,
            lambda b, i, rows: own[b, rows].astype(WIDE),
            ups,
            downs,
            staging,
            keep_output,
        )

    run(
        [
            exchange_rows(links, place, lambda q: blocks.at[q], lambda q: all_out.at[q]),
            outputs(),
            exchange_line(
                links, place, lambda b: gate_own.at[b], lambda b: gate_out.at[b]
            ),
            scatter_rows(
                links,
                place,
                lambda q, h: up_partial.at[strip(2 * q + h, half)],
                up_buffers,
                keep_up,
            ),
        ]
    )
    mine.wait()
    kept.wait()


def first_norm_back(
    count, grad_partial, x_all, grad_middle, vectors, proj_partial, up_own, sums_in, channel_in,
    hidden_in, block_in, grad_out, proj_out, up_out, width_sums, channel_sums, block_out, hidden_sums,
    theirs, ours, added,
    row_buffer, x, result, sums, proj_own, proj_ups, proj_downs, proj_staging, proj_low, width_table,
    width_line, width_part, channel_table, channel_line, hidden_table, block_buffers, block_sum, block_ups, block_downs,
    block_staging, block_low, send, recv, local,
):
    place = Place(count)
    links = Links(send, recv, local)
    greet(place, rows=True, line=True, cores=True)
    row, z, col = place.row, place.dp, place.col
    quarter, full = grad_middle.shape
    narrow = full // 4
    gain = vectors[0:1, :]
    load_x = links.keep(x_all.at[strip(4 * col + row, quarter)], x)
    load_proj = [links.keep(proj_partial.at[:, b], proj_own.at[b]) for b in range(count)]
    kept = links.keep(up_own.at[z], up_out.at[z])

    def tokens():
        share = links.copy(grad_partial.at[place.other], theirs, col=place.other)
        share.start()
        load = links.keep(grad_partial.at[col], ours)
        yield 1
        share.wait_recv()
        load.wait()

        def add(rows):
            for q in range(4):
                total = ours[q, rows].astype(WIDE) + theirs[q, rows].astype(WIDE)
                added[q, rows] = total.astype(LOW)

        by_rows(quarter, add)
        load_x.wait()
        sums[0:3, :] = sums_in[0:3, :]
        sums[3:, :] = jnp.zeros((sums.shape[0] - 3, full), WIDE)
        half = quarter // 2

        def back(h, rows, grad):
            here = pl.ds(pl.multiple_of(rows.start + half * h, 16), rows.size)
            value = x[here].astype(WIDE)
            total = grad_middle[here] + norm_rule(rows, grad, value, gain, sums, 3)
            for q in range(4):
                result[q, here] = total[:, q * narrow : (q + 1) * narrow]

        yield from scatter_rows(
            links,
            place,
            lambda q, h: added.at[q, pl.ds(half * h, half)],
            row_buffer,
            back,
        )
        share.wait_send()
        mine = links.keep(result.at[row], grad_out.at[row])
        yield from exchange_rows(
            links, place, lambda q: result.at[q], lambda q: grad_out.at[q]
        )
        mine.wait()
        for q in range(4):
            width_part[q] = sums[:, q * narrow : (q + 1) * narrow]
        own = links.keep(width_part.at[row], width_table.at[row])
        yield from exchange_rows(
            links, place, lambda q: width_part.at[q], lambda q: width_table.at[q]
        )
        own.wait()
        width_line[z] = width_table[0] + width_table[1] + width_table[2] + width_table[3]
        yield from exchange_line(
            links, place, lambda b: width_line.at[z], lambda b: width_line.at[b]
        )
        total = width_line[0]
        for b in range(1, count):
            total = total + width_line[b]
        width_sums[0] = total
        yield 1
        last = links.copy(width_sums.at[0], width_sums.at[1], col=place.other)
        last.start()
        yield 1
        last.wait_recv()
        last.wait_send()

    def projections():
        for load in load_proj:
            load.wait()

        def keep_proj(i, rows, value):
            proj_low[i, rows] = value.astype(LOW)

        yield from scatter_line(
            links,
            place,
            lambda s: None,
            lambda b, i, rows: proj_own[b, i, rows].astype(WIDE),
            proj_ups,
            proj_downs,
            proj_staging,
            keep_proj,
        )
        mine = links.keep(proj_low.at[row], proj_out.at[row])
        yield from exchange_rows(
            links, place, lambda q: proj_low.at[q], lambda q: proj_out.at[q]
        )
        mine.wait()

    def hidden():
        own = links.keep(hidden_in, hidden_table.at[row])
        yield from exchange_rows(
            links, place, lambda q: hidden_in, lambda q: hidden_table.at[q]
        )
        own.wait()
        hidden_sums[...] = hidden_table[0] + hidden_table[1] + hidden_table[2] + hidden_table[3]

    def channels():
        own = links.keep(channel_in, channel_table.at[row])
        yield from exchange_rows(
            links, place, lambda q: channel_in, lambda q: channel_table.at[q]
        )
        own.wait()
        channel_line[z] = (
            channel_table[0] + channel_table[1] + channel_table[2] + channel_table[3]
        )
        yield from exchange_line(
            links, place, lambda b: channel_line.at[z], lambda b: channel_line.at[b]
        )
        total = channel_line[0]
        for b in range(1, count):
            total = total + channel_line[b]
        channel_sums[...] = total

    def blocks():
        def keep_rows(h, rows, value):
            block_sum[h, rows] = value

        yield from scatter_rows(
            links,
            place,
            lambda q, h: block_in.at[q, h],
            block_buffers,
            keep_rows,
        )
        length = block_sum.shape[1] * 2 // count
        middle = count // 2

        def term(b, i, rows):
            at = pl.multiple_of(lax.rem(b, middle) * length + rows.start, 8)
            return block_sum[lax.div(b, middle), pl.ds(at, rows.size)]

        def keep_line(i, rows, value):
            block_low[rows] = value.astype(LOW)

        yield from scatter_line(
            links, place, lambda s: None, term, block_ups, block_downs, block_staging, keep_line
        )
        mine = links.keep(block_low, block_out.at[row])
        yield from exchange_rows(links, place, lambda q: block_low, lambda q: block_out.at[q])
        mine.wait()

    run(
        [
            tokens(),
            projections(),
            exchange_line(links, place, lambda b: up_own.at[b], lambda b: up_out.at[b]),
            channels(),
            hidden(),
            blocks(),
        ]
    )
    kept.wait()


def times(piece, matrix):
    return jnp.dot(piece, matrix, preferred_element_type=WIDE)


def times_flipped(piece, matrix):
    return lax.dot_general(piece, matrix, (((1,), (1,)), ((), ())), preferred_element_type=WIDE)


def left_product(left, right):
    return lax.dot_general(left, right, (((0,), (0,)), ((), ())), preferred_element_type=WIDE)


def side_by_side(blocks):
    return jnp.concatenate([blocks[i] for i in range(blocks.shape[0])], axis=1)


def columns(matrix, parts):
    width = matrix.shape[1] // parts
    return jnp.stack([matrix[:, i * width : (i + 1) * width] for i in range(parts)])


def padded_rows(rows, height, width):
    return jnp.pad(rows, ((0, height - rows.shape[0]), (0, width - rows.shape[1])))


def round_up(size, step):
    return -(-size // step) * step


def shards(
    inputs,
    positions,
    branch_matrix,
    gelu_matrix,
    output_matrix,
    gate_matrix,
    up_matrix,
    down_matrix,
    input_blocks,
    decay_blocks,
    conv_taps,
    conv_bias,
    branch_bias,
    gelu_bias,
    input_bias,
    decay_bias,
    decay_param,
    output_bias,
    gate_bias,
    up_bias,
    down_bias,
    norm_first,
    norm_second,
    cotangent,
):
    count, rows_count, cores = lax.axis_size("dp"), lax.axis_size("row"), lax.axis_size("col")
    place_dp, place_row = lax.axis_index("dp"), lax.axis_index("row")
    tall, narrow = inputs.shape
    quarter, full, tokens = tall // rows_count, narrow * rows_count, tall * cores
    depth, width = branch_matrix.shape
    part = width // rows_count
    hidden_part = down_matrix.shape[0]
    heads, block_part, block = input_blocks.shape
    taps = conv_taps.shape[0]
    steps = positions.shape[0]
    share = block_part // rows_count
    remote, local = 64 + 24 * count, 40 + 6 * count

    wxy = jnp.concatenate(
        (columns(branch_matrix.astype(LOW), rows_count), columns(gelu_matrix.astype(LOW), rows_count)),
        axis=2,
    )
    blocks_low = jnp.concatenate((input_blocks, decay_blocks), axis=0).astype(LOW)
    blk = lax.dynamic_slice_in_dim(blocks_low, place_row * share, share, 1).reshape(
        2 * heads * share, block
    )
    channel_rows = jnp.concatenate(
        (
            conv_taps,
            jnp.stack((conv_bias, branch_bias, gelu_bias, input_bias, decay_bias, decay_param)),
        ),
        axis=0,
    )
    channel_size = channel_rows.shape[1]
    cvec = padded_rows(
        channel_rows.astype(LOW).astype(WIDE),
        round_up(taps + 6, 8),
        round_up(channel_size, 128),
    )
    wvec = padded_rows(
        jnp.stack((norm_first, output_bias, down_bias, norm_second)).astype(LOW).astype(WIDE),
        8,
        round_up(depth, 128),
    )
    x_all, cot_all, wxy_all, wout_all, gate_all, up_all, down_all, blk_all, cvec_all, wvec_all = call(
        functools.partial(gather_inputs, count),
        "gather_inputs",
        1,
        [
            (array, False)
            for array in (
                inputs,
                cotangent,
                wxy,
                output_matrix.astype(LOW),
                columns(gate_matrix.astype(LOW), count),
                columns(up_matrix.astype(LOW), count),
                down_matrix.astype(LOW),
                blk,
                cvec,
                wvec,
            )
        ],
        [
            ((tokens, full), LOW, False),
            ((cores * count * quarter, full), LOW, False),
            ((rows_count, count, depth, 2 * part), LOW, False),
            ((count,) + output_matrix.shape, LOW, False),
            ((rows_count, count, depth, hidden_part), LOW, False),
            ((rows_count, count, depth, hidden_part), LOW, False),
            ((hidden_part, full), LOW, False),
            ((count, rows_count) + blk.shape, LOW, False),
            ((count,) + cvec.shape, WIDE, False),
            ((rows_count, count) + wvec.shape, WIDE, False),
        ],
        [],
        remote,
        local,
    )
    wxy_all = wxy_all.reshape(full, 2 * part)
    wout_all = wout_all.reshape(width, narrow)
    gate_all = gate_all.reshape(full, hidden_part)
    up_all = up_all.reshape(full, hidden_part)
    blocks = (
        blk_all.reshape(count, rows_count, 2 * heads, share, block)
        .transpose(2, 0, 1, 3, 4)
        .reshape(2 * heads, block, block)
    )
    channel_all = side_by_side(cvec_all[:, : taps + 6, :channel_size])
    gelu_shift, decay_raw = channel_all[taps + 2], channel_all[taps + 5]
    vectors = jnp.concatenate(
        (channel_all[: taps + 5], -8.0 * jax.nn.softplus(decay_raw)[None, :]), axis=0
    )
    width_all = jnp.concatenate(
        [wvec_all[q, b, :, :depth] for q in range(rows_count) for b in range(count)], axis=1
    )

    resid = x_all.astype(WIDE)
    inverse = lax.rsqrt(jnp.mean(resid * resid, axis=1, keepdims=True) + epsilon)
    normed_first = (resid * inverse * (1.0 + width_all[0])).astype(LOW)
    projected = jnp.pad(times(normed_first, wxy_all), ((8, 0), (0, 0)))
    (projected_here,) = call(
        functools.partial(spread_projected, count),
        "spread_projected",
        2,
        [(projected, False)],
        [((rows_count, steps + 8, 2 * part), WIDE, False)],
        [],
        remote,
        local,
    )
    branch = side_by_side(projected_here[:, :, :part])
    gelu_in = side_by_side(projected_here[:, 8:, part:]) + gelu_shift
    side, gelu_pull = jax.vjp(jax.nn.gelu, gelu_in)

    spots = positions[:, None]
    wide_tokens = ((steps, width), WIDE, True)
    tokens_scratch = pltpu.VMEM((steps, width), WIDE)
    eight_rows = pltpu.VMEM((8, width), WIDE)
    table_rows = pltpu.VMEM((rows_count, 8, width), WIDE)
    conv, input_gate, decay_gate, state, entering, mixed_all = call(
        functools.partial(recurrence_forward, count, taps),
        "recurrence_forward",
        3,
        [(array, True) for array in (branch, side, spots, vectors, blocks)],
        [wide_tokens] * 4 + [((8, width), WIDE, True), ((tokens, width), LOW, False)],
        [
            tokens_scratch,
            tokens_scratch,
            eight_rows,
            table_rows,
            pltpu.VMEM((steps, width), LOW),
        ],
        remote,
        local,
    )

    middle, normed_second = call(
        functools.partial(output_and_norm, count),
        "output_and_norm",
        4,
        [(times(mixed_all, wout_all), False), (inputs, True), (width_all, True)],
        [((quarter, full), WIDE, True), ((cores * count * quarter, full), LOW, False)],
        [
            pltpu.VMEM((tall, narrow), WIDE),
            pltpu.VMEM((tall, narrow), WIDE),
            pltpu.VMEM((tall, narrow), WIDE),
            pltpu.VMEM((quarter, full), WIDE),
            pltpu.VMEM((quarter, full), LOW),
        ],
        remote,
        local,
    )

    def feed(gate_value, up_value):
        return jax.nn.gelu(gate_value) * up_value

    hidden_value, feed_pull = jax.vjp(
        feed,
        times(normed_second, gate_all) + gate_bias.astype(LOW).astype(WIDE),
        times(normed_second, up_all) + up_bias.astype(LOW).astype(WIDE),
    )
    hidden = hidden_value.astype(LOW)
    grad_gate, grad_up = feed_pull(times_flipped(cot_all, down_all))
    grad_gate_low, grad_up_low = grad_gate.astype(LOW), grad_up.astype(LOW)
    by_device = (cores, count, quarter, full)
    grad_normed_second = (
        (times_flipped(grad_gate_low, gate_all) + times_flipped(grad_up_low, up_all))
        .astype(LOW)
        .reshape(by_device)
    )
    down_partial = left_product(hidden, cot_all).astype(LOW)
    token_scratch = [
        pltpu.VMEM((count, quarter, full), LOW),
        pltpu.VMEM((count, quarter, full), LOW),
        *line_buffers(count, 1, quarter, full),
    ]
    token_low = pltpu.VMEM((quarter, full), LOW)
    grad_middle, grad_middle_all, width_sums, down_grad = call(
        functools.partial(second_norm_back, count),
        "second_norm_back",
        5,
        [
            (grad_normed_second, False),
            (cot_all, False),
            (middle, True),
            (width_all, True),
            (down_partial, False),
        ],
        [
            ((quarter, full), WIDE, True),
            ((tokens, narrow), LOW, False),
            ((8, full), WIDE, True),
            ((hidden_part, narrow), WIDE, True),
        ],
        token_scratch + [token_low, token_low, row_buffers(hidden_part, narrow)],
        remote,
        local,
    )
    gate_partial = left_product(normed_second, grad_gate_low).astype(LOW)
    up_partial = left_product(normed_second, grad_up_low).astype(LOW)
    forward_partial = times(hidden, down_all).astype(LOW).reshape(by_device)

    mixed_partial = times_flipped(grad_middle_all, wout_all).astype(LOW)
    output_partial = left_product(mixed_all, grad_middle_all).astype(LOW)
    grad_mixed, layer_out, gate_own = call(
        functools.partial(mixed_and_output, count),
        "mixed_and_output",
        6,
        [
            (mixed_partial, False),
            (forward_partial, False),
            (middle, True),
            (width_all, True),
            (gate_partial, False),
        ],
        [
            ((2, steps // 2, width), WIDE, True),
            ((rows_count, quarter, narrow), LOW, False),
            ((2, narrow // 2, hidden_part), LOW, True),
        ],
        [row_buffers(steps, width)]
        + token_scratch
        + [token_low, row_buffers(narrow, hidden_part)],
        remote,
        local,
    )
    grad_mixed = grad_mixed.reshape(steps, width)

    grad_gelu = gelu_pull(grad_mixed * state)[0]
    grad_branch_low, channel_part, block_sums = call(
        functools.partial(recurrence_backward, count, taps),
        "recurrence_backward",
        7,
        [
            (array, True)
            for array in (
                branch,
                side,
                spots,
                vectors,
                blocks,
                conv,
                input_gate,
                decay_gate,
                state,
                entering,
                grad_mixed,
            )
        ],
        [
            ((steps, width), LOW, True),
            ((round_up(taps + 6, 8), width), WIDE, True),
            ((2 * heads, block, block), WIDE, True),
        ],
        [
            tokens_scratch,
            tokens_scratch,
            tokens_scratch,
            eight_rows,
            table_rows,
            pltpu.VMEM((2, 8, width), WIDE),
            eight_rows,
            pltpu.VMEM((steps + 8, block), WIDE),
            pltpu.VMEM((steps + 8, block), WIDE),
        ],
        remote,
        local,
    )
    grad_gelu_low = grad_gelu.astype(LOW)
    projected_grads = jnp.concatenate(
        (columns(grad_branch_low, rows_count), columns(grad_gelu_low, rows_count)), axis=2
    )
    grad_projected, up_own, output_grad, gate_blocks = call(
        functools.partial(spread_gradients, count),
        "spread_gradients",
        8,
        [
            (projected_grads, False),
            (up_partial, False),
            (output_partial.reshape((count,) + output_matrix.shape), False),
            (gate_own.reshape(count, depth, hidden_part), False),
        ],
        [
            ((rows_count, steps, 2 * part), LOW, False),
            ((2, narrow // 2, hidden_part), LOW, True),
            (output_matrix.shape, WIDE, True),
            ((count, depth, hidden_part), LOW, False),
        ],
        [
            row_buffers(narrow, hidden_part),
            *line_buffers(count, 1, *output_matrix.shape),
            pltpu.VMEM((count,) + output_matrix.shape, LOW),
        ],
        remote,
        local,
    )
    grad_projected = grad_projected.reshape(tokens, 2 * part)
    proj_partial = left_product(normed_first, grad_projected).astype(LOW)
    grad_normed_first = times_flipped(grad_projected, wxy_all).astype(LOW)
    channel_part = channel_part.at[taps + 5].set(jnp.sum(grad_gelu, axis=0))
    hidden_part_sums = padded_rows(
        jnp.stack((jnp.sum(grad_gate, axis=0), jnp.sum(grad_up, axis=0))),
        8,
        round_up(hidden_part, 128),
    )
    block_in = (
        block_sums.astype(LOW)
        .reshape(2 * heads, count, rows_count, share, block)
        .transpose(2, 1, 0, 3, 4)
        .reshape(rows_count, 2, count // 2 * 2 * heads * share, block)
    )
    channel_shape, hidden_shape = channel_part.shape, hidden_part_sums.shape
    block_rows = 2 * heads * share
    input_grad, proj_grad, up_blocks, width_sums, channel_sums, block_grads, hidden_sums = call(
        functools.partial(first_norm_back, count),
        "first_norm_back",
        9,
        [
            (grad_normed_first.reshape(cores, rows_count, quarter, full), False),
            (x_all, False),
            (grad_middle, True),
            (width_all, True),
            (proj_partial.reshape(rows_count, count, depth, 2 * part), False),
            (up_own.reshape(count, depth, hidden_part), False),
            (width_sums, True),
            (channel_part, True),
            (hidden_part_sums, True),
            (block_in, False),
        ],
        [
            ((rows_count, quarter, narrow), WIDE, False),
            ((rows_count, depth, 2 * part), LOW, False),
            ((count, depth, hidden_part), LOW, False),
            ((2, 8, narrow), WIDE, True),
            (channel_shape, WIDE, True),
            ((rows_count, block_rows, block), LOW, False),
            (hidden_shape, WIDE, True),
        ],
        [
            pltpu.VMEM((rows_count, quarter, full), LOW),
            pltpu.VMEM((rows_count, quarter, full), LOW),
            pltpu.VMEM((rows_count, quarter, full), LOW),
            row_buffers(quarter, full),
            token_low,
            pltpu.VMEM((rows_count, quarter, narrow), WIDE),
            pltpu.VMEM((8, full), WIDE),
            pltpu.VMEM((count, rows_count, depth, 2 * part), LOW),
            *line_buffers(count, rows_count, depth, 2 * part),
            pltpu.VMEM((rows_count, depth, 2 * part), LOW),
            pltpu.VMEM((rows_count, 8, narrow), WIDE),
            pltpu.VMEM((count, 8, narrow), WIDE),
            pltpu.VMEM((rows_count, 8, narrow), WIDE),
            pltpu.VMEM((rows_count,) + channel_shape, WIDE),
            pltpu.VMEM((count,) + channel_shape, WIDE),
            pltpu.VMEM((rows_count,) + hidden_shape, WIDE),
            row_buffers(2 * block_in.shape[2], block),
            pltpu.VMEM((2, block_in.shape[2], block), WIDE),
            *line_buffers(count, 1, block_rows, block),
            pltpu.VMEM((block_rows, block), LOW),
        ],
        remote,
        local,
    )
    branch_grad = side_by_side(proj_grad[:, :, :part]).astype(WIDE)
    gelu_grad = side_by_side(proj_grad[:, :, part:]).astype(WIDE)
    block_grads = (
        block_grads.reshape(rows_count, 2 * heads, share, block)
        .transpose(1, 0, 2, 3)
        .reshape(2 * heads, block_part, block)
        .astype(WIDE)
    )
    channel_sums = lax.dynamic_slice_in_dim(channel_sums, place_dp * channel_size, channel_size, 1)
    width_sums = lax.dynamic_slice_in_dim(
        width_sums[0] + width_sums[1], place_dp * depth, depth, 1
    )
    decay_raw_here = lax.dynamic_slice_in_dim(decay_raw, place_dp * channel_size, channel_size, 0)
    decay_param_grad = -8.0 * channel_sums[taps + 4] * jax.nn.sigmoid(decay_raw_here)

    return (
        layer_out.reshape(tall, narrow),
        input_grad.reshape(tall, narrow),
        branch_grad,
        gelu_grad,
        output_grad,
        side_by_side(gate_blocks).astype(WIDE),
        side_by_side(up_blocks).astype(WIDE),
        down_grad,
        block_grads[:heads],
        block_grads[heads:],
        channel_sums[:taps],
        channel_sums[taps],
        channel_sums[taps + 1],
        channel_sums[taps + 5],
        channel_sums[taps + 2],
        channel_sums[taps + 3],
        decay_param_grad,
        width_sums[1],
        hidden_sums[0, :hidden_part],
        hidden_sums[1, :hidden_part],
        width_sums[2],
        width_sums[3],
        width_sums[0],
    )


def solution(mesh):
    in_specs = (
        P(("dp", "col"), "row"),
        P(("dp", "row")),
        P(("row", "dp"), "col"),
        P(("row", "dp"), "col"),
        P(("col", "dp"), "row"),
        P(("row", "dp"), "col"),
        P(("row", "dp"), "col"),
        P(("col", "dp"), "row"),
        P("col", "dp", None),
        P("col", "dp", None),
        P(None, ("col", "dp")),
        P(("col", "dp")),
        P(("col", "dp")),
        P(("col", "dp")),
        P(("col", "dp")),
        P(("col", "dp")),
        P(("col", "dp")),
        P(("row", "dp")),
        P(("col", "dp")),
        P(("col", "dp")),
        P(("row", "dp")),
        P(("row", "dp")),
        P(("row", "dp")),
        P(("dp", "col"), "row"),
    )
    out_specs = (
        P(("dp", "col"), "row"),
        P(("dp", "col"), "row"),
        P(("row", "dp"), "col"),
        P(("row", "dp"), "col"),
        P(("col", "dp"), "row"),
        P(("row", "dp"), "col"),
        P(("row", "dp"), "col"),
        P(("col", "dp"), "row"),
        P("col", "dp", None),
        P("col", "dp", None),
        P(None, ("col", "dp")),
        P(("col", "dp")),
        P(("col", "dp")),
        P(("col", "dp")),
        P(("col", "dp")),
        P(("col", "dp")),
        P(("col", "dp")),
        P(("row", "dp")),
        P(("col", "dp")),
        P(("col", "dp")),
        P(("row", "dp")),
        P(("row", "dp")),
        P(("row", "dp")),
    )
    return jax.shard_map(shards, mesh=mesh, in_specs=in_specs, out_specs=out_specs, check_vma=False)
```

```python
import functools

import jax
import jax.numpy as jnp
from jax import lax
from jax.experimental import pallas as pl
from jax.experimental.pallas import tpu as pltpu
from jax.sharding import PartitionSpec as P

epsilon = 1e-06
ROOT = (2.0 / 3.141592653589793) ** 0.5
CUBE = 0.044715
LOW = jnp.bfloat16
WIDE = jnp.float32
MESH = pl.DeviceIdType.MESH
VMEM = pl.BlockSpec(memory_space=pltpu.VMEM)
ANY = pl.BlockSpec(memory_space=pl.ANY)


class Links:
    def __init__(self, send, recv, local):
        self.send, self.recv, self.local = send, recv, local
        self.sent = self.kept = 0

    def copy(self, src, dst, **where):
        k, self.sent = self.sent, self.sent + 1
        return pltpu.make_async_remote_copy(
            src_ref=src,
            dst_ref=dst,
            send_sem=self.send.at[k],
            recv_sem=self.recv.at[k],
            device_id=where,
            device_id_type=MESH,
        )

    def keep(self, src, dst):
        k, self.kept = self.kept, self.kept + 1
        copy = pltpu.make_async_copy(src, dst, self.local.at[k])
        copy.start()
        return copy


class Relay:
    def __init__(self, links, src, buffer, dst):
        self.links, self.buffer, self.dst, self.store = links, buffer, dst, None
        self.load = links.keep(src, buffer)

    def pass_on(self):
        if self.store is None:
            self.load.wait()
            self.store = self.links.keep(self.buffer, self.dst)

    def wait(self):
        self.pass_on()
        self.store.wait()


class Place:
    def __init__(self, count_dp):
        self.row, self.dp, self.col = (lax.axis_index(name) for name in ("row", "dp", "col"))
        self.count = count_dp
        first, second = lax.rem(self.row, 2), lax.div(self.row, 2)
        self.near = [self.row, self.row + 1 - 2 * first, self.row + 2 - 4 * second, 3 - self.row]
        self.other = 1 - self.col

    def turn(self, index):
        return lax.rem(index + self.count, self.count)


def greet(place, rows=False, line=False, cores=False):
    barrier = pltpu.get_barrier_semaphore()
    partners = []
    if rows:
        partners += [{"row": place.near[k]} for k in range(1, 4)]
    if line:
        partners += [{"dp": place.turn(place.dp + k)} for k in range(1, place.count)]
    if cores:
        partners += [{"col": place.other}]
    for where in partners:
        pl.semaphore_signal(barrier, inc=1, device_id=where, device_id_type=MESH)
    pl.semaphore_wait(barrier, len(partners))


def run(tasks):
    live = list(tasks)
    while live:
        live = [task for task in live if next(task, None) is not None]


def chain(*tasks):
    for task in tasks:
        yield from task


def when(condition, action):
    pl.when(condition)(lambda: action() and None)


def halves(size):
    first = -(-size // 32) * 16
    return (pl.ds(0, first), pl.ds(first, size - first))


def by_rows(count, body):
    step = 16 if count % 16 == 0 else count

    def lap(i, carry):
        body(pl.ds(pl.multiple_of(i * step, step), step))
        return carry

    lax.fori_loop(0, count // step, lap, 0)


def by_pieces(pieces, height, body):
    def lap(i, carry):
        by_rows(height, lambda rows: body(i, rows))
        return carry

    if pieces == 1:
        by_rows(height, lambda rows: body(0, rows))
    else:
        lax.fori_loop(0, pieces, lap, 0)


def gather_rows(links, place, own, piece):
    row, near, side, _ = place.near
    out = [
        links.copy(own(0), piece(row, 0), row=near),
        links.copy(own(1), piece(row, 1), row=side),
        links.copy(own(1), piece(row, 1), row=near),
        links.copy(own(0), piece(row, 0), row=side),
    ]
    for copy in out:
        copy.start()
    yield 1
    out[0].wait_recv()
    out.append(links.copy(piece(near, 0), piece(near, 0), row=side))
    out[4].start()
    out[1].wait_recv()
    out.append(links.copy(piece(side, 1), piece(side, 1), row=near))
    out[5].start()
    yield 1
    for copy in out[2:]:
        copy.wait_recv()
    for copy in out:
        copy.wait_send()


def exchange_rows(links, place, source, target):
    out = [
        links.copy(source(place.near[k]), target(place.row), row=place.near[k])
        for k in range(1, 4)
    ]
    for copy in out:
        copy.start()
    yield 1
    for copy in out:
        copy.wait_recv()
    for copy in out:
        copy.wait_send()


def exchange_line(links, place, source, target):
    out = []
    for k in range(1, place.count):
        far = place.turn(place.dp + k)
        out.append(links.copy(source(far), target(place.dp), dp=far))
    for copy in out:
        copy.start()
    yield 1
    for copy in out:
        copy.wait_recv()
    for copy in out:
        copy.wait_send()


def gather_line(links, place, own, piece, share=False):
    z, count, turn = place.dp, place.count, place.turn
    ups, downs, shared = [], [], []

    def pass_on(block, valid):
        copy = links.copy(piece(block), piece(block), col=place.other)
        when(valid, copy.start)
        shared.append((copy, valid))

    if share:
        copy = links.copy(own, piece(z), col=place.other)
        copy.start()
        shared.append((copy, z >= 0))
    for step in range(1, count + 1):
        if step > 1:
            yield 1
            below, above = z >= step - 1, z <= count - step
            when(below, ups[-1].wait_recv)
            when(above, downs[-1].wait_recv)
        if step < count:
            low, high = turn(z - step + 1), turn(z + step - 1)
            ups.append(
                links.copy(own if step == 1 else piece(low), piece(low), dp=turn(z + 1))
            )
            downs.append(
                links.copy(own if step == 1 else piece(high), piece(high), dp=turn(z - 1))
            )
            when((z >= step - 1) & (z < count - 1), ups[-1].start)
            when((z <= count - step) & (z > 0), downs[-1].start)
        if step > 1 and share:
            pass_on(turn(z - step + 1), below)
            pass_on(turn(z + step - 1), above)
    yield 1
    for copy, valid in shared:
        when(valid, copy.wait_recv)
    for step in range(1, count):
        when((z >= step - 1) & (z < count - 1), ups[step - 1].wait_send)
        when((z <= count - step) & (z > 0), downs[step - 1].wait_send)
    for copy, valid in shared:
        when(valid, copy.wait_send)


class LineGather:
    def __init__(self, links, place, own, piece):
        self.links, self.place, self.own, self.piece = links, place, own, piece
        self.ups, self.downs, self.shared = [None], [None], []

    def send(self, step):
        z, count, turn = self.place.dp, self.place.count, self.place.turn
        low, high = turn(z - step + 1), turn(z + step - 1)
        for copies, block, target, valid in (
            (self.ups, low, turn(z + 1), (z >= step - 1) & (z < count - 1)),
            (self.downs, high, turn(z - 1), (z <= count - step) & (z > 0)),
        ):
            source = self.own if step == 1 else self.piece(block)
            copy = self.links.copy(source, self.piece(block), dp=target)
            copies.append((copy, valid))
            when(valid, copy.start)

    def share(self, blocks, own=None):
        out = []
        for block, valid in blocks:
            source = self.piece(block) if own is None else own
            copy = self.links.copy(source, self.piece(block), col=self.place.other)
            when(valid, copy.start)
            out.append((copy, valid))
        self.shared.append(out)

    def start(self):
        self.send(1)
        self.share([(self.place.dp, self.place.dp >= 0)], self.own)

    def step(self, step):
        z, count, turn = self.place.dp, self.place.count, self.place.turn
        below, above = z >= step, z <= count - 1 - step
        when(below, self.ups[step][0].wait_recv)
        when(above, self.downs[step][0].wait_recv)
        if step < count - 1:
            self.send(step + 1)
        self.share([(turn(z - step), below), (turn(z + step), above)])

    def ready(self, step):
        for copy, valid in self.shared[step]:
            when(valid, copy.wait_recv)

    def close(self):
        for copy, valid in self.ups[1:] + self.downs[1:] + sum(self.shared, []):
            when(valid, copy.wait_send)


def scatter_rows(links, place, part, buffers, result):
    row, near, side, far = place.near
    heights = [part(row, h).shape[0] for h in range(2)]

    def buffer(i, h):
        return buffers.at[i, pl.ds(0, heights[h])]

    out = [
        links.copy(part(far, 0), buffer(5, 0), row=side),
        links.copy(part(far, 1), buffer(7, 1), row=near),
        links.copy(part(side, 0), buffer(4, 0), row=side),
        links.copy(part(near, 1), buffer(6, 1), row=near),
    ]
    for copy in out:
        copy.start()
    loads = [
        links.keep(part(near, 0), buffer(0, 0)),
        links.keep(part(side, 1), buffer(1, 1)),
        links.keep(part(row, 0), buffer(2, 0)),
        links.keep(part(row, 1), buffer(3, 1)),
    ]
    yield 1
    for h, target in ((0, near), (1, side)):
        loads[h].wait()
        out[h].wait_recv()

        def add(rows, h=h):
            total = buffers[h, rows].astype(WIDE) + buffers[5 + 2 * h, rows].astype(WIDE)
            buffers[h, rows] = total.astype(LOW)

        by_rows(heights[h], add)
        out.append(links.copy(buffer(h, h), buffer(8 + h, h), row=target))
        out[-1].start()
        yield 1
    for h in range(2):
        loads[2 + h].wait()
        out[2 + h].wait_recv()
        out[4 + h].wait_recv()

        def finish(rows, h=h):
            result(
                h,
                rows,
                buffers[2 + h, rows].astype(WIDE)
                + buffers[4 + 2 * h, rows].astype(WIDE)
                + buffers[8 + h, rows].astype(WIDE),
            )

        by_rows(heights[h], finish)
    for copy in out:
        copy.wait_send()


def row_buffers(size, width):
    return pltpu.VMEM((10, halves(size)[0].size, width), LOW)


def scatter_line(links, place, ready, term, ups_in, downs_in, staging, result):
    z, count, turn = place.dp, place.count, place.turn
    pieces, height = ups_in.shape[1:3]
    ups, downs = [None], [None]

    def sends_up(t):
        return (z <= t - 1) & (z < count - 1)

    def sends_down(t):
        return (z >= count - t) & (z > 0)

    def fill(slot, block, arrived):
        def body(i, rows):
            value = term(block, i, rows)
            if arrived is not None:
                value = value + arrived[i, rows].astype(WIDE)
            staging[slot, i, rows] = value.astype(LOW)

        by_pieces(pieces, height, body)

    for t in range(1, count):
        ready(t)
        ready(count - t)
        for which in range(2):
            copies, into = ((ups, ups_in), (downs, downs_in))[which]
            sends = (sends_up, sends_down)[which]
            first = (z == 0, z == count - 1)[which]
            block = (turn(z - t), turn(z + t))[which]
            target = (turn(z + 1), turn(z - 1))[which]
            slot = 2 * which + t % 2
            if t > 2:
                when(sends(t - 2), copies[t - 2].wait_send)
            copy = links.copy(staging.at[slot], into.at[t - 1], dp=target)
            copies.append(copy)

            def begin(copy=copy, slot=slot, block=block):
                fill(slot, block, None)
                copy.start()

            when(sends(t) & first, begin)
            if t > 1:

                def go_on(copy=copy, slot=slot, block=block, before=copies[t - 1], into=into, t=t):
                    before.wait_recv()
                    fill(slot, block, into.at[t - 2])
                    copy.start()

                when(sends(t) & jnp.logical_not(first), go_on)
        yield 1
    ready(0)
    last = count - 1
    from_below, from_above = ups_in.at[last - 1], downs_in.at[last - 1]
    when(z > 0, ups[last].wait_recv)
    when(z < last, downs[last].wait_recv)

    def finish(below, above):
        def body(i, rows):
            value = term(z, i, rows)
            if below:
                value = value + from_below[i, rows].astype(WIDE)
            if above:
                value = value + from_above[i, rows].astype(WIDE)
            result(i, rows, value)

        by_pieces(pieces, height, body)

    when(z == 0, lambda: finish(False, True))
    when((z > 0) & (z < last), lambda: finish(True, True))
    when(z == last, lambda: finish(True, False))
    for t in range(max(1, count - 2), count):
        when(sends_up(t), ups[t].wait_send)
        when(sends_down(t), downs[t].wait_send)


def line_buffers(count, pieces, height, width):
    return [pltpu.VMEM((slots, pieces, height, width), LOW) for slots in (count - 1, count - 1, 4)]


def token_scatter(links, place, partial, ours, theirs, buffers, result):
    out, loads = [], []
    for s in list(range(1, place.count)) + [0]:
        block = place.turn(place.dp - s)
        out.append(
            links.copy(partial.at[block, place.other], theirs.at[block], col=place.other)
        )
        out[-1].start()
        loads.append(links.keep(partial.at[block, place.col], ours.at[block]))
    waited = set()

    def ready(s):
        if s not in waited:
            waited.add(s)
            at = s - 1 if s else place.count - 1
            out[at].wait_recv()
            loads[at].wait()

    def term(block, i, rows):
        return ours[block, rows].astype(WIDE) + theirs[block, rows].astype(WIDE)

    yield 1
    yield from scatter_line(
        links, place, ready, term, *buffers, lambda i, rows, value: result(rows, value)
    )
    for copy in out:
        copy.wait_send()


def call(kernel, name, number, ins, outs, scratch, remote, local):
    return pl.pallas_call(
        kernel,
        in_specs=[VMEM if inside else ANY for _, inside in ins],
        out_specs=[VMEM if inside else ANY for _, _, inside in outs],
        out_shape=[jax.ShapeDtypeStruct(shape, kind) for shape, kind, _ in outs],
        scratch_shapes=list(scratch)
        + [
            pltpu.SemaphoreType.DMA((remote,)),
            pltpu.SemaphoreType.DMA((remote,)),
            pltpu.SemaphoreType.DMA((local,)),
        ],
        compiler_params=pltpu.CompilerParams(
            collective_id=number, has_side_effects=True, vmem_limit_bytes=58 * 1024 * 1024
        ),
        name=name,
    )(*[array for array, _ in ins])


def lanes(index, width):
    return pl.ds(pl.multiple_of(index * width, 128), width)


def strip(index, height, step=16):
    return pl.ds(pl.multiple_of(index * height, step), height)


def combine(earlier, later):
    return (earlier[0] * later[0], later[0] * earlier[1] + later[1])


def scan_rows(decay, value, reverse):
    count = decay.shape[0]
    rows = lax.broadcasted_iota(jnp.int32, decay.shape, 0)
    reach = 1
    while reach < count:
        turn = count - reach if reverse else reach
        inside = rows < count - reach if reverse else rows >= reach
        decay_far = jnp.where(inside, pltpu.roll(decay, turn, 0), 1.0)
        value_far = jnp.where(inside, pltpu.roll(value, turn, 0), 0.0)
        value = decay * value_far + value
        decay = decay * decay_far
        reach *= 2
    return decay, value


def minus_expm1(v):
    series = 1.0 + v / 9.0
    for k in range(8, 1, -1):
        series = 1.0 + (v / k) * series
    return jnp.where(v > -0.5, -v * series, 1.0 - jnp.exp(v))


def each_head(heads, width, body):
    def lap(h, carry):
        body(h, pl.ds(pl.multiple_of(h * width, 128), width))
        return carry

    lax.fori_loop(0, heads, lap, 0)


def carry_over(links, place, ends, table, reverse):
    run([exchange_rows(links, place, lambda q: ends, lambda q: table.at[q])])
    row = place.row
    state = jnp.zeros((1, ends.shape[1]), WIDE)
    for k in range(4):
        q = 3 - k if reverse else k

        def entry(i):
            return table[q, i : i + 1, :]

        reached = q > row if reverse else q < row
        state = jnp.where(reached, entry(0) * state + entry(1), state)
    return state


def recurrence_backward(
    count, taps, proj, side, spots, vectors, blocks, conv_in, in_gate, dec_gate, state_in, entering,
    grad_mixed, branch_out, sums_out, blocks_out, reach, local_grad, branch, ends, table, heads_in,
    heads_here, padded, spread, send, recv, local,
):
    place = Place(count)
    links = Links(send, recv, local)
    greet(place, rows=True)
    tokens, width = side.shape
    heads, block = blocks.shape[0] // 2, blocks.shape[1]
    spot = spots[...]
    starting = spot == 0
    ends[...] = jnp.zeros(ends.shape, WIDE)

    def backwards(h, at):
        rate = vectors[taps + 5 : taps + 6, at]
        decay = jnp.where(starting, 0.0, jnp.exp(rate * dec_gate[:, at]))
        padded[0:tokens, :] = decay
        padded[tokens:, :] = jnp.ones((8, block), WIDE)
        far, grad = scan_rows(padded[1 : tokens + 1, :], grad_mixed[:, at] * side[:, at], True)
        reach[:, at] = far
        local_grad[:, at] = grad
        ends[0:1, at] = decay[0:1, :] * far[0:1, :]
        ends[1:2, at] = decay[0:1, :] * grad[0:1, :]

    each_head(heads, block, backwards)
    own = links.keep(ends, table.at[place.row])
    own.wait()
    heads_here[0:1, :] = carry_over(links, place, ends, table, True)

    def one_head(h, at):
        def vector(i):
            return vectors[i : i + 1, at]

        grad_state = local_grad[:, at] + reach[:, at] * heads_here[0:1, at]
        padded[8:, :] = state_in[:, at]
        padded[7:8, :] = entering[0:1, at]
        grad_decay = grad_state * padded[7 : 7 + tokens, :]
        input_gate, decay_gate, conv = in_gate[:, at], dec_gate[:, at], conv_in[:, at]
        rate = vector(taps + 5)
        log_decay = rate * decay_gate
        decay = jnp.exp(log_decay)
        multiplier = jnp.where(starting, 1.0, jnp.sqrt(minus_expm1(2.0 * log_decay)))
        grad_gated = grad_state * conv
        grad_log = jnp.where(
            starting, 0.0, decay * (grad_decay - grad_gated * input_gate * (decay / multiplier))
        )
        grad_in = grad_gated * multiplier * (input_gate * (1.0 - input_gate))
        grad_gate = grad_log * decay_gate
        grad_dec = grad_gate * rate * (1.0 - decay_gate)
        low = conv.astype(LOW)
        low_in, low_dec = grad_in.astype(LOW), grad_dec.astype(LOW)
        across = (((1,), (1,)), ((), ()))
        along = (((0,), (0,)), ((), ()))
        grad_conv = (
            grad_state * multiplier * input_gate
            + lax.dot_general(low_in, blocks[h], across, preferred_element_type=WIDE)
            + lax.dot_general(low_dec, blocks[heads + h], across, preferred_element_type=WIDE)
        )
        blocks_out[h] = lax.dot_general(low, low_in, along, preferred_element_type=WIDE)
        blocks_out[heads + h] = lax.dot_general(low, low_dec, along, preferred_element_type=WIDE)
        spread[0:8, :] = jnp.zeros((8, block), WIDE)
        spread[8:, :] = vector(0) * grad_conv
        shift = vector(taps + 1)

        def total(values):
            return jnp.sum(values, axis=0, keepdims=True)

        sums_out[0:1, at] = total(grad_conv * (proj[8:, at] + shift))
        for k in range(1, taps):
            kept = jnp.where(spot >= k, grad_conv, 0.0)
            sums_out[k : k + 1, at] = total(kept * (proj[8 - k : 8 - k + tokens, at] + shift))
            spread[8 - k : 8 - k + tokens, :] += vector(k) * kept
        branch[:, at] = spread[8:, :]
        heads_in[0, :, at] = spread[0:8, :]
        sums_out[taps : taps + 1, at] = total(grad_conv)
        sums_out[taps + 1 : taps + 2, at] = total(spread[...])
        sums_out[taps + 2 : taps + 3, at] = total(grad_in)
        sums_out[taps + 3 : taps + 4, at] = total(grad_dec)
        sums_out[taps + 4 : taps + 5, at] = total(grad_gate)
        sums_out[taps + 5 :, at] = jnp.zeros((sums_out.shape[0] - taps - 5, block), WIDE)

    each_head(heads, block, one_head)
    row = place.row
    before = lax.rem(row + 3, 4)
    owed = links.copy(heads_in.at[0], heads_in.at[1], row=before)
    owed.start()
    owed.wait_recv()
    owed.wait_send()

    def finish(h, at):
        last = jnp.where(row < 3, heads_in[1, :, at], 0.0)
        branch[tokens - 8 :, at] += last
        branch_out[:, at] = branch[:, at].astype(LOW)

    each_head(heads, block, finish)


def norm_rule(rows, grad, value, gain, sums, at):
    full = value.shape[1]
    inverse = lax.rsqrt(jnp.sum(value * value, axis=1, keepdims=True) / full + epsilon)
    scaled = grad * (1.0 + gain)
    inner = jnp.sum(scaled * value, axis=1, keepdims=True)
    sums[at : at + 1, :] += jnp.sum(grad * value * inverse, axis=0, keepdims=True)
    return inverse * scaled - value * (inverse * inverse * inverse) * (inner / full)


def second_norm_back(
    count, grad_partial, cot_all, middle, vectors, down_partial, grad_middle, grad_all, sums, down_out,
    ours, theirs, ups, downs, staging, cot, low, buffers, send, recv, local,
):
    place = Place(count)
    links = Links(send, recv, local)
    greet(place, rows=True, line=True, cores=True)
    row, z, col = place.row, place.dp, place.col
    quarter, full = middle.shape
    narrow = full // 4
    tall = 4 * quarter
    down_halves = halves(down_partial.shape[0])
    sums[...] = jnp.zeros(sums.shape, WIDE)
    gain = vectors[3:4, :]
    load = links.keep(cot_all.at[strip(2 * z + col, quarter)], cot)

    def back(rows, grad):
        own = cot[rows].astype(WIDE)
        total = own + norm_rule(rows, grad, middle[rows], gain, sums, 0)
        sums[1:2, :] += jnp.sum(total, axis=0, keepdims=True)
        sums[2:3, :] += jnp.sum(own, axis=0, keepdims=True)
        grad_middle[rows] = total
        low[rows] = total.astype(LOW)

    def tokens():
        load.wait()
        yield from token_scatter(
            links, place, grad_partial, ours, theirs, (ups, downs, staging), back
        )

        def block(q):
            return grad_all.at[strip(4 * col + q, quarter)]

        mine = links.keep(low.at[:, lanes(row, narrow)], block(row))
        yield from exchange_rows(
            links, place, lambda q: low.at[:, lanes(q, narrow)], block
        )
        mine.wait()
        both = grad_all.at[strip(col, tall)]
        share = links.copy(both, both, col=place.other)
        share.start()
        yield 1
        share.wait_recv()
        share.wait_send()

    def keep_down(h, rows, value):
        down_out[pl.ds(pl.multiple_of(down_halves[h].start + rows.start, 16), rows.size)] = value

    run(
        [
            tokens(),
            scatter_rows(
                links,
                place,
                lambda q, h: down_partial.at[down_halves[h], lanes(q, narrow)],
                buffers,
                keep_down,
            ),
        ]
    )


def mixed_and_output(
    count, mixed_partial, out_partial, middle, vectors, gate_partial, mixed_out, layer_out, gate_out,
    mixed_buffers, ours, theirs, ups, downs, staging, low, gate_buffers, send, recv, local,
):
    place = Place(count)
    links = Links(send, recv, local)
    greet(place, rows=True, line=True, cores=True)
    row = place.row
    quarter, full = middle.shape
    narrow = full // 4
    shift = vectors[2:3, :]
    half = mixed_partial.shape[0] // 8
    gate_half = gate_partial.shape[0] // 8

    def keep_mixed(h, rows, value):
        mixed_out[h, rows] = value

    def keep_gate(h, rows, value):
        gate_out[h, rows] = value.astype(LOW)

    def finish(rows, value):
        low[rows] = (middle[rows] + value + shift).astype(LOW)

    def tokens():
        yield from token_scatter(
            links, place, out_partial, ours, theirs, (ups, downs, staging), finish
        )
        mine = links.keep(low.at[:, lanes(row, narrow)], layer_out.at[row])
        yield from exchange_rows(
            links, place, lambda q: low.at[:, lanes(q, narrow)], lambda q: layer_out.at[q]
        )
        mine.wait()

    run(
        [
            scatter_rows(
                links,
                place,
                lambda q, h: mixed_partial.at[strip(2 * q + h, half)],
                mixed_buffers,
                keep_mixed,
            ),
            tokens(),
            scatter_rows(
                links,
                place,
                lambda q, h: gate_partial.at[strip(2 * q + h, gate_half)],
                gate_buffers,
                keep_gate,
            ),
        ]
    )


def spread_gradients(
    count, blocks, up_partial, output_partial, gate_own, all_out, up_out, output_out, gate_out,
    up_buffers, ups, downs, staging, own, send, recv, local,
):
    place = Place(count)
    links = Links(send, recv, local)
    greet(place, rows=True, line=True)
    row, z = place.row, place.dp
    half = up_partial.shape[0] // 8
    mine = links.keep(blocks.at[row], all_out.at[row])
    kept = links.keep(gate_own.at[z], gate_out.at[z])
    load = links.keep(output_partial, own)

    def keep_up(h, rows, value):
        up_out[h, rows] = value.astype(LOW)

    def keep_output(i, rows, value):
        output_out[rows] = value

    def outputs():
        load.wait()
        yield from scatter_line(
            links,
            place,
            lambda s: None,
            lambda b, i, rows: own[b, rows].astype(WIDE),
            ups,
            downs,
            staging,
            keep_output,
        )

    run(
        [
            exchange_rows(links, place, lambda q: blocks.at[q], lambda q: all_out.at[q]),
            outputs(),
            exchange_line(
                links, place, lambda b: gate_own.at[b], lambda b: gate_out.at[b]
            ),
            scatter_rows(
                links,
                place,
                lambda q, h: up_partial.at[strip(2 * q + h, half)],
                up_buffers,
                keep_up,
            ),
        ]
    )
    mine.wait()
    kept.wait()


def first_norm_back(
    count, grad_partial, x_own, grad_middle, vectors, proj_partial, up_own, sums_in, channel_in,
    hidden_in, block_in, grad_out, proj_out, up_out, width_sums, channel_sums, block_out, hidden_sums,
    theirs, ours, added,
    row_buffer, x, result, sums, proj_own, proj_ups, proj_downs, proj_staging, proj_low, width_table,
    width_line, width_part, channel_table, channel_line, hidden_table, block_buffers, block_sum, block_ups, block_downs,
    block_staging, block_low, send, recv, local,
):
    place = Place(count)
    links = Links(send, recv, local)
    greet(place, rows=True, line=True, cores=True)
    row, z, col = place.row, place.dp, place.col
    quarter, full = grad_middle.shape
    narrow = full // 4
    gain = vectors[0:1, :]
    load_x = links.keep(x_own, x)
    load_proj = [links.keep(proj_partial.at[:, b], proj_own.at[b]) for b in range(count)]
    kept = links.keep(up_own.at[z], up_out.at[z])

    def tokens():
        share = links.copy(grad_partial.at[place.other], theirs, col=place.other)
        share.start()
        load = links.keep(grad_partial.at[col], ours)
        yield 1
        share.wait_recv()
        load.wait()

        def add(rows):
            for q in range(4):
                total = ours[q, rows].astype(WIDE) + theirs[q, rows].astype(WIDE)
                added[q, rows] = total.astype(LOW)

        by_rows(quarter, add)
        load_x.wait()
        sums[0:3, :] = sums_in[0:3, :]
        sums[3:, :] = jnp.zeros((sums.shape[0] - 3, full), WIDE)
        half = quarter // 2

        def back(h, rows, grad):
            here = pl.ds(pl.multiple_of(rows.start + half * h, 16), rows.size)
            value = x[here].astype(WIDE)
            total = grad_middle[here] + norm_rule(rows, grad, value, gain, sums, 3)
            for q in range(4):
                result[q, here] = total[:, q * narrow : (q + 1) * narrow]

        yield from scatter_rows(
            links,
            place,
            lambda q, h: added.at[q, pl.ds(half * h, half)],
            row_buffer,
            back,
        )
        share.wait_send()
        mine = links.keep(result.at[row], grad_out.at[row])
        yield from exchange_rows(
            links, place, lambda q: result.at[q], lambda q: grad_out.at[q]
        )
        mine.wait()
        for q in range(4):
            width_part[q] = sums[:, q * narrow : (q + 1) * narrow]
        own = links.keep(width_part.at[row], width_table.at[row])
        yield from exchange_rows(
            links, place, lambda q: width_part.at[q], lambda q: width_table.at[q]
        )
        own.wait()
        width_line[z] = width_table[0] + width_table[1] + width_table[2] + width_table[3]
        yield from exchange_line(
            links, place, lambda b: width_line.at[z], lambda b: width_line.at[b]
        )
        total = width_line[0]
        for b in range(1, count):
            total = total + width_line[b]
        width_sums[0] = total
        yield 1
        last = links.copy(width_sums.at[0], width_sums.at[1], col=place.other)
        last.start()
        yield 1
        last.wait_recv()
        last.wait_send()

    def projections():
        for load in load_proj:
            load.wait()

        def keep_proj(i, rows, value):
            proj_low[i, rows] = value.astype(LOW)

        yield from scatter_line(
            links,
            place,
            lambda s: None,
            lambda b, i, rows: proj_own[b, i, rows].astype(WIDE),
            proj_ups,
            proj_downs,
            proj_staging,
            keep_proj,
        )
        mine = links.keep(proj_low.at[row], proj_out.at[row])
        yield from exchange_rows(
            links, place, lambda q: proj_low.at[q], lambda q: proj_out.at[q]
        )
        mine.wait()

    def hidden():
        own = links.keep(hidden_in, hidden_table.at[row])
        yield from exchange_rows(
            links, place, lambda q: hidden_in, lambda q: hidden_table.at[q]
        )
        own.wait()
        hidden_sums[...] = hidden_table[0] + hidden_table[1] + hidden_table[2] + hidden_table[3]

    def channels():
        own = links.keep(channel_in, channel_table.at[row])
        yield from exchange_rows(
            links, place, lambda q: channel_in, lambda q: channel_table.at[q]
        )
        own.wait()
        channel_line[z] = (
            channel_table[0] + channel_table[1] + channel_table[2] + channel_table[3]
        )
        yield from exchange_line(
            links, place, lambda b: channel_line.at[z], lambda b: channel_line.at[b]
        )
        total = channel_line[0]
        for b in range(1, count):
            total = total + channel_line[b]
        channel_sums[...] = total

    def blocks():
        def keep_rows(h, rows, value):
            block_sum[h, rows] = value

        yield from scatter_rows(
            links,
            place,
            lambda q, h: block_in.at[q, h],
            block_buffers,
            keep_rows,
        )
        length = block_sum.shape[1] * 2 // count
        middle = count // 2

        def term(b, i, rows):
            at = pl.multiple_of(lax.rem(b, middle) * length + rows.start, 8)
            return block_sum[lax.div(b, middle), pl.ds(at, rows.size)]

        def keep_line(i, rows, value):
            block_low[rows] = value.astype(LOW)

        yield from scatter_line(
            links, place, lambda s: None, term, block_ups, block_downs, block_staging, keep_line
        )
        mine = links.keep(block_low, block_out.at[row])
        yield from exchange_rows(links, place, lambda q: block_low, lambda q: block_out.at[q])
        mine.wait()

    run(
        [
            tokens(),
            projections(),
            exchange_line(links, place, lambda b: up_own.at[b], lambda b: up_out.at[b]),
            channels(),
            hidden(),
            blocks(),
        ]
    )
    kept.wait()


def advance(*tasks):
    for task in tasks:
        next(task, None)


def finish(*tasks):
    run(tasks)


def gelu(v):
    return 0.5 * v * (1.0 + jnp.tanh(ROOT * (v + CUBE * (v * v * v))))


def gelu_slope(v):
    t = jnp.tanh(ROOT * (v + CUBE * (v * v * v)))
    return 0.5 * (1.0 + t) + 0.5 * v * (1.0 - t * t) * (ROOT * (1.0 + 3.0 * CUBE * (v * v)))


def block_of(blocks, h):
    width = blocks.shape[-1]
    return blocks[h].reshape(width, width)


def forward(
    count, taps, x, cot, wxy, wout, wgate, wup, wdown, blk, cvec, wvec, spots,
    nf_out, x_out, cot_own, wxy_out, wout_out, gate_own, up_own, down_all, blocks_out, vectors_out,
    width_out, branch_out, gelu_out, side_out, conv_out, in_out, dec_out, state_out, entering_out,
    mixed_out, middle_out, normed_out,
    x_all, nf, wxy_all, wout_all, blocks, cvec_all, wvec_all, vectors, width, stage, arrived, branch,
    gelu_in, side, conv, in_gate, dec_gate, state, running, local_state, ends, table, entering, mixed,
    mixed_all, partial, theirs, here, wide, middle, normed, gate_here, up_here, down_here, cot_here,
    send, recv, local,
):
    place = Place(count)
    links = Links(send, recv, local)
    row, z, col = place.row, place.dp, place.col
    greet(place, rows=True, line=True, cores=True)
    tall, narrow = x.shape
    full = 4 * narrow
    half, quarter = tall // 2, tall // 4
    depth, part = wxy.shape[1], wxy.shape[2] // 2
    tokens, steps = 2 * tall, tall // 2
    heads, block = blocks.shape[0] // 2, blocks.shape[-1]
    share = blocks.shape[3]
    kept = []

    def keep(src, dst):
        kept.append(links.keep(src, dst))
        return kept[-1]

    def projections():
        def at(q, b):
            return wxy_all.at[q, strip(b, depth, 8)]

        mine = links.keep(wxy.at[row], at(row, z))
        yield from exchange_rows(links, place, lambda q: wxy.at[q], lambda q: at(q, z))
        mine.wait()

        def piece(b):
            return wxy_all.at[:, strip(b, depth, 8)]

        yield from gather_line(links, place, piece(z), piece)

    def inputs():
        def at(q, core):
            return x_all.at[strip(core, tall), lanes(q, narrow)]

        mine = links.keep(x, at(row, col))
        shared = [links.copy(x, at(row, col), col=place.other)]
        shared[0].start()
        yield from gather_rows(
            links,
            place,
            lambda h: x.at[pl.ds(half * h, half)],
            lambda q, h: x_all.at[strip(2 * col + h, half), lanes(q, narrow)],
        )
        for k in range(1, 4):
            q = place.near[k]
            shared.append(links.copy(at(q, col), at(q, col), col=place.other))
            shared[-1].start()
        yield 1
        mine.wait()
        for copy in shared:
            copy.wait_recv()
        for copy in shared:
            copy.wait_send()

    def channel_vectors():
        keep(cvec, cvec_all.at[z])
        yield from exchange_line(links, place, lambda b: cvec, lambda b: cvec_all.at[b])

    def width_vectors():
        mine = links.keep(wvec, wvec_all.at[row, z])
        yield from exchange_line(links, place, lambda b: wvec, lambda b: wvec_all.at[row, b])
        mine.wait()
        yield from exchange_rows(
            links, place, lambda q: wvec_all.at[row], lambda q: wvec_all.at[q]
        )

    def gate_blocks():
        split = blocks.shape[2] > 1
        own = row if split else 0
        mine = links.keep(blk, blocks.at[:, z, own])
        yield from exchange_line(links, place, lambda b: blk, lambda b: blocks.at[:, b, own])
        mine.wait()
        middle = count // 2
        if split:

            def at(q, h):
                return blocks.at[:, pl.ds(middle * h, middle), q]

            yield from gather_rows(links, place, lambda h: at(row, h), at)

    def hidden_rows():
        parts = halves(wdown.shape[0])
        mine = Relay(links, wdown, down_here, down_all.at[:, lanes(row, narrow)])
        kept.append(mine)
        yield from gather_rows(
            links,
            place,
            lambda h: wdown.at[parts[h]],
            lambda q, h: down_all.at[parts[h], lanes(q, narrow)],
        )

    def cotangent_rows():
        def spot(q):
            return cot_own.at[:, lanes(q, narrow)]

        mine = Relay(links, cot.at[strip(row, quarter)], cot_here, spot(row))
        yield from exchange_rows(links, place, lambda q: cot.at[strip(q, quarter)], spot)
        mine.wait()

    def hidden_columns(matrix, buffer, own):
        mine = Relay(links, matrix.at[z], buffer, own.at[z])
        yield from exchange_line(links, place, lambda b: matrix.at[b], lambda b: own.at[b])
        mine.wait()

    def output_rows():
        at = wout.shape[0]
        mine = links.keep(wout, wout_all.at[strip(z, at)])
        yield from gather_line(links, place, wout, lambda b: wout_all.at[strip(b, at)])
        mine.wait()

    weights, rows_in = projections(), inputs()
    vectors_in, widths_in, blocks_in = channel_vectors(), width_vectors(), gate_blocks()
    cot_in, output_in, down_in = cotangent_rows(), output_rows(), hidden_rows()
    gate_in = hidden_columns(wgate, gate_here, gate_own)
    up_in = hidden_columns(wup, up_here, up_own)
    advance(weights, rows_in, widths_in, vectors_in, blocks_in, cot_in)
    advance(weights, widths_in, vectors_in, blocks_in)
    finish(widths_in, vectors_in)
    for copy in kept:
        copy.wait()
    kept.clear()

    for b in range(count):
        size = vectors.shape[1] // count
        vectors[:, b * size : (b + 1) * size] = cvec_all[b, :, :size]
        for q in range(4):
            at = q * narrow + b * depth
            width[:, at : at + depth] = wvec_all[q, b, :, :depth]
    keep(vectors, vectors_out)
    keep(width, width_out)
    advance(rows_in)
    advance(weights)
    finish(rows_in)
    advance(down_in)
    keep(x_all.at[strip(4 * col + row, quarter)], x_out)

    nf[0:16, :] = jnp.zeros((16, full), LOW)

    def first_norm(rows):
        value = x_all[rows].astype(WIDE)
        mean = jnp.sum(value * value, axis=1, keepdims=True) / full
        value = value * lax.rsqrt(mean + epsilon) * (1.0 + width[0:1, :])
        nf[pl.ds(pl.multiple_of(rows.start + 16, 16), rows.size)] = value.astype(LOW)

    by_rows(tokens, first_norm)
    keep(nf.at[pl.ds(16, tokens)], nf_out)
    advance(weights, blocks_in, cot_in)
    finish(blocks_in)
    keep(blocks, blocks_out)
    finish(weights, cot_in)
    keep(wxy_all, wxy_out)

    advance(output_in)
    advance(down_in)
    out = []
    for k in (3, 2, 1, 0):
        q = place.near[k]

        def product(k=k, q=q):
            stage[k] = jnp.dot(
                nf[pl.ds(pl.multiple_of(q * steps, 16), steps + 16), :],
                wxy_all[...].astype(LOW).reshape(full, 2 * part),
                preferred_element_type=WIDE,
            )

        product()
        source = stage.at[k, pl.ds(8, steps + 8)]
        if k:
            out.append(links.copy(source, arrived.at[row], row=q))
            out[-1].start()
        else:
            mine = links.keep(source, arrived.at[row])
    advance(output_in, gate_in)
    mine.wait()
    for copy in out:
        copy.wait_recv()
    finish(down_in)
    for copy in out:
        copy.wait_send()

    spot = spots[...]
    starting = spot == 0
    for q in range(4):
        at = slice(q * part, (q + 1) * part)
        branch[:, at] = arrived[q, :, :part]
        gelu_in[:, at] = arrived[q, 8:, part:] + vectors[taps + 2 : taps + 3, at]
    keep(branch, branch_out)
    keep(gelu_in, gelu_out)
    ends[...] = jnp.zeros(ends.shape, WIDE)
    entering[...] = jnp.zeros(ends.shape, WIDE)

    def one_head(h, at):
        def vector(i):
            return vectors[i : i + 1, at]

        conv_here = vector(taps) + vector(0) * (branch[8:, at] + vector(taps + 1))
        for k in range(1, taps):
            earlier = branch[8 - k : 8 - k + steps, at] + vector(taps + 1)
            conv_here = conv_here + vector(k) * jnp.where(spot >= k, earlier, 0.0)
        conv[:, at] = conv_here
        low = conv_here.astype(LOW)
        input_gate = jax.nn.sigmoid(
            jnp.dot(low, block_of(blocks, h), preferred_element_type=WIDE) + vector(taps + 3)
        )
        decay_gate = jax.nn.sigmoid(
            jnp.dot(low, block_of(blocks, heads + h), preferred_element_type=WIDE)
            + vector(taps + 4)
        )
        in_gate[:, at] = input_gate
        dec_gate[:, at] = decay_gate
        log_decay = vector(taps + 5) * decay_gate
        decay = jnp.where(starting, 0.0, jnp.exp(log_decay))
        multiplier = jnp.where(starting, 1.0, jnp.sqrt(minus_expm1(2.0 * log_decay)))
        reach, value = scan_rows(decay, multiplier * input_gate * conv_here, False)
        running[:, at] = reach
        local_state[:, at] = value
        ends[0:1, at] = reach[steps - 1 :, :]
        ends[1:2, at] = value[steps - 1 :, :]
        side[:, at] = gelu(gelu_in[:, at])

    each_head(heads, block, one_head)
    for scratch, output in (
        (conv, conv_out), (in_gate, in_out), (dec_gate, dec_out), (side, side_out),
    ):
        keep(scratch, output)
    own = links.keep(ends, table.at[row])
    advance(output_in)
    own.wait()
    entering[0:1, :] = carry_over(links, place, ends, table, False)

    def mix(h, at):
        value = local_state[:, at] + running[:, at] * entering[0:1, at]
        state[:, at] = value
        mixed[:, at] = (value * side[:, at]).astype(LOW)

    each_head(heads, block, mix)
    mine = links.keep(mixed, mixed_all.at[strip(row, steps)])
    mixes = gather_rows(
        links,
        place,
        lambda h: mixed.at[pl.ds(steps // 2 * h, steps // 2)],
        lambda q, h: mixed_all.at[strip(2 * q + h, steps // 2)],
    )
    advance(mixes)
    keep(state, state_out)
    keep(entering, entering_out)
    finish(output_in)
    keep(wout_all, wout_out)
    advance(mixes, up_in)
    finish(mixes)
    mine.wait()
    keep(mixed_all, mixed_out)

    def product_rows(first):
        def body(i, carry):
            rows = pl.ds(pl.multiple_of(first * tall + i * steps, 16), steps)
            partial[rows] = jnp.dot(mixed_all[rows], wout_all[...], preferred_element_type=WIDE)
            return carry

        lax.fori_loop(0, tall // steps, body, 0)

    product_rows(place.other)
    swap = links.copy(partial.at[strip(place.other, tall)], theirs, col=place.other)
    swap.start()
    product_rows(col)
    swap.wait_recv()

    def add(rows):
        at = pl.ds(pl.multiple_of(col * tall + rows.start, 16), rows.size)
        here[rows] = partial[at] + theirs[rows] + x_all[at, lanes(row, narrow)].astype(WIDE)

    by_rows(tall, add)

    def quarter_of(q):
        return here.at[strip(q, quarter)]

    mine = links.keep(quarter_of(row), wide.at[:, lanes(row, narrow)])
    middles = exchange_rows(links, place, quarter_of, lambda q: wide.at[:, lanes(q, narrow)])
    advance(middles)
    mine.wait()
    finish(middles)
    swap.wait_send()

    def second_norm(rows):
        value = wide[rows] + width[1:2, :]
        middle[rows] = value
        mean = jnp.sum(value * value, axis=1, keepdims=True) / full
        normed[rows] = (value * lax.rsqrt(mean + epsilon) * (1.0 + width[3:4, :])).astype(LOW)

    by_rows(quarter, second_norm)
    keep(middle, middle_out)
    keep(normed, normed_out)
    finish(gate_in, up_in)
    for copy in kept:
        copy.wait()


def feed_forward(
    count, normed, cot, wgate, up_own, wdown, biases, normed_all, cot_all, gate_all, up_all, hidden_out,
    gate_out, up_out, sums, gate_w, up_w, down_w, piece, gate_v, up_v, grad_v, hidden, grad_gate,
    grad_up, cot_here, normed_here, send, recv, local,
):
    place = Place(count)
    links = Links(send, recv, local)
    row, z, col = place.row, place.dp, place.col
    greet(place, rows=True, line=True, cores=True)
    quarter, full = normed.shape
    narrow, pair = full // 4, 2 * quarter
    units = wdown.shape[0]
    middle = count // 2
    kept = [
        links.keep(wgate, gate_w.at[row]),
        links.keep(up_own, up_w.at[row]),
    ]
    load = links.keep(wdown, down_w)

    def tokens(own, buffer, whole):
        def at(b):
            return whole.at[strip(2 * b + col, quarter)]

        relay = Relay(links, own, buffer, at(z))
        return LineGather(links, place, own, at), relay

    def columns_of(own, whole):
        yield from gather_rows(
            links,
            place,
            lambda h: own.at[pl.ds(middle * h, middle)],
            lambda q, h: whole.at[q, pl.ds(middle * h, middle)],
        )

    def neighbours(step, body):
        if step == 0:
            body(z)
            return

        def lap(i, carry):
            b = z - step + 2 * step * i
            pl.when((b >= 0) & (b < count))(lambda: body(place.turn(b)))
            return carry

        lax.fori_loop(0, 2, lap, 0)

    def with_piece(source, body):
        k, links.kept = links.kept, links.kept + 1

        def inner(b):
            load = pltpu.make_async_copy(source.at[strip(b, pair)], piece, links.local.at[k])
            load.start()
            load.wait()
            body(strip(b, pair))

        return inner

    def inward(whole, i, values):
        def body(rows):
            weight = whole[...].astype(LOW).reshape(full, units)
            values[rows] = (
                jnp.dot(piece[...], weight, preferred_element_type=WIDE) + biases[i : i + 1, :]
            )

        return body

    def backward(rows):
        grad_v[rows] = lax.dot_general(
            piece[...], down_w[...], (((1,), (1,)), ((), ())), preferred_element_type=WIDE
        )

    def outward(rows):
        def body(inner):
            at = pl.ds(pl.multiple_of(rows.start + inner.start, 16), inner.size)
            gate, up, grad = gate_v[at], up_v[at], grad_v[at]
            t = jnp.tanh(ROOT * (gate + CUBE * (gate * gate * gate)))
            side = 0.5 * gate * (1.0 + t)
            slope = 0.5 * (1.0 + t) + 0.5 * gate * (1.0 - t * t) * (
                ROOT * (1.0 + 3.0 * CUBE * (gate * gate))
            )
            hidden[at] = (side * up).astype(LOW)
            gate, up = grad * up * slope, grad * side
            grad_gate[at] = gate.astype(LOW)
            grad_up[at] = up.astype(LOW)
            sums[0:1, :] += jnp.sum(gate, axis=0, keepdims=True)
            sums[1:2, :] += jnp.sum(up, axis=0, keepdims=True)

        by_rows(pair, body)

    gates, ups = columns_of(wgate, gate_w), columns_of(up_own, up_w)
    cots, cot_relay = tokens(cot, cot_here, cot_all)
    norms, norm_relay = tokens(normed, normed_here, normed_all)
    cots.start()
    advance(gates, ups)
    cot_relay.wait()
    sums[...] = jnp.zeros(sums.shape, WIDE)
    load.wait()
    cots.ready(0)
    back = with_piece(cot_all, backward)
    neighbours(0, back)
    into = with_piece(normed_all, inward(gate_w, 0, gate_v))
    for step in range(1, count):
        cots.step(step)
        if step == 1:
            norms.start()
        else:
            norms.step(step - 1)
        cots.ready(step)
        neighbours(step, back)
    advance(gates, ups)
    norm_relay.wait()
    finish(gates)
    for copy in kept:
        copy.wait()
    kept.clear()
    kept.append(links.keep(gate_w, gate_all))
    for step in range(count - 1):
        norms.ready(step)
        neighbours(step, into)
    norms.step(count - 1)
    norms.ready(count - 1)
    neighbours(count - 1, into)
    finish(ups)
    kept.append(links.keep(up_w, up_all))
    into_up = with_piece(normed_all, inward(up_w, 1, up_v))

    def last(b, carry):
        into_up(b)
        outward(strip(b, pair))
        return carry

    lax.fori_loop(0, count, last, 0)
    cots.close()
    norms.close()
    kept.append(links.keep(hidden, hidden_out))
    kept.append(links.keep(grad_gate, gate_out))
    kept.append(links.keep(grad_up, up_out))
    for copy in kept:
        copy.wait()


def times(piece, matrix):
    return jnp.dot(piece, matrix, preferred_element_type=WIDE)


def times_flipped(piece, matrix):
    return lax.dot_general(piece, matrix, (((1,), (1,)), ((), ())), preferred_element_type=WIDE)


def left_product(left, right):
    return lax.dot_general(left, right, (((0,), (0,)), ((), ())), preferred_element_type=WIDE)


def side_by_side(blocks):
    return jnp.concatenate([blocks[i] for i in range(blocks.shape[0])], axis=1)


def columns(matrix, parts):
    width = matrix.shape[1] // parts
    return jnp.stack([matrix[:, i * width : (i + 1) * width] for i in range(parts)])


def padded_rows(rows, height, width):
    return jnp.pad(rows, ((0, height - rows.shape[0]), (0, width - rows.shape[1])))


def rounded(values):
    return lax.reduce_precision(values, 8, 7)


def round_up(size, step):
    return -(-size // step) * step


def shards(
    inputs,
    positions,
    branch_matrix,
    gelu_matrix,
    output_matrix,
    gate_matrix,
    up_matrix,
    down_matrix,
    input_blocks,
    decay_blocks,
    conv_taps,
    conv_bias,
    branch_bias,
    gelu_bias,
    input_bias,
    decay_bias,
    decay_param,
    output_bias,
    gate_bias,
    up_bias,
    down_bias,
    norm_first,
    norm_second,
    cotangent,
):
    count, rows_count, cores = lax.axis_size("dp"), lax.axis_size("row"), lax.axis_size("col")
    place_dp, place_row = lax.axis_index("dp"), lax.axis_index("row")
    tall, narrow = inputs.shape
    quarter, full, tokens = tall // rows_count, narrow * rows_count, tall * cores
    depth, width = branch_matrix.shape
    part = width // rows_count
    hidden_part = down_matrix.shape[0]
    heads, block_part, block = input_blocks.shape
    taps = conv_taps.shape[0]
    steps = positions.shape[0]
    splits = rows_count if block_part % (16 * rows_count) == 0 else 1
    share = block_part // splits
    back_share = block_part // rows_count
    remote, local = 64 + 24 * count, 40 + 6 * count

    wxy = jnp.concatenate(
        (columns(branch_matrix.astype(LOW), rows_count), columns(gelu_matrix.astype(LOW), rows_count)),
        axis=2,
    )
    if depth % 16:
        wxy = wxy.astype(WIDE)
    blocks_low = jnp.concatenate((input_blocks, decay_blocks), axis=0).astype(LOW)
    blk = lax.dynamic_slice_in_dim(
        blocks_low, place_row * share if splits > 1 else 0, share, 1
    )
    channel_rows = jnp.concatenate(
        (
            conv_taps,
            jnp.stack((conv_bias, branch_bias, gelu_bias, input_bias, decay_bias)),
        ),
        axis=0,
    )
    decay_raw = rounded(decay_param)
    channel_rows = jnp.concatenate(
        (rounded(channel_rows), -8.0 * jax.nn.softplus(decay_raw)[None, :]), axis=0
    )
    channel_size = channel_rows.shape[1]
    cvec = padded_rows(
        channel_rows,
        round_up(taps + 6, 8),
        round_up(channel_size, 128),
    )
    wvec = padded_rows(
        rounded(jnp.stack((norm_first, output_bias, down_bias, norm_second))),
        8,
        round_up(depth, 128),
    )
    spots = positions[:, None]
    heads_all = 2 * heads
    whole_tokens = ((tokens, full), LOW, False)
    wide_tokens = ((steps, width), WIDE, False)
    nf_shape = pltpu.VMEM((16 + tokens, full), LOW)
    wxy_kind = wxy.dtype
    tokens_scratch = pltpu.VMEM((steps, width), WIDE)
    eight_rows = pltpu.VMEM((8, width), WIDE)
    table_rows = pltpu.VMEM((rows_count, 8, width), WIDE)
    blocks_shape = (heads_all, count, splits, share, block)
    hidden_shape = (rows_count, count, depth, hidden_part)
    here_scratch = pltpu.VMEM((tall, narrow), WIDE)
    (
        normed_first, x_own, cot_own, wxy_all, wout_all, gate_own, up_own, down_all, blocks, vectors,
        width_all, branch, gelu_in, side, conv, input_gate, decay_gate, state, entering, mixed_all,
        middle, normed_own,
    ) = call(
        functools.partial(forward, count, taps),
        "forward",
        1,
        [
            (inputs, False),
            (cotangent, False),
            (wxy, False),
            (output_matrix.astype(LOW), False),
            (columns(gate_matrix.astype(LOW), count).astype(wxy_kind), False),
            (columns(up_matrix.astype(LOW), count).astype(wxy_kind), False),
            (down_matrix.astype(LOW), False),
            (blk, False),
            (cvec, False),
            (wvec, False),
            (spots, True),
        ],
        [
            whole_tokens,
            ((quarter, full), LOW, False),
            ((quarter, full), LOW, False),
            ((rows_count, count * depth, 2 * part), wxy_kind, False),
            ((width, narrow), LOW, False),
            (hidden_shape[1:], wxy_kind, False),
            (hidden_shape[1:], wxy_kind, False),
            ((hidden_part, full), LOW, False),
            (blocks_shape, LOW, False),
            ((cvec.shape[0], width), WIDE, False),
            ((8, full), WIDE, False),
            ((steps + 8, width), WIDE, False),
            wide_tokens,
            wide_tokens,
            wide_tokens,
            wide_tokens,
            wide_tokens,
            wide_tokens,
            ((8, width), WIDE, False),
            ((tokens, width), LOW, False),
            ((quarter, full), WIDE, False),
            ((quarter, full), LOW, False),
        ],
        [
            pltpu.VMEM((tokens, full), LOW),
            nf_shape,
            pltpu.VMEM((rows_count, count * depth, 2 * part), wxy_kind),
            pltpu.VMEM((width, narrow), LOW),
            pltpu.VMEM(blocks_shape, LOW),
            pltpu.VMEM((count,) + cvec.shape, WIDE),
            pltpu.VMEM((rows_count, count) + wvec.shape, WIDE),
            pltpu.VMEM((cvec.shape[0], width), WIDE),
            pltpu.VMEM((8, full), WIDE),
            pltpu.VMEM((rows_count, steps + 16, 2 * part), WIDE),
            pltpu.VMEM((rows_count, steps + 8, 2 * part), WIDE),
            pltpu.VMEM((steps + 8, width), WIDE),
            tokens_scratch,
            tokens_scratch,
            tokens_scratch,
            tokens_scratch,
            tokens_scratch,
            tokens_scratch,
            tokens_scratch,
            tokens_scratch,
            eight_rows,
            table_rows,
            eight_rows,
            pltpu.VMEM((steps, width), LOW),
            pltpu.VMEM((tokens, width), LOW),
            pltpu.VMEM((tokens, narrow), WIDE),
            here_scratch,
            here_scratch,
            pltpu.VMEM((quarter, full), WIDE),
            pltpu.VMEM((quarter, full), WIDE),
            pltpu.VMEM((quarter, full), LOW),
            pltpu.VMEM((depth, hidden_part), wxy_kind),
            pltpu.VMEM((depth, hidden_part), wxy_kind),
            pltpu.VMEM((hidden_part, narrow), LOW),
            pltpu.VMEM((quarter, narrow), LOW),
        ],
        remote,
        local,
    )
    wxy_all = wxy_all.reshape(full, 2 * part).astype(LOW)
    blocks = blocks.reshape(heads_all, block, block)
    gelu_pull = jax.vjp(jax.nn.gelu, gelu_in)[1]

    hidden_tokens = cores * count * quarter
    units_rows = ((hidden_tokens, hidden_part), LOW, False)
    biases = padded_rows(rounded(jnp.stack((gate_bias, up_bias))), 8, hidden_part)
    weight_scratch = pltpu.VMEM(hidden_shape, wxy_kind)
    units_wide = pltpu.VMEM((hidden_tokens, hidden_part), WIDE)
    units_low = pltpu.VMEM((hidden_tokens, hidden_part), LOW)
    (
        normed_second, cot_all, gate_all, up_all, hidden, grad_gate_low, grad_up_low, hidden_part_sums,
    ) = call(
        functools.partial(feed_forward, count),
        "feed_forward",
        2,
        [
            (normed_own, False),
            (cot_own, False),
            (gate_own, False),
            (up_own, False),
            (down_all, False),
            (biases, True),
        ],
        [
            ((hidden_tokens, full), LOW, False),
            ((hidden_tokens, full), LOW, False),
            (hidden_shape, wxy_kind, False),
            (hidden_shape, wxy_kind, False),
            units_rows,
            units_rows,
            units_rows,
            ((8, hidden_part), WIDE, True),
        ],
        [
            weight_scratch,
            weight_scratch,
            pltpu.VMEM((hidden_part, full), LOW),
            pltpu.VMEM((cores * quarter, full), LOW),
            units_wide,
            units_wide,
            units_wide,
            units_low,
            units_low,
            units_low,
            pltpu.VMEM((quarter, full), LOW),
            pltpu.VMEM((quarter, full), LOW),
        ],
        remote,
        local,
    )
    gate_all = gate_all.reshape(full, hidden_part).astype(LOW)
    up_all = up_all.reshape(full, hidden_part).astype(LOW)
    by_device = (count, cores, quarter, full)
    grad_normed_second = (
        (times_flipped(grad_gate_low, gate_all) + times_flipped(grad_up_low, up_all))
        .astype(LOW)
        .reshape(by_device)
    )
    down_partial = left_product(hidden, cot_all).astype(LOW)
    token_scratch = [
        pltpu.VMEM((count, quarter, full), LOW),
        pltpu.VMEM((count, quarter, full), LOW),
        *line_buffers(count, 1, quarter, full),
    ]
    token_low = pltpu.VMEM((quarter, full), LOW)
    grad_middle, grad_middle_all, width_sums, down_grad = call(
        functools.partial(second_norm_back, count),
        "second_norm_back",
        5,
        [
            (grad_normed_second, False),
            (cot_all, False),
            (middle, True),
            (width_all, True),
            (down_partial, False),
        ],
        [
            ((quarter, full), WIDE, True),
            ((tokens, narrow), LOW, False),
            ((8, full), WIDE, True),
            ((hidden_part, narrow), WIDE, True),
        ],
        token_scratch + [token_low, token_low, row_buffers(hidden_part, narrow)],
        remote,
        local,
    )
    gate_partial = left_product(normed_second, grad_gate_low).astype(LOW)
    up_partial = left_product(normed_second, grad_up_low).astype(LOW)
    forward_partial = times(hidden, down_all).astype(LOW).reshape(by_device)

    mixed_partial = times_flipped(grad_middle_all, wout_all).astype(LOW)
    output_partial = left_product(mixed_all, grad_middle_all).astype(LOW)
    grad_mixed, layer_out, gate_own = call(
        functools.partial(mixed_and_output, count),
        "mixed_and_output",
        6,
        [
            (mixed_partial, False),
            (forward_partial, False),
            (middle, True),
            (width_all, True),
            (gate_partial, False),
        ],
        [
            ((2, steps // 2, width), WIDE, True),
            ((rows_count, quarter, narrow), LOW, False),
            ((2, narrow // 2, hidden_part), LOW, True),
        ],
        [row_buffers(steps, width)]
        + token_scratch
        + [token_low, row_buffers(narrow, hidden_part)],
        remote,
        local,
    )
    grad_mixed = grad_mixed.reshape(steps, width)

    grad_gelu = gelu_pull(grad_mixed * state)[0]
    grad_branch_low, channel_part, block_sums = call(
        functools.partial(recurrence_backward, count, taps),
        "recurrence_backward",
        7,
        [
            (array, True)
            for array in (
                branch,
                side,
                spots,
                vectors,
                blocks,
                conv,
                input_gate,
                decay_gate,
                state,
                entering,
                grad_mixed,
            )
        ],
        [
            ((steps, width), LOW, True),
            ((round_up(taps + 6, 8), width), WIDE, True),
            ((2 * heads, block, block), WIDE, True),
        ],
        [
            tokens_scratch,
            tokens_scratch,
            tokens_scratch,
            eight_rows,
            table_rows,
            pltpu.VMEM((2, 8, width), WIDE),
            eight_rows,
            pltpu.VMEM((steps + 8, block), WIDE),
            pltpu.VMEM((steps + 8, block), WIDE),
        ],
        remote,
        local,
    )
    grad_gelu_low = grad_gelu.astype(LOW)
    projected_grads = jnp.concatenate(
        (columns(grad_branch_low, rows_count), columns(grad_gelu_low, rows_count)), axis=2
    )
    grad_projected, up_own, output_grad, gate_blocks = call(
        functools.partial(spread_gradients, count),
        "spread_gradients",
        8,
        [
            (projected_grads, False),
            (up_partial, False),
            (output_partial.reshape((count,) + output_matrix.shape), False),
            (gate_own.reshape(count, depth, hidden_part), False),
        ],
        [
            ((rows_count, steps, 2 * part), LOW, False),
            ((2, narrow // 2, hidden_part), LOW, True),
            (output_matrix.shape, WIDE, True),
            ((count, depth, hidden_part), LOW, False),
        ],
        [
            row_buffers(narrow, hidden_part),
            *line_buffers(count, 1, *output_matrix.shape),
            pltpu.VMEM((count,) + output_matrix.shape, LOW),
        ],
        remote,
        local,
    )
    grad_projected = grad_projected.reshape(tokens, 2 * part)
    proj_partial = left_product(normed_first, grad_projected).astype(LOW)
    grad_normed_first = times_flipped(grad_projected, wxy_all).astype(LOW)
    channel_part = channel_part.at[taps + 5].set(jnp.sum(grad_gelu, axis=0))
    hidden_part_sums = padded_rows(hidden_part_sums, 8, round_up(hidden_part, 128))
    block_in = (
        block_sums.astype(LOW)
        .reshape(2 * heads, count, rows_count, back_share, block)
        .transpose(2, 1, 0, 3, 4)
        .reshape(rows_count, 2, count // 2 * 2 * heads * back_share, block)
    )
    channel_shape, sums_shape = channel_part.shape, hidden_part_sums.shape
    block_rows = 2 * heads * back_share
    input_grad, proj_grad, up_blocks, width_sums, channel_sums, block_grads, hidden_sums = call(
        functools.partial(first_norm_back, count),
        "first_norm_back",
        9,
        [
            (grad_normed_first.reshape(cores, rows_count, quarter, full), False),
            (x_own, False),
            (grad_middle, True),
            (width_all, True),
            (proj_partial.reshape(rows_count, count, depth, 2 * part), False),
            (up_own.reshape(count, depth, hidden_part), False),
            (width_sums, True),
            (channel_part, True),
            (hidden_part_sums, True),
            (block_in, False),
        ],
        [
            ((rows_count, quarter, narrow), WIDE, False),
            ((rows_count, depth, 2 * part), LOW, False),
            ((count, depth, hidden_part), LOW, False),
            ((2, 8, narrow), WIDE, True),
            (channel_shape, WIDE, True),
            ((rows_count, block_rows, block), LOW, False),
            (sums_shape, WIDE, True),
        ],
        [
            pltpu.VMEM((rows_count, quarter, full), LOW),
            pltpu.VMEM((rows_count, quarter, full), LOW),
            pltpu.VMEM((rows_count, quarter, full), LOW),
            row_buffers(quarter, full),
            token_low,
            pltpu.VMEM((rows_count, quarter, narrow), WIDE),
            pltpu.VMEM((8, full), WIDE),
            pltpu.VMEM((count, rows_count, depth, 2 * part), LOW),
            *line_buffers(count, rows_count, depth, 2 * part),
            pltpu.VMEM((rows_count, depth, 2 * part), LOW),
            pltpu.VMEM((rows_count, 8, narrow), WIDE),
            pltpu.VMEM((count, 8, narrow), WIDE),
            pltpu.VMEM((rows_count, 8, narrow), WIDE),
            pltpu.VMEM((rows_count,) + channel_shape, WIDE),
            pltpu.VMEM((count,) + channel_shape, WIDE),
            pltpu.VMEM((rows_count,) + sums_shape, WIDE),
            row_buffers(2 * block_in.shape[2], block),
            pltpu.VMEM((2, block_in.shape[2], block), WIDE),
            *line_buffers(count, 1, block_rows, block),
            pltpu.VMEM((block_rows, block), LOW),
        ],
        remote,
        local,
    )
    branch_grad = side_by_side(proj_grad[:, :, :part]).astype(WIDE)
    gelu_grad = side_by_side(proj_grad[:, :, part:]).astype(WIDE)
    block_grads = (
        block_grads.reshape(rows_count, 2 * heads, back_share, block)
        .transpose(1, 0, 2, 3)
        .reshape(2 * heads, block_part, block)
        .astype(WIDE)
    )
    channel_sums = lax.dynamic_slice_in_dim(channel_sums, place_dp * channel_size, channel_size, 1)
    width_sums = lax.dynamic_slice_in_dim(
        width_sums[0] + width_sums[1], place_dp * depth, depth, 1
    )
    decay_param_grad = -8.0 * channel_sums[taps + 4] * jax.nn.sigmoid(decay_raw)

    return (
        layer_out.reshape(tall, narrow),
        input_grad.reshape(tall, narrow),
        branch_grad,
        gelu_grad,
        output_grad,
        side_by_side(gate_blocks).astype(WIDE),
        side_by_side(up_blocks).astype(WIDE),
        down_grad,
        block_grads[:heads],
        block_grads[heads:],
        channel_sums[:taps],
        channel_sums[taps],
        channel_sums[taps + 1],
        channel_sums[taps + 5],
        channel_sums[taps + 2],
        channel_sums[taps + 3],
        decay_param_grad,
        width_sums[1],
        hidden_sums[0, :hidden_part],
        hidden_sums[1, :hidden_part],
        width_sums[2],
        width_sums[3],
        width_sums[0],
    )


def solution(mesh):
    in_specs = (
        P(("dp", "col"), "row"),
        P(("dp", "row")),
        P(("row", "dp"), "col"),
        P(("row", "dp"), "col"),
        P(("col", "dp"), "row"),
        P(("row", "dp"), "col"),
        P(("row", "dp"), "col"),
        P(("col", "dp"), "row"),
        P("col", "dp", None),
        P("col", "dp", None),
        P(None, ("col", "dp")),
        P(("col", "dp")),
        P(("col", "dp")),
        P(("col", "dp")),
        P(("col", "dp")),
        P(("col", "dp")),
        P(("col", "dp")),
        P(("row", "dp")),
        P(("col", "dp")),
        P(("col", "dp")),
        P(("row", "dp")),
        P(("row", "dp")),
        P(("row", "dp")),
        P(("dp", "col"), "row"),
    )
    out_specs = (
        P(("dp", "col"), "row"),
        P(("dp", "col"), "row"),
        P(("row", "dp"), "col"),
        P(("row", "dp"), "col"),
        P(("col", "dp"), "row"),
        P(("row", "dp"), "col"),
        P(("row", "dp"), "col"),
        P(("col", "dp"), "row"),
        P("col", "dp", None),
        P("col", "dp", None),
        P(None, ("col", "dp")),
        P(("col", "dp")),
        P(("col", "dp")),
        P(("col", "dp")),
        P(("col", "dp")),
        P(("col", "dp")),
        P(("col", "dp")),
        P(("row", "dp")),
        P(("col", "dp")),
        P(("col", "dp")),
        P(("row", "dp")),
        P(("row", "dp")),
        P(("row", "dp")),
    )
    return jax.shard_map(shards, mesh=mesh, in_specs=in_specs, out_specs=out_specs, check_vma=False)
```

```python
import functools

import jax
import jax.numpy as jnp
from jax import lax
from jax.experimental import pallas as pl
from jax.experimental.pallas import tpu as pltpu
from jax.sharding import PartitionSpec as P

epsilon = 1e-06
ROOT = (2.0 / 3.141592653589793) ** 0.5
CUBE = 0.044715
LOW = jnp.bfloat16
WIDE = jnp.float32
MESH = pl.DeviceIdType.MESH
VMEM = pl.BlockSpec(memory_space=pltpu.VMEM)
ANY = pl.BlockSpec(memory_space=pl.ANY)


def times(piece, matrix):
    return jnp.dot(piece, matrix, preferred_element_type=WIDE)


def times_flipped(piece, matrix):
    return lax.dot_general(piece, matrix, (((1,), (1,)), ((), ())), preferred_element_type=WIDE)


def left_product(left, right):
    return lax.dot_general(left, right, (((0,), (0,)), ((), ())), preferred_element_type=WIDE)


class Links:
    def __init__(self, send, recv, local):
        self.send, self.recv, self.local = send, recv, local
        self.sent = self.kept = 0

    def copy(self, src, dst, **where):
        k, self.sent = self.sent, self.sent + 1
        return pltpu.make_async_remote_copy(
            src_ref=src,
            dst_ref=dst,
            send_sem=self.send.at[k],
            recv_sem=self.recv.at[k],
            device_id=where,
            device_id_type=MESH,
        )

    def keep(self, src, dst):
        k, self.kept = self.kept, self.kept + 1
        copy = pltpu.make_async_copy(src, dst, self.local.at[k])
        copy.start()
        return copy


class Relay:
    def __init__(self, links, src, buffer, dst):
        self.links, self.buffer, self.dst, self.store = links, buffer, dst, None
        self.load = links.keep(src, buffer)

    def pass_on(self):
        if self.store is None:
            self.load.wait()
            self.store = self.links.keep(self.buffer, self.dst)

    def wait(self):
        self.pass_on()
        self.store.wait()


class Place:
    def __init__(self, count_dp):
        self.row, self.dp, self.col = (lax.axis_index(name) for name in ("row", "dp", "col"))
        self.count = count_dp
        first, second = lax.rem(self.row, 2), lax.div(self.row, 2)
        self.near = [self.row, self.row + 1 - 2 * first, self.row + 2 - 4 * second, 3 - self.row]
        self.other = 1 - self.col

    def turn(self, index):
        return lax.rem(index + self.count, self.count)


def greet(place, rows=False, line=False, cores=False):
    barrier = pltpu.get_barrier_semaphore()
    partners = []
    if rows:
        partners += [{"row": place.near[k]} for k in range(1, 4)]
    if line:
        partners += [{"dp": place.turn(place.dp + k)} for k in range(1, place.count)]
    if cores:
        partners += [{"col": place.other}]
    for where in partners:
        pl.semaphore_signal(barrier, inc=1, device_id=where, device_id_type=MESH)
    pl.semaphore_wait(barrier, len(partners))


def run(tasks):
    live = list(tasks)
    while live:
        live = [task for task in live if next(task, None) is not None]


def advance(*tasks):
    for task in tasks:
        next(task, None)


def finish(*tasks):
    run(tasks)


def chain(*tasks):
    for task in tasks:
        yield from task


def when(condition, action):
    pl.when(condition)(lambda: action() and None)


def halves(size):
    first = -(-size // 32) * 16
    return (pl.ds(0, first), pl.ds(first, size - first))


def by_rows(count, body):
    step = 16 if count % 16 == 0 else count

    def lap(i, carry):
        body(pl.ds(pl.multiple_of(i * step, step), step))
        return carry

    lax.fori_loop(0, count // step, lap, 0)


def by_pieces(pieces, height, body):
    def lap(i, carry):
        by_rows(height, lambda rows: body(i, rows))
        return carry

    if pieces == 1:
        by_rows(height, lambda rows: body(0, rows))
    else:
        lax.fori_loop(0, pieces, lap, 0)


def gather_rows(links, place, own, piece):
    row, near, side, _ = place.near
    out = [
        links.copy(own(0), piece(row, 0), row=near),
        links.copy(own(1), piece(row, 1), row=side),
        links.copy(own(1), piece(row, 1), row=near),
        links.copy(own(0), piece(row, 0), row=side),
    ]
    for copy in out:
        copy.start()
    yield 1
    out[0].wait_recv()
    out.append(links.copy(piece(near, 0), piece(near, 0), row=side))
    out[4].start()
    out[1].wait_recv()
    out.append(links.copy(piece(side, 1), piece(side, 1), row=near))
    out[5].start()
    yield 1
    for copy in out[2:]:
        copy.wait_recv()
    for copy in out:
        copy.wait_send()


def exchange_rows(links, place, source, target):
    out = [
        links.copy(source(place.near[k]), target(place.row), row=place.near[k])
        for k in range(1, 4)
    ]
    for copy in out:
        copy.start()
    yield 1
    for copy in out:
        copy.wait_recv()
    for copy in out:
        copy.wait_send()


def exchange_line(links, place, source, target):
    out = []
    for k in range(1, place.count):
        far = place.turn(place.dp + k)
        out.append(links.copy(source(far), target(place.dp), dp=far))
    for copy in out:
        copy.start()
    yield 1
    for copy in out:
        copy.wait_recv()
    for copy in out:
        copy.wait_send()


def gather_line(links, place, own, piece, share=False):
    z, count, turn = place.dp, place.count, place.turn
    ups, downs, shared = [], [], []

    def pass_on(block, valid):
        copy = links.copy(piece(block), piece(block), col=place.other)
        when(valid, copy.start)
        shared.append((copy, valid))

    if share:
        copy = links.copy(own, piece(z), col=place.other)
        copy.start()
        shared.append((copy, z >= 0))
    for step in range(1, count + 1):
        if step > 1:
            yield 1
            below, above = z >= step - 1, z <= count - step
            when(below, ups[-1].wait_recv)
            when(above, downs[-1].wait_recv)
        if step < count:
            low, high = turn(z - step + 1), turn(z + step - 1)
            ups.append(
                links.copy(own if step == 1 else piece(low), piece(low), dp=turn(z + 1))
            )
            downs.append(
                links.copy(own if step == 1 else piece(high), piece(high), dp=turn(z - 1))
            )
            when((z >= step - 1) & (z < count - 1), ups[-1].start)
            when((z <= count - step) & (z > 0), downs[-1].start)
        if step > 1 and share:
            pass_on(turn(z - step + 1), below)
            pass_on(turn(z + step - 1), above)
    yield 1
    for copy, valid in shared:
        when(valid, copy.wait_recv)
    for step in range(1, count):
        when((z >= step - 1) & (z < count - 1), ups[step - 1].wait_send)
        when((z <= count - step) & (z > 0), downs[step - 1].wait_send)
    for copy, valid in shared:
        when(valid, copy.wait_send)


class LineGather:
    def __init__(self, links, place, own, piece):
        self.links, self.place, self.own, self.piece = links, place, own, piece
        self.ups, self.downs, self.shared = [None], [None], []

    def send(self, step):
        z, count, turn = self.place.dp, self.place.count, self.place.turn
        low, high = turn(z - step + 1), turn(z + step - 1)
        for copies, block, target, valid in (
            (self.ups, low, turn(z + 1), (z >= step - 1) & (z < count - 1)),
            (self.downs, high, turn(z - 1), (z <= count - step) & (z > 0)),
        ):
            source = self.own if step == 1 else self.piece(block)
            copy = self.links.copy(source, self.piece(block), dp=target)
            copies.append((copy, valid))
            when(valid, copy.start)

    def share(self, blocks, own=None):
        out = []
        for block, valid in blocks:
            source = self.piece(block) if own is None else own
            copy = self.links.copy(source, self.piece(block), col=self.place.other)
            when(valid, copy.start)
            out.append((copy, valid))
        self.shared.append(out)

    def start(self):
        self.send(1)
        self.share([(self.place.dp, self.place.dp >= 0)], self.own)

    def step(self, step):
        z, count, turn = self.place.dp, self.place.count, self.place.turn
        below, above = z >= step, z <= count - 1 - step
        when(below, self.ups[step][0].wait_recv)
        when(above, self.downs[step][0].wait_recv)
        if step < count - 1:
            self.send(step + 1)
        self.share([(turn(z - step), below), (turn(z + step), above)])

    def ready(self, step):
        for copy, valid in self.shared[step]:
            when(valid, copy.wait_recv)

    def close(self):
        for copy, valid in self.ups[1:] + self.downs[1:] + sum(self.shared, []):
            when(valid, copy.wait_send)


def scatter_rows(links, place, part, buffers, result, prepare=None, gentle=False):
    row, near, side, far = place.near
    if prepare is not None:
        prepare(far)
    heights = [part(row, h).shape[0] for h in range(2)]

    def buffer(i, h):
        return buffers.at[i, pl.ds(0, heights[h])]

    out = [
        links.copy(part(far, 0), buffer(5, 0), row=side),
        links.copy(part(far, 1), buffer(7, 1), row=near),
        links.copy(part(side, 0), buffer(4, 0), row=side),
        links.copy(part(near, 1), buffer(6, 1), row=near),
    ]
    for i, copy in enumerate(out):
        if i == 2 and gentle:
            yield 1
        if i > 1 and prepare is not None:
            prepare(near if i == 3 else side)
        copy.start()
    if prepare is not None:
        prepare(row)
    loads = [
        links.keep(part(near, 0), buffer(0, 0)),
        links.keep(part(side, 1), buffer(1, 1)),
        links.keep(part(row, 0), buffer(2, 0)),
        links.keep(part(row, 1), buffer(3, 1)),
    ]
    yield 1
    for h, target in ((0, near), (1, side)):
        loads[h].wait()
        out[h].wait_recv()

        def add(rows, h=h):
            total = buffers[h, rows].astype(WIDE) + buffers[5 + 2 * h, rows].astype(WIDE)
            buffers[h, rows] = total.astype(LOW)

        by_rows(heights[h], add)
        out.append(links.copy(buffer(h, h), buffer(8 + h, h), row=target))
        out[-1].start()
        yield 1
    for h in range(2):
        loads[2 + h].wait()
        out[2 + h].wait_recv()
        out[4 + h].wait_recv()

        def finish(rows, h=h):
            result(
                h,
                rows,
                buffers[2 + h, rows].astype(WIDE)
                + buffers[4 + 2 * h, rows].astype(WIDE)
                + buffers[8 + h, rows].astype(WIDE),
            )

        by_rows(heights[h], finish)
    for copy in out:
        copy.wait_send()


def row_buffers(size, width):
    return pltpu.VMEM((10, halves(size)[0].size, width), LOW)


def scatter_line(links, place, ready, term, ups_in, downs_in, staging, result):
    z, count, turn = place.dp, place.count, place.turn
    pieces, height = ups_in.shape[1:3]
    ups, downs = [None], [None]

    def sends_up(t):
        return (z <= t - 1) & (z < count - 1)

    def sends_down(t):
        return (z >= count - t) & (z > 0)

    def fill(slot, block, arrived):
        def body(i, rows):
            value = term(block, i, rows)
            if arrived is not None:
                value = value + arrived[i, rows].astype(WIDE)
            staging[slot, i, rows] = value.astype(LOW)

        by_pieces(pieces, height, body)

    for t in range(1, count):
        ready(t)
        ready(count - t)
        for which in range(2):
            copies, into = ((ups, ups_in), (downs, downs_in))[which]
            sends = (sends_up, sends_down)[which]
            first = (z == 0, z == count - 1)[which]
            block = (turn(z - t), turn(z + t))[which]
            target = (turn(z + 1), turn(z - 1))[which]
            slot = 2 * which + t % 2
            if t > 2:
                when(sends(t - 2), copies[t - 2].wait_send)
            copy = links.copy(staging.at[slot], into.at[t - 1], dp=target)
            copies.append(copy)

            def begin(copy=copy, slot=slot, block=block):
                fill(slot, block, None)
                copy.start()

            when(sends(t) & first, begin)
            if t > 1:

                def go_on(copy=copy, slot=slot, block=block, before=copies[t - 1], into=into, t=t):
                    before.wait_recv()
                    fill(slot, block, into.at[t - 2])
                    copy.start()

                when(sends(t) & jnp.logical_not(first), go_on)
        yield 1
    ready(0)
    last = count - 1
    from_below, from_above = ups_in.at[last - 1], downs_in.at[last - 1]
    when(z > 0, ups[last].wait_recv)
    when(z < last, downs[last].wait_recv)

    def finish(below, above):
        def body(i, rows):
            value = term(z, i, rows)
            if below:
                value = value + from_below[i, rows].astype(WIDE)
            if above:
                value = value + from_above[i, rows].astype(WIDE)
            result(i, rows, value)

        by_pieces(pieces, height, body)

    when(z == 0, lambda: finish(False, True))
    when((z > 0) & (z < last), lambda: finish(True, True))
    when(z == last, lambda: finish(True, False))
    for t in range(max(1, count - 2), count):
        when(sends_up(t), ups[t].wait_send)
        when(sends_down(t), downs[t].wait_send)


def scatter_line_in_parts(links, place, ready, term, ups_in, downs_in, staging, result):
    def part(i):
        return scatter_line(
            links,
            place,
            ready,
            lambda b, _, rows: term(b, i, rows),
            ups_in.at[:, pl.ds(i, 1)],
            downs_in.at[:, pl.ds(i, 1)],
            staging.at[:, pl.ds(i, 1)],
            lambda _, rows, value: result(i, rows, value),
        )

    live = [part(i) for i in range(ups_in.shape[1])]
    while live:
        live = [task for task in live if next(task, None) is not None]
        yield 1


def line_buffers(count, pieces, height, width):
    return [pltpu.VMEM((slots, pieces, height, width), LOW) for slots in (count - 1, count - 1, 4)]


def token_scatter(links, place, partial, ours, theirs, buffers, result, prepare=None):
    out, loads = [], []
    for s in list(range(1, place.count)) + [0]:
        block = place.turn(place.dp - s)
        if prepare is not None:
            prepare(block)
        out.append(
            links.copy(partial.at[block, place.other], theirs.at[block], col=place.other)
        )
        out[-1].start()
        loads.append(links.keep(partial.at[block, place.col], ours.at[block]))
    waited = set()

    def ready(s):
        if s not in waited:
            waited.add(s)
            at = s - 1 if s else place.count - 1
            out[at].wait_recv()
            loads[at].wait()

    height = buffers[0].shape[2]

    def at(i, rows):
        return pl.ds(pl.multiple_of(rows.start + i * height, 16), rows.size)

    def term(block, i, rows):
        here = at(i, rows)
        return ours[block, here].astype(WIDE) + theirs[block, here].astype(WIDE)

    yield 1
    yield from scatter_line_in_parts(
        links, place, ready, term, *buffers, lambda i, rows, value: result(at(i, rows), value)
    )
    for copy in out:
        copy.wait_send()


def call(kernel, name, number, ins, outs, scratch, remote, local):
    return pl.pallas_call(
        kernel,
        in_specs=[VMEM if inside else ANY for _, inside in ins],
        out_specs=[VMEM if inside else ANY for _, _, inside in outs],
        out_shape=[jax.ShapeDtypeStruct(shape, kind) for shape, kind, _ in outs],
        scratch_shapes=list(scratch)
        + [
            pltpu.SemaphoreType.DMA((remote,)),
            pltpu.SemaphoreType.DMA((remote,)),
            pltpu.SemaphoreType.DMA((local,)),
        ],
        compiler_params=pltpu.CompilerParams(
            collective_id=number, has_side_effects=True, vmem_limit_bytes=58 * 1024 * 1024
        ),
        name=name,
    )(*[array for array, _ in ins])


def lanes(index, width):
    return pl.ds(pl.multiple_of(index * width, 128), width)


def strip(index, height, step=16):
    return pl.ds(pl.multiple_of(index * height, step), height)


def combine(earlier, later):
    return (earlier[0] * later[0], later[0] * earlier[1] + later[1])


def scan_rows(decay, value, reverse):
    count = decay.shape[0]
    rows = lax.broadcasted_iota(jnp.int32, decay.shape, 0)
    reach = 1
    while reach < count:
        turn = count - reach if reverse else reach
        inside = rows < count - reach if reverse else rows >= reach
        decay_far = jnp.where(inside, pltpu.roll(decay, turn, 0), 1.0)
        value_far = jnp.where(inside, pltpu.roll(value, turn, 0), 0.0)
        value = decay * value_far + value
        decay = decay * decay_far
        reach *= 2
    return decay, value


def minus_expm1(v):
    series = 1.0 + v / 9.0
    for k in range(8, 1, -1):
        series = 1.0 + (v / k) * series
    return jnp.where(v > -0.5, -v * series, 1.0 - jnp.exp(v))


def each_head(heads, width, body):
    def lap(h, carry):
        body(h, pl.ds(pl.multiple_of(h * width, 128), width))
        return carry

    lax.fori_loop(0, heads, lap, 0)


def carry_over(links, place, ends, table, reverse):
    run([exchange_rows(links, place, lambda q: ends, lambda q: table.at[q])])
    row = place.row
    state = jnp.zeros((1, ends.shape[1]), WIDE)
    for k in range(4):
        q = 3 - k if reverse else k

        def entry(i):
            return table[q, i : i + 1, :]

        reached = q > row if reverse else q < row
        state = jnp.where(reached, entry(0) * state + entry(1), state)
    return state


def recurrence_backward(
    count, taps, proj, side, spots, vectors, blocks, conv_in, in_gate, dec_gate, state_in, entering,
    grad_mixed, branch_out, sums_out, blocks_out, reach, local_grad, branch, ends, table, heads_in,
    heads_here, padded, spread, send, recv, local, links=None, between=lambda: None,
):
    place = Place(count)
    if links is None:
        links = Links(send, recv, local)
        greet(place, rows=True)
    tokens, width = side.shape
    heads, block = blocks.shape[0] // 2, blocks.shape[1]
    spot = spots[...]
    starting = spot == 0
    ends[...] = jnp.zeros(ends.shape, WIDE)

    def backwards(h, at):
        rate = vectors[taps + 5 : taps + 6, at]
        decay = jnp.where(starting, 0.0, jnp.exp(rate * dec_gate[:, at]))
        padded[0:tokens, :] = decay
        padded[tokens:, :] = jnp.ones((8, block), WIDE)
        far, grad = scan_rows(padded[1 : tokens + 1, :], grad_mixed[:, at] * side[:, at], True)
        reach[:, at] = far
        local_grad[:, at] = grad
        ends[0:1, at] = decay[0:1, :] * far[0:1, :]
        ends[1:2, at] = decay[0:1, :] * grad[0:1, :]

    each_head(heads, block, backwards)
    own = links.keep(ends, table.at[place.row])
    own.wait()
    heads_here[0:1, :] = carry_over(links, place, ends, table, True)
    between()

    def one_head(h, at):
        def vector(i):
            return vectors[i : i + 1, at]

        grad_state = local_grad[:, at] + reach[:, at] * heads_here[0:1, at]
        padded[8:, :] = state_in[:, at]
        padded[7:8, :] = entering[0:1, at]
        grad_decay = grad_state * padded[7 : 7 + tokens, :]
        input_gate, decay_gate, conv = in_gate[:, at], dec_gate[:, at], conv_in[:, at]
        rate = vector(taps + 5)
        log_decay = rate * decay_gate
        decay = jnp.exp(log_decay)
        multiplier = jnp.where(starting, 1.0, jnp.sqrt(minus_expm1(2.0 * log_decay)))
        grad_gated = grad_state * conv
        grad_log = jnp.where(
            starting, 0.0, decay * (grad_decay - grad_gated * input_gate * (decay / multiplier))
        )
        grad_in = grad_gated * multiplier * (input_gate * (1.0 - input_gate))
        grad_gate = grad_log * decay_gate
        grad_dec = grad_gate * rate * (1.0 - decay_gate)
        low = conv.astype(LOW)
        low_in, low_dec = grad_in.astype(LOW), grad_dec.astype(LOW)
        across = (((1,), (1,)), ((), ()))
        along = (((0,), (0,)), ((), ()))
        grad_conv = (
            grad_state * multiplier * input_gate
            + lax.dot_general(low_in, blocks[h], across, preferred_element_type=WIDE)
            + lax.dot_general(low_dec, blocks[heads + h], across, preferred_element_type=WIDE)
        )
        blocks_out[h] = lax.dot_general(low, low_in, along, preferred_element_type=WIDE)
        blocks_out[heads + h] = lax.dot_general(low, low_dec, along, preferred_element_type=WIDE)
        spread[0:8, :] = jnp.zeros((8, block), WIDE)
        spread[8:, :] = vector(0) * grad_conv
        shift = vector(taps + 1)

        def total(values):
            return jnp.sum(values, axis=0, keepdims=True)

        sums_out[0:1, at] = total(grad_conv * (proj[8:, at] + shift))
        for k in range(1, taps):
            kept = jnp.where(spot >= k, grad_conv, 0.0)
            sums_out[k : k + 1, at] = total(kept * (proj[8 - k : 8 - k + tokens, at] + shift))
            spread[8 - k : 8 - k + tokens, :] += vector(k) * kept
        branch[:, at] = spread[8:, :]
        heads_in[0, :, at] = spread[0:8, :]
        sums_out[taps : taps + 1, at] = total(grad_conv)
        sums_out[taps + 1 : taps + 2, at] = total(spread[...])
        sums_out[taps + 2 : taps + 3, at] = total(grad_in)
        sums_out[taps + 3 : taps + 4, at] = total(grad_dec)
        sums_out[taps + 4 : taps + 5, at] = total(grad_gate)
        sums_out[taps + 5 :, at] = jnp.zeros((sums_out.shape[0] - taps - 5, block), WIDE)

    each_head(heads, block, one_head)
    row = place.row
    before = lax.rem(row + 3, 4)
    owed = links.copy(heads_in.at[0], heads_in.at[1], row=before)
    owed.start()
    owed.wait_recv()
    owed.wait_send()
    between()

    def finish(h, at):
        last = jnp.where(row < 3, heads_in[1, :, at], 0.0)
        branch[tokens - 8 :, at] += last
        branch_out[:, at] = branch[:, at].astype(LOW)

    each_head(heads, block, finish)


def recurrence_back_inside(
    count, taps, proj, side, gelu_in, spots, vectors, blocks, conv_in, in_gate, dec_gate, state_in,
    entering, grad_mixed, output_partial, up_own, sums_out, blocks_out, all_out, output_out, up_out, branch_low, gelu_low, stage, reach, local_grad, branch, ends, table, heads_in,
    heads_here, padded, spread, ups, downs, staging, own, up_here, send, recv, local,
):
    place = Place(count)
    links = Links(send, recv, local)
    greet(place, rows=True, line=True)
    row, z = place.row, place.dp
    part = stage.shape[2] // 2
    kept = Relay(links, up_own.at[z], up_here, up_out.at[z])
    load = links.keep(output_partial, own)

    output_half = ups.shape[2]

    def output_rows(i, rows):
        return pl.ds(pl.multiple_of(rows.start + i * output_half, 16), rows.size)

    def keep_output(i, rows, value):
        output_out[output_rows(i, rows)] = value

    output_sum = scatter_line_in_parts(
        links,
        place,
        lambda s: None,
        lambda b, i, rows: own[b, output_rows(i, rows)].astype(WIDE),
        ups,
        downs,
        staging,
        keep_output,
    )
    up_line = exchange_line(links, place, lambda b: up_own.at[b], lambda b: up_out.at[b])
    load.wait()
    advance(output_sum, up_line)
    kept.pass_on()

    def gelu_back(h, at):
        grad = grad_mixed[:, at] * state_in[:, at] * gelu_slope(gelu_in[:, at])
        gelu_low[:, at] = grad.astype(LOW)
        spread[0:1, :] = jnp.sum(grad, axis=0, keepdims=True)
        sums_out[taps + 5 : taps + 6, at] = spread[0:1, :]

    recurrence_backward(
        count, taps, proj, side, spots, vectors, blocks, conv_in, in_gate, dec_gate, state_in, entering,
        grad_mixed, branch_low, sums_out, blocks_out, reach, local_grad, branch, ends, table, heads_in,
        heads_here, padded, spread, None, None, None, links, lambda: advance(output_sum),
    )
    each_head(blocks.shape[0] // 2, blocks.shape[1], gelu_back)
    for q in range(4):
        at = slice(q * part, (q + 1) * part)
        stage[q, :, :part] = branch_low[:, at]
        stage[q, :, part:] = gelu_low[:, at]
    mine = links.keep(stage.at[row], all_out.at[row])
    spread_out = exchange_rows(links, place, lambda q: stage.at[q], lambda q: all_out.at[q])
    run([spread_out, output_sum, up_line])
    mine.wait()
    kept.wait()


def norm_rule(rows, grad, value, gain, sums, at):
    full = value.shape[1]
    inverse = lax.rsqrt(jnp.sum(value * value, axis=1, keepdims=True) / full + epsilon)
    scaled = grad * (1.0 + gain)
    inner = jnp.sum(scaled * value, axis=1, keepdims=True)
    sums[at : at + 1, :] += jnp.sum(grad * value * inverse, axis=0, keepdims=True)
    return inverse * scaled - value * (inverse * inverse * inverse) * (inner / full)


def second_norm_back_inside(
    count, grad_gate, grad_up, gate_all, up_all, normed, cot_all, middle, vectors, grad_middle, grad_all,
    sums, gate_out, ours, theirs, ups, downs, staging, cot, low, buffers, gate_v, up_v, gate_w, up_w,
    tile, partial, gate_partial, send, recv, local,
):
    place = Place(count)
    links = Links(send, recv, local)
    greet(place, rows=True, line=True, cores=True)
    loads = [links.keep(grad_gate, gate_v), links.keep(grad_up, up_v)]
    pieces = [
        (links.keep(gate_all.at[q], gate_w.at[q]), links.keep(up_all.at[q], up_w.at[q]))
        for q in range(4)
    ]
    quarter, full = middle.shape
    narrow, units = full // 4, gate_v.shape[1]
    for load in loads:
        load.wait()
    first = [True]

    def tokens(block):
        rows = strip(block, 2 * quarter)

        def lap(q, carry):
            total = sum(
                times_flipped(values[rows, :], weight[q].astype(LOW).reshape(narrow, units))
                for values, weight in ((gate_v, gate_w), (up_v, up_w))
            ).astype(LOW)
            for core in range(2):
                partial[block, core, :, lanes(q, narrow)] = total[
                    core * quarter : (core + 1) * quarter
                ]
            return carry

        if first:
            first.clear()
            for q in range(4):
                for load in pieces[q]:
                    load.wait()
                lap(q, 0)
        else:
            lax.fori_loop(0, 4, lap, 0)

    k, links.kept = links.kept, links.kept + 1

    def gate(q):
        load = pltpu.make_async_copy(normed.at[:, lanes(q, narrow)], tile, links.local.at[k])
        load.start()
        load.wait()
        gate_partial[strip(q, narrow)] = left_product(tile[...], gate_v[...]).astype(LOW)

    second_norm_back(
        count, partial, cot_all, middle, vectors, gate_partial, grad_middle, grad_all, sums, gate_out,
        ours, theirs, ups, downs, staging, cot, low, buffers, None, None, None, links, tokens, gate,
    )


def second_norm_back(
    count, grad_partial, cot_all, middle, vectors, gate_partial, grad_middle, grad_all, sums, gate_out,
    ours, theirs, ups, downs, staging, cot, low, buffers, send, recv, local, links=None,
    prepare_tokens=None, prepare_gate=None,
):
    place = Place(count)
    if links is None:
        links = Links(send, recv, local)
        greet(place, rows=True, line=True, cores=True)
    row, z, col = place.row, place.dp, place.col
    quarter, full = middle.shape
    narrow = full // 4
    tall = 4 * quarter
    half = gate_partial.shape[0] // 8
    sums[...] = jnp.zeros(sums.shape, WIDE)
    gain = vectors[3:4, :]
    load = links.keep(cot_all.at[strip(2 * z + col, quarter)], cot)

    def back(rows, grad):
        own = cot[rows].astype(WIDE)
        total = own + norm_rule(rows, grad, middle[rows], gain, sums, 0)
        sums[1:2, :] += jnp.sum(total, axis=0, keepdims=True)
        sums[2:3, :] += jnp.sum(own, axis=0, keepdims=True)
        grad_middle[rows] = total
        low[rows] = total.astype(LOW)

    def tokens():
        load.wait()
        yield from token_scatter(
            links, place, grad_partial, ours, theirs, (ups, downs, staging), back, prepare_tokens
        )

        def block(q):
            return grad_all.at[strip(4 * col + q, quarter)]

        mine = links.keep(low.at[:, lanes(row, narrow)], block(row))
        yield from exchange_rows(
            links, place, lambda q: low.at[:, lanes(q, narrow)], block
        )
        mine.wait()
        both = grad_all.at[strip(col, tall)]
        share = links.copy(both, both, col=place.other)
        share.start()
        yield 1
        share.wait_recv()
        share.wait_send()

    def keep_gate(h, rows, value):
        gate_out[h, rows] = value.astype(LOW)

    tokens_back = tokens()
    gate_back = scatter_rows(
        links,
        place,
        lambda q, h: gate_partial.at[strip(2 * q + h, half)],
        buffers,
        keep_gate,
        prepare_gate,
    )
    advance(tokens_back)
    advance(tokens_back)
    run([gate_back, tokens_back])


def mixed_and_output_inside(
    count, grad_all, wout, mixed_all, normed, cot_all, grad_up, hidden, out_partial, middle, vectors, gate_own,
    mixed_out, layer_out, up_out, gate_out, output_out, down_out, mixed_buffers, ours, theirs, ups, downs,
    staging, low, up_buffers, gate_here, grad_v, wout_v, mixed_v, tile, up_v, hidden_v, mixed_partial,
    up_partial, output_v, down_v, send, recv, local,
):
    place = Place(count)
    links = Links(send, recv, local)
    greet(place, rows=True, line=True, cores=True)
    loads = [
        links.keep(source, target)
        for source, target in (
            (grad_all, grad_v), (wout, wout_v), (grad_up, up_v), (mixed_all, mixed_v),
            (hidden, hidden_v),
        )
    ]
    steps = mixed_partial.shape[0] // 4
    narrow = grad_v.shape[1]
    for load in loads[:2]:
        load.wait()

    def mixed(q):
        rows = strip(q, steps)
        mixed_partial[rows] = times_flipped(grad_v[rows, :], wout_v[...]).astype(LOW)

    k, links.kept = links.kept, links.kept + 1

    def fetch(source, q):
        load = pltpu.make_async_copy(source.at[:, lanes(q, narrow)], tile, links.local.at[k])
        load.start()
        load.wait()

    def up(q):
        fetch(normed, q)
        up_partial[strip(q, narrow)] = left_product(tile[...], up_v[...]).astype(LOW)

    def ready():
        for load in loads[2:]:
            load.wait()

    def others():
        output_v[...] = left_product(mixed_v[...], grad_v[...]).astype(LOW)
        stores = [links.keep(output_v, output_out)]

        def lap(q, carry):
            fetch(cot_all, q)
            down_v[:, lanes(q, narrow)] = left_product(hidden_v[...], tile[...]).astype(LOW)
            return carry

        lax.fori_loop(0, 4, lap, 0)
        stores.append(links.keep(down_v, down_out))
        yield 1
        for store in stores:
            store.wait()

    mixed_and_output(
        count, mixed_partial, out_partial, middle, vectors, up_partial, gate_own, mixed_out, layer_out,
        up_out, gate_out, mixed_buffers, ours, theirs, ups, downs, staging, low, up_buffers, gate_here, None,
        None, None, links, ready, mixed, up, others(),
    )


def mixed_and_output(
    count, mixed_partial, out_partial, middle, vectors, up_partial, gate_own, mixed_out, layer_out, up_out,
    gate_out, mixed_buffers, ours, theirs, ups, downs, staging, low, up_buffers, gate_here, send, recv,
    local, links=None, ready=None, prepare_mixed=None, prepare_up=None, others=None,
):
    place = Place(count)
    if links is None:
        links = Links(send, recv, local)
        greet(place, rows=True, line=True, cores=True)
    row = place.row
    quarter, full = middle.shape
    narrow = full // 4
    shift = vectors[2:3, :]
    half = mixed_partial.shape[0] // 8
    up_half = up_partial.shape[0] // 8
    kept = Relay(links, gate_own.at[place.dp], gate_here, gate_out.at[place.dp])

    def keep_mixed(h, rows, value):
        mixed_out[h, rows] = value

    def keep_up(h, rows, value):
        up_out[h, rows] = value.astype(LOW)

    def finish(rows, value):
        low[rows] = (middle[rows] + value + shift).astype(LOW)

    def tokens():
        yield from token_scatter(
            links, place, out_partial, ours, theirs, (ups, downs, staging), finish
        )
        mine = links.keep(low.at[:, lanes(row, narrow)], layer_out.at[row])
        yield from exchange_rows(
            links, place, lambda q: low.at[:, lanes(q, narrow)], lambda q: layer_out.at[q]
        )
        mine.wait()

    outs = tokens()
    mixes = scatter_rows(
        links,
        place,
        lambda q, h: mixed_partial.at[strip(2 * q + h, half)],
        mixed_buffers,
        keep_mixed,
        prepare_mixed,
    )
    sums_up = scatter_rows(
        links,
        place,
        lambda q, h: up_partial.at[strip(2 * q + h, up_half)],
        up_buffers,
        keep_up,
        prepare_up,
    )
    gates = exchange_line(links, place, lambda b: gate_own.at[b], lambda b: gate_out.at[b])
    advance(outs, mixes, outs)
    kept.pass_on()
    if ready is not None:
        ready()
    advance(sums_up, mixes, outs, gates)
    if others is not None:
        advance(others)
    advance(mixes)
    run([outs, sums_up, mixes, gates] + ([others] if others is not None else []))
    kept.wait()


def spread_gradients(
    count, blocks, output_partial, up_own, all_out, output_out, up_out, ups, downs, staging, own, send, recv, local,
):
    place = Place(count)
    links = Links(send, recv, local)
    greet(place, rows=True, line=True)
    row, z = place.row, place.dp
    mine = links.keep(blocks.at[row], all_out.at[row])
    kept = links.keep(up_own.at[z], up_out.at[z])
    load = links.keep(output_partial, own)

    output_half = ups.shape[2]

    def output_rows(i, rows):
        return pl.ds(pl.multiple_of(rows.start + i * output_half, 16), rows.size)

    def keep_output(i, rows, value):
        output_out[output_rows(i, rows)] = value

    def outputs():
        load.wait()
        yield from scatter_line_in_parts(
            links,
            place,
            lambda s: None,
            lambda b, i, rows: own[b, output_rows(i, rows)].astype(WIDE),
            ups,
            downs,
            staging,
            keep_output,
        )

    run(
        [
            exchange_rows(links, place, lambda q: blocks.at[q], lambda q: all_out.at[q]),
            outputs(),
            exchange_line(links, place, lambda b: up_own.at[b], lambda b: up_out.at[b]),
        ]
    )
    mine.wait()
    kept.wait()


def first_norm_back(
    count, grad_partial, x_own, grad_middle, vectors, proj_partial, down_partial, sums_in,
    channel_in, hidden_in, block_in, grad_out, proj_out, down_out, width_sums, channel_sums, block_out, hidden_sums,
    theirs, ours, added,
    row_buffer, x, result, sums, proj_own, proj_ups, proj_downs, proj_staging, proj_low, width_table,
    width_line, width_part, channel_table, channel_line, hidden_table, block_buffers, block_sum, block_ups, block_downs,
    block_staging, block_low, down_buffers, send, recv, local, links=None, prepare_tokens=None, prepare_proj=None,
):
    place = Place(count)
    if links is None:
        links = Links(send, recv, local)
        greet(place, rows=True, line=True, cores=True)
    row, z, col = place.row, place.dp, place.col
    quarter, full = grad_middle.shape
    narrow = full // 4
    gain = vectors[0:1, :]
    load_x = links.keep(x_own, x)
    if prepare_proj is None:
        load_proj = [links.keep(proj_partial.at[:, b], proj_own.at[b]) for b in range(count)]

    parts = halves(down_partial.shape[0])

    def keep_down(h, rows, value):
        down_out[pl.ds(pl.multiple_of(parts[h].start + rows.start, 16), rows.size)] = value

    down_sum = scatter_rows(
        links,
        place,
        lambda q, h: down_partial.at[parts[h], lanes(q, narrow)],
        down_buffers,
        keep_down,
    )

    def tokens():
        if prepare_tokens is not None:
            prepare_tokens(place.other)
        share = links.copy(grad_partial.at[place.other], theirs, col=place.other)
        share.start()
        if prepare_tokens is not None:
            prepare_tokens(col)
        load = links.keep(grad_partial.at[col], ours)
        yield 1
        share.wait_recv()
        load.wait()

        def add(rows):
            for q in range(4):
                total = ours[q, rows].astype(WIDE) + theirs[q, rows].astype(WIDE)
                added[q, rows] = total.astype(LOW)

        by_rows(quarter, add)
        load_x.wait()
        sums[0:3, :] = sums_in[0:3, :]
        sums[3:, :] = jnp.zeros((sums.shape[0] - 3, full), WIDE)
        half = quarter // 2

        def back(h, rows, grad):
            here = pl.ds(pl.multiple_of(rows.start + half * h, 16), rows.size)
            value = x[here].astype(WIDE)
            total = grad_middle[here] + norm_rule(rows, grad, value, gain, sums, 3)
            for q in range(4):
                result[q, here] = total[:, q * narrow : (q + 1) * narrow]

        yield from scatter_rows(
            links,
            place,
            lambda q, h: added.at[q, pl.ds(half * h, half)],
            row_buffer,
            back,
        )
        share.wait_send()
        mine = links.keep(result.at[row], grad_out.at[row])
        yield from exchange_rows(
            links, place, lambda q: result.at[q], lambda q: grad_out.at[q]
        )
        mine.wait()
        for q in range(4):
            width_part[q] = sums[:, q * narrow : (q + 1) * narrow]
        own = links.keep(width_part.at[row], width_table.at[row])
        yield from exchange_rows(
            links, place, lambda q: width_part.at[q], lambda q: width_table.at[q]
        )
        own.wait()
        width_line[z] = width_table[0] + width_table[1] + width_table[2] + width_table[3]
        yield from exchange_line(
            links, place, lambda b: width_line.at[z], lambda b: width_line.at[b]
        )
        total = width_line[0]
        for b in range(1, count):
            total = total + width_line[b]
        width_sums[0] = total
        yield 1
        last = links.copy(width_sums.at[0], width_sums.at[1], col=place.other)
        last.start()
        yield 1
        last.wait_recv()
        last.wait_send()

    def projections():
        if prepare_proj is None:
            for load in load_proj:
                load.wait()
        else:
            prepare_proj()

        def keep_proj(i, rows, value):
            proj_low[i, rows] = value.astype(LOW)

        yield from scatter_line_in_parts(
            links,
            place,
            lambda s: None,
            lambda b, i, rows: proj_own[b, i, rows].astype(WIDE),
            proj_ups,
            proj_downs,
            proj_staging,
            keep_proj,
        )
        mine = links.keep(proj_low.at[row], proj_out.at[row])
        yield from exchange_rows(
            links, place, lambda q: proj_low.at[q], lambda q: proj_out.at[q]
        )
        mine.wait()

    def hidden():
        own = links.keep(hidden_in, hidden_table.at[row])
        yield from exchange_rows(
            links, place, lambda q: hidden_in, lambda q: hidden_table.at[q]
        )
        own.wait()
        hidden_sums[...] = hidden_table[0] + hidden_table[1] + hidden_table[2] + hidden_table[3]

    def channels():
        own = links.keep(channel_in, channel_table.at[row])
        yield from exchange_rows(
            links, place, lambda q: channel_in, lambda q: channel_table.at[q]
        )
        own.wait()
        channel_line[z] = (
            channel_table[0] + channel_table[1] + channel_table[2] + channel_table[3]
        )
        yield from exchange_line(
            links, place, lambda b: channel_line.at[z], lambda b: channel_line.at[b]
        )
        total = channel_line[0]
        for b in range(1, count):
            total = total + channel_line[b]
        channel_sums[...] = total

    def blocks():
        def keep_rows(h, rows, value):
            block_sum[h, rows] = value

        yield from scatter_rows(
            links,
            place,
            lambda q, h: block_in.at[q, h],
            block_buffers,
            keep_rows,
        )
        length = block_sum.shape[1] * 2 // count
        middle = count // 2

        def term(b, i, rows):
            at = pl.multiple_of(lax.rem(b, middle) * length + rows.start, 8)
            return block_sum[lax.div(b, middle), pl.ds(at, rows.size)]

        def keep_line(i, rows, value):
            block_low[rows] = value.astype(LOW)

        yield from scatter_line_in_parts(
            links, place, lambda s: None, term, block_ups, block_downs, block_staging, keep_line
        )
        mine = links.keep(block_low, block_out.at[row])
        yield from exchange_rows(links, place, lambda q: block_low, lambda q: block_out.at[q])
        mine.wait()

    proj_sum, token_sum = projections(), tokens()
    small = [channels(), hidden(), blocks()]
    advance(down_sum, proj_sum, token_sum, *small)
    advance(token_sum)
    run([proj_sum, token_sum, down_sum] + small)


def first_norm_back_inside(
    count, grad_proj, wxy, nf, x_own, grad_middle, vectors, down_partial, *refs
):
    rest, (grad_v, wxy_v, nf_v, partial, send, recv, local) = refs[:-7], refs[-7:]
    proj_own = rest[18]
    place = Place(count)
    links = Links(send, recv, local)
    greet(place, rows=True, line=True, cores=True)
    loads = [
        links.keep(source, target)
        for source, target in ((grad_proj, grad_v), (nf, nf_v), (wxy, wxy_v))
    ]
    quarter, full = grad_middle.shape
    narrow, tall = full // 4, 4 * quarter
    depth = proj_own.shape[2]

    def tokens(core):
        def lap(q, carry):
            total = times_flipped(
                grad_v[strip(core, tall), :], wxy_v[strip(q, narrow), :]
            ).astype(LOW)
            for r in range(4):
                partial[core, r, :, lanes(q, narrow)] = total[r * quarter : (r + 1) * quarter]
            return carry

        lax.fori_loop(0, 4, lap, 0)

    def proj():
        for load in loads:
            load.wait()

        def lap(q, carry):
            total = left_product(nf_v[:, lanes(q, narrow)], grad_v[...]).astype(LOW)
            for b in range(count):
                proj_own[b, q] = total[b * depth : (b + 1) * depth]
            return carry

        lax.fori_loop(0, 4, lap, 0)

    first_norm_back(
        count, partial, x_own, grad_middle, vectors, None, down_partial, *rest, None, None, None, links,
        tokens, proj,
    )


def gelu(v):
    return 0.5 * v * (1.0 + jnp.tanh(ROOT * (v + CUBE * (v * v * v))))


def gelu_slope(v):
    t = jnp.tanh(ROOT * (v + CUBE * (v * v * v)))
    return 0.5 * (1.0 + t) + 0.5 * v * (1.0 - t * t) * (ROOT * (1.0 + 3.0 * CUBE * (v * v)))


def block_of(blocks, h):
    width = blocks.shape[-1]
    return blocks[h].reshape(width, width)


def forward(
    count, taps, x, cot, wxy, wout, wgate, wup, wdown, blk, cvec, wvec, spots,
    nf_out, x_out, cot_own, wxy_out, wout_out, gate_own, up_own, down_all, blocks_out, vectors_out,
    width_out, branch_out, gelu_out, side_out, conv_out, in_out, dec_out, state_out, entering_out,
    mixed_out, middle_out, normed_out,
    x_all, nf, wxy_all, wout_all, blocks, cvec_all, wvec_all, vectors, width, stage, arrived, branch,
    gelu_in, side, conv, in_gate, dec_gate, state, running, local_state, ends, table, entering, mixed,
    mixed_all, partial, theirs, here, wide, middle, normed, gate_here, up_here, down_here, cot_here,
    send, recv, local,
):
    place = Place(count)
    links = Links(send, recv, local)
    row, z, col = place.row, place.dp, place.col
    greet(place, rows=True, line=True, cores=True)
    tall, narrow = x.shape
    full = 4 * narrow
    half, quarter = tall // 2, tall // 4
    depth, part = wxy.shape[1], wxy.shape[2] // 2
    tokens, steps = 2 * tall, tall // 2
    heads, block = blocks.shape[0] // 2, blocks.shape[-1]
    share = blocks.shape[3]
    kept = []

    def keep(src, dst):
        kept.append(links.keep(src, dst))
        return kept[-1]

    def projections():
        def at(q, b):
            return wxy_all.at[q, strip(b, depth, 8)]

        mine = links.keep(wxy.at[row], at(row, z))
        yield from exchange_rows(links, place, lambda q: wxy.at[q], lambda q: at(q, z))
        mine.wait()

        def piece(b):
            return wxy_all.at[:, strip(b, depth, 8)]

        yield from gather_line(links, place, piece(z), piece)

    def inputs():
        def at(q, core):
            return x_all.at[strip(core, tall), lanes(q, narrow)]

        mine = links.keep(x, at(row, col))
        shared = [links.copy(x, at(row, col), col=place.other)]
        shared[0].start()
        yield from gather_rows(
            links,
            place,
            lambda h: x.at[pl.ds(half * h, half)],
            lambda q, h: x_all.at[strip(2 * col + h, half), lanes(q, narrow)],
        )
        for k in range(1, 4):
            q = place.near[k]
            shared.append(links.copy(at(q, col), at(q, col), col=place.other))
            shared[-1].start()
        yield 1
        mine.wait()
        for copy in shared:
            copy.wait_recv()
        for copy in shared:
            copy.wait_send()

    def channel_vectors():
        keep(cvec, cvec_all.at[z])
        yield from exchange_line(links, place, lambda b: cvec, lambda b: cvec_all.at[b])

    def width_vectors():
        mine = links.keep(wvec, wvec_all.at[row, z])
        yield from exchange_line(links, place, lambda b: wvec, lambda b: wvec_all.at[row, b])
        mine.wait()
        yield from exchange_rows(
            links, place, lambda q: wvec_all.at[row], lambda q: wvec_all.at[q]
        )

    def gate_blocks():
        split = blocks.shape[2] > 1
        own = row if split else 0
        mine = links.keep(blk, blocks.at[:, z, own])
        yield from exchange_line(links, place, lambda b: blk, lambda b: blocks.at[:, b, own])
        mine.wait()
        middle = count // 2
        if split:

            def at(q, h):
                return blocks.at[:, pl.ds(middle * h, middle), q]

            yield from gather_rows(links, place, lambda h: at(row, h), at)

    def hidden_rows():
        parts = halves(wdown.shape[0])
        mine = Relay(links, wdown, down_here, down_all.at[:, lanes(row, narrow)])
        kept.append(mine)
        yield from gather_rows(
            links,
            place,
            lambda h: wdown.at[parts[h]],
            lambda q, h: down_all.at[parts[h], lanes(q, narrow)],
        )

    def cotangent_rows():
        def spot(q):
            return cot_own.at[:, lanes(q, narrow)]

        mine = Relay(links, cot.at[strip(row, quarter)], cot_here, spot(row))
        yield from exchange_rows(links, place, lambda q: cot.at[strip(q, quarter)], spot)
        mine.wait()

    def hidden_columns(matrix, buffer, own):
        mine = Relay(links, matrix.at[z], buffer, own.at[z])
        yield from exchange_line(links, place, lambda b: matrix.at[b], lambda b: own.at[b])
        mine.wait()

    def output_rows():
        at = wout.shape[0]
        mine = links.keep(wout, wout_all.at[strip(z, at)])
        yield from gather_line(links, place, wout, lambda b: wout_all.at[strip(b, at)])
        mine.wait()

    weights, rows_in = projections(), inputs()
    vectors_in, widths_in, blocks_in = channel_vectors(), width_vectors(), gate_blocks()
    cot_in, output_in, down_in = cotangent_rows(), output_rows(), hidden_rows()
    gate_in = hidden_columns(wgate, gate_here, gate_own)
    up_in = hidden_columns(wup, up_here, up_own)
    advance(weights, rows_in, widths_in, vectors_in, blocks_in, cot_in)
    advance(weights, widths_in, vectors_in, blocks_in)
    finish(widths_in, vectors_in)
    for copy in kept:
        copy.wait()
    kept.clear()

    for b in range(count):
        size = vectors.shape[1] // count
        vectors[:, b * size : (b + 1) * size] = cvec_all[b, :, :size]
        for q in range(4):
            at = q * narrow + b * depth
            width[:, at : at + depth] = wvec_all[q, b, :, :depth]
    keep(vectors, vectors_out)
    keep(width, width_out)
    advance(rows_in)
    advance(weights)
    finish(rows_in)
    advance(down_in)
    keep(x_all.at[strip(4 * col + row, quarter)], x_out)

    nf[0:16, :] = jnp.zeros((16, full), LOW)

    def first_norm(rows):
        value = x_all[rows].astype(WIDE)
        mean = jnp.sum(value * value, axis=1, keepdims=True) / full
        value = value * lax.rsqrt(mean + epsilon) * (1.0 + width[0:1, :])
        nf[pl.ds(pl.multiple_of(rows.start + 16, 16), rows.size)] = value.astype(LOW)

    by_rows(tokens, first_norm)
    keep(nf.at[pl.ds(16, tokens)], nf_out)
    advance(weights, blocks_in, cot_in)
    finish(blocks_in)
    keep(blocks, blocks_out)
    finish(weights, cot_in)
    keep(wxy_all, wxy_out)

    advance(output_in)
    advance(down_in)
    out = []
    for k in (3, 2, 1, 0):
        q = place.near[k]

        def product(k=k, q=q):
            stage[k] = jnp.dot(
                nf[pl.ds(pl.multiple_of(q * steps, 16), steps + 16), :],
                wxy_all[...].astype(LOW).reshape(full, 2 * part),
                preferred_element_type=WIDE,
            )

        product()
        source = stage.at[k, pl.ds(8, steps + 8)]
        if k:
            out.append(links.copy(source, arrived.at[row], row=q))
            out[-1].start()
        else:
            mine = links.keep(source, arrived.at[row])
    advance(output_in, gate_in)
    mine.wait()
    for copy in out:
        copy.wait_recv()
    finish(down_in)
    for copy in out:
        copy.wait_send()

    spot = spots[...]
    starting = spot == 0
    for q in range(4):
        at = slice(q * part, (q + 1) * part)
        branch[:, at] = arrived[q, :, :part]
        gelu_in[:, at] = arrived[q, 8:, part:] + vectors[taps + 2 : taps + 3, at]
    keep(branch, branch_out)
    keep(gelu_in, gelu_out)
    ends[...] = jnp.zeros(ends.shape, WIDE)
    entering[...] = jnp.zeros(ends.shape, WIDE)

    def one_head(h, at):
        def vector(i):
            return vectors[i : i + 1, at]

        conv_here = vector(taps) + vector(0) * (branch[8:, at] + vector(taps + 1))
        for k in range(1, taps):
            earlier = branch[8 - k : 8 - k + steps, at] + vector(taps + 1)
            conv_here = conv_here + vector(k) * jnp.where(spot >= k, earlier, 0.0)
        conv[:, at] = conv_here
        low = conv_here.astype(LOW)
        input_gate = jax.nn.sigmoid(
            jnp.dot(low, block_of(blocks, h), preferred_element_type=WIDE) + vector(taps + 3)
        )
        decay_gate = jax.nn.sigmoid(
            jnp.dot(low, block_of(blocks, heads + h), preferred_element_type=WIDE)
            + vector(taps + 4)
        )
        in_gate[:, at] = input_gate
        dec_gate[:, at] = decay_gate
        log_decay = vector(taps + 5) * decay_gate
        decay = jnp.where(starting, 0.0, jnp.exp(log_decay))
        multiplier = jnp.where(starting, 1.0, jnp.sqrt(minus_expm1(2.0 * log_decay)))
        reach, value = scan_rows(decay, multiplier * input_gate * conv_here, False)
        running[:, at] = reach
        local_state[:, at] = value
        ends[0:1, at] = reach[steps - 1 :, :]
        ends[1:2, at] = value[steps - 1 :, :]
        side[:, at] = gelu(gelu_in[:, at])

    each_head(heads, block, one_head)
    for scratch, output in (
        (conv, conv_out), (in_gate, in_out), (dec_gate, dec_out), (side, side_out),
    ):
        keep(scratch, output)
    own = links.keep(ends, table.at[row])
    advance(output_in)
    own.wait()
    entering[0:1, :] = carry_over(links, place, ends, table, False)

    def mix(h, at):
        value = local_state[:, at] + running[:, at] * entering[0:1, at]
        state[:, at] = value
        mixed[:, at] = (value * side[:, at]).astype(LOW)

    each_head(heads, block, mix)
    mine = links.keep(mixed, mixed_all.at[strip(row, steps)])
    mixes = gather_rows(
        links,
        place,
        lambda h: mixed.at[pl.ds(steps // 2 * h, steps // 2)],
        lambda q, h: mixed_all.at[strip(2 * q + h, steps // 2)],
    )
    advance(mixes)
    keep(state, state_out)
    keep(entering, entering_out)
    finish(output_in)
    keep(wout_all, wout_out)
    advance(mixes, up_in)
    finish(mixes)
    mine.wait()
    keep(mixed_all, mixed_out)

    def product_rows(first):
        def body(i, carry):
            rows = pl.ds(pl.multiple_of(first * tall + i * steps, 16), steps)
            partial[rows] = jnp.dot(mixed_all[rows], wout_all[...], preferred_element_type=WIDE)
            return carry

        lax.fori_loop(0, tall // steps, body, 0)

    product_rows(place.other)
    swap = links.copy(partial.at[strip(place.other, tall)], theirs, col=place.other)
    swap.start()
    product_rows(col)
    swap.wait_recv()

    def add(rows):
        at = pl.ds(pl.multiple_of(col * tall + rows.start, 16), rows.size)
        here[rows] = partial[at] + theirs[rows] + x_all[at, lanes(row, narrow)].astype(WIDE)

    by_rows(tall, add)

    def quarter_of(q):
        return here.at[strip(q, quarter)]

    mine = links.keep(quarter_of(row), wide.at[:, lanes(row, narrow)])
    middles = exchange_rows(links, place, quarter_of, lambda q: wide.at[:, lanes(q, narrow)])
    advance(middles)
    mine.wait()
    finish(middles)
    swap.wait_send()

    def second_norm(rows):
        value = wide[rows] + width[1:2, :]
        middle[rows] = value
        mean = jnp.sum(value * value, axis=1, keepdims=True) / full
        normed[rows] = (value * lax.rsqrt(mean + epsilon) * (1.0 + width[3:4, :])).astype(LOW)

    by_rows(quarter, second_norm)
    keep(middle, middle_out)
    keep(normed, normed_out)
    finish(gate_in, up_in)
    for copy in kept:
        copy.wait()


def feed_forward(
    count, normed, cot, wgate, up_own, wdown, biases, normed_all, cot_all, gate_all, up_all, hidden_out,
    gate_out, up_out, sums, gate_w, up_w, down_w, piece, gate_v, up_v, grad_v, hidden, grad_gate,
    grad_up, cot_here, normed_here, send, recv, local,
):
    place = Place(count)
    links = Links(send, recv, local)
    row, z, col = place.row, place.dp, place.col
    greet(place, rows=True, line=True, cores=True)
    quarter, full = normed.shape
    narrow, pair = full // 4, 2 * quarter
    units = wdown.shape[0]
    middle = count // 2
    kept = [
        links.keep(wgate, gate_w.at[row]),
        links.keep(up_own, up_w.at[row]),
    ]
    load = links.keep(wdown, down_w)

    def tokens(own, buffer, whole):
        def at(b):
            return whole.at[strip(2 * b + col, quarter)]

        relay = Relay(links, own, buffer, at(z))
        return LineGather(links, place, own, at), relay

    def columns_of(own, whole):
        yield from gather_rows(
            links,
            place,
            lambda h: own.at[pl.ds(middle * h, middle)],
            lambda q, h: whole.at[q, pl.ds(middle * h, middle)],
        )

    def neighbours(step, body):
        if step == 0:
            body(z)
            return

        def lap(i, carry):
            b = z - step + 2 * step * i
            pl.when((b >= 0) & (b < count))(lambda: body(place.turn(b)))
            return carry

        lax.fori_loop(0, 2, lap, 0)

    def with_piece(source, body):
        k, links.kept = links.kept, links.kept + 1

        def inner(b):
            load = pltpu.make_async_copy(source.at[strip(b, pair)], piece, links.local.at[k])
            load.start()
            load.wait()
            body(strip(b, pair))

        return inner

    def inward(whole, i, values):
        def body(rows):
            weight = whole[...].astype(LOW).reshape(full, units)
            values[rows] = (
                jnp.dot(piece[...], weight, preferred_element_type=WIDE) + biases[i : i + 1, :]
            )

        return body

    def backward(rows):
        grad_v[rows] = lax.dot_general(
            piece[...], down_w[...], (((1,), (1,)), ((), ())), preferred_element_type=WIDE
        )

    def outward(rows):
        def body(inner):
            at = pl.ds(pl.multiple_of(rows.start + inner.start, 16), inner.size)
            gate, up, grad = gate_v[at], up_v[at], grad_v[at]
            t = jnp.tanh(ROOT * (gate + CUBE * (gate * gate * gate)))
            side = 0.5 * gate * (1.0 + t)
            slope = 0.5 * (1.0 + t) + 0.5 * gate * (1.0 - t * t) * (
                ROOT * (1.0 + 3.0 * CUBE * (gate * gate))
            )
            hidden[at] = (side * up).astype(LOW)
            gate, up = grad * up * slope, grad * side
            grad_gate[at] = gate.astype(LOW)
            grad_up[at] = up.astype(LOW)
            sums[0:1, :] += jnp.sum(gate, axis=0, keepdims=True)
            sums[1:2, :] += jnp.sum(up, axis=0, keepdims=True)

        by_rows(pair, body)

    gates, ups = columns_of(wgate, gate_w), columns_of(up_own, up_w)
    cots, cot_relay = tokens(cot, cot_here, cot_all)
    norms, norm_relay = tokens(normed, normed_here, normed_all)
    cots.start()
    advance(gates, ups)
    cot_relay.wait()
    sums[...] = jnp.zeros(sums.shape, WIDE)
    load.wait()
    cots.ready(0)
    back = with_piece(cot_all, backward)
    neighbours(0, back)
    into = with_piece(normed_all, inward(gate_w, 0, gate_v))
    for step in range(1, count):
        cots.step(step)
        if step == 1:
            norms.start()
        else:
            norms.step(step - 1)
        cots.ready(step)
        neighbours(step, back)
    advance(gates, ups)
    norm_relay.wait()
    finish(gates)
    for copy in kept:
        copy.wait()
    kept.clear()
    kept.append(links.keep(gate_w, gate_all))
    for step in range(count - 1):
        norms.ready(step)
        neighbours(step, into)
    norms.step(count - 1)
    norms.ready(count - 1)
    neighbours(count - 1, into)
    finish(ups)
    kept.append(links.keep(up_w, up_all))
    into_up = with_piece(normed_all, inward(up_w, 1, up_v))

    def last(b, carry):
        into_up(b)
        outward(strip(b, pair))
        return carry

    lax.fori_loop(0, count, last, 0)
    cots.close()
    norms.close()
    kept.append(links.keep(hidden, hidden_out))
    kept.append(links.keep(grad_gate, gate_out))
    kept.append(links.keep(grad_up, up_out))
    for copy in kept:
        copy.wait()


def side_by_side(blocks):
    return jnp.concatenate([blocks[i] for i in range(blocks.shape[0])], axis=1)


def columns(matrix, parts):
    width = matrix.shape[1] // parts
    return jnp.stack([matrix[:, i * width : (i + 1) * width] for i in range(parts)])


def padded_rows(rows, height, width):
    return jnp.pad(rows, ((0, height - rows.shape[0]), (0, width - rows.shape[1])))


def rounded(values):
    return lax.reduce_precision(values, 8, 7)


def round_up(size, step):
    return -(-size // step) * step


def shards(
    inputs,
    positions,
    branch_matrix,
    gelu_matrix,
    output_matrix,
    gate_matrix,
    up_matrix,
    down_matrix,
    input_blocks,
    decay_blocks,
    conv_taps,
    conv_bias,
    branch_bias,
    gelu_bias,
    input_bias,
    decay_bias,
    decay_param,
    output_bias,
    gate_bias,
    up_bias,
    down_bias,
    norm_first,
    norm_second,
    cotangent,
):
    count, rows_count, cores = lax.axis_size("dp"), lax.axis_size("row"), lax.axis_size("col")
    place_dp, place_row = lax.axis_index("dp"), lax.axis_index("row")
    tall, narrow = inputs.shape
    quarter, full, tokens = tall // rows_count, narrow * rows_count, tall * cores
    depth, width = branch_matrix.shape
    part = width // rows_count
    hidden_part = down_matrix.shape[0]
    heads, block_part, block = input_blocks.shape
    taps = conv_taps.shape[0]
    steps = positions.shape[0]
    splits = rows_count if block_part % (16 * rows_count) == 0 else 1
    share = block_part // splits
    back_share = block_part // rows_count
    remote, local = 64 + 24 * count, 40 + 6 * count

    wxy = jnp.concatenate(
        (columns(branch_matrix.astype(LOW), rows_count), columns(gelu_matrix.astype(LOW), rows_count)),
        axis=2,
    )
    if depth % 16:
        wxy = wxy.astype(WIDE)
    blocks_low = jnp.concatenate((input_blocks, decay_blocks), axis=0).astype(LOW)
    blk = lax.dynamic_slice_in_dim(
        blocks_low, place_row * share if splits > 1 else 0, share, 1
    )
    channel_rows = jnp.concatenate(
        (
            conv_taps,
            jnp.stack((conv_bias, branch_bias, gelu_bias, input_bias, decay_bias)),
        ),
        axis=0,
    )
    decay_raw = rounded(decay_param)
    channel_rows = jnp.concatenate(
        (rounded(channel_rows), -8.0 * jax.nn.softplus(decay_raw)[None, :]), axis=0
    )
    channel_size = channel_rows.shape[1]
    cvec = padded_rows(
        channel_rows,
        round_up(taps + 6, 8),
        round_up(channel_size, 128),
    )
    wvec = padded_rows(
        rounded(jnp.stack((norm_first, output_bias, down_bias, norm_second))),
        8,
        round_up(depth, 128),
    )
    spots = positions[:, None]
    heads_all = 2 * heads
    whole_tokens = ((tokens, full), LOW, False)
    wide_tokens = ((steps, width), WIDE, False)
    nf_shape = pltpu.VMEM((16 + tokens, full), LOW)
    wxy_kind = wxy.dtype
    tokens_scratch = pltpu.VMEM((steps, width), WIDE)
    eight_rows = pltpu.VMEM((8, width), WIDE)
    table_rows = pltpu.VMEM((rows_count, 8, width), WIDE)
    blocks_shape = (heads_all, count, splits, share, block)
    hidden_shape = (rows_count, count, depth, hidden_part)
    here_scratch = pltpu.VMEM((tall, narrow), WIDE)
    (
        normed_first, x_own, cot_own, wxy_all, wout_all, gate_own, up_own, down_all, blocks, vectors,
        width_all, branch, gelu_in, side, conv, input_gate, decay_gate, state, entering, mixed_all,
        middle, normed_own,
    ) = call(
        functools.partial(forward, count, taps),
        "forward",
        1,
        [
            (inputs, False),
            (cotangent, False),
            (wxy, False),
            (output_matrix.astype(LOW), False),
            (columns(gate_matrix.astype(LOW), count).astype(wxy_kind), False),
            (columns(up_matrix.astype(LOW), count).astype(wxy_kind), False),
            (down_matrix.astype(LOW), False),
            (blk, False),
            (cvec, False),
            (wvec, False),
            (spots, True),
        ],
        [
            whole_tokens,
            ((quarter, full), LOW, False),
            ((quarter, full), LOW, False),
            ((rows_count, count * depth, 2 * part), wxy_kind, False),
            ((width, narrow), LOW, False),
            (hidden_shape[1:], wxy_kind, False),
            (hidden_shape[1:], wxy_kind, False),
            ((hidden_part, full), LOW, False),
            (blocks_shape, LOW, False),
            ((cvec.shape[0], width), WIDE, False),
            ((8, full), WIDE, False),
            ((steps + 8, width), WIDE, False),
            wide_tokens,
            wide_tokens,
            wide_tokens,
            wide_tokens,
            wide_tokens,
            wide_tokens,
            ((8, width), WIDE, False),
            ((tokens, width), LOW, False),
            ((quarter, full), WIDE, False),
            ((quarter, full), LOW, False),
        ],
        [
            pltpu.VMEM((tokens, full), LOW),
            nf_shape,
            pltpu.VMEM((rows_count, count * depth, 2 * part), wxy_kind),
            pltpu.VMEM((width, narrow), LOW),
            pltpu.VMEM(blocks_shape, LOW),
            pltpu.VMEM((count,) + cvec.shape, WIDE),
            pltpu.VMEM((rows_count, count) + wvec.shape, WIDE),
            pltpu.VMEM((cvec.shape[0], width), WIDE),
            pltpu.VMEM((8, full), WIDE),
            pltpu.VMEM((rows_count, steps + 16, 2 * part), WIDE),
            pltpu.VMEM((rows_count, steps + 8, 2 * part), WIDE),
            pltpu.VMEM((steps + 8, width), WIDE),
            tokens_scratch,
            tokens_scratch,
            tokens_scratch,
            tokens_scratch,
            tokens_scratch,
            tokens_scratch,
            tokens_scratch,
            tokens_scratch,
            eight_rows,
            table_rows,
            eight_rows,
            pltpu.VMEM((steps, width), LOW),
            pltpu.VMEM((tokens, width), LOW),
            pltpu.VMEM((tokens, narrow), WIDE),
            here_scratch,
            here_scratch,
            pltpu.VMEM((quarter, full), WIDE),
            pltpu.VMEM((quarter, full), WIDE),
            pltpu.VMEM((quarter, full), LOW),
            pltpu.VMEM((depth, hidden_part), wxy_kind),
            pltpu.VMEM((depth, hidden_part), wxy_kind),
            pltpu.VMEM((hidden_part, narrow), LOW),
            pltpu.VMEM((quarter, narrow), LOW),
        ],
        remote,
        local,
    )
    wxy_all = wxy_all.reshape(full, 2 * part).astype(LOW)
    blocks = blocks.reshape(heads_all, block, block)
    gelu_pull = jax.vjp(jax.nn.gelu, gelu_in)[1]

    hidden_tokens = cores * count * quarter
    units_rows = ((hidden_tokens, hidden_part), LOW, False)
    biases = padded_rows(rounded(jnp.stack((gate_bias, up_bias))), 8, hidden_part)
    weight_scratch = pltpu.VMEM(hidden_shape, wxy_kind)
    units_wide = pltpu.VMEM((hidden_tokens, hidden_part), WIDE)
    units_low = pltpu.VMEM((hidden_tokens, hidden_part), LOW)
    (
        normed_second, cot_all, gate_all, up_all, hidden, grad_gate_low, grad_up_low, hidden_part_sums,
    ) = call(
        functools.partial(feed_forward, count),
        "feed_forward",
        2,
        [
            (normed_own, False),
            (cot_own, False),
            (gate_own, False),
            (up_own, False),
            (down_all, False),
            (biases, True),
        ],
        [
            ((hidden_tokens, full), LOW, False),
            ((hidden_tokens, full), LOW, False),
            (hidden_shape, wxy_kind, False),
            (hidden_shape, wxy_kind, False),
            units_rows,
            units_rows,
            units_rows,
            ((8, hidden_part), WIDE, True),
        ],
        [
            weight_scratch,
            weight_scratch,
            pltpu.VMEM((hidden_part, full), LOW),
            pltpu.VMEM((cores * quarter, full), LOW),
            units_wide,
            units_wide,
            units_wide,
            units_low,
            units_low,
            units_low,
            pltpu.VMEM((quarter, full), LOW),
            pltpu.VMEM((quarter, full), LOW),
        ],
        remote,
        local,
    )
    by_device = (count, cores, quarter, full)
    token_scratch = [
        pltpu.VMEM((count, quarter, full), LOW),
        pltpu.VMEM((count, quarter, full), LOW),
        *line_buffers(count, 2, quarter // 2, full),
    ]
    token_low = pltpu.VMEM((quarter, full), LOW)
    back_outs = [
        ((quarter, full), WIDE, True),
        ((tokens, narrow), LOW, False),
        ((8, full), WIDE, True),
        ((2, narrow // 2, hidden_part), LOW, True),
    ]
    back_scratch = token_scratch + [token_low, token_low, row_buffers(narrow, hidden_part)]
    inside = count <= 4
    if inside:
        grad_middle, grad_middle_all, width_sums, gate_own = call(
            functools.partial(second_norm_back_inside, count),
            "second_norm_back",
            5,
            [
                (grad_gate_low, False),
                (grad_up_low, False),
                (gate_all, False),
                (up_all, False),
                (normed_second, False),
                (cot_all, False),
                (middle, True),
                (width_all, True),
            ],
            back_outs,
            back_scratch
            + [
                units_low,
                units_low,
                weight_scratch,
                weight_scratch,
                pltpu.VMEM((hidden_tokens, narrow), LOW),
                pltpu.VMEM(by_device, LOW),
                pltpu.VMEM((full, hidden_part), LOW),
            ],
            remote,
            local,
        )
    else:
        gate_all = gate_all.reshape(full, hidden_part).astype(LOW)
        up_all = up_all.reshape(full, hidden_part).astype(LOW)
        grad_normed_second = (
            (times_flipped(grad_gate_low, gate_all) + times_flipped(grad_up_low, up_all))
            .astype(LOW)
            .reshape(by_device)
        )
        grad_middle, grad_middle_all, width_sums, gate_own = call(
            functools.partial(second_norm_back, count),
            "second_norm_back",
            5,
            [
                (grad_normed_second, False),
                (cot_all, False),
                (middle, True),
                (width_all, True),
                (left_product(normed_second, grad_gate_low).astype(LOW), False),
            ],
            back_outs,
            back_scratch,
            remote,
            local,
        )
    forward_partial = times(hidden, down_all).astype(LOW).reshape(by_device)

    mixed_outs = [
        ((2, steps // 2, width), WIDE, True),
        ((rows_count, quarter, narrow), LOW, False),
        ((2, narrow // 2, hidden_part), LOW, True),
        ((count, depth, hidden_part), LOW, False),
    ]
    mixed_scratch = (
        [row_buffers(steps, width)]
        + token_scratch
        + [token_low, row_buffers(narrow, hidden_part), pltpu.VMEM((depth, hidden_part), LOW)]
    )
    gate_own = gate_own.reshape(count, depth, hidden_part)
    if inside:
        grad_mixed, layer_out, up_own, gate_blocks, output_partial, down_partial = call(
            functools.partial(mixed_and_output_inside, count),
            "mixed_and_output",
            6,
            [
                (grad_middle_all, False),
                (wout_all, False),
                (mixed_all, False),
                (normed_second, False),
                (cot_all, False),
                (grad_up_low, False),
                (hidden, False),
                (forward_partial, False),
                (middle, True),
                (width_all, True),
                (gate_own, False),
            ],
            mixed_outs + [((width, narrow), LOW, False), ((hidden_part, full), LOW, False)],
            mixed_scratch
            + [
                pltpu.VMEM((tokens, narrow), LOW),
                pltpu.VMEM((width, narrow), LOW),
                pltpu.VMEM((tokens, width), LOW),
                pltpu.VMEM((hidden_tokens, narrow), LOW),
                units_low,
                units_low,
                pltpu.VMEM((tokens, width), LOW),
                pltpu.VMEM((full, hidden_part), LOW),
                pltpu.VMEM((width, narrow), LOW),
                pltpu.VMEM((hidden_part, full), LOW),
            ],
            remote,
            local,
        )
    else:
        down_partial = left_product(hidden, cot_all).astype(LOW)
        output_partial = left_product(mixed_all, grad_middle_all).astype(LOW)
        grad_mixed, layer_out, up_own, gate_blocks = call(
            functools.partial(mixed_and_output, count),
            "mixed_and_output",
            6,
            [
                (times_flipped(grad_middle_all, wout_all).astype(LOW), False),
                (forward_partial, False),
                (middle, True),
                (width_all, True),
                (left_product(normed_second, grad_up_low).astype(LOW), False),
                (gate_own, False),
            ],
            mixed_outs,
            mixed_scratch,
            remote,
            local,
        )
    up_own = up_own.reshape(count, depth, hidden_part)
    grad_mixed = grad_mixed.reshape(steps, width)

    sums_rows = round_up(taps + 6, 8)
    output_parts = 2 if output_matrix.shape[0] % 32 == 0 else 1
    if inside:
        channel_part, block_sums, grad_projected, output_grad, up_blocks = call(
            functools.partial(recurrence_back_inside, count, taps),
            "recurrence_backward",
            7,
            [
                (array, True)
                for array in (
                    branch,
                    side,
                    gelu_in,
                    spots,
                    vectors,
                    blocks,
                    conv,
                    input_gate,
                    decay_gate,
                    state,
                    entering,
                    grad_mixed,
                )
            ]
            + [
                (output_partial.reshape((count,) + output_matrix.shape), False),
                (up_own, False),
            ],
            [
                ((sums_rows, width), WIDE, True),
                ((2 * heads, block, block), WIDE, True),
                ((rows_count, steps, 2 * part), LOW, False),
                (output_matrix.shape, WIDE, True),
                ((count, depth, hidden_part), LOW, False),
            ],
            [
                pltpu.VMEM((steps, width), LOW),
                pltpu.VMEM((steps, width), LOW),
                pltpu.VMEM((rows_count, steps, 2 * part), LOW),
                tokens_scratch,
                tokens_scratch,
                tokens_scratch,
                eight_rows,
                table_rows,
                pltpu.VMEM((2, 8, width), WIDE),
                eight_rows,
                pltpu.VMEM((steps + 8, block), WIDE),
                pltpu.VMEM((steps + 8, block), WIDE),
                *line_buffers(count, output_parts, output_matrix.shape[0] // output_parts, narrow),
                pltpu.VMEM((count,) + output_matrix.shape, LOW),
                pltpu.VMEM((depth, hidden_part), LOW),
            ],
            remote,
            local,
        )
        grad_projected = grad_projected.reshape(tokens, 2 * part)
    else:
        grad_gelu = gelu_pull(grad_mixed * state)[0]
        grad_branch_low, channel_part, block_sums = call(
            functools.partial(recurrence_backward, count, taps),
            "recurrence_backward",
            7,
            [
                (array, True)
                for array in (
                    branch,
                    side,
                    spots,
                    vectors,
                    blocks,
                    conv,
                    input_gate,
                    decay_gate,
                    state,
                    entering,
                    grad_mixed,
                )
            ],
            [
                ((steps, width), LOW, True),
                ((round_up(taps + 6, 8), width), WIDE, True),
                ((2 * heads, block, block), WIDE, True),
            ],
            [
                tokens_scratch,
                tokens_scratch,
                tokens_scratch,
                eight_rows,
                table_rows,
                pltpu.VMEM((2, 8, width), WIDE),
                eight_rows,
                pltpu.VMEM((steps + 8, block), WIDE),
                pltpu.VMEM((steps + 8, block), WIDE),
            ],
            remote,
            local,
        )
        grad_gelu_low = grad_gelu.astype(LOW)
        projected_grads = jnp.concatenate(
            (columns(grad_branch_low, rows_count), columns(grad_gelu_low, rows_count)), axis=2
        )
        grad_projected, output_grad, up_blocks = call(
            functools.partial(spread_gradients, count),
            "spread_gradients",
            8,
            [
                (projected_grads, False),
                (output_partial.reshape((count,) + output_matrix.shape), False),
                (up_own, False),
            ],
            [
                ((rows_count, steps, 2 * part), LOW, False),
                (output_matrix.shape, WIDE, True),
                ((count, depth, hidden_part), LOW, False),
            ],
            [
                *line_buffers(count, output_parts, output_matrix.shape[0] // output_parts, narrow),
                pltpu.VMEM((count,) + output_matrix.shape, LOW),
            ],
            remote,
            local,
        )
        grad_projected = grad_projected.reshape(tokens, 2 * part)
        channel_part = channel_part.at[taps + 5].set(jnp.sum(grad_gelu, axis=0))
    hidden_part_sums = padded_rows(hidden_part_sums, 8, round_up(hidden_part, 128))
    block_in = (
        block_sums.astype(LOW)
        .reshape(2 * heads, count, rows_count, back_share, block)
        .transpose(2, 1, 0, 3, 4)
        .reshape(rows_count, 2, count // 2 * 2 * heads * back_share, block)
    )
    channel_shape, sums_shape = channel_part.shape, hidden_part_sums.shape
    block_rows = 2 * heads * back_share
    first_outs = [
        ((rows_count, quarter, narrow), WIDE, False),
        ((rows_count, depth, 2 * part), LOW, False),
        ((hidden_part, narrow), WIDE, True),
        ((2, 8, narrow), WIDE, True),
        (channel_shape, WIDE, True),
        ((rows_count, block_rows, block), LOW, False),
        (sums_shape, WIDE, True),
    ]
    first_scratch = [
        pltpu.VMEM((rows_count, quarter, full), LOW),
        pltpu.VMEM((rows_count, quarter, full), LOW),
        pltpu.VMEM((rows_count, quarter, full), LOW),
        row_buffers(quarter, full),
        token_low,
        pltpu.VMEM((rows_count, quarter, narrow), WIDE),
        pltpu.VMEM((8, full), WIDE),
        pltpu.VMEM((count, rows_count, depth, 2 * part), LOW),
        *line_buffers(count, rows_count, depth, 2 * part),
        pltpu.VMEM((rows_count, depth, 2 * part), LOW),
        pltpu.VMEM((rows_count, 8, narrow), WIDE),
        pltpu.VMEM((count, 8, narrow), WIDE),
        pltpu.VMEM((rows_count, 8, narrow), WIDE),
        pltpu.VMEM((rows_count,) + channel_shape, WIDE),
        pltpu.VMEM((count,) + channel_shape, WIDE),
        pltpu.VMEM((rows_count,) + sums_shape, WIDE),
        row_buffers(2 * block_in.shape[2], block),
        pltpu.VMEM((2, block_in.shape[2], block), WIDE),
        *line_buffers(count, 1, block_rows, block),
        pltpu.VMEM((block_rows, block), LOW),
        row_buffers(hidden_part, narrow),
    ]
    sums_in = [
        (width_sums, True),
        (channel_part, True),
        (hidden_part_sums, True),
        (block_in, False),
    ]
    if inside:
        first_kernel, first_ins = first_norm_back_inside, [
            (grad_projected, False),
            (wxy_all, False),
            (normed_first, False),
            (x_own, False),
            (grad_middle, True),
            (width_all, True),
            (down_partial, False),
        ]
        first_scratch += [
            pltpu.VMEM((tokens, 2 * part), LOW),
            pltpu.VMEM((full, 2 * part), LOW),
            pltpu.VMEM((tokens, full), LOW),
            pltpu.VMEM((cores, rows_count, quarter, full), LOW),
        ]
    else:
        first_kernel, first_ins = first_norm_back, [
            (
                times_flipped(grad_projected, wxy_all)
                .astype(LOW)
                .reshape(cores, rows_count, quarter, full),
                False,
            ),
            (x_own, False),
            (grad_middle, True),
            (width_all, True),
            (
                left_product(normed_first, grad_projected)
                .astype(LOW)
                .reshape(rows_count, count, depth, 2 * part),
                False,
            ),
            (down_partial, False),
        ]
    input_grad, proj_grad, down_grad, width_sums, channel_sums, block_grads, hidden_sums = call(
        functools.partial(first_kernel, count),
        "first_norm_back",
        9,
        first_ins + sums_in,
        first_outs,
        first_scratch,
        remote,
        local,
    )
    branch_grad = side_by_side(proj_grad[:, :, :part]).astype(WIDE)
    gelu_grad = side_by_side(proj_grad[:, :, part:]).astype(WIDE)
    block_grads = (
        block_grads.reshape(rows_count, 2 * heads, back_share, block)
        .transpose(1, 0, 2, 3)
        .reshape(2 * heads, block_part, block)
        .astype(WIDE)
    )
    channel_sums = lax.dynamic_slice_in_dim(channel_sums, place_dp * channel_size, channel_size, 1)
    width_sums = lax.dynamic_slice_in_dim(
        width_sums[0] + width_sums[1], place_dp * depth, depth, 1
    )
    decay_param_grad = -8.0 * channel_sums[taps + 4] * jax.nn.sigmoid(decay_raw)

    return (
        layer_out.reshape(tall, narrow),
        input_grad.reshape(tall, narrow),
        branch_grad,
        gelu_grad,
        output_grad,
        side_by_side(gate_blocks).astype(WIDE),
        side_by_side(up_blocks).astype(WIDE),
        down_grad,
        block_grads[:heads],
        block_grads[heads:],
        channel_sums[:taps],
        channel_sums[taps],
        channel_sums[taps + 1],
        channel_sums[taps + 5],
        channel_sums[taps + 2],
        channel_sums[taps + 3],
        decay_param_grad,
        width_sums[1],
        hidden_sums[0, :hidden_part],
        hidden_sums[1, :hidden_part],
        width_sums[2],
        width_sums[3],
        width_sums[0],
    )


def solution(mesh):
    in_specs = (
        P(("dp", "col"), "row"),
        P(("dp", "row")),
        P(("row", "dp"), "col"),
        P(("row", "dp"), "col"),
        P(("col", "dp"), "row"),
        P(("row", "dp"), "col"),
        P(("row", "dp"), "col"),
        P(("col", "dp"), "row"),
        P("col", "dp", None),
        P("col", "dp", None),
        P(None, ("col", "dp")),
        P(("col", "dp")),
        P(("col", "dp")),
        P(("col", "dp")),
        P(("col", "dp")),
        P(("col", "dp")),
        P(("col", "dp")),
        P(("row", "dp")),
        P(("col", "dp")),
        P(("col", "dp")),
        P(("row", "dp")),
        P(("row", "dp")),
        P(("row", "dp")),
        P(("dp", "col"), "row"),
    )
    out_specs = (
        P(("dp", "col"), "row"),
        P(("dp", "col"), "row"),
        P(("row", "dp"), "col"),
        P(("row", "dp"), "col"),
        P(("col", "dp"), "row"),
        P(("row", "dp"), "col"),
        P(("row", "dp"), "col"),
        P(("col", "dp"), "row"),
        P("col", "dp", None),
        P("col", "dp", None),
        P(None, ("col", "dp")),
        P(("col", "dp")),
        P(("col", "dp")),
        P(("col", "dp")),
        P(("col", "dp")),
        P(("col", "dp")),
        P(("col", "dp")),
        P(("row", "dp")),
        P(("col", "dp")),
        P(("col", "dp")),
        P(("row", "dp")),
        P(("row", "dp")),
        P(("row", "dp")),
    )
    return jax.shard_map(shards, mesh=mesh, in_specs=in_specs, out_specs=out_specs, check_vma=False)
```

```python
import functools

import jax
import jax.numpy as jnp
from jax import lax
from jax.experimental import pallas as pl
from jax.experimental.pallas import tpu as pltpu
from jax.sharding import PartitionSpec as P

epsilon = 1e-06
ROOT = (2.0 / 3.141592653589793) ** 0.5
CUBE = 0.044715
LOW = jnp.bfloat16
WIDE = jnp.float32
MESH = pl.DeviceIdType.MESH
VMEM = pl.BlockSpec(memory_space=pltpu.VMEM)
ANY = pl.BlockSpec(memory_space=pl.ANY)


def times(piece, matrix):
    return jnp.dot(piece, matrix, preferred_element_type=WIDE)


def times_flipped(piece, matrix):
    return lax.dot_general(piece, matrix, (((1,), (1,)), ((), ())), preferred_element_type=WIDE)


def left_product(left, right):
    return lax.dot_general(left, right, (((0,), (0,)), ((), ())), preferred_element_type=WIDE)


class Links:
    def __init__(self, send, recv, local):
        self.send, self.recv, self.local = send, recv, local
        self.sent = self.kept = 0

    def copy(self, src, dst, **where):
        k, self.sent = self.sent, self.sent + 1
        return pltpu.make_async_remote_copy(
            src_ref=src,
            dst_ref=dst,
            send_sem=self.send.at[k],
            recv_sem=self.recv.at[k],
            device_id=where,
            device_id_type=MESH,
        )

    def keep(self, src, dst):
        k, self.kept = self.kept, self.kept + 1
        copy = pltpu.make_async_copy(src, dst, self.local.at[k])
        copy.start()
        return copy


class Relay:
    def __init__(self, links, src, buffer, dst):
        self.links, self.buffer, self.dst, self.store = links, buffer, dst, None
        self.load = links.keep(src, buffer)

    def pass_on(self):
        if self.store is None:
            self.load.wait()
            self.store = self.links.keep(self.buffer, self.dst)

    def wait(self):
        self.pass_on()
        self.store.wait()


class Place:
    def __init__(self, count_dp):
        self.row, self.dp, self.col = (lax.axis_index(name) for name in ("row", "dp", "col"))
        self.count = count_dp
        first, second = lax.rem(self.row, 2), lax.div(self.row, 2)
        self.near = [self.row, self.row + 1 - 2 * first, self.row + 2 - 4 * second, 3 - self.row]
        self.other = 1 - self.col

    def turn(self, index):
        return lax.rem(index + self.count, self.count)


def greet(place, rows=False, line=False, cores=False):
    barrier = pltpu.get_barrier_semaphore()
    partners = []
    if rows:
        partners += [{"row": place.near[k]} for k in range(1, 4)]
    if line:
        partners += [{"dp": place.turn(place.dp + k)} for k in range(1, place.count)]
    if cores:
        partners += [{"col": place.other}]
    for where in partners:
        pl.semaphore_signal(barrier, inc=1, device_id=where, device_id_type=MESH)
    pl.semaphore_wait(barrier, len(partners))


def run(tasks):
    live = list(tasks)
    while live:
        live = [task for task in live if next(task, None) is not None]


def advance(*tasks):
    for task in tasks:
        next(task, None)


def finish(*tasks):
    run(tasks)


def chain(*tasks):
    for task in tasks:
        yield from task


def when(condition, action):
    pl.when(condition)(lambda: action() and None)


def halves(size):
    first = -(-size // 32) * 16
    return (pl.ds(0, first), pl.ds(first, size - first))


def by_rows(count, body):
    step = 16 if count % 16 == 0 else count

    def lap(i, carry):
        body(pl.ds(pl.multiple_of(i * step, step), step))
        return carry

    lax.fori_loop(0, count // step, lap, 0)


def by_pieces(pieces, height, body):
    def lap(i, carry):
        by_rows(height, lambda rows: body(i, rows))
        return carry

    if pieces == 1:
        by_rows(height, lambda rows: body(0, rows))
    else:
        lax.fori_loop(0, pieces, lap, 0)


def gather_rows(links, place, own, piece):
    row, near, side, _ = place.near
    out = [
        links.copy(own(0), piece(row, 0), row=near),
        links.copy(own(1), piece(row, 1), row=side),
        links.copy(own(1), piece(row, 1), row=near),
        links.copy(own(0), piece(row, 0), row=side),
    ]
    for copy in out:
        copy.start()
    yield 1
    out[0].wait_recv()
    out.append(links.copy(piece(near, 0), piece(near, 0), row=side))
    out[4].start()
    out[1].wait_recv()
    out.append(links.copy(piece(side, 1), piece(side, 1), row=near))
    out[5].start()
    yield 1
    for copy in out[2:]:
        copy.wait_recv()
    for copy in out:
        copy.wait_send()


def exchange_rows(links, place, source, target):
    out = [
        links.copy(source(place.near[k]), target(place.row), row=place.near[k])
        for k in range(1, 4)
    ]
    for copy in out:
        copy.start()
    yield 1
    for copy in out:
        copy.wait_recv()
    for copy in out:
        copy.wait_send()


def exchange_line(links, place, source, target):
    out = []
    for k in range(1, place.count):
        far = place.turn(place.dp + k)
        out.append(links.copy(source(far), target(place.dp), dp=far))
    for copy in out:
        copy.start()
    yield 1
    for copy in out:
        copy.wait_recv()
    for copy in out:
        copy.wait_send()


def gather_line(links, place, own, piece, share=False):
    z, count, turn = place.dp, place.count, place.turn
    ups, downs, shared = [], [], []

    def pass_on(block, valid):
        copy = links.copy(piece(block), piece(block), col=place.other)
        when(valid, copy.start)
        shared.append((copy, valid))

    if share:
        copy = links.copy(own, piece(z), col=place.other)
        copy.start()
        shared.append((copy, z >= 0))
    for step in range(1, count + 1):
        if step > 1:
            yield 1
            below, above = z >= step - 1, z <= count - step
            when(below, ups[-1].wait_recv)
            when(above, downs[-1].wait_recv)
        if step < count:
            low, high = turn(z - step + 1), turn(z + step - 1)
            ups.append(
                links.copy(own if step == 1 else piece(low), piece(low), dp=turn(z + 1))
            )
            downs.append(
                links.copy(own if step == 1 else piece(high), piece(high), dp=turn(z - 1))
            )
            when((z >= step - 1) & (z < count - 1), ups[-1].start)
            when((z <= count - step) & (z > 0), downs[-1].start)
        if step > 1 and share:
            pass_on(turn(z - step + 1), below)
            pass_on(turn(z + step - 1), above)
    yield 1
    for copy, valid in shared:
        when(valid, copy.wait_recv)
    for step in range(1, count):
        when((z >= step - 1) & (z < count - 1), ups[step - 1].wait_send)
        when((z <= count - step) & (z > 0), downs[step - 1].wait_send)
    for copy, valid in shared:
        when(valid, copy.wait_send)


class LineGather:
    def __init__(self, links, place, own, piece):
        self.links, self.place, self.own, self.piece = links, place, own, piece
        self.ups, self.downs, self.shared = [None], [None], []

    def send(self, step):
        z, count, turn = self.place.dp, self.place.count, self.place.turn
        low, high = turn(z - step + 1), turn(z + step - 1)
        for copies, block, target, valid in (
            (self.ups, low, turn(z + 1), (z >= step - 1) & (z < count - 1)),
            (self.downs, high, turn(z - 1), (z <= count - step) & (z > 0)),
        ):
            source = self.own if step == 1 else self.piece(block)
            copy = self.links.copy(source, self.piece(block), dp=target)
            copies.append((copy, valid))
            when(valid, copy.start)

    def share(self, blocks, own=None):
        out = []
        for block, valid in blocks:
            source = self.piece(block) if own is None else own
            copy = self.links.copy(source, self.piece(block), col=self.place.other)
            when(valid, copy.start)
            out.append((copy, valid))
        self.shared.append(out)

    def start(self):
        self.send(1)
        self.share([(self.place.dp, self.place.dp >= 0)], self.own)

    def step(self, step):
        z, count, turn = self.place.dp, self.place.count, self.place.turn
        below, above = z >= step, z <= count - 1 - step
        when(below, self.ups[step][0].wait_recv)
        when(above, self.downs[step][0].wait_recv)
        if step < count - 1:
            self.send(step + 1)
        self.share([(turn(z - step), below), (turn(z + step), above)])

    def ready(self, step):
        for copy, valid in self.shared[step]:
            when(valid, copy.wait_recv)

    def close(self):
        for copy, valid in self.ups[1:] + self.downs[1:] + sum(self.shared, []):
            when(valid, copy.wait_send)


def scatter_rows(links, place, part, buffers, result, prepare=None, gentle=False):
    row, near, side, far = place.near
    if prepare is not None:
        prepare(far)
    heights = [part(row, h).shape[0] for h in range(2)]

    def buffer(i, h):
        return buffers.at[i, pl.ds(0, heights[h])]

    out = [
        links.copy(part(far, 0), buffer(5, 0), row=side),
        links.copy(part(far, 1), buffer(7, 1), row=near),
        links.copy(part(side, 0), buffer(4, 0), row=side),
        links.copy(part(near, 1), buffer(6, 1), row=near),
    ]
    for i, copy in enumerate(out):
        if i == 2 and gentle:
            yield 1
        if i > 1 and prepare is not None:
            prepare(near if i == 3 else side)
        copy.start()
    if prepare is not None:
        prepare(row)
    loads = [
        links.keep(part(near, 0), buffer(0, 0)),
        links.keep(part(side, 1), buffer(1, 1)),
        links.keep(part(row, 0), buffer(2, 0)),
        links.keep(part(row, 1), buffer(3, 1)),
    ]
    yield 1
    for h, target in ((0, near), (1, side)):
        loads[h].wait()
        out[h].wait_recv()

        def add(rows, h=h):
            total = buffers[h, rows].astype(WIDE) + buffers[5 + 2 * h, rows].astype(WIDE)
            buffers[h, rows] = total.astype(LOW)

        by_rows(heights[h], add)
        out.append(links.copy(buffer(h, h), buffer(8 + h, h), row=target))
        out[-1].start()
        yield 1
    for h in range(2):
        loads[2 + h].wait()
        out[2 + h].wait_recv()
        out[4 + h].wait_recv()

        def finish(rows, h=h):
            result(
                h,
                rows,
                buffers[2 + h, rows].astype(WIDE)
                + buffers[4 + 2 * h, rows].astype(WIDE)
                + buffers[8 + h, rows].astype(WIDE),
            )

        by_rows(heights[h], finish)
    for copy in out:
        copy.wait_send()


def row_buffers(size, width):
    return pltpu.VMEM((10, halves(size)[0].size, width), LOW)


def scatter_line(links, place, ready, term, ups_in, downs_in, staging, result):
    z, count, turn = place.dp, place.count, place.turn
    pieces, height = ups_in.shape[1:3]
    ups, downs = [None], [None]

    def sends_up(t):
        return (z <= t - 1) & (z < count - 1)

    def sends_down(t):
        return (z >= count - t) & (z > 0)

    def fill(slot, block, arrived):
        def body(i, rows):
            value = term(block, i, rows)
            if arrived is not None:
                value = value + arrived[i, rows].astype(WIDE)
            staging[slot, i, rows] = value.astype(LOW)

        by_pieces(pieces, height, body)

    for t in range(1, count):
        ready(t)
        ready(count - t)
        for which in range(2):
            copies, into = ((ups, ups_in), (downs, downs_in))[which]
            sends = (sends_up, sends_down)[which]
            first = (z == 0, z == count - 1)[which]
            block = (turn(z - t), turn(z + t))[which]
            target = (turn(z + 1), turn(z - 1))[which]
            slot = 2 * which + t % 2
            if t > 2:
                when(sends(t - 2), copies[t - 2].wait_send)
            copy = links.copy(staging.at[slot], into.at[t - 1], dp=target)
            copies.append(copy)

            def begin(copy=copy, slot=slot, block=block):
                fill(slot, block, None)
                copy.start()

            when(sends(t) & first, begin)
            if t > 1:

                def go_on(copy=copy, slot=slot, block=block, before=copies[t - 1], into=into, t=t):
                    before.wait_recv()
                    fill(slot, block, into.at[t - 2])
                    copy.start()

                when(sends(t) & jnp.logical_not(first), go_on)
        yield 1
    ready(0)
    last = count - 1
    from_below, from_above = ups_in.at[last - 1], downs_in.at[last - 1]
    when(z > 0, ups[last].wait_recv)
    when(z < last, downs[last].wait_recv)

    def finish(below, above):
        def body(i, rows):
            value = term(z, i, rows)
            if below:
                value = value + from_below[i, rows].astype(WIDE)
            if above:
                value = value + from_above[i, rows].astype(WIDE)
            result(i, rows, value)

        by_pieces(pieces, height, body)

    when(z == 0, lambda: finish(False, True))
    when((z > 0) & (z < last), lambda: finish(True, True))
    when(z == last, lambda: finish(True, False))
    for t in range(max(1, count - 2), count):
        when(sends_up(t), ups[t].wait_send)
        when(sends_down(t), downs[t].wait_send)


def scatter_line_in_parts(links, place, ready, term, ups_in, downs_in, staging, result):
    def part(i):
        return scatter_line(
            links,
            place,
            ready,
            lambda b, _, rows: term(b, i, rows),
            ups_in.at[:, pl.ds(i, 1)],
            downs_in.at[:, pl.ds(i, 1)],
            staging.at[:, pl.ds(i, 1)],
            lambda _, rows, value: result(i, rows, value),
        )

    live = [part(i) for i in range(ups_in.shape[1])]
    while live:
        live = [task for task in live if next(task, None) is not None]
        yield 1


def line_buffers(count, pieces, height, width):
    return [pltpu.VMEM((slots, pieces, height, width), LOW) for slots in (count - 1, count - 1, 4)]


def token_scatter(links, place, partial, ours, theirs, buffers, result, prepare=None):
    out, loads = [], []
    for s in list(range(1, place.count)) + [0]:
        block = place.turn(place.dp - s)
        if prepare is not None:
            prepare(block)
        out.append(
            links.copy(partial.at[block, place.other], theirs.at[block], col=place.other)
        )
        out[-1].start()
        loads.append(links.keep(partial.at[block, place.col], ours.at[block]))
    waited = set()

    def ready(s):
        if s not in waited:
            waited.add(s)
            at = s - 1 if s else place.count - 1
            out[at].wait_recv()
            loads[at].wait()

    height = buffers[0].shape[2]

    def at(i, rows):
        return pl.ds(pl.multiple_of(rows.start + i * height, 16), rows.size)

    def term(block, i, rows):
        here = at(i, rows)
        return ours[block, here].astype(WIDE) + theirs[block, here].astype(WIDE)

    yield 1
    yield from scatter_line_in_parts(
        links, place, ready, term, *buffers, lambda i, rows, value: result(at(i, rows), value)
    )
    for copy in out:
        copy.wait_send()


def call(kernel, name, number, ins, outs, scratch, remote, local):
    return pl.pallas_call(
        kernel,
        in_specs=[VMEM if inside else ANY for _, inside in ins],
        out_specs=[VMEM if inside else ANY for _, _, inside in outs],
        out_shape=[jax.ShapeDtypeStruct(shape, kind) for shape, kind, _ in outs],
        scratch_shapes=list(scratch)
        + [
            pltpu.SemaphoreType.DMA((remote,)),
            pltpu.SemaphoreType.DMA((remote,)),
            pltpu.SemaphoreType.DMA((local,)),
        ],
        compiler_params=pltpu.CompilerParams(
            collective_id=number, has_side_effects=True, vmem_limit_bytes=58 * 1024 * 1024
        ),
        name=name,
    )(*[array for array, _ in ins])


def lanes(index, width):
    return pl.ds(pl.multiple_of(index * width, 128), width)


def strip(index, height, step=16):
    return pl.ds(pl.multiple_of(index * height, step), height)


def combine(earlier, later):
    return (earlier[0] * later[0], later[0] * earlier[1] + later[1])


def scan_rows(decay, value, reverse):
    count = decay.shape[0]
    rows = lax.broadcasted_iota(jnp.int32, decay.shape, 0)
    reach = 1
    while reach < count:
        turn = count - reach if reverse else reach
        inside = rows < count - reach if reverse else rows >= reach
        decay_far = jnp.where(inside, pltpu.roll(decay, turn, 0), 1.0)
        value_far = jnp.where(inside, pltpu.roll(value, turn, 0), 0.0)
        value = decay * value_far + value
        decay = decay * decay_far
        reach *= 2
    return decay, value


def minus_expm1(v):
    series = 1.0 + v / 9.0
    for k in range(8, 1, -1):
        series = 1.0 + (v / k) * series
    return jnp.where(v > -0.5, -v * series, 1.0 - jnp.exp(v))


def each_head(heads, width, body):
    def lap(h, carry):
        body(h, pl.ds(pl.multiple_of(h * width, 128), width))
        return carry

    lax.fori_loop(0, heads, lap, 0)


def carry_over(links, place, ends, table, reverse):
    run([exchange_rows(links, place, lambda q: ends, lambda q: table.at[q])])
    row = place.row
    state = jnp.zeros((1, ends.shape[1]), WIDE)
    for k in range(4):
        q = 3 - k if reverse else k

        def entry(i):
            return table[q, i : i + 1, :]

        reached = q > row if reverse else q < row
        state = jnp.where(reached, entry(0) * state + entry(1), state)
    return state


def recurrence_backward(
    count, taps, proj, side, spots, vectors, blocks, conv_in, in_gate, dec_gate, state_in, entering,
    grad_mixed, branch_out, sums_out, blocks_out, reach, local_grad, branch, ends, table, heads_in,
    heads_here, padded, spread, send, recv, local, links=None, between=lambda: None,
):
    place = Place(count)
    if links is None:
        links = Links(send, recv, local)
        greet(place, rows=True)
    tokens, width = side.shape
    heads, block = blocks.shape[0] // 2, blocks.shape[1]
    spot = spots[...]
    starting = spot == 0
    ends[...] = jnp.zeros(ends.shape, WIDE)

    def backwards(h, at):
        rate = vectors[taps + 5 : taps + 6, at]
        decay = jnp.where(starting, 0.0, jnp.exp(rate * dec_gate[:, at]))
        padded[0:tokens, :] = decay
        padded[tokens:, :] = jnp.ones((8, block), WIDE)
        far, grad = scan_rows(padded[1 : tokens + 1, :], grad_mixed[:, at] * side[:, at], True)
        reach[:, at] = far
        local_grad[:, at] = grad
        ends[0:1, at] = decay[0:1, :] * far[0:1, :]
        ends[1:2, at] = decay[0:1, :] * grad[0:1, :]

    each_head(heads, block, backwards)
    own = links.keep(ends, table.at[place.row])
    own.wait()
    heads_here[0:1, :] = carry_over(links, place, ends, table, True)
    between()

    def one_head(h, at):
        def vector(i):
            return vectors[i : i + 1, at]

        grad_state = local_grad[:, at] + reach[:, at] * heads_here[0:1, at]
        padded[8:, :] = state_in[:, at]
        padded[7:8, :] = entering[0:1, at]
        grad_decay = grad_state * padded[7 : 7 + tokens, :]
        input_gate, decay_gate, conv = in_gate[:, at], dec_gate[:, at], conv_in[:, at]
        rate = vector(taps + 5)
        log_decay = rate * decay_gate
        decay = jnp.exp(log_decay)
        multiplier = jnp.where(starting, 1.0, jnp.sqrt(minus_expm1(2.0 * log_decay)))
        grad_gated = grad_state * conv
        grad_log = jnp.where(
            starting, 0.0, decay * (grad_decay - grad_gated * input_gate * (decay / multiplier))
        )
        grad_in = grad_gated * multiplier * (input_gate * (1.0 - input_gate))
        grad_gate = grad_log * decay_gate
        grad_dec = grad_gate * rate * (1.0 - decay_gate)
        low = conv.astype(LOW)
        low_in, low_dec = grad_in.astype(LOW), grad_dec.astype(LOW)
        across = (((1,), (1,)), ((), ()))
        along = (((0,), (0,)), ((), ()))
        grad_conv = (
            grad_state * multiplier * input_gate
            + lax.dot_general(low_in, blocks[h], across, preferred_element_type=WIDE)
            + lax.dot_general(low_dec, blocks[heads + h], across, preferred_element_type=WIDE)
        )
        blocks_out[h] = lax.dot_general(low, low_in, along, preferred_element_type=WIDE)
        blocks_out[heads + h] = lax.dot_general(low, low_dec, along, preferred_element_type=WIDE)
        spread[0:8, :] = jnp.zeros((8, block), WIDE)
        spread[8:, :] = vector(0) * grad_conv
        shift = vector(taps + 1)

        def total(values):
            return jnp.sum(values, axis=0, keepdims=True)

        sums_out[0:1, at] = total(grad_conv * (proj[8:, at] + shift))
        for k in range(1, taps):
            kept = jnp.where(spot >= k, grad_conv, 0.0)
            sums_out[k : k + 1, at] = total(kept * (proj[8 - k : 8 - k + tokens, at] + shift))
            spread[8 - k : 8 - k + tokens, :] += vector(k) * kept
        branch[:, at] = spread[8:, :]
        heads_in[0, :, at] = spread[0:8, :]
        sums_out[taps : taps + 1, at] = total(grad_conv)
        sums_out[taps + 1 : taps + 2, at] = total(spread[...])
        sums_out[taps + 2 : taps + 3, at] = total(grad_in)
        sums_out[taps + 3 : taps + 4, at] = total(grad_dec)
        sums_out[taps + 4 : taps + 5, at] = total(grad_gate)
        sums_out[taps + 5 :, at] = jnp.zeros((sums_out.shape[0] - taps - 5, block), WIDE)

    each_head(heads, block, one_head)
    row = place.row
    before = lax.rem(row + 3, 4)
    owed = links.copy(heads_in.at[0], heads_in.at[1], row=before)
    owed.start()
    owed.wait_recv()
    owed.wait_send()
    between()

    def finish(h, at):
        last = jnp.where(row < 3, heads_in[1, :, at], 0.0)
        branch[tokens - 8 :, at] += last
        branch_out[:, at] = branch[:, at].astype(LOW)

    each_head(heads, block, finish)


def recurrence_back_inside(
    count, taps, proj, side, gelu_in, spots, vectors, blocks, conv_in, in_gate, dec_gate, state_in,
    entering, grad_mixed, output_partial, up_own, sums_out, blocks_out, all_out, output_out, up_out, branch_low, gelu_low, stage, reach, local_grad, branch, ends, table, heads_in,
    heads_here, padded, spread, ups, downs, staging, own, up_here, send, recv, local,
):
    place = Place(count)
    links = Links(send, recv, local)
    greet(place, rows=True, line=True)
    row, z = place.row, place.dp
    part = stage.shape[2] // 2
    kept = Relay(links, up_own.at[z], up_here, up_out.at[z])
    load = links.keep(output_partial, own)

    output_half = ups.shape[2]

    def output_rows(i, rows):
        return pl.ds(pl.multiple_of(rows.start + i * output_half, 16), rows.size)

    def keep_output(i, rows, value):
        output_out[output_rows(i, rows)] = value

    output_sum = scatter_line_in_parts(
        links,
        place,
        lambda s: None,
        lambda b, i, rows: own[b, output_rows(i, rows)].astype(WIDE),
        ups,
        downs,
        staging,
        keep_output,
    )
    up_line = exchange_line(links, place, lambda b: up_own.at[b], lambda b: up_out.at[b])
    load.wait()
    advance(output_sum, up_line)
    kept.pass_on()

    def gelu_back(h, at):
        grad = grad_mixed[:, at] * state_in[:, at] * gelu_slope(gelu_in[:, at])
        gelu_low[:, at] = grad.astype(LOW)
        spread[0:1, :] = jnp.sum(grad, axis=0, keepdims=True)
        sums_out[taps + 5 : taps + 6, at] = spread[0:1, :]

    recurrence_backward(
        count, taps, proj, side, spots, vectors, blocks, conv_in, in_gate, dec_gate, state_in, entering,
        grad_mixed, branch_low, sums_out, blocks_out, reach, local_grad, branch, ends, table, heads_in,
        heads_here, padded, spread, None, None, None, links, lambda: advance(output_sum),
    )
    each_head(blocks.shape[0] // 2, blocks.shape[1], gelu_back)
    for q in range(4):
        at = slice(q * part, (q + 1) * part)
        stage[q, :, :part] = branch_low[:, at]
        stage[q, :, part:] = gelu_low[:, at]
    mine = links.keep(stage.at[row], all_out.at[row])
    spread_out = exchange_rows(links, place, lambda q: stage.at[q], lambda q: all_out.at[q])
    run([spread_out, output_sum, up_line])
    mine.wait()
    kept.wait()


def norm_rule(rows, grad, value, gain, sums, at):
    full = value.shape[1]
    inverse = lax.rsqrt(jnp.sum(value * value, axis=1, keepdims=True) / full + epsilon)
    scaled = grad * (1.0 + gain)
    inner = jnp.sum(scaled * value, axis=1, keepdims=True)
    sums[at : at + 1, :] += jnp.sum(grad * value * inverse, axis=0, keepdims=True)
    return inverse * scaled - value * (inverse * inverse * inverse) * (inner / full)


def second_norm_back_inside(
    count, grad_gate, grad_up, gate_all, up_all, normed, hidden, down_all, cot_all, middle, vectors,
    grad_middle, grad_all, sums, gate_out, forward_out, ours, theirs, ups, downs, staging, cot, low, buffers,
    gate_v, up_v, gate_w, up_w, tile, partial, gate_partial, hidden_v, down_tile, forward_tile, send, recv,
    local,
):
    place = Place(count)
    links = Links(send, recv, local)
    greet(place, rows=True, line=True, cores=True)
    loads = [links.keep(grad_gate, gate_v), links.keep(grad_up, up_v)]
    pieces = [
        (links.keep(gate_all.at[q], gate_w.at[q]), links.keep(up_all.at[q], up_w.at[q]))
        for q in range(4)
    ]
    quarter, full = middle.shape
    narrow, units = full // 4, gate_v.shape[1]
    for load in loads:
        load.wait()
    first = [True]

    def tokens(block):
        rows = strip(block, 2 * quarter)

        def lap(q, carry):
            total = sum(
                times_flipped(values[rows, :], weight[q].astype(LOW).reshape(narrow, units))
                for values, weight in ((gate_v, gate_w), (up_v, up_w))
            ).astype(LOW)
            for core in range(2):
                partial[block, core, :, lanes(q, narrow)] = total[
                    core * quarter : (core + 1) * quarter
                ]
            return carry

        if first:
            first.clear()
            for q in range(4):
                for load in pieces[q]:
                    load.wait()
                lap(q, 0)
        else:
            lax.fori_loop(0, 4, lap, 0)

    k, links.kept = links.kept, links.kept + 1

    def gate(q):
        load = pltpu.make_async_copy(normed.at[:, lanes(q, narrow)], tile, links.local.at[k])
        load.start()
        load.wait()
        gate_partial[strip(q, narrow)] = left_product(tile[...], gate_v[...]).astype(LOW)

    k_down, links.kept = links.kept, links.kept + 1
    load_hidden = links.keep(hidden, hidden_v)

    def forward_sum():
        load_hidden.wait()
        store = None
        for q in range(4):
            load = pltpu.make_async_copy(
                down_all.at[:, lanes(q, narrow)], down_tile, links.local.at[k_down]
            )
            load.start()
            load.wait()
            if store is not None:
                store.wait()
            forward_tile[...] = times(hidden_v[...], down_tile[...]).astype(LOW)
            store = links.keep(forward_tile, forward_out.at[:, lanes(q, narrow)])
            yield 1
        store.wait()

    second_norm_back(
        count, partial, cot_all, middle, vectors, gate_partial, grad_middle, grad_all, sums, gate_out,
        ours, theirs, ups, downs, staging, cot, low, buffers, None, None, None, links, tokens, gate,
        [forward_sum()],
    )


def second_norm_back(
    count, grad_partial, cot_all, middle, vectors, gate_partial, grad_middle, grad_all, sums, gate_out,
    ours, theirs, ups, downs, staging, cot, low, buffers, send, recv, local, links=None,
    prepare_tokens=None, prepare_gate=None, others=(),
):
    place = Place(count)
    if links is None:
        links = Links(send, recv, local)
        greet(place, rows=True, line=True, cores=True)
    row, z, col = place.row, place.dp, place.col
    quarter, full = middle.shape
    narrow = full // 4
    tall = 4 * quarter
    half = gate_partial.shape[0] // 8
    sums[...] = jnp.zeros(sums.shape, WIDE)
    gain = vectors[3:4, :]
    load = links.keep(cot_all.at[strip(2 * z + col, quarter)], cot)

    def back(rows, grad):
        own = cot[rows].astype(WIDE)
        total = own + norm_rule(rows, grad, middle[rows], gain, sums, 0)
        sums[1:2, :] += jnp.sum(total, axis=0, keepdims=True)
        sums[2:3, :] += jnp.sum(own, axis=0, keepdims=True)
        grad_middle[rows] = total
        low[rows] = total.astype(LOW)

    def tokens():
        load.wait()
        yield from token_scatter(
            links, place, grad_partial, ours, theirs, (ups, downs, staging), back, prepare_tokens
        )

        def block(q):
            return grad_all.at[strip(4 * col + q, quarter)]

        mine = links.keep(low.at[:, lanes(row, narrow)], block(row))
        yield from exchange_rows(
            links, place, lambda q: low.at[:, lanes(q, narrow)], block
        )
        mine.wait()
        both = grad_all.at[strip(col, tall)]
        share = links.copy(both, both, col=place.other)
        share.start()
        yield 1
        share.wait_recv()
        share.wait_send()

    def keep_gate(h, rows, value):
        gate_out[h, rows] = value.astype(LOW)

    tokens_back = tokens()
    gate_back = scatter_rows(
        links,
        place,
        lambda q, h: gate_partial.at[strip(2 * q + h, half)],
        buffers,
        keep_gate,
        prepare_gate,
    )
    advance(tokens_back)
    advance(tokens_back)
    run([gate_back, tokens_back, *others])


def mixed_and_output_inside(
    count, grad_all, wout, mixed_all, normed, cot_all, grad_up, hidden, out_partial, middle, vectors, gate_own,
    mixed_out, layer_out, up_out, gate_out, output_out, down_out, mixed_buffers, ours, theirs, ups, downs,
    staging, low, up_buffers, gate_here, grad_v, wout_v, mixed_v, tile, up_v, hidden_v, mixed_partial,
    up_partial, output_v, down_v, send, recv, local,
):
    place = Place(count)
    links = Links(send, recv, local)
    greet(place, rows=True, line=True, cores=True)
    loads = [
        links.keep(source, target)
        for source, target in (
            (grad_all, grad_v), (wout, wout_v), (grad_up, up_v), (mixed_all, mixed_v),
            (hidden, hidden_v),
        )
    ]
    steps = mixed_partial.shape[0] // 4
    narrow = grad_v.shape[1]
    for load in loads[:2]:
        load.wait()

    def mixed(q):
        rows = strip(q, steps)
        mixed_partial[rows] = times_flipped(grad_v[rows, :], wout_v[...]).astype(LOW)

    k, links.kept = links.kept, links.kept + 1

    def fetch(source, q):
        load = pltpu.make_async_copy(source.at[:, lanes(q, narrow)], tile, links.local.at[k])
        load.start()
        load.wait()

    def up(q):
        fetch(normed, q)
        up_partial[strip(q, narrow)] = left_product(tile[...], up_v[...]).astype(LOW)

    def ready():
        for load in loads[2:]:
            load.wait()

    def others():
        output_v[...] = left_product(mixed_v[...], grad_v[...]).astype(LOW)
        stores = [links.keep(output_v, output_out)]

        def lap(q, carry):
            fetch(cot_all, q)
            down_v[:, lanes(q, narrow)] = left_product(hidden_v[...], tile[...]).astype(LOW)
            return carry

        lax.fori_loop(0, 4, lap, 0)
        stores.append(links.keep(down_v, down_out))
        yield 1
        for store in stores:
            store.wait()

    mixed_and_output(
        count, mixed_partial, out_partial, middle, vectors, up_partial, gate_own, mixed_out, layer_out,
        up_out, gate_out, mixed_buffers, ours, theirs, ups, downs, staging, low, up_buffers, gate_here, None,
        None, None, links, ready, mixed, up, others(),
    )


def mixed_and_output(
    count, mixed_partial, out_partial, middle, vectors, up_partial, gate_own, mixed_out, layer_out, up_out,
    gate_out, mixed_buffers, ours, theirs, ups, downs, staging, low, up_buffers, gate_here, send, recv,
    local, links=None, ready=None, prepare_mixed=None, prepare_up=None, others=None,
):
    place = Place(count)
    if links is None:
        links = Links(send, recv, local)
        greet(place, rows=True, line=True, cores=True)
    row = place.row
    quarter, full = middle.shape
    narrow = full // 4
    shift = vectors[2:3, :]
    half = mixed_partial.shape[0] // 8
    up_half = up_partial.shape[0] // 8
    kept = Relay(links, gate_own.at[place.dp], gate_here, gate_out.at[place.dp])

    def keep_mixed(h, rows, value):
        mixed_out[h, rows] = value

    def keep_up(h, rows, value):
        up_out[h, rows] = value.astype(LOW)

    def finish(rows, value):
        low[rows] = (middle[rows] + value + shift).astype(LOW)

    def tokens():
        yield from token_scatter(
            links, place, out_partial, ours, theirs, (ups, downs, staging), finish
        )
        mine = links.keep(low.at[:, lanes(row, narrow)], layer_out.at[row])
        yield from exchange_rows(
            links, place, lambda q: low.at[:, lanes(q, narrow)], lambda q: layer_out.at[q]
        )
        mine.wait()

    outs = tokens()
    mixes = scatter_rows(
        links,
        place,
        lambda q, h: mixed_partial.at[strip(2 * q + h, half)],
        mixed_buffers,
        keep_mixed,
        prepare_mixed,
    )
    sums_up = scatter_rows(
        links,
        place,
        lambda q, h: up_partial.at[strip(2 * q + h, up_half)],
        up_buffers,
        keep_up,
        prepare_up,
    )
    gates = exchange_line(links, place, lambda b: gate_own.at[b], lambda b: gate_out.at[b])
    advance(gates, outs, mixes, outs)
    kept.pass_on()
    if ready is not None:
        ready()
    advance(sums_up, mixes, outs)
    if others is not None:
        advance(others)
    advance(mixes)
    run([outs, sums_up, mixes, gates] + ([others] if others is not None else []))
    kept.wait()


def spread_gradients(
    count, blocks, output_partial, up_own, all_out, output_out, up_out, ups, downs, staging, own, send, recv, local,
):
    place = Place(count)
    links = Links(send, recv, local)
    greet(place, rows=True, line=True)
    row, z = place.row, place.dp
    mine = links.keep(blocks.at[row], all_out.at[row])
    kept = links.keep(up_own.at[z], up_out.at[z])
    load = links.keep(output_partial, own)

    output_half = ups.shape[2]

    def output_rows(i, rows):
        return pl.ds(pl.multiple_of(rows.start + i * output_half, 16), rows.size)

    def keep_output(i, rows, value):
        output_out[output_rows(i, rows)] = value

    def outputs():
        load.wait()
        yield from scatter_line_in_parts(
            links,
            place,
            lambda s: None,
            lambda b, i, rows: own[b, output_rows(i, rows)].astype(WIDE),
            ups,
            downs,
            staging,
            keep_output,
        )

    run(
        [
            exchange_rows(links, place, lambda q: blocks.at[q], lambda q: all_out.at[q]),
            outputs(),
            exchange_line(links, place, lambda b: up_own.at[b], lambda b: up_out.at[b]),
        ]
    )
    mine.wait()
    kept.wait()


def first_norm_back(
    count, grad_partial, x_own, grad_middle, vectors, proj_partial, down_partial, sums_in,
    channel_in, hidden_in, block_in, grad_out, proj_out, down_out, width_sums, channel_sums, block_out, hidden_sums,
    theirs, ours, added,
    row_buffer, x, result, sums, proj_own, proj_ups, proj_downs, proj_staging, proj_low, width_table,
    width_line, width_part, channel_table, channel_line, hidden_table, block_table, block_part, block_line, block_low,
    down_buffers, send, recv, local, links=None, prepare_tokens=None, prepare_proj=None,
):
    place = Place(count)
    if links is None:
        links = Links(send, recv, local)
        greet(place, rows=True, line=True, cores=True)
    row, z, col = place.row, place.dp, place.col
    quarter, full = grad_middle.shape
    narrow = full // 4
    gain = vectors[0:1, :]
    load_x = links.keep(x_own, x)
    if prepare_proj is None:
        load_proj = [links.keep(proj_partial.at[:, b], proj_own.at[b]) for b in range(count)]

    parts = halves(down_partial.shape[0])

    def keep_down(h, rows, value):
        down_out[pl.ds(pl.multiple_of(parts[h].start + rows.start, 16), rows.size)] = value

    down_sum = scatter_rows(
        links,
        place,
        lambda q, h: down_partial.at[parts[h], lanes(q, narrow)],
        down_buffers,
        keep_down,
    )

    def tokens():
        if prepare_tokens is not None:
            prepare_tokens(place.other)
        share = links.copy(grad_partial.at[place.other], theirs, col=place.other)
        share.start()
        if prepare_tokens is not None:
            prepare_tokens(col)
        load = links.keep(grad_partial.at[col], ours)
        yield 1
        share.wait_recv()
        load.wait()

        def add(rows):
            for q in range(4):
                total = ours[q, rows].astype(WIDE) + theirs[q, rows].astype(WIDE)
                added[q, rows] = total.astype(LOW)

        by_rows(quarter, add)
        load_x.wait()
        sums[0:3, :] = sums_in[0:3, :]
        sums[3:, :] = jnp.zeros((sums.shape[0] - 3, full), WIDE)
        half = quarter // 2

        def back(h, rows, grad):
            here = pl.ds(pl.multiple_of(rows.start + half * h, 16), rows.size)
            value = x[here].astype(WIDE)
            total = grad_middle[here] + norm_rule(rows, grad, value, gain, sums, 3)
            for q in range(4):
                result[q, here] = total[:, q * narrow : (q + 1) * narrow].astype(LOW)

        yield from scatter_rows(
            links,
            place,
            lambda q, h: added.at[q, pl.ds(half * h, half)],
            row_buffer,
            back,
        )
        share.wait_send()
        mine = links.keep(result.at[row], grad_out.at[row])
        for q in range(4):
            width_part[q] = sums[:, q * narrow : (q + 1) * narrow]
        own = links.keep(width_part.at[row], width_table.at[row])
        vectors_out = exchange_rows(
            links, place, lambda q: width_part.at[q], lambda q: width_table.at[q]
        )
        results_out = exchange_rows(
            links, place, lambda q: result.at[q], lambda q: grad_out.at[q]
        )
        advance(vectors_out, results_out)
        yield 1
        finish(vectors_out)
        own.wait()
        width_line[z] = width_table[0] + width_table[1] + width_table[2] + width_table[3]
        yield from exchange_line(
            links, place, lambda b: width_line.at[z], lambda b: width_line.at[b]
        )
        total = width_line[0]
        for b in range(1, count):
            total = total + width_line[b]
        width_sums[0] = total
        yield 1
        last = links.copy(width_sums.at[0], width_sums.at[1], col=place.other)
        last.start()
        yield 1
        last.wait_recv()
        last.wait_send()
        finish(results_out)
        mine.wait()

    def projections():
        if prepare_proj is None:
            for load in load_proj:
                load.wait()
        else:
            prepare_proj()

        def keep_proj(i, rows, value):
            proj_low[i, rows] = value.astype(LOW)

        yield from scatter_line_in_parts(
            links,
            place,
            lambda s: None,
            lambda b, i, rows: proj_own[b, i, rows].astype(WIDE),
            proj_ups,
            proj_downs,
            proj_staging,
            keep_proj,
        )
        mine = links.keep(proj_low.at[row], proj_out.at[row])
        yield from exchange_rows(
            links, place, lambda q: proj_low.at[q], lambda q: proj_out.at[q]
        )
        mine.wait()

    def hidden():
        own = links.keep(hidden_in, hidden_table.at[row])
        yield from exchange_rows(
            links, place, lambda q: hidden_in, lambda q: hidden_table.at[q]
        )
        own.wait()
        hidden_sums[...] = hidden_table[0] + hidden_table[1] + hidden_table[2] + hidden_table[3]

    def channels():
        own = links.keep(channel_in, channel_table.at[row])
        yield from exchange_rows(
            links, place, lambda q: channel_in, lambda q: channel_table.at[q]
        )
        own.wait()
        channel_line[z] = (
            channel_table[0] + channel_table[1] + channel_table[2] + channel_table[3]
        )
        yield from exchange_line(
            links, place, lambda b: channel_line.at[z], lambda b: channel_line.at[b]
        )
        total = channel_line[0]
        for b in range(1, count):
            total = total + channel_line[b]
        channel_sums[...] = total

    def blocks():
        own = links.keep(block_in.at[row], block_table.at[row])
        yield from exchange_rows(
            links, place, lambda q: block_in.at[q], lambda q: block_table.at[q]
        )
        own.wait()

        for b in range(count):
            block_part[b] = sum(block_table[q, b].astype(WIDE) for q in range(4)).astype(LOW)
        own = links.keep(block_part.at[z], block_line.at[z])
        yield from exchange_line(
            links, place, lambda b: block_part.at[b], lambda b: block_line.at[b]
        )
        own.wait()
        block_low[...] = sum(block_line[b].astype(WIDE) for b in range(count)).astype(LOW)
        own = links.keep(block_low, block_out.at[row])
        yield from exchange_rows(links, place, lambda q: block_low, lambda q: block_out.at[q])
        own.wait()

    proj_sum, token_sum = projections(), tokens()
    small = [channels(), hidden(), blocks()]
    advance(down_sum, proj_sum, token_sum, *small)
    advance(token_sum)
    run([proj_sum, token_sum, down_sum] + small)


def first_norm_back_inside(
    count, grad_proj, wxy, nf, x_own, grad_middle, vectors, down_partial, *refs
):
    rest, (grad_v, wxy_v, nf_v, partial, send, recv, local) = refs[:-7], refs[-7:]
    proj_own = rest[18]
    place = Place(count)
    links = Links(send, recv, local)
    greet(place, rows=True, line=True, cores=True)
    loads = [
        links.keep(source, target)
        for source, target in ((grad_proj, grad_v), (nf, nf_v), (wxy, wxy_v))
    ]
    quarter, full = grad_middle.shape
    narrow, tall = full // 4, 4 * quarter
    depth = proj_own.shape[2]

    def tokens(core):
        def lap(q, carry):
            total = times_flipped(
                grad_v[strip(core, tall), :], wxy_v[strip(q, narrow), :]
            ).astype(LOW)
            for r in range(4):
                partial[core, r, :, lanes(q, narrow)] = total[r * quarter : (r + 1) * quarter]
            return carry

        lax.fori_loop(0, 4, lap, 0)

    def proj():
        for load in loads:
            load.wait()

        def lap(q, carry):
            total = left_product(nf_v[:, lanes(q, narrow)], grad_v[...]).astype(LOW)
            for b in range(count):
                proj_own[b, q] = total[b * depth : (b + 1) * depth]
            return carry

        lax.fori_loop(0, 4, lap, 0)

    first_norm_back(
        count, partial, x_own, grad_middle, vectors, None, down_partial, *rest, None, None, None, links,
        tokens, proj,
    )


def gelu(v):
    return 0.5 * v * (1.0 + jnp.tanh(ROOT * (v + CUBE * (v * v * v))))


def gelu_slope(v):
    t = jnp.tanh(ROOT * (v + CUBE * (v * v * v)))
    return 0.5 * (1.0 + t) + 0.5 * v * (1.0 - t * t) * (ROOT * (1.0 + 3.0 * CUBE * (v * v)))


def block_of(blocks, h):
    width = blocks.shape[-1]
    return blocks[h].reshape(width, width)


def forward(
    count, taps, x, cot, wxy, wout, wgate, wup, wdown, blk, cvec, wvec, spots,
    nf_out, x_out, cot_all, wxy_out, wout_out, gate_all, up_own, down_all, blocks_out, vectors_out,
    width_out, branch_out, gelu_out, side_out, conv_out, in_out, dec_out, state_out, entering_out,
    mixed_out, middle_out, normed_out,
    x_all, nf, wxy_all, wout_all, blocks, cvec_all, wvec_all, vectors, width, stage, arrived, branch,
    gelu_in, side, conv, in_gate, dec_gate, state, running, local_state, ends, table, entering, mixed,
    mixed_all, partial, theirs, here, wide, middle, normed, gate_here, up_here, down_here, cot_here,
    send, recv, local,
):
    place = Place(count)
    links = Links(send, recv, local)
    row, z, col = place.row, place.dp, place.col
    greet(place, rows=True, line=True, cores=True)
    tall, narrow = x.shape
    full = 4 * narrow
    half, quarter = tall // 2, tall // 4
    depth, part = wxy.shape[1], wxy.shape[2] // 2
    tokens, steps = 2 * tall, tall // 2
    heads, block = blocks.shape[0] // 2, blocks.shape[-1]
    share = blocks.shape[3]
    kept = []

    def keep(src, dst):
        kept.append(links.keep(src, dst))
        return kept[-1]

    def projections():
        def at(q, b):
            return wxy_all.at[q, strip(b, depth, 8)]

        mine = links.keep(wxy.at[row], at(row, z))
        yield from exchange_rows(links, place, lambda q: wxy.at[q], lambda q: at(q, z))
        mine.wait()

        def piece(b):
            return wxy_all.at[:, strip(b, depth, 8)]

        yield from gather_line(links, place, piece(z), piece)

    def inputs():
        def at(q, core):
            return x_all.at[strip(core, tall), lanes(q, narrow)]

        mine = links.keep(x, at(row, col))
        shared = [links.copy(x, at(row, col), col=place.other)]
        shared[0].start()
        yield from gather_rows(
            links,
            place,
            lambda h: x.at[pl.ds(half * h, half)],
            lambda q, h: x_all.at[strip(2 * col + h, half), lanes(q, narrow)],
        )
        for k in range(1, 4):
            q = place.near[k]
            shared.append(links.copy(at(q, col), at(q, col), col=place.other))
            shared[-1].start()
        yield 1
        mine.wait()
        for copy in shared:
            copy.wait_recv()
        for copy in shared:
            copy.wait_send()

    def channel_vectors():
        keep(cvec, cvec_all.at[z])
        yield from exchange_line(links, place, lambda b: cvec, lambda b: cvec_all.at[b])

    def width_vectors():
        mine = links.keep(wvec, wvec_all.at[row, z])
        yield from exchange_line(links, place, lambda b: wvec, lambda b: wvec_all.at[row, b])
        mine.wait()
        yield from exchange_rows(
            links, place, lambda q: wvec_all.at[row], lambda q: wvec_all.at[q]
        )

    def gate_blocks():
        split = blocks.shape[2] > 1
        own = row if split else 0
        mine = links.keep(blk, blocks.at[:, z, own])
        yield from exchange_line(links, place, lambda b: blk, lambda b: blocks.at[:, b, own])
        mine.wait()
        middle = count // 2
        if split:

            def at(q, h):
                return blocks.at[:, pl.ds(middle * h, middle), q]

            yield from gather_rows(links, place, lambda h: at(row, h), at)

    def hidden_rows():
        parts = halves(wdown.shape[0])
        mine = Relay(links, wdown, down_here, down_all.at[:, lanes(row, narrow)])
        kept.append(mine)
        yield from gather_rows(
            links,
            place,
            lambda h: wdown.at[parts[h]],
            lambda q, h: down_all.at[parts[h], lanes(q, narrow)],
        )

    def cotangent_rows():
        def spot(q):
            return cot_all.at[strip(2 * z + col, quarter), lanes(q, narrow)]

        mine = Relay(links, cot.at[strip(row, quarter)], cot_here, spot(row))
        yield from exchange_rows(links, place, lambda q: cot.at[strip(q, quarter)], spot)
        mine.wait()

    def hidden_columns(matrix, buffer, own):
        mine = Relay(links, matrix.at[z], buffer, own.at[z])
        yield from exchange_line(links, place, lambda b: matrix.at[b], lambda b: own.at[b])
        mine.wait()

    def all_hidden_columns(matrix, buffer, whole):
        yield from hidden_columns(matrix, buffer, whole.at[row])
        middle = count // 2

        def at(q, h):
            return whole.at[q, pl.ds(middle * h, middle)]

        yield from gather_rows(links, place, lambda h: at(row, h), at)

    def cot_block(b):
        return cot_all.at[strip(2 * b + col, quarter)]

    def output_rows():
        at = wout.shape[0]
        mine = links.keep(wout, wout_all.at[strip(z, at)])
        yield from gather_line(links, place, wout, lambda b: wout_all.at[strip(b, at)])
        mine.wait()

    weights, rows_in = projections(), inputs()
    vectors_in, widths_in, blocks_in = channel_vectors(), width_vectors(), gate_blocks()
    cot_in, output_in, down_in = cotangent_rows(), output_rows(), hidden_rows()
    gate_in = all_hidden_columns(wgate, gate_here, gate_all)
    cots = LineGather(links, place, cot_block(z), cot_block)
    up_in = hidden_columns(wup, up_here, up_own)
    advance(weights, rows_in, widths_in, vectors_in, blocks_in, cot_in)
    advance(weights, widths_in, vectors_in, blocks_in)
    finish(widths_in, vectors_in)
    for copy in kept:
        copy.wait()
    kept.clear()

    for b in range(count):
        size = vectors.shape[1] // count
        vectors[:, b * size : (b + 1) * size] = cvec_all[b, :, :size]
        for q in range(4):
            at = q * narrow + b * depth
            width[:, at : at + depth] = wvec_all[q, b, :, :depth]
    keep(vectors, vectors_out)
    keep(width, width_out)
    advance(rows_in)
    advance(weights)
    finish(rows_in)
    advance(down_in)
    keep(x_all.at[strip(4 * col + row, quarter)], x_out)

    nf[0:16, :] = jnp.zeros((16, full), LOW)

    def first_norm(rows):
        value = x_all[rows].astype(WIDE)
        mean = jnp.sum(value * value, axis=1, keepdims=True) / full
        value = value * lax.rsqrt(mean + epsilon) * (1.0 + width[0:1, :])
        nf[pl.ds(pl.multiple_of(rows.start + 16, 16), rows.size)] = value.astype(LOW)

    by_rows(tokens, first_norm)
    keep(nf.at[pl.ds(16, tokens)], nf_out)
    advance(weights, blocks_in, cot_in)
    finish(blocks_in)
    keep(blocks, blocks_out)
    finish(weights, cot_in)
    keep(wxy_all, wxy_out)

    advance(output_in)
    advance(down_in)
    out = []
    for k in (3, 2, 1, 0):
        q = place.near[k]

        def product(k=k, q=q):
            stage[k] = jnp.dot(
                nf[pl.ds(pl.multiple_of(q * steps, 16), steps + 16), :],
                wxy_all[...].astype(LOW).reshape(full, 2 * part),
                preferred_element_type=WIDE,
            )

        product()
        source = stage.at[k, pl.ds(8, steps + 8)]
        if k:
            out.append(links.copy(source, arrived.at[row], row=q))
            out[-1].start()
        else:
            mine = links.keep(source, arrived.at[row])
    advance(output_in, gate_in)
    mine.wait()
    for copy in out:
        copy.wait_recv()
    finish(down_in)
    for copy in out:
        copy.wait_send()
    cots.start()

    spot = spots[...]
    starting = spot == 0
    for q in range(4):
        at = slice(q * part, (q + 1) * part)
        branch[:, at] = arrived[q, :, :part]
        gelu_in[:, at] = arrived[q, 8:, part:] + vectors[taps + 2 : taps + 3, at]
    keep(branch, branch_out)
    keep(gelu_in, gelu_out)
    ends[...] = jnp.zeros(ends.shape, WIDE)
    entering[...] = jnp.zeros(ends.shape, WIDE)

    def one_head(h, at):
        def vector(i):
            return vectors[i : i + 1, at]

        conv_here = vector(taps) + vector(0) * (branch[8:, at] + vector(taps + 1))
        for k in range(1, taps):
            earlier = branch[8 - k : 8 - k + steps, at] + vector(taps + 1)
            conv_here = conv_here + vector(k) * jnp.where(spot >= k, earlier, 0.0)
        conv[:, at] = conv_here
        low = conv_here.astype(LOW)
        input_gate = jax.nn.sigmoid(
            jnp.dot(low, block_of(blocks, h), preferred_element_type=WIDE) + vector(taps + 3)
        )
        decay_gate = jax.nn.sigmoid(
            jnp.dot(low, block_of(blocks, heads + h), preferred_element_type=WIDE)
            + vector(taps + 4)
        )
        in_gate[:, at] = input_gate
        dec_gate[:, at] = decay_gate
        log_decay = vector(taps + 5) * decay_gate
        decay = jnp.where(starting, 0.0, jnp.exp(log_decay))
        multiplier = jnp.where(starting, 1.0, jnp.sqrt(minus_expm1(2.0 * log_decay)))
        reach, value = scan_rows(decay, multiplier * input_gate * conv_here, False)
        running[:, at] = reach
        local_state[:, at] = value
        ends[0:1, at] = reach[steps - 1 :, :]
        ends[1:2, at] = value[steps - 1 :, :]
        side[:, at] = gelu(gelu_in[:, at])

    each_head(heads, block, one_head)
    for scratch, output in (
        (conv, conv_out), (in_gate, in_out), (dec_gate, dec_out), (side, side_out),
    ):
        keep(scratch, output)
    own = links.keep(ends, table.at[row])
    advance(output_in)
    own.wait()
    entering[0:1, :] = carry_over(links, place, ends, table, False)

    def mix(h, at):
        value = local_state[:, at] + running[:, at] * entering[0:1, at]
        state[:, at] = value
        mixed[:, at] = (value * side[:, at]).astype(LOW)

    each_head(heads, block, mix)
    mine = links.keep(mixed, mixed_all.at[strip(row, steps)])
    mixes = gather_rows(
        links,
        place,
        lambda h: mixed.at[pl.ds(steps // 2 * h, steps // 2)],
        lambda q, h: mixed_all.at[strip(2 * q + h, steps // 2)],
    )
    advance(mixes)
    keep(state, state_out)
    keep(entering, entering_out)
    finish(output_in)
    keep(wout_all, wout_out)
    advance(mixes, up_in)
    finish(mixes)
    mine.wait()
    cots.step(1)
    advance(gate_in)
    keep(mixed_all, mixed_out)

    def product_rows(first):
        def body(i, carry):
            rows = pl.ds(pl.multiple_of(first * tall + i * steps, 16), steps)
            partial[rows] = jnp.dot(mixed_all[rows], wout_all[...], preferred_element_type=WIDE)
            return carry

        lax.fori_loop(0, tall // steps, body, 0)

    product_rows(place.other)
    swap = links.copy(partial.at[strip(place.other, tall)], theirs, col=place.other)
    swap.start()
    product_rows(col)
    swap.wait_recv()

    def add(rows):
        at = pl.ds(pl.multiple_of(col * tall + rows.start, 16), rows.size)
        here[rows] = partial[at] + theirs[rows] + x_all[at, lanes(row, narrow)].astype(WIDE)

    by_rows(tall, add)

    def quarter_of(q):
        return here.at[strip(q, quarter)]

    mine = links.keep(quarter_of(row), wide.at[:, lanes(row, narrow)])
    middles = exchange_rows(links, place, quarter_of, lambda q: wide.at[:, lanes(q, narrow)])
    advance(middles)
    mine.wait()
    finish(middles)
    swap.wait_send()

    def second_norm(rows):
        value = wide[rows] + width[1:2, :]
        middle[rows] = value
        mean = jnp.sum(value * value, axis=1, keepdims=True) / full
        normed[rows] = (value * lax.rsqrt(mean + epsilon) * (1.0 + width[3:4, :])).astype(LOW)

    by_rows(quarter, second_norm)
    keep(middle, middle_out)
    keep(normed, normed_out)
    advance(gate_in)
    for step in range(2, count):
        cots.step(step)
    finish(gate_in, up_in)
    for step in range(count):
        cots.ready(step)
    cots.close()
    for copy in kept:
        copy.wait()


def feed_forward(
    count, normed, cot_all, gate_all, up_own, wdown, biases, normed_all, up_all, hidden_out, gate_out,
    up_out, sums, gate_w, up_w, down_w, piece, gate_v, up_v, grad_v, hidden, grad_gate, grad_up, normed_here,
    send, recv, local,
):
    place = Place(count)
    links = Links(send, recv, local)
    row, z, col = place.row, place.dp, place.col
    greet(place, rows=True, line=True, cores=True)
    quarter, full = normed.shape
    narrow, pair = full // 4, 2 * quarter
    units = wdown.shape[0]
    middle = count // 2
    load = links.keep(wdown, down_w)
    kept = [links.keep(gate_all, gate_w), links.keep(up_own, up_w.at[row])]

    def tokens(own, buffer, whole):
        def at(b):
            return whole.at[strip(2 * b + col, quarter)]

        relay = Relay(links, own, buffer, at(z))
        return LineGather(links, place, own, at), relay

    def columns_of(own, whole):
        yield from gather_rows(
            links,
            place,
            lambda h: own.at[pl.ds(middle * h, middle)],
            lambda q, h: whole.at[q, pl.ds(middle * h, middle)],
        )

    def neighbours(step, body):
        if step == 0:
            body(z)
            return

        def lap(i, carry):
            b = z - step + 2 * step * i
            pl.when((b >= 0) & (b < count))(lambda: body(place.turn(b)))
            return carry

        lax.fori_loop(0, 2, lap, 0)

    def with_piece(source, body):
        k, links.kept = links.kept, links.kept + 1

        def inner(b):
            load = pltpu.make_async_copy(source.at[strip(b, pair)], piece, links.local.at[k])
            load.start()
            load.wait()
            body(strip(b, pair))

        return inner

    def inward(whole, i, values):
        def body(rows):
            weight = whole[...].astype(LOW).reshape(full, units)
            values[rows] = (
                jnp.dot(piece[...], weight, preferred_element_type=WIDE) + biases[i : i + 1, :]
            )

        return body

    def backward(rows):
        grad_v[rows] = lax.dot_general(
            piece[...], down_w[...], (((1,), (1,)), ((), ())), preferred_element_type=WIDE
        )

    def outward(rows):
        def body(inner):
            at = pl.ds(pl.multiple_of(rows.start + inner.start, 16), inner.size)
            gate, up, grad = gate_v[at], up_v[at], grad_v[at]
            t = jnp.tanh(ROOT * (gate + CUBE * (gate * gate * gate)))
            side = 0.5 * gate * (1.0 + t)
            slope = 0.5 * (1.0 + t) + 0.5 * gate * (1.0 - t * t) * (
                ROOT * (1.0 + 3.0 * CUBE * (gate * gate))
            )
            hidden[at] = (side * up).astype(LOW)
            gate, up = grad * up * slope, grad * side
            grad_gate[at] = gate.astype(LOW)
            grad_up[at] = up.astype(LOW)
            sums[0:1, :] += jnp.sum(gate, axis=0, keepdims=True)
            sums[1:2, :] += jnp.sum(up, axis=0, keepdims=True)

        by_rows(pair, body)

    ups = columns_of(up_own, up_w)
    norms, norm_relay = tokens(normed, normed_here, normed_all)
    norms.start()
    advance(ups)
    norm_relay.wait()
    sums[...] = jnp.zeros(sums.shape, WIDE)
    load.wait()
    back = with_piece(cot_all, backward)
    into = with_piece(normed_all, inward(gate_w, 0, gate_v))

    def backs(first, last):
        def lap(b, carry):
            back(b)
            return carry

        lax.fori_loop(first, last, lap, 0)

    backs(0, middle)
    norms.step(1)
    backs(middle, count)
    for copy in kept:
        copy.wait()
    kept.clear()
    for step in range(count):
        if step > 1:
            norms.step(step)
        if step == 2:
            advance(ups)
        norms.ready(step)
        neighbours(step, into)
    finish(ups)
    kept.append(links.keep(up_w, up_all))
    into_up = with_piece(normed_all, inward(up_w, 1, up_v))

    def last(b, carry):
        into_up(b)
        outward(strip(b, pair))
        return carry

    lax.fori_loop(0, count, last, 0)
    norms.close()
    kept.append(links.keep(hidden, hidden_out))
    kept.append(links.keep(grad_gate, gate_out))
    kept.append(links.keep(grad_up, up_out))
    for copy in kept:
        copy.wait()


def side_by_side(blocks):
    return jnp.concatenate([blocks[i] for i in range(blocks.shape[0])], axis=1)


def columns(matrix, parts):
    width = matrix.shape[1] // parts
    return jnp.stack([matrix[:, i * width : (i + 1) * width] for i in range(parts)])


def padded_rows(rows, height, width):
    return jnp.pad(rows, ((0, height - rows.shape[0]), (0, width - rows.shape[1])))


def rounded(values):
    return lax.reduce_precision(values, 8, 7)


def round_up(size, step):
    return -(-size // step) * step


def shards(
    inputs,
    positions,
    branch_matrix,
    gelu_matrix,
    output_matrix,
    gate_matrix,
    up_matrix,
    down_matrix,
    input_blocks,
    decay_blocks,
    conv_taps,
    conv_bias,
    branch_bias,
    gelu_bias,
    input_bias,
    decay_bias,
    decay_param,
    output_bias,
    gate_bias,
    up_bias,
    down_bias,
    norm_first,
    norm_second,
    cotangent,
):
    count, rows_count, cores = lax.axis_size("dp"), lax.axis_size("row"), lax.axis_size("col")
    place_dp, place_row = lax.axis_index("dp"), lax.axis_index("row")
    tall, narrow = inputs.shape
    quarter, full, tokens = tall // rows_count, narrow * rows_count, tall * cores
    depth, width = branch_matrix.shape
    part = width // rows_count
    hidden_part = down_matrix.shape[0]
    heads, block_part, block = input_blocks.shape
    taps = conv_taps.shape[0]
    steps = positions.shape[0]
    splits = rows_count if block_part % (16 * rows_count) == 0 else 1
    share = block_part // splits
    back_share = block_part // rows_count
    remote, local = 64 + 24 * count, 40 + 6 * count

    wxy = jnp.concatenate(
        (columns(branch_matrix.astype(LOW), rows_count), columns(gelu_matrix.astype(LOW), rows_count)),
        axis=2,
    )
    if depth % 16:
        wxy = wxy.astype(WIDE)
    blocks_low = jnp.concatenate((input_blocks, decay_blocks), axis=0).astype(LOW)
    blk = lax.dynamic_slice_in_dim(
        blocks_low, place_row * share if splits > 1 else 0, share, 1
    )
    channel_rows = jnp.concatenate(
        (
            conv_taps,
            jnp.stack((conv_bias, branch_bias, gelu_bias, input_bias, decay_bias)),
        ),
        axis=0,
    )
    decay_raw = rounded(decay_param)
    channel_rows = jnp.concatenate(
        (rounded(channel_rows), -8.0 * jax.nn.softplus(decay_raw)[None, :]), axis=0
    )
    channel_size = channel_rows.shape[1]
    cvec = padded_rows(
        channel_rows,
        round_up(taps + 6, 8),
        round_up(channel_size, 128),
    )
    wvec = padded_rows(
        rounded(jnp.stack((norm_first, output_bias, down_bias, norm_second))),
        8,
        round_up(depth, 128),
    )
    spots = positions[:, None]
    heads_all = 2 * heads
    whole_tokens = ((tokens, full), LOW, False)
    wide_tokens = ((steps, width), WIDE, False)
    nf_shape = pltpu.VMEM((16 + tokens, full), LOW)
    wxy_kind = wxy.dtype
    tokens_scratch = pltpu.VMEM((steps, width), WIDE)
    eight_rows = pltpu.VMEM((8, width), WIDE)
    table_rows = pltpu.VMEM((rows_count, 8, width), WIDE)
    blocks_shape = (heads_all, count, splits, share, block)
    hidden_shape = (rows_count, count, depth, hidden_part)
    here_scratch = pltpu.VMEM((tall, narrow), WIDE)
    (
        normed_first, x_own, cot_all, wxy_all, wout_all, gate_all, up_own, down_all, blocks, vectors,
        width_all, branch, gelu_in, side, conv, input_gate, decay_gate, state, entering, mixed_all,
        middle, normed_own,
    ) = call(
        functools.partial(forward, count, taps),
        "forward",
        1,
        [
            (inputs, False),
            (cotangent, False),
            (wxy, False),
            (output_matrix.astype(LOW), False),
            (columns(gate_matrix.astype(LOW), count).astype(wxy_kind), False),
            (columns(up_matrix.astype(LOW), count).astype(wxy_kind), False),
            (down_matrix.astype(LOW), False),
            (blk, False),
            (cvec, False),
            (wvec, False),
            (spots, True),
        ],
        [
            whole_tokens,
            ((quarter, full), LOW, False),
            ((cores * count * quarter, full), LOW, False),
            ((rows_count, count * depth, 2 * part), wxy_kind, False),
            ((width, narrow), LOW, False),
            (hidden_shape, wxy_kind, False),
            (hidden_shape[1:], wxy_kind, False),
            ((hidden_part, full), LOW, False),
            (blocks_shape, LOW, False),
            ((cvec.shape[0], width), WIDE, False),
            ((8, full), WIDE, False),
            ((steps + 8, width), WIDE, False),
            wide_tokens,
            wide_tokens,
            wide_tokens,
            wide_tokens,
            wide_tokens,
            wide_tokens,
            ((8, width), WIDE, False),
            ((tokens, width), LOW, False),
            ((quarter, full), WIDE, False),
            ((quarter, full), LOW, False),
        ],
        [
            pltpu.VMEM((tokens, full), LOW),
            nf_shape,
            pltpu.VMEM((rows_count, count * depth, 2 * part), wxy_kind),
            pltpu.VMEM((width, narrow), LOW),
            pltpu.VMEM(blocks_shape, LOW),
            pltpu.VMEM((count,) + cvec.shape, WIDE),
            pltpu.VMEM((rows_count, count) + wvec.shape, WIDE),
            pltpu.VMEM((cvec.shape[0], width), WIDE),
            pltpu.VMEM((8, full), WIDE),
            pltpu.VMEM((rows_count, steps + 16, 2 * part), WIDE),
            pltpu.VMEM((rows_count, steps + 8, 2 * part), WIDE),
            pltpu.VMEM((steps + 8, width), WIDE),
            tokens_scratch,
            tokens_scratch,
            tokens_scratch,
            tokens_scratch,
            tokens_scratch,
            tokens_scratch,
            tokens_scratch,
            tokens_scratch,
            eight_rows,
            table_rows,
            eight_rows,
            pltpu.VMEM((steps, width), LOW),
            pltpu.VMEM((tokens, width), LOW),
            pltpu.VMEM((tokens, narrow), WIDE),
            here_scratch,
            here_scratch,
            pltpu.VMEM((quarter, full), WIDE),
            pltpu.VMEM((quarter, full), WIDE),
            pltpu.VMEM((quarter, full), LOW),
            pltpu.VMEM((depth, hidden_part), wxy_kind),
            pltpu.VMEM((depth, hidden_part), wxy_kind),
            pltpu.VMEM((hidden_part, narrow), LOW),
            pltpu.VMEM((quarter, narrow), LOW),
        ],
        remote,
        local,
    )
    wxy_all = wxy_all.reshape(full, 2 * part).astype(LOW)
    blocks = blocks.reshape(heads_all, block, block)
    gelu_pull = jax.vjp(jax.nn.gelu, gelu_in)[1]

    hidden_tokens = cores * count * quarter
    units_rows = ((hidden_tokens, hidden_part), LOW, False)
    biases = padded_rows(rounded(jnp.stack((gate_bias, up_bias))), 8, hidden_part)
    weight_scratch = pltpu.VMEM(hidden_shape, wxy_kind)
    units_wide = pltpu.VMEM((hidden_tokens, hidden_part), WIDE)
    units_low = pltpu.VMEM((hidden_tokens, hidden_part), LOW)
    (
        normed_second, up_all, hidden, grad_gate_low, grad_up_low, hidden_part_sums,
    ) = call(
        functools.partial(feed_forward, count),
        "feed_forward",
        2,
        [
            (normed_own, False),
            (cot_all, False),
            (gate_all, False),
            (up_own, False),
            (down_all, False),
            (biases, True),
        ],
        [
            ((hidden_tokens, full), LOW, False),
            (hidden_shape, wxy_kind, False),
            units_rows,
            units_rows,
            units_rows,
            ((8, hidden_part), WIDE, True),
        ],
        [
            weight_scratch,
            weight_scratch,
            pltpu.VMEM((hidden_part, full), LOW),
            pltpu.VMEM((cores * quarter, full), LOW),
            units_wide,
            units_wide,
            units_wide,
            units_low,
            units_low,
            units_low,
            pltpu.VMEM((quarter, full), LOW),
        ],
        remote,
        local,
    )
    by_device = (count, cores, quarter, full)
    token_scratch = [
        pltpu.VMEM((count, quarter, full), LOW),
        pltpu.VMEM((count, quarter, full), LOW),
        *line_buffers(count, 2, quarter // 2, full),
    ]
    token_low = pltpu.VMEM((quarter, full), LOW)
    back_outs = [
        ((quarter, full), WIDE, True),
        ((tokens, narrow), LOW, False),
        ((8, full), WIDE, True),
        ((2, narrow // 2, hidden_part), LOW, True),
    ]
    back_scratch = token_scratch + [token_low, token_low, row_buffers(narrow, hidden_part)]
    inside = count <= 4
    if inside:
        grad_middle, grad_middle_all, width_sums, gate_own, forward_partial = call(
            functools.partial(second_norm_back_inside, count),
            "second_norm_back",
            5,
            [
                (grad_gate_low, False),
                (grad_up_low, False),
                (gate_all, False),
                (up_all, False),
                (normed_second, False),
                (hidden, False),
                (down_all, False),
                (cot_all, False),
                (middle, True),
                (width_all, True),
            ],
            back_outs + [((hidden_tokens, full), LOW, False)],
            back_scratch
            + [
                units_low,
                units_low,
                weight_scratch,
                weight_scratch,
                pltpu.VMEM((hidden_tokens, narrow), LOW),
                pltpu.VMEM(by_device, LOW),
                pltpu.VMEM((full, hidden_part), LOW),
                units_low,
                pltpu.VMEM((hidden_part, narrow), LOW),
                pltpu.VMEM((hidden_tokens, narrow), LOW),
            ],
            remote,
            local,
        )
    else:
        forward_partial = times(hidden, down_all).astype(LOW)
        gate_all = gate_all.reshape(full, hidden_part).astype(LOW)
        up_all = up_all.reshape(full, hidden_part).astype(LOW)
        grad_normed_second = (
            (times_flipped(grad_gate_low, gate_all) + times_flipped(grad_up_low, up_all))
            .astype(LOW)
            .reshape(by_device)
        )
        grad_middle, grad_middle_all, width_sums, gate_own = call(
            functools.partial(second_norm_back, count),
            "second_norm_back",
            5,
            [
                (grad_normed_second, False),
                (cot_all, False),
                (middle, True),
                (width_all, True),
                (left_product(normed_second, grad_gate_low).astype(LOW), False),
            ],
            back_outs,
            back_scratch,
            remote,
            local,
        )
    forward_partial = forward_partial.reshape(by_device)

    mixed_outs = [
        ((2, steps // 2, width), WIDE, True),
        ((rows_count, quarter, narrow), LOW, False),
        ((2, narrow // 2, hidden_part), LOW, True),
        ((count, depth, hidden_part), LOW, False),
    ]
    mixed_scratch = (
        [row_buffers(steps, width)]
        + token_scratch
        + [token_low, row_buffers(narrow, hidden_part), pltpu.VMEM((depth, hidden_part), LOW)]
    )
    gate_own = gate_own.reshape(count, depth, hidden_part)
    if inside:
        grad_mixed, layer_out, up_own, gate_blocks, output_partial, down_partial = call(
            functools.partial(mixed_and_output_inside, count),
            "mixed_and_output",
            6,
            [
                (grad_middle_all, False),
                (wout_all, False),
                (mixed_all, False),
                (normed_second, False),
                (cot_all, False),
                (grad_up_low, False),
                (hidden, False),
                (forward_partial, False),
                (middle, True),
                (width_all, True),
                (gate_own, False),
            ],
            mixed_outs + [((width, narrow), LOW, False), ((hidden_part, full), LOW, False)],
            mixed_scratch
            + [
                pltpu.VMEM((tokens, narrow), LOW),
                pltpu.VMEM((width, narrow), LOW),
                pltpu.VMEM((tokens, width), LOW),
                pltpu.VMEM((hidden_tokens, narrow), LOW),
                units_low,
                units_low,
                pltpu.VMEM((tokens, width), LOW),
                pltpu.VMEM((full, hidden_part), LOW),
                pltpu.VMEM((width, narrow), LOW),
                pltpu.VMEM((hidden_part, full), LOW),
            ],
            remote,
            local,
        )
    else:
        down_partial = left_product(hidden, cot_all).astype(LOW)
        output_partial = left_product(mixed_all, grad_middle_all).astype(LOW)
        grad_mixed, layer_out, up_own, gate_blocks = call(
            functools.partial(mixed_and_output, count),
            "mixed_and_output",
            6,
            [
                (times_flipped(grad_middle_all, wout_all).astype(LOW), False),
                (forward_partial, False),
                (middle, True),
                (width_all, True),
                (left_product(normed_second, grad_up_low).astype(LOW), False),
                (gate_own, False),
            ],
            mixed_outs,
            mixed_scratch,
            remote,
            local,
        )
    up_own = up_own.reshape(count, depth, hidden_part)
    grad_mixed = grad_mixed.reshape(steps, width)

    sums_rows = round_up(taps + 6, 8)
    output_parts = 2 if output_matrix.shape[0] % 32 == 0 else 1
    if inside:
        channel_part, block_sums, grad_projected, output_grad, up_blocks = call(
            functools.partial(recurrence_back_inside, count, taps),
            "recurrence_backward",
            7,
            [
                (array, True)
                for array in (
                    branch,
                    side,
                    gelu_in,
                    spots,
                    vectors,
                    blocks,
                    conv,
                    input_gate,
                    decay_gate,
                    state,
                    entering,
                    grad_mixed,
                )
            ]
            + [
                (output_partial.reshape((count,) + output_matrix.shape), False),
                (up_own, False),
            ],
            [
                ((sums_rows, width), WIDE, True),
                ((2 * heads, block, block), WIDE, True),
                ((rows_count, steps, 2 * part), LOW, False),
                (output_matrix.shape, WIDE, True),
                ((count, depth, hidden_part), LOW, False),
            ],
            [
                pltpu.VMEM((steps, width), LOW),
                pltpu.VMEM((steps, width), LOW),
                pltpu.VMEM((rows_count, steps, 2 * part), LOW),
                tokens_scratch,
                tokens_scratch,
                tokens_scratch,
                eight_rows,
                table_rows,
                pltpu.VMEM((2, 8, width), WIDE),
                eight_rows,
                pltpu.VMEM((steps + 8, block), WIDE),
                pltpu.VMEM((steps + 8, block), WIDE),
                *line_buffers(count, output_parts, output_matrix.shape[0] // output_parts, narrow),
                pltpu.VMEM((count,) + output_matrix.shape, LOW),
                pltpu.VMEM((depth, hidden_part), LOW),
            ],
            remote,
            local,
        )
        grad_projected = grad_projected.reshape(tokens, 2 * part)
    else:
        grad_gelu = gelu_pull(grad_mixed * state)[0]
        grad_branch_low, channel_part, block_sums = call(
            functools.partial(recurrence_backward, count, taps),
            "recurrence_backward",
            7,
            [
                (array, True)
                for array in (
                    branch,
                    side,
                    spots,
                    vectors,
                    blocks,
                    conv,
                    input_gate,
                    decay_gate,
                    state,
                    entering,
                    grad_mixed,
                )
            ],
            [
                ((steps, width), LOW, True),
                ((round_up(taps + 6, 8), width), WIDE, True),
                ((2 * heads, block, block), WIDE, True),
            ],
            [
                tokens_scratch,
                tokens_scratch,
                tokens_scratch,
                eight_rows,
                table_rows,
                pltpu.VMEM((2, 8, width), WIDE),
                eight_rows,
                pltpu.VMEM((steps + 8, block), WIDE),
                pltpu.VMEM((steps + 8, block), WIDE),
            ],
            remote,
            local,
        )
        grad_gelu_low = grad_gelu.astype(LOW)
        projected_grads = jnp.concatenate(
            (columns(grad_branch_low, rows_count), columns(grad_gelu_low, rows_count)), axis=2
        )
        grad_projected, output_grad, up_blocks = call(
            functools.partial(spread_gradients, count),
            "spread_gradients",
            8,
            [
                (projected_grads, False),
                (output_partial.reshape((count,) + output_matrix.shape), False),
                (up_own, False),
            ],
            [
                ((rows_count, steps, 2 * part), LOW, False),
                (output_matrix.shape, WIDE, True),
                ((count, depth, hidden_part), LOW, False),
            ],
            [
                *line_buffers(count, output_parts, output_matrix.shape[0] // output_parts, narrow),
                pltpu.VMEM((count,) + output_matrix.shape, LOW),
            ],
            remote,
            local,
        )
        grad_projected = grad_projected.reshape(tokens, 2 * part)
        channel_part = channel_part.at[taps + 5].set(jnp.sum(grad_gelu, axis=0))
    hidden_part_sums = padded_rows(hidden_part_sums, 8, round_up(hidden_part, 128))
    block_in = (
        block_sums.astype(LOW)
        .reshape(2 * heads, count, rows_count, back_share, block)
        .transpose(2, 1, 0, 3, 4)
        .reshape(rows_count, count, 2 * heads * back_share, block)
    )
    channel_shape, sums_shape = channel_part.shape, hidden_part_sums.shape
    block_rows = 2 * heads * back_share
    first_outs = [
        ((rows_count, quarter, narrow), LOW, False),
        ((rows_count, depth, 2 * part), LOW, False),
        ((hidden_part, narrow), WIDE, True),
        ((2, 8, narrow), WIDE, True),
        (channel_shape, WIDE, True),
        ((rows_count, block_rows, block), LOW, False),
        (sums_shape, WIDE, True),
    ]
    first_scratch = [
        pltpu.VMEM((rows_count, quarter, full), LOW),
        pltpu.VMEM((rows_count, quarter, full), LOW),
        pltpu.VMEM((rows_count, quarter, full), LOW),
        row_buffers(quarter, full),
        token_low,
        pltpu.VMEM((rows_count, quarter, narrow), LOW),
        pltpu.VMEM((8, full), WIDE),
        pltpu.VMEM((count, rows_count, depth, 2 * part), LOW),
        *line_buffers(count, rows_count, depth, 2 * part),
        pltpu.VMEM((rows_count, depth, 2 * part), LOW),
        pltpu.VMEM((rows_count, 8, narrow), WIDE),
        pltpu.VMEM((count, 8, narrow), WIDE),
        pltpu.VMEM((rows_count, 8, narrow), WIDE),
        pltpu.VMEM((rows_count,) + channel_shape, WIDE),
        pltpu.VMEM((count,) + channel_shape, WIDE),
        pltpu.VMEM((rows_count,) + sums_shape, WIDE),
        pltpu.VMEM(block_in.shape, LOW),
        pltpu.VMEM(block_in.shape[1:], LOW),
        pltpu.VMEM(block_in.shape[1:], LOW),
        pltpu.VMEM((block_rows, block), LOW),
        row_buffers(hidden_part, narrow),
    ]
    sums_in = [
        (width_sums, True),
        (channel_part, True),
        (hidden_part_sums, True),
        (block_in, False),
    ]
    if inside:
        first_kernel, first_ins = first_norm_back_inside, [
            (grad_projected, False),
            (wxy_all, False),
            (normed_first, False),
            (x_own, False),
            (grad_middle, True),
            (width_all, True),
            (down_partial, False),
        ]
        first_scratch += [
            pltpu.VMEM((tokens, 2 * part), LOW),
            pltpu.VMEM((full, 2 * part), LOW),
            pltpu.VMEM((tokens, full), LOW),
            pltpu.VMEM((cores, rows_count, quarter, full), LOW),
        ]
    else:
        first_kernel, first_ins = first_norm_back, [
            (
                times_flipped(grad_projected, wxy_all)
                .astype(LOW)
                .reshape(cores, rows_count, quarter, full),
                False,
            ),
            (x_own, False),
            (grad_middle, True),
            (width_all, True),
            (
                left_product(normed_first, grad_projected)
                .astype(LOW)
                .reshape(rows_count, count, depth, 2 * part),
                False,
            ),
            (down_partial, False),
        ]
    input_grad, proj_grad, down_grad, width_sums, channel_sums, block_grads, hidden_sums = call(
        functools.partial(first_kernel, count),
        "first_norm_back",
        9,
        first_ins + sums_in,
        first_outs,
        first_scratch,
        remote,
        local,
    )
    branch_grad = side_by_side(proj_grad[:, :, :part].astype(WIDE))
    gelu_grad = side_by_side(proj_grad[:, :, part:].astype(WIDE))
    block_grads = (
        block_grads.reshape(rows_count, 2 * heads, back_share, block)
        .transpose(1, 0, 2, 3)
        .reshape(2 * heads, block_part, block)
        .astype(WIDE)
    )
    channel_sums = lax.dynamic_slice_in_dim(channel_sums, place_dp * channel_size, channel_size, 1)
    width_sums = lax.dynamic_slice_in_dim(
        width_sums[0] + width_sums[1], place_dp * depth, depth, 1
    )
    decay_param_grad = -8.0 * channel_sums[taps + 4] * jax.nn.sigmoid(decay_raw)

    return (
        layer_out.reshape(tall, narrow),
        input_grad.reshape(tall, narrow).astype(WIDE),
        branch_grad,
        gelu_grad,
        output_grad,
        side_by_side(gate_blocks.astype(WIDE)),
        side_by_side(up_blocks.astype(WIDE)),
        down_grad,
        block_grads[:heads],
        block_grads[heads:],
        channel_sums[:taps],
        channel_sums[taps],
        channel_sums[taps + 1],
        channel_sums[taps + 5],
        channel_sums[taps + 2],
        channel_sums[taps + 3],
        decay_param_grad,
        width_sums[1],
        hidden_sums[0, :hidden_part],
        hidden_sums[1, :hidden_part],
        width_sums[2],
        width_sums[3],
        width_sums[0],
    )


def solution(mesh):
    in_specs = (
        P(("dp", "col"), "row"),
        P(("dp", "row")),
        P(("row", "dp"), "col"),
        P(("row", "dp"), "col"),
        P(("col", "dp"), "row"),
        P(("row", "dp"), "col"),
        P(("row", "dp"), "col"),
        P(("col", "dp"), "row"),
        P("col", "dp", None),
        P("col", "dp", None),
        P(None, ("col", "dp")),
        P(("col", "dp")),
        P(("col", "dp")),
        P(("col", "dp")),
        P(("col", "dp")),
        P(("col", "dp")),
        P(("col", "dp")),
        P(("row", "dp")),
        P(("col", "dp")),
        P(("col", "dp")),
        P(("row", "dp")),
        P(("row", "dp")),
        P(("row", "dp")),
        P(("dp", "col"), "row"),
    )
    out_specs = (
        P(("dp", "col"), "row"),
        P(("dp", "col"), "row"),
        P(("row", "dp"), "col"),
        P(("row", "dp"), "col"),
        P(("col", "dp"), "row"),
        P(("row", "dp"), "col"),
        P(("row", "dp"), "col"),
        P(("col", "dp"), "row"),
        P("col", "dp", None),
        P("col", "dp", None),
        P(None, ("col", "dp")),
        P(("col", "dp")),
        P(("col", "dp")),
        P(("col", "dp")),
        P(("col", "dp")),
        P(("col", "dp")),
        P(("col", "dp")),
        P(("row", "dp")),
        P(("col", "dp")),
        P(("col", "dp")),
        P(("row", "dp")),
        P(("row", "dp")),
        P(("row", "dp")),
    )
    return jax.shard_map(shards, mesh=mesh, in_specs=in_specs, out_specs=out_specs, check_vma=False)
```

```python
import functools

import jax
import jax.numpy as jnp
from jax import lax
from jax.experimental import pallas as pl
from jax.experimental.pallas import tpu as pltpu
from jax.sharding import PartitionSpec as P

epsilon = 1e-06
ROOT = (2.0 / 3.141592653589793) ** 0.5
CUBE = 0.044715
LOW = jnp.bfloat16
WIDE = jnp.float32
MESH = pl.DeviceIdType.MESH
VMEM = pl.BlockSpec(memory_space=pltpu.VMEM)
ANY = pl.BlockSpec(memory_space=pl.ANY)


def times(piece, matrix):
    return jnp.dot(piece, matrix, preferred_element_type=WIDE)


def times_flipped(piece, matrix):
    return lax.dot_general(piece, matrix, (((1,), (1,)), ((), ())), preferred_element_type=WIDE)


def left_product(left, right):
    return lax.dot_general(left, right, (((0,), (0,)), ((), ())), preferred_element_type=WIDE)


class Links:
    def __init__(self, send, recv, local):
        self.send, self.recv, self.local = send, recv, local
        self.sent = self.kept = 0

    def copy(self, src, dst, **where):
        k, self.sent = self.sent, self.sent + 1
        return pltpu.make_async_remote_copy(
            src_ref=src,
            dst_ref=dst,
            send_sem=self.send.at[k],
            recv_sem=self.recv.at[k],
            device_id=where,
            device_id_type=MESH,
        )

    def keep(self, src, dst):
        k, self.kept = self.kept, self.kept + 1
        copy = pltpu.make_async_copy(src, dst, self.local.at[k])
        copy.start()
        return copy


class Relay:
    def __init__(self, links, src, buffer, dst):
        self.links, self.buffer, self.dst, self.store = links, buffer, dst, None
        self.load = links.keep(src, buffer)

    def pass_on(self):
        if self.store is None:
            self.load.wait()
            self.store = self.links.keep(self.buffer, self.dst)

    def wait(self):
        self.pass_on()
        self.store.wait()


class Place:
    def __init__(self, count_dp):
        self.row, self.dp, self.col = (lax.axis_index(name) for name in ("row", "dp", "col"))
        self.count = count_dp
        first, second = lax.rem(self.row, 2), lax.div(self.row, 2)
        self.near = [self.row, self.row + 1 - 2 * first, self.row + 2 - 4 * second, 3 - self.row]
        self.other = 1 - self.col

    def turn(self, index):
        return lax.rem(index + self.count, self.count)


def greet(place, rows=False, line=False, cores=False):
    barrier = pltpu.get_barrier_semaphore()
    partners = []
    if rows:
        partners += [{"row": place.near[k]} for k in range(1, 4)]
    if line:
        partners += [{"dp": place.turn(place.dp + k)} for k in range(1, place.count)]
    if cores:
        partners += [{"col": place.other}]
    for where in partners:
        pl.semaphore_signal(barrier, inc=1, device_id=where, device_id_type=MESH)
    pl.semaphore_wait(barrier, len(partners))


def run(tasks):
    live = list(tasks)
    while live:
        live = [task for task in live if next(task, None) is not None]


def advance(*tasks):
    for task in tasks:
        next(task, None)


def finish(*tasks):
    run(tasks)


def chain(*tasks):
    for task in tasks:
        yield from task


def when(condition, action):
    pl.when(condition)(lambda: action() and None)


def halves(size):
    first = -(-size // 32) * 16
    return (pl.ds(0, first), pl.ds(first, size - first))


def by_rows(count, body):
    step = 16 if count % 16 == 0 else count

    def lap(i, carry):
        body(pl.ds(pl.multiple_of(i * step, step), step))
        return carry

    lax.fori_loop(0, count // step, lap, 0)


def by_pieces(pieces, height, body):
    def lap(i, carry):
        by_rows(height, lambda rows: body(i, rows))
        return carry

    if pieces == 1:
        by_rows(height, lambda rows: body(0, rows))
    else:
        lax.fori_loop(0, pieces, lap, 0)


def gather_rows(links, place, own, piece):
    row, near, side, _ = place.near
    out = [
        links.copy(own(0), piece(row, 0), row=near),
        links.copy(own(1), piece(row, 1), row=side),
        links.copy(own(1), piece(row, 1), row=near),
        links.copy(own(0), piece(row, 0), row=side),
    ]
    for copy in out:
        copy.start()
    yield 1
    out[0].wait_recv()
    out.append(links.copy(piece(near, 0), piece(near, 0), row=side))
    out[4].start()
    out[1].wait_recv()
    out.append(links.copy(piece(side, 1), piece(side, 1), row=near))
    out[5].start()
    yield 1
    for copy in out[2:]:
        copy.wait_recv()
    for copy in out:
        copy.wait_send()


def exchange_rows(links, place, source, target):
    out = [
        links.copy(source(place.near[k]), target(place.row), row=place.near[k])
        for k in range(1, 4)
    ]
    for copy in out:
        copy.start()
    yield 1
    for copy in out:
        copy.wait_recv()
    for copy in out:
        copy.wait_send()


def exchange_line(links, place, source, target):
    out = []
    for k in range(1, place.count):
        far = place.turn(place.dp + k)
        out.append(links.copy(source(far), target(place.dp), dp=far))
    for copy in out:
        copy.start()
    yield 1
    for copy in out:
        copy.wait_recv()
    for copy in out:
        copy.wait_send()


def gather_line(links, place, own, piece, share=False):
    z, count, turn = place.dp, place.count, place.turn
    ups, downs, shared = [], [], []

    def pass_on(block, valid):
        copy = links.copy(piece(block), piece(block), col=place.other)
        when(valid, copy.start)
        shared.append((copy, valid))

    if share:
        copy = links.copy(own, piece(z), col=place.other)
        copy.start()
        shared.append((copy, z >= 0))
    for step in range(1, count + 1):
        if step > 1:
            yield 1
            below, above = z >= step - 1, z <= count - step
            when(below, ups[-1].wait_recv)
            when(above, downs[-1].wait_recv)
        if step < count:
            low, high = turn(z - step + 1), turn(z + step - 1)
            ups.append(
                links.copy(own if step == 1 else piece(low), piece(low), dp=turn(z + 1))
            )
            downs.append(
                links.copy(own if step == 1 else piece(high), piece(high), dp=turn(z - 1))
            )
            when((z >= step - 1) & (z < count - 1), ups[-1].start)
            when((z <= count - step) & (z > 0), downs[-1].start)
        if step > 1 and share:
            pass_on(turn(z - step + 1), below)
            pass_on(turn(z + step - 1), above)
    yield 1
    for copy, valid in shared:
        when(valid, copy.wait_recv)
    for step in range(1, count):
        when((z >= step - 1) & (z < count - 1), ups[step - 1].wait_send)
        when((z <= count - step) & (z > 0), downs[step - 1].wait_send)
    for copy, valid in shared:
        when(valid, copy.wait_send)


class LineGather:
    def __init__(self, links, place, own, piece):
        self.links, self.place, self.own, self.piece = links, place, own, piece
        self.ups, self.downs, self.shared = [None], [None], []

    def send(self, step):
        z, count, turn = self.place.dp, self.place.count, self.place.turn
        low, high = turn(z - step + 1), turn(z + step - 1)
        for copies, block, target, valid in (
            (self.ups, low, turn(z + 1), (z >= step - 1) & (z < count - 1)),
            (self.downs, high, turn(z - 1), (z <= count - step) & (z > 0)),
        ):
            source = self.own if step == 1 else self.piece(block)
            copy = self.links.copy(source, self.piece(block), dp=target)
            copies.append((copy, valid))
            when(valid, copy.start)

    def share(self, blocks, own=None):
        out = []
        for block, valid in blocks:
            source = self.piece(block) if own is None else own
            copy = self.links.copy(source, self.piece(block), col=self.place.other)
            when(valid, copy.start)
            out.append((copy, valid))
        self.shared.append(out)

    def start(self):
        self.send(1)
        self.share([(self.place.dp, self.place.dp >= 0)], self.own)

    def step(self, step):
        z, count, turn = self.place.dp, self.place.count, self.place.turn
        below, above = z >= step, z <= count - 1 - step
        when(below, self.ups[step][0].wait_recv)
        when(above, self.downs[step][0].wait_recv)
        if step < count - 1:
            self.send(step + 1)
        self.share([(turn(z - step), below), (turn(z + step), above)])

    def ready(self, step):
        for copy, valid in self.shared[step]:
            when(valid, copy.wait_recv)

    def close(self):
        for copy, valid in self.ups[1:] + self.downs[1:] + sum(self.shared, []):
            when(valid, copy.wait_send)


def scatter_rows(links, place, part, buffers, result, prepare=None, gentle=False):
    row, near, side, far = place.near
    if prepare is not None:
        prepare(far)
    heights = [part(row, h).shape[0] for h in range(2)]

    def buffer(i, h):
        return buffers.at[i, pl.ds(0, heights[h])]

    out = [
        links.copy(part(far, 0), buffer(5, 0), row=side),
        links.copy(part(far, 1), buffer(7, 1), row=near),
        links.copy(part(side, 0), buffer(4, 0), row=side),
        links.copy(part(near, 1), buffer(6, 1), row=near),
    ]
    for i, copy in enumerate(out):
        if i == 2 and gentle:
            yield 1
        if i > 1 and prepare is not None:
            prepare(near if i == 3 else side)
        copy.start()
    if prepare is not None:
        prepare(row)
    loads = [
        links.keep(part(near, 0), buffer(0, 0)),
        links.keep(part(side, 1), buffer(1, 1)),
        links.keep(part(row, 0), buffer(2, 0)),
        links.keep(part(row, 1), buffer(3, 1)),
    ]
    yield 1
    for h, target in ((0, near), (1, side)):
        loads[h].wait()
        out[h].wait_recv()

        def add(rows, h=h):
            total = buffers[h, rows].astype(WIDE) + buffers[5 + 2 * h, rows].astype(WIDE)
            buffers[h, rows] = total.astype(LOW)

        by_rows(heights[h], add)
        out.append(links.copy(buffer(h, h), buffer(8 + h, h), row=target))
        out[-1].start()
        yield 1
    for h in range(2):
        loads[2 + h].wait()
        out[2 + h].wait_recv()
        out[4 + h].wait_recv()

        def finish(rows, h=h):
            result(
                h,
                rows,
                buffers[2 + h, rows].astype(WIDE)
                + buffers[4 + 2 * h, rows].astype(WIDE)
                + buffers[8 + h, rows].astype(WIDE),
            )

        by_rows(heights[h], finish)
    for copy in out:
        copy.wait_send()


def row_buffers(size, width):
    return pltpu.VMEM((10, halves(size)[0].size, width), LOW)


def scatter_line(links, place, ready, term, ups_in, downs_in, staging, result):
    z, count, turn = place.dp, place.count, place.turn
    pieces, height = ups_in.shape[1:3]
    ups, downs = [None], [None]

    def sends_up(t):
        return (z <= t - 1) & (z < count - 1)

    def sends_down(t):
        return (z >= count - t) & (z > 0)

    def fill(slot, block, arrived):
        def body(i, rows):
            value = term(block, i, rows)
            if arrived is not None:
                value = value + arrived[i, rows].astype(WIDE)
            staging[slot, i, rows] = value.astype(LOW)

        by_pieces(pieces, height, body)

    for t in range(1, count):
        ready(t)
        ready(count - t)
        for which in range(2):
            copies, into = ((ups, ups_in), (downs, downs_in))[which]
            sends = (sends_up, sends_down)[which]
            first = (z == 0, z == count - 1)[which]
            block = (turn(z - t), turn(z + t))[which]
            target = (turn(z + 1), turn(z - 1))[which]
            slot = 2 * which + t % 2
            if t > 2:
                when(sends(t - 2), copies[t - 2].wait_send)
            copy = links.copy(staging.at[slot], into.at[t - 1], dp=target)
            copies.append(copy)

            def begin(copy=copy, slot=slot, block=block):
                fill(slot, block, None)
                copy.start()

            when(sends(t) & first, begin)
            if t > 1:

                def go_on(copy=copy, slot=slot, block=block, before=copies[t - 1], into=into, t=t):
                    before.wait_recv()
                    fill(slot, block, into.at[t - 2])
                    copy.start()

                when(sends(t) & jnp.logical_not(first), go_on)
        yield 1
    ready(0)
    last = count - 1
    from_below, from_above = ups_in.at[last - 1], downs_in.at[last - 1]
    when(z > 0, ups[last].wait_recv)
    when(z < last, downs[last].wait_recv)

    def finish(below, above):
        def body(i, rows):
            value = term(z, i, rows)
            if below:
                value = value + from_below[i, rows].astype(WIDE)
            if above:
                value = value + from_above[i, rows].astype(WIDE)
            result(i, rows, value)

        by_pieces(pieces, height, body)

    when(z == 0, lambda: finish(False, True))
    when((z > 0) & (z < last), lambda: finish(True, True))
    when(z == last, lambda: finish(True, False))
    for t in range(max(1, count - 2), count):
        when(sends_up(t), ups[t].wait_send)
        when(sends_down(t), downs[t].wait_send)


def scatter_line_in_parts(links, place, ready, term, ups_in, downs_in, staging, result):
    def part(i):
        return scatter_line(
            links,
            place,
            ready,
            lambda b, _, rows: term(b, i, rows),
            ups_in.at[:, pl.ds(i, 1)],
            downs_in.at[:, pl.ds(i, 1)],
            staging.at[:, pl.ds(i, 1)],
            lambda _, rows, value: result(i, rows, value),
        )

    live = [part(i) for i in range(ups_in.shape[1])]
    while live:
        live = [task for task in live if next(task, None) is not None]
        yield 1


def line_buffers(count, pieces, height, width):
    return [pltpu.VMEM((slots, pieces, height, width), LOW) for slots in (count - 1, count - 1, 4)]


def token_scatter(links, place, partial, ours, theirs, buffers, result, prepare=None):
    out, loads = [], []
    for s in list(range(1, place.count)) + [0]:
        block = place.turn(place.dp - s)
        if prepare is not None:
            prepare(block)
        out.append(
            links.copy(partial.at[block, place.other], theirs.at[block], col=place.other)
        )
        out[-1].start()
        loads.append(links.keep(partial.at[block, place.col], ours.at[block]))
    waited = set()

    def ready(s):
        if s not in waited:
            waited.add(s)
            at = s - 1 if s else place.count - 1
            out[at].wait_recv()
            loads[at].wait()

    height = buffers[0].shape[2]

    def at(i, rows):
        return pl.ds(pl.multiple_of(rows.start + i * height, 16), rows.size)

    def term(block, i, rows):
        here = at(i, rows)
        return ours[block, here].astype(WIDE) + theirs[block, here].astype(WIDE)

    yield 1
    yield from scatter_line_in_parts(
        links, place, ready, term, *buffers, lambda i, rows, value: result(at(i, rows), value)
    )
    for copy in out:
        copy.wait_send()


def call(kernel, name, number, ins, outs, scratch, remote, local):
    return pl.pallas_call(
        kernel,
        in_specs=[VMEM if inside else ANY for _, inside in ins],
        out_specs=[VMEM if inside else ANY for _, _, inside in outs],
        out_shape=[jax.ShapeDtypeStruct(shape, kind) for shape, kind, _ in outs],
        scratch_shapes=list(scratch)
        + [
            pltpu.SemaphoreType.DMA((remote,)),
            pltpu.SemaphoreType.DMA((remote,)),
            pltpu.SemaphoreType.DMA((local,)),
        ],
        compiler_params=pltpu.CompilerParams(
            collective_id=number, has_side_effects=True, vmem_limit_bytes=58 * 1024 * 1024
        ),
        name=name,
    )(*[array for array, _ in ins])


def lanes(index, width):
    return pl.ds(pl.multiple_of(index * width, 128), width)


def strip(index, height, step=16):
    return pl.ds(pl.multiple_of(index * height, step), height)


def combine(earlier, later):
    return (earlier[0] * later[0], later[0] * earlier[1] + later[1])


def scan_rows(decay, value, reverse):
    count = decay.shape[0]
    rows = lax.broadcasted_iota(jnp.int32, decay.shape, 0)
    reach = 1
    while reach < count:
        turn = count - reach if reverse else reach
        inside = rows < count - reach if reverse else rows >= reach
        decay_far = jnp.where(inside, pltpu.roll(decay, turn, 0), 1.0)
        value_far = jnp.where(inside, pltpu.roll(value, turn, 0), 0.0)
        value = decay * value_far + value
        decay = decay * decay_far
        reach *= 2
    return decay, value


def minus_expm1(v):
    series = 1.0 + v / 9.0
    for k in range(8, 1, -1):
        series = 1.0 + (v / k) * series
    return jnp.where(v > -0.5, -v * series, 1.0 - jnp.exp(v))


def each_head(heads, width, body):
    def lap(h, carry):
        body(h, pl.ds(pl.multiple_of(h * width, 128), width))
        return carry

    lax.fori_loop(0, heads, lap, 0)


def carry_over(links, place, ends, table, reverse):
    run([exchange_rows(links, place, lambda q: ends, lambda q: table.at[q])])
    row = place.row
    state = jnp.zeros((1, ends.shape[1]), WIDE)
    for k in range(4):
        q = 3 - k if reverse else k

        def entry(i):
            return table[q, i : i + 1, :]

        reached = q > row if reverse else q < row
        state = jnp.where(reached, entry(0) * state + entry(1), state)
    return state


def recurrence_backward(
    count, taps, proj, side, spots, vectors, blocks, conv_in, in_gate, dec_gate, state_in, entering,
    grad_mixed, branch_out, sums_out, blocks_out, reach, local_grad, branch, ends, table, heads_in,
    heads_here, padded, spread, send, recv, local, links=None, between=lambda: None,
):
    place = Place(count)
    if links is None:
        links = Links(send, recv, local)
        greet(place, rows=True)
    tokens, width = side.shape
    heads, block = blocks.shape[0] // 2, blocks.shape[1]
    spot = spots[...]
    starting = spot == 0
    ends[...] = jnp.zeros(ends.shape, WIDE)

    def backwards(h, at):
        rate = vectors[taps + 5 : taps + 6, at]
        decay = jnp.where(starting, 0.0, jnp.exp(rate * dec_gate[:, at]))
        padded[0:tokens, :] = decay
        padded[tokens:, :] = jnp.ones((8, block), WIDE)
        far, grad = scan_rows(padded[1 : tokens + 1, :], grad_mixed[:, at] * side[:, at], True)
        reach[:, at] = far
        local_grad[:, at] = grad
        ends[0:1, at] = decay[0:1, :] * far[0:1, :]
        ends[1:2, at] = decay[0:1, :] * grad[0:1, :]

    each_head(heads, block, backwards)
    own = links.keep(ends, table.at[place.row])
    own.wait()
    heads_here[0:1, :] = carry_over(links, place, ends, table, True)
    between()

    def one_head(h, at):
        def vector(i):
            return vectors[i : i + 1, at]

        grad_state = local_grad[:, at] + reach[:, at] * heads_here[0:1, at]
        padded[8:, :] = state_in[:, at]
        padded[7:8, :] = entering[0:1, at]
        grad_decay = grad_state * padded[7 : 7 + tokens, :]
        input_gate, decay_gate, conv = in_gate[:, at], dec_gate[:, at], conv_in[:, at]
        rate = vector(taps + 5)
        log_decay = rate * decay_gate
        decay = jnp.exp(log_decay)
        multiplier = jnp.where(starting, 1.0, jnp.sqrt(minus_expm1(2.0 * log_decay)))
        grad_gated = grad_state * conv
        grad_log = jnp.where(
            starting, 0.0, decay * (grad_decay - grad_gated * input_gate * (decay / multiplier))
        )
        grad_in = grad_gated * multiplier * (input_gate * (1.0 - input_gate))
        grad_gate = grad_log * decay_gate
        grad_dec = grad_gate * rate * (1.0 - decay_gate)
        low = conv.astype(LOW)
        low_in, low_dec = grad_in.astype(LOW), grad_dec.astype(LOW)
        across = (((1,), (1,)), ((), ()))
        along = (((0,), (0,)), ((), ()))
        grad_conv = (
            grad_state * multiplier * input_gate
            + lax.dot_general(low_in, blocks[h], across, preferred_element_type=WIDE)
            + lax.dot_general(low_dec, blocks[heads + h], across, preferred_element_type=WIDE)
        )
        blocks_out[h] = lax.dot_general(low, low_in, along, preferred_element_type=WIDE)
        blocks_out[heads + h] = lax.dot_general(low, low_dec, along, preferred_element_type=WIDE)
        spread[0:8, :] = jnp.zeros((8, block), WIDE)
        spread[8:, :] = vector(0) * grad_conv
        shift = vector(taps + 1)

        def total(values):
            return jnp.sum(values, axis=0, keepdims=True)

        sums_out[0:1, at] = total(grad_conv * (proj[8:, at] + shift))
        for k in range(1, taps):
            kept = jnp.where(spot >= k, grad_conv, 0.0)
            sums_out[k : k + 1, at] = total(kept * (proj[8 - k : 8 - k + tokens, at] + shift))
            spread[8 - k : 8 - k + tokens, :] += vector(k) * kept
        branch[:, at] = spread[8:, :]
        heads_in[0, :, at] = spread[0:8, :]
        sums_out[taps : taps + 1, at] = total(grad_conv)
        sums_out[taps + 1 : taps + 2, at] = total(spread[...])
        sums_out[taps + 2 : taps + 3, at] = total(grad_in)
        sums_out[taps + 3 : taps + 4, at] = total(grad_dec)
        sums_out[taps + 4 : taps + 5, at] = total(grad_gate)
        sums_out[taps + 5 :, at] = jnp.zeros((sums_out.shape[0] - taps - 5, block), WIDE)

    each_head(heads, block, one_head)
    row = place.row
    before = lax.rem(row + 3, 4)
    owed = links.copy(heads_in.at[0], heads_in.at[1], row=before)
    owed.start()
    owed.wait_recv()
    owed.wait_send()
    between()

    def finish(h, at):
        last = jnp.where(row < 3, heads_in[1, :, at], 0.0)
        branch[tokens - 8 :, at] += last
        branch_out[:, at] = branch[:, at].astype(LOW)

    each_head(heads, block, finish)


def recurrence_back_inside(
    count, taps, proj_hbm, side_hbm, gelu_hbm, spots, vectors, blocks_hbm, conv_hbm, in_hbm, dec_hbm,
    state_hbm, entering, mixed_hbm, output_partial, up_own, sums_out, blocks_out, all_out, output_out, up_out, branch_low, gelu_low, stage, reach, local_grad, branch, ends, table, heads_in,
    heads_here, padded, spread, ups, downs, staging, own, up_here, proj, side, gelu_in, blocks, conv_in,
    in_gate, dec_gate, state_in, grad_mixed, send, recv, local,
):
    place = Place(count)
    links = Links(send, recv, local)
    load = links.keep(output_partial, own)
    arrays = [
        links.keep(source, target)
        for source, target in (
            (dec_hbm, dec_gate), (mixed_hbm, grad_mixed), (side_hbm, side), (state_hbm, state_in),
            (blocks_hbm, blocks), (conv_hbm, conv_in), (in_hbm, in_gate), (proj_hbm, proj),
            (gelu_hbm, gelu_in),
        )
    ]
    greet(place, rows=True, line=True)
    row, z = place.row, place.dp
    part = stage.shape[2] // 2
    kept = Relay(links, up_own.at[z], up_here, up_out.at[z])

    output_half = ups.shape[2]

    def output_rows(i, rows):
        return pl.ds(pl.multiple_of(rows.start + i * output_half, 16), rows.size)

    def keep_output(i, rows, value):
        output_out[output_rows(i, rows)] = value

    output_sum = scatter_line_in_parts(
        links,
        place,
        lambda s: None,
        lambda b, i, rows: own[b, output_rows(i, rows)].astype(WIDE),
        ups,
        downs,
        staging,
        keep_output,
    )
    up_line = exchange_line(links, place, lambda b: up_own.at[b], lambda b: up_out.at[b])
    load.wait()
    advance(output_sum, up_line)
    kept.pass_on()
    for array in arrays:
        array.wait()

    def gelu_back(h, at):
        grad = grad_mixed[:, at] * state_in[:, at] * gelu_slope(gelu_in[:, at])
        gelu_low[:, at] = grad.astype(LOW)
        spread[0:1, :] = jnp.sum(grad, axis=0, keepdims=True)
        sums_out[taps + 5 : taps + 6, at] = spread[0:1, :]

    recurrence_backward(
        count, taps, proj, side, spots, vectors, blocks, conv_in, in_gate, dec_gate, state_in, entering,
        grad_mixed, branch_low, sums_out, blocks_out, reach, local_grad, branch, ends, table, heads_in,
        heads_here, padded, spread, None, None, None, links, lambda: advance(output_sum),
    )
    each_head(blocks.shape[0] // 2, blocks.shape[1], gelu_back)
    for q in range(4):
        at = slice(q * part, (q + 1) * part)
        stage[q, :, :part] = branch_low[:, at]
        stage[q, :, part:] = gelu_low[:, at]
    mine = links.keep(stage.at[row], all_out.at[row])
    spread_out = exchange_rows(links, place, lambda q: stage.at[q], lambda q: all_out.at[q])
    run([spread_out, output_sum, up_line])
    mine.wait()
    kept.wait()


def norm_rule(rows, grad, value, gain, sums, at):
    full = value.shape[1]
    inverse = lax.rsqrt(jnp.sum(value * value, axis=1, keepdims=True) / full + epsilon)
    scaled = grad * (1.0 + gain)
    inner = jnp.sum(scaled * value, axis=1, keepdims=True)
    sums[at : at + 1, :] += jnp.sum(grad * value * inverse, axis=0, keepdims=True)
    return inverse * scaled - value * (inverse * inverse * inverse) * (inner / full)


def second_norm_back_inside(
    count, grad_gate, grad_up, gate_all, up_all, normed, hidden, down_all, cot_all, middle, vectors,
    grad_middle, grad_all, sums, gate_out, forward_out, ours, theirs, ups, downs, staging, cot, low, buffers,
    gate_v, up_v, gate_w, up_w, tile, partial, gate_partial, hidden_v, down_tile, forward_tile, send, recv,
    local,
):
    place = Place(count)
    links = Links(send, recv, local)
    loads = [links.keep(grad_gate, gate_v), links.keep(grad_up, up_v)]
    pieces = [
        (links.keep(gate_all.at[q], gate_w.at[q]), links.keep(up_all.at[q], up_w.at[q]))
        for q in range(4)
    ]
    greet(place, rows=True, line=True, cores=True)
    quarter, full = middle.shape
    narrow, units = full // 4, gate_v.shape[1]
    for load in loads:
        load.wait()
    first = [True]

    def tokens(block):
        rows = strip(block, 2 * quarter)

        def lap(q, carry):
            total = sum(
                times_flipped(values[rows, :], weight[q].astype(LOW).reshape(narrow, units))
                for values, weight in ((gate_v, gate_w), (up_v, up_w))
            ).astype(LOW)
            for core in range(2):
                partial[block, core, :, lanes(q, narrow)] = total[
                    core * quarter : (core + 1) * quarter
                ]
            return carry

        if first:
            first.clear()
            for q in range(4):
                for load in pieces[q]:
                    load.wait()
                lap(q, 0)
        else:
            lax.fori_loop(0, 4, lap, 0)

    k, links.kept = links.kept, links.kept + 1

    def gate(q):
        load = pltpu.make_async_copy(normed.at[:, lanes(q, narrow)], tile, links.local.at[k])
        load.start()
        load.wait()
        gate_partial[strip(q, narrow)] = left_product(tile[...], gate_v[...]).astype(LOW)

    k_down, links.kept = links.kept, links.kept + 1
    load_hidden = links.keep(hidden, hidden_v)

    def forward_sum():
        load_hidden.wait()
        store = None
        for q in range(4):
            load = pltpu.make_async_copy(
                down_all.at[:, lanes(q, narrow)], down_tile, links.local.at[k_down]
            )
            load.start()
            load.wait()
            if store is not None:
                store.wait()
            forward_tile[...] = times(hidden_v[...], down_tile[...]).astype(LOW)
            store = links.keep(forward_tile, forward_out.at[:, lanes(q, narrow)])
            yield 1
        store.wait()

    second_norm_back(
        count, partial, cot_all, middle, vectors, gate_partial, grad_middle, grad_all, sums, gate_out,
        ours, theirs, ups, downs, staging, cot, low, buffers, None, None, None, links, tokens, gate,
        [forward_sum()],
    )


def second_norm_back(
    count, grad_partial, cot_all, middle, vectors, gate_partial, grad_middle, grad_all, sums, gate_out,
    ours, theirs, ups, downs, staging, cot, low, buffers, send, recv, local, links=None,
    prepare_tokens=None, prepare_gate=None, others=(),
):
    place = Place(count)
    if links is None:
        links = Links(send, recv, local)
        greet(place, rows=True, line=True, cores=True)
    row, z, col = place.row, place.dp, place.col
    quarter, full = middle.shape
    narrow = full // 4
    tall = 4 * quarter
    half = gate_partial.shape[0] // 8
    sums[...] = jnp.zeros(sums.shape, WIDE)
    gain = vectors[3:4, :]
    load = links.keep(cot_all.at[strip(2 * z + col, quarter)], cot)

    def back(rows, grad):
        own = cot[rows].astype(WIDE)
        total = own + norm_rule(rows, grad, middle[rows], gain, sums, 0)
        sums[1:2, :] += jnp.sum(total, axis=0, keepdims=True)
        sums[2:3, :] += jnp.sum(own, axis=0, keepdims=True)
        grad_middle[rows] = total
        low[rows] = total.astype(LOW)

    def tokens():
        load.wait()
        yield from token_scatter(
            links, place, grad_partial, ours, theirs, (ups, downs, staging), back, prepare_tokens
        )

        def block(q):
            return grad_all.at[strip(4 * col + q, quarter)]

        mine = links.keep(low.at[:, lanes(row, narrow)], block(row))
        yield from exchange_rows(
            links, place, lambda q: low.at[:, lanes(q, narrow)], block
        )
        mine.wait()
        both = grad_all.at[strip(col, tall)]
        share = links.copy(both, both, col=place.other)
        share.start()
        yield 1
        share.wait_recv()
        share.wait_send()

    def keep_gate(h, rows, value):
        gate_out[h, rows] = value.astype(LOW)

    tokens_back = tokens()
    gate_back = scatter_rows(
        links,
        place,
        lambda q, h: gate_partial.at[strip(2 * q + h, half)],
        buffers,
        keep_gate,
        prepare_gate,
    )
    advance(tokens_back)
    advance(tokens_back)
    run([gate_back, tokens_back, *others])


def mixed_and_output_inside(
    count, grad_all, wout, mixed_all, normed, cot_all, grad_up, hidden, out_partial, middle, vectors, gate_own,
    mixed_out, layer_out, up_out, gate_out, output_out, down_out, mixed_buffers, ours, theirs, ups, downs,
    staging, low, up_buffers, gate_here, grad_v, wout_v, mixed_v, tile, up_v, hidden_v, mixed_partial,
    up_partial, output_v, down_v, send, recv, local,
):
    place = Place(count)
    links = Links(send, recv, local)
    loads = [
        links.keep(source, target)
        for source, target in (
            (grad_all, grad_v), (wout, wout_v), (grad_up, up_v), (mixed_all, mixed_v),
            (hidden, hidden_v),
        )
    ]
    greet(place, rows=True, line=True, cores=True)
    steps = mixed_partial.shape[0] // 4
    narrow = grad_v.shape[1]
    for load in loads[:2]:
        load.wait()

    def mixed(q):
        rows = strip(q, steps)
        mixed_partial[rows] = times_flipped(grad_v[rows, :], wout_v[...]).astype(LOW)

    k, links.kept = links.kept, links.kept + 1

    def fetch(source, q):
        load = pltpu.make_async_copy(source.at[:, lanes(q, narrow)], tile, links.local.at[k])
        load.start()
        load.wait()

    def up(q):
        fetch(normed, q)
        up_partial[strip(q, narrow)] = left_product(tile[...], up_v[...]).astype(LOW)

    def ready():
        for load in loads[2:]:
            load.wait()

    def others():
        output_v[...] = left_product(mixed_v[...], grad_v[...]).astype(LOW)
        stores = [links.keep(output_v, output_out)]

        def lap(q, carry):
            fetch(cot_all, q)
            down_v[:, lanes(q, narrow)] = left_product(hidden_v[...], tile[...]).astype(LOW)
            return carry

        lax.fori_loop(0, 4, lap, 0)
        stores.append(links.keep(down_v, down_out))
        yield 1
        for store in stores:
            store.wait()

    mixed_and_output(
        count, mixed_partial, out_partial, middle, vectors, up_partial, gate_own, mixed_out, layer_out,
        up_out, gate_out, mixed_buffers, ours, theirs, ups, downs, staging, low, up_buffers, gate_here, None,
        None, None, links, ready, mixed, up, others(),
    )


def mixed_and_output(
    count, mixed_partial, out_partial, middle, vectors, up_partial, gate_own, mixed_out, layer_out, up_out,
    gate_out, mixed_buffers, ours, theirs, ups, downs, staging, low, up_buffers, gate_here, send, recv,
    local, links=None, ready=None, prepare_mixed=None, prepare_up=None, others=None,
):
    place = Place(count)
    if links is None:
        links = Links(send, recv, local)
        greet(place, rows=True, line=True, cores=True)
    row = place.row
    quarter, full = middle.shape
    narrow = full // 4
    shift = vectors[2:3, :]
    half = mixed_partial.shape[0] // 8
    up_half = up_partial.shape[0] // 8
    kept = Relay(links, gate_own.at[place.dp], gate_here, gate_out.at[place.dp])

    def keep_mixed(h, rows, value):
        mixed_out[h, rows] = value

    def keep_up(h, rows, value):
        up_out[h, rows] = value.astype(LOW)

    def finish(rows, value):
        low[rows] = (middle[rows] + value + shift).astype(LOW)

    def tokens():
        yield from token_scatter(
            links, place, out_partial, ours, theirs, (ups, downs, staging), finish
        )
        mine = links.keep(low.at[:, lanes(row, narrow)], layer_out.at[row])
        yield from exchange_rows(
            links, place, lambda q: low.at[:, lanes(q, narrow)], lambda q: layer_out.at[q]
        )
        mine.wait()

    outs = tokens()
    mixes = scatter_rows(
        links,
        place,
        lambda q, h: mixed_partial.at[strip(2 * q + h, half)],
        mixed_buffers,
        keep_mixed,
        prepare_mixed,
    )
    sums_up = scatter_rows(
        links,
        place,
        lambda q, h: up_partial.at[strip(2 * q + h, up_half)],
        up_buffers,
        keep_up,
        prepare_up,
    )
    gates = exchange_line(links, place, lambda b: gate_own.at[b], lambda b: gate_out.at[b])
    advance(gates, outs, mixes, outs)
    kept.pass_on()
    if ready is not None:
        ready()
    advance(sums_up, mixes, outs)
    if others is not None:
        advance(others)
    advance(mixes)
    run([outs, sums_up, mixes, gates] + ([others] if others is not None else []))
    kept.wait()


def spread_gradients(
    count, blocks, output_partial, up_own, all_out, output_out, up_out, ups, downs, staging, own, send, recv, local,
):
    place = Place(count)
    links = Links(send, recv, local)
    greet(place, rows=True, line=True)
    row, z = place.row, place.dp
    mine = links.keep(blocks.at[row], all_out.at[row])
    kept = links.keep(up_own.at[z], up_out.at[z])
    load = links.keep(output_partial, own)

    output_half = ups.shape[2]

    def output_rows(i, rows):
        return pl.ds(pl.multiple_of(rows.start + i * output_half, 16), rows.size)

    def keep_output(i, rows, value):
        output_out[output_rows(i, rows)] = value

    def outputs():
        load.wait()
        yield from scatter_line_in_parts(
            links,
            place,
            lambda s: None,
            lambda b, i, rows: own[b, output_rows(i, rows)].astype(WIDE),
            ups,
            downs,
            staging,
            keep_output,
        )

    run(
        [
            exchange_rows(links, place, lambda q: blocks.at[q], lambda q: all_out.at[q]),
            outputs(),
            exchange_line(links, place, lambda b: up_own.at[b], lambda b: up_out.at[b]),
        ]
    )
    mine.wait()
    kept.wait()


def first_norm_back(
    count, grad_partial, x_own, grad_middle, vectors, proj_partial, down_partial, sums_in,
    channel_in, hidden_in, block_in, grad_out, proj_out, down_out, width_sums, channel_sums, block_out, hidden_sums,
    theirs, ours, added,
    row_buffer, x, result, sums, proj_own, proj_ups, proj_downs, proj_staging, proj_low, width_table,
    width_line, width_part, channel_table, channel_line, hidden_table, block_table, block_part, block_line, block_low,
    down_buffers, send, recv, local, links=None, prepare_tokens=None, prepare_proj=None,
):
    place = Place(count)
    if links is None:
        links = Links(send, recv, local)
        greet(place, rows=True, line=True, cores=True)
    row, z, col = place.row, place.dp, place.col
    quarter, full = grad_middle.shape
    narrow = full // 4
    gain = vectors[0:1, :]
    load_x = links.keep(x_own, x)
    if prepare_proj is None:
        load_proj = [links.keep(proj_partial.at[:, b], proj_own.at[b]) for b in range(count)]

    parts = halves(down_partial.shape[0])

    def keep_down(h, rows, value):
        down_out[pl.ds(pl.multiple_of(parts[h].start + rows.start, 16), rows.size)] = value

    down_sum = scatter_rows(
        links,
        place,
        lambda q, h: down_partial.at[parts[h], lanes(q, narrow)],
        down_buffers,
        keep_down,
    )

    def tokens():
        if prepare_tokens is not None:
            prepare_tokens(place.other)
        share = links.copy(grad_partial.at[place.other], theirs, col=place.other)
        share.start()
        if prepare_tokens is not None:
            prepare_tokens(col)
        load = links.keep(grad_partial.at[col], ours)
        yield 1
        share.wait_recv()
        load.wait()

        def add(rows):
            for q in range(4):
                total = ours[q, rows].astype(WIDE) + theirs[q, rows].astype(WIDE)
                added[q, rows] = total.astype(LOW)

        by_rows(quarter, add)
        load_x.wait()
        sums[0:3, :] = sums_in[0:3, :]
        sums[3:, :] = jnp.zeros((sums.shape[0] - 3, full), WIDE)
        half = quarter // 2

        def back(h, rows, grad):
            here = pl.ds(pl.multiple_of(rows.start + half * h, 16), rows.size)
            value = x[here].astype(WIDE)
            total = grad_middle[here] + norm_rule(rows, grad, value, gain, sums, 3)
            for q in range(4):
                result[q, here] = total[:, q * narrow : (q + 1) * narrow].astype(LOW)

        yield from scatter_rows(
            links,
            place,
            lambda q, h: added.at[q, pl.ds(half * h, half)],
            row_buffer,
            back,
        )
        share.wait_send()
        mine = links.keep(result.at[row], grad_out.at[row])
        for q in range(4):
            width_part[q] = sums[:, q * narrow : (q + 1) * narrow]
        own = links.keep(width_part.at[row], width_table.at[row])
        vectors_out = exchange_rows(
            links, place, lambda q: width_part.at[q], lambda q: width_table.at[q]
        )
        results_out = exchange_rows(
            links, place, lambda q: result.at[q], lambda q: grad_out.at[q]
        )
        advance(vectors_out, results_out)
        yield 1
        finish(vectors_out)
        own.wait()
        width_line[z] = width_table[0] + width_table[1] + width_table[2] + width_table[3]
        yield from exchange_line(
            links, place, lambda b: width_line.at[z], lambda b: width_line.at[b]
        )
        total = width_line[0]
        for b in range(1, count):
            total = total + width_line[b]
        width_sums[0] = total
        yield 1
        last = links.copy(width_sums.at[0], width_sums.at[1], col=place.other)
        last.start()
        yield 1
        last.wait_recv()
        last.wait_send()
        finish(results_out)
        mine.wait()

    def projections():
        if prepare_proj is None:
            for load in load_proj:
                load.wait()
        else:
            prepare_proj()

        def keep_proj(i, rows, value):
            proj_low[i, rows] = value.astype(LOW)

        yield from scatter_line_in_parts(
            links,
            place,
            lambda s: None,
            lambda b, i, rows: proj_own[b, i, rows].astype(WIDE),
            proj_ups,
            proj_downs,
            proj_staging,
            keep_proj,
        )
        mine = links.keep(proj_low.at[row], proj_out.at[row])
        yield from exchange_rows(
            links, place, lambda q: proj_low.at[q], lambda q: proj_out.at[q]
        )
        mine.wait()

    def hidden():
        own = links.keep(hidden_in, hidden_table.at[row])
        yield from exchange_rows(
            links, place, lambda q: hidden_in, lambda q: hidden_table.at[q]
        )
        own.wait()
        hidden_sums[...] = hidden_table[0] + hidden_table[1] + hidden_table[2] + hidden_table[3]

    def channels():
        own = links.keep(channel_in, channel_table.at[row])
        yield from exchange_rows(
            links, place, lambda q: channel_in, lambda q: channel_table.at[q]
        )
        own.wait()
        channel_line[z] = (
            channel_table[0] + channel_table[1] + channel_table[2] + channel_table[3]
        )
        yield from exchange_line(
            links, place, lambda b: channel_line.at[z], lambda b: channel_line.at[b]
        )
        total = channel_line[0]
        for b in range(1, count):
            total = total + channel_line[b]
        channel_sums[...] = total

    def blocks():
        own = links.keep(block_in.at[row], block_table.at[row])
        yield from exchange_rows(
            links, place, lambda q: block_in.at[q], lambda q: block_table.at[q]
        )
        own.wait()

        for b in range(count):
            block_part[b] = sum(block_table[q, b].astype(WIDE) for q in range(4)).astype(LOW)
        own = links.keep(block_part.at[z], block_line.at[z])
        yield from exchange_line(
            links, place, lambda b: block_part.at[b], lambda b: block_line.at[b]
        )
        own.wait()
        block_low[...] = sum(block_line[b].astype(WIDE) for b in range(count)).astype(LOW)
        own = links.keep(block_low, block_out.at[row])
        yield from exchange_rows(links, place, lambda q: block_low, lambda q: block_out.at[q])
        own.wait()

    proj_sum, token_sum = projections(), tokens()
    small = [channels(), hidden(), blocks()]
    advance(down_sum, proj_sum, token_sum, *small)
    advance(token_sum)
    run([proj_sum, token_sum, down_sum] + small)


def first_norm_back_inside(
    count, grad_proj, wxy, nf, x_own, grad_middle, vectors, down_partial, *refs
):
    rest, (grad_v, wxy_v, nf_v, partial, send, recv, local) = refs[:-7], refs[-7:]
    proj_own = rest[18]
    place = Place(count)
    links = Links(send, recv, local)
    loads = [
        links.keep(source, target)
        for source, target in ((grad_proj, grad_v), (nf, nf_v), (wxy, wxy_v))
    ]
    greet(place, rows=True, line=True, cores=True)
    quarter, full = grad_middle.shape
    narrow, tall = full // 4, 4 * quarter
    depth = proj_own.shape[2]

    def tokens(core):
        def lap(q, carry):
            total = times_flipped(
                grad_v[strip(core, tall), :], wxy_v[strip(q, narrow), :]
            ).astype(LOW)
            for r in range(4):
                partial[core, r, :, lanes(q, narrow)] = total[r * quarter : (r + 1) * quarter]
            return carry

        lax.fori_loop(0, 4, lap, 0)

    def proj():
        for load in loads:
            load.wait()

        def lap(q, carry):
            total = left_product(nf_v[:, lanes(q, narrow)], grad_v[...]).astype(LOW)
            for b in range(count):
                proj_own[b, q] = total[b * depth : (b + 1) * depth]
            return carry

        lax.fori_loop(0, 4, lap, 0)

    first_norm_back(
        count, partial, x_own, grad_middle, vectors, None, down_partial, *rest, None, None, None, links,
        tokens, proj,
    )


def gelu(v):
    return 0.5 * v * (1.0 + jnp.tanh(ROOT * (v + CUBE * (v * v * v))))


def gelu_slope(v):
    t = jnp.tanh(ROOT * (v + CUBE * (v * v * v)))
    return 0.5 * (1.0 + t) + 0.5 * v * (1.0 - t * t) * (ROOT * (1.0 + 3.0 * CUBE * (v * v)))


def block_of(blocks, h):
    width = blocks.shape[-1]
    return blocks[h].reshape(width, width)


def forward(
    count, taps, x, cot, wxy, wout, wgate, wup, wdown, blk, cvec, wvec, spots,
    nf_out, x_out, cot_all, wxy_out, wout_out, gate_all, up_own, down_all, blocks_out, vectors_out,
    width_out, branch_out, gelu_out, side_out, conv_out, in_out, dec_out, state_out, entering_out,
    mixed_out, middle_out, normed_out,
    x_all, nf, wxy_all, wout_all, blocks, cvec_all, wvec_all, vectors, width, stage, arrived, branch,
    gelu_in, side, conv, in_gate, dec_gate, state, running, local_state, ends, table, entering, mixed,
    mixed_all, partial, theirs, here, wide, middle, normed, gate_here, up_here, down_here, cot_here,
    send, recv, local,
):
    place = Place(count)
    links = Links(send, recv, local)
    row, z, col = place.row, place.dp, place.col
    greet(place, rows=True, line=True, cores=True)
    tall, narrow = x.shape
    full = 4 * narrow
    half, quarter = tall // 2, tall // 4
    depth, part = wxy.shape[1], wxy.shape[2] // 2
    tokens, steps = 2 * tall, tall // 2
    heads, block = blocks.shape[0] // 2, blocks.shape[-1]
    share = blocks.shape[3]
    kept = []

    def keep(src, dst):
        kept.append(links.keep(src, dst))
        return kept[-1]

    def projections():
        def at(q, b):
            return wxy_all.at[q, strip(b, depth, 8)]

        mine = links.keep(wxy.at[row], at(row, z))
        yield from exchange_rows(links, place, lambda q: wxy.at[q], lambda q: at(q, z))
        mine.wait()

        def piece(b):
            return wxy_all.at[:, strip(b, depth, 8)]

        yield from gather_line(links, place, piece(z), piece)

    def inputs():
        def at(q, core):
            return x_all.at[strip(core, tall), lanes(q, narrow)]

        mine = links.keep(x, at(row, col))
        shared = [links.copy(x, at(row, col), col=place.other)]
        shared[0].start()
        yield from gather_rows(
            links,
            place,
            lambda h: x.at[pl.ds(half * h, half)],
            lambda q, h: x_all.at[strip(2 * col + h, half), lanes(q, narrow)],
        )
        for k in range(1, 4):
            q = place.near[k]
            shared.append(links.copy(at(q, col), at(q, col), col=place.other))
            shared[-1].start()
        yield 1
        mine.wait()
        for copy in shared:
            copy.wait_recv()
        for copy in shared:
            copy.wait_send()

    def channel_vectors():
        keep(cvec, cvec_all.at[z])
        yield from exchange_line(links, place, lambda b: cvec, lambda b: cvec_all.at[b])

    def width_vectors():
        mine = links.keep(wvec, wvec_all.at[row, z])
        yield from exchange_line(links, place, lambda b: wvec, lambda b: wvec_all.at[row, b])
        mine.wait()
        yield from exchange_rows(
            links, place, lambda q: wvec_all.at[row], lambda q: wvec_all.at[q]
        )

    def gate_blocks():
        split = blocks.shape[2] > 1
        own = row if split else 0
        mine = links.keep(blk, blocks.at[:, z, own])
        yield from exchange_line(links, place, lambda b: blk, lambda b: blocks.at[:, b, own])
        mine.wait()
        middle = count // 2
        if split:

            def at(q, h):
                return blocks.at[:, pl.ds(middle * h, middle), q]

            yield from gather_rows(links, place, lambda h: at(row, h), at)

    def hidden_rows():
        parts = halves(wdown.shape[0])
        mine = Relay(links, wdown, down_here, down_all.at[:, lanes(row, narrow)])
        kept.append(mine)
        yield from gather_rows(
            links,
            place,
            lambda h: wdown.at[parts[h]],
            lambda q, h: down_all.at[parts[h], lanes(q, narrow)],
        )

    def cotangent_rows():
        def spot(q):
            return cot_all.at[strip(2 * z + col, quarter), lanes(q, narrow)]

        mine = Relay(links, cot.at[strip(row, quarter)], cot_here, spot(row))
        yield from exchange_rows(links, place, lambda q: cot.at[strip(q, quarter)], spot)
        mine.wait()

    def hidden_columns(matrix, buffer, own):
        mine = Relay(links, matrix.at[z], buffer, own.at[z])
        yield from exchange_line(links, place, lambda b: matrix.at[b], lambda b: own.at[b])
        mine.wait()

    def all_hidden_columns(matrix, buffer, whole):
        yield from hidden_columns(matrix, buffer, whole.at[row])
        middle = count // 2

        def at(q, h):
            return whole.at[q, pl.ds(middle * h, middle)]

        yield from gather_rows(links, place, lambda h: at(row, h), at)

    def cot_block(b):
        return cot_all.at[strip(2 * b + col, quarter)]

    def output_rows():
        at = wout.shape[0]
        mine = links.keep(wout, wout_all.at[strip(z, at)])
        yield from gather_line(links, place, wout, lambda b: wout_all.at[strip(b, at)])
        mine.wait()

    weights, rows_in = projections(), inputs()
    vectors_in, widths_in, blocks_in = channel_vectors(), width_vectors(), gate_blocks()
    cot_in, output_in, down_in = cotangent_rows(), output_rows(), hidden_rows()
    gate_in = all_hidden_columns(wgate, gate_here, gate_all)
    cots = LineGather(links, place, cot_block(z), cot_block)
    up_in = hidden_columns(wup, up_here, up_own)
    advance(weights, rows_in, widths_in, vectors_in, blocks_in, cot_in)
    advance(weights, widths_in, vectors_in, blocks_in)
    finish(widths_in, vectors_in)
    for copy in kept:
        copy.wait()
    kept.clear()

    for b in range(count):
        size = vectors.shape[1] // count
        vectors[:, b * size : (b + 1) * size] = cvec_all[b, :, :size]
        for q in range(4):
            at = q * narrow + b * depth
            width[:, at : at + depth] = wvec_all[q, b, :, :depth]
    keep(vectors, vectors_out)
    keep(width, width_out)
    advance(rows_in)
    advance(weights)
    finish(rows_in)
    advance(down_in)
    keep(x_all.at[strip(4 * col + row, quarter)], x_out)

    nf[0:16, :] = jnp.zeros((16, full), LOW)

    def first_norm(rows):
        value = x_all[rows].astype(WIDE)
        mean = jnp.sum(value * value, axis=1, keepdims=True) / full
        value = value * lax.rsqrt(mean + epsilon) * (1.0 + width[0:1, :])
        nf[pl.ds(pl.multiple_of(rows.start + 16, 16), rows.size)] = value.astype(LOW)

    by_rows(tokens, first_norm)
    keep(nf.at[pl.ds(16, tokens)], nf_out)
    advance(weights, blocks_in, cot_in)
    finish(blocks_in)
    keep(blocks, blocks_out)
    finish(weights, cot_in)
    keep(wxy_all, wxy_out)

    advance(output_in)
    advance(down_in)
    out = []
    for k in (3, 2, 1, 0):
        q = place.near[k]

        def product(k=k, q=q):
            stage[k] = jnp.dot(
                nf[pl.ds(pl.multiple_of(q * steps, 16), steps + 16), :],
                wxy_all[...].astype(LOW).reshape(full, 2 * part),
                preferred_element_type=WIDE,
            )

        product()
        source = stage.at[k, pl.ds(8, steps + 8)]
        if k:
            out.append(links.copy(source, arrived.at[row], row=q))
            out[-1].start()
        else:
            mine = links.keep(source, arrived.at[row])
    advance(output_in, gate_in)
    mine.wait()
    for copy in out:
        copy.wait_recv()
    finish(down_in)
    for copy in out:
        copy.wait_send()
    cots.start()

    spot = spots[...]
    starting = spot == 0
    for q in range(4):
        at = slice(q * part, (q + 1) * part)
        branch[:, at] = arrived[q, :, :part]
        gelu_in[:, at] = arrived[q, 8:, part:] + vectors[taps + 2 : taps + 3, at]
    keep(branch, branch_out)
    keep(gelu_in, gelu_out)
    ends[...] = jnp.zeros(ends.shape, WIDE)
    entering[...] = jnp.zeros(ends.shape, WIDE)

    def one_head(h, at):
        def vector(i):
            return vectors[i : i + 1, at]

        conv_here = vector(taps) + vector(0) * (branch[8:, at] + vector(taps + 1))
        for k in range(1, taps):
            earlier = branch[8 - k : 8 - k + steps, at] + vector(taps + 1)
            conv_here = conv_here + vector(k) * jnp.where(spot >= k, earlier, 0.0)
        conv[:, at] = conv_here
        low = conv_here.astype(LOW)
        input_gate = jax.nn.sigmoid(
            jnp.dot(low, block_of(blocks, h), preferred_element_type=WIDE) + vector(taps + 3)
        )
        decay_gate = jax.nn.sigmoid(
            jnp.dot(low, block_of(blocks, heads + h), preferred_element_type=WIDE)
            + vector(taps + 4)
        )
        in_gate[:, at] = input_gate
        dec_gate[:, at] = decay_gate
        log_decay = vector(taps + 5) * decay_gate
        decay = jnp.where(starting, 0.0, jnp.exp(log_decay))
        multiplier = jnp.where(starting, 1.0, jnp.sqrt(minus_expm1(2.0 * log_decay)))
        reach, value = scan_rows(decay, multiplier * input_gate * conv_here, False)
        running[:, at] = reach
        local_state[:, at] = value
        ends[0:1, at] = reach[steps - 1 :, :]
        ends[1:2, at] = value[steps - 1 :, :]
        side[:, at] = gelu(gelu_in[:, at])

    each_head(heads, block, one_head)
    for scratch, output in (
        (conv, conv_out), (in_gate, in_out), (dec_gate, dec_out), (side, side_out),
    ):
        keep(scratch, output)
    own = links.keep(ends, table.at[row])
    advance(output_in)
    own.wait()
    entering[0:1, :] = carry_over(links, place, ends, table, False)

    def mix(h, at):
        value = local_state[:, at] + running[:, at] * entering[0:1, at]
        state[:, at] = value
        mixed[:, at] = (value * side[:, at]).astype(LOW)

    each_head(heads, block, mix)
    mine = links.keep(mixed, mixed_all.at[strip(row, steps)])
    mixes = gather_rows(
        links,
        place,
        lambda h: mixed.at[pl.ds(steps // 2 * h, steps // 2)],
        lambda q, h: mixed_all.at[strip(2 * q + h, steps // 2)],
    )
    advance(mixes)
    keep(state, state_out)
    keep(entering, entering_out)
    finish(output_in)
    keep(wout_all, wout_out)
    advance(mixes, up_in)
    finish(mixes)
    mine.wait()
    cots.step(1)
    advance(gate_in)
    keep(mixed_all, mixed_out)

    def product_rows(first):
        def body(i, carry):
            rows = pl.ds(pl.multiple_of(first * tall + i * steps, 16), steps)
            partial[rows] = jnp.dot(mixed_all[rows], wout_all[...], preferred_element_type=WIDE)
            return carry

        lax.fori_loop(0, tall // steps, body, 0)

    product_rows(place.other)
    swap = links.copy(partial.at[strip(place.other, tall)], theirs, col=place.other)
    swap.start()
    product_rows(col)
    swap.wait_recv()

    def add(rows):
        at = pl.ds(pl.multiple_of(col * tall + rows.start, 16), rows.size)
        here[rows] = partial[at] + theirs[rows] + x_all[at, lanes(row, narrow)].astype(WIDE)

    by_rows(tall, add)

    def quarter_of(q):
        return here.at[strip(q, quarter)]

    mine = links.keep(quarter_of(row), wide.at[:, lanes(row, narrow)])
    middles = exchange_rows(links, place, quarter_of, lambda q: wide.at[:, lanes(q, narrow)])
    advance(middles)
    mine.wait()
    finish(middles)
    swap.wait_send()

    def second_norm(rows):
        value = wide[rows] + width[1:2, :]
        middle[rows] = value
        mean = jnp.sum(value * value, axis=1, keepdims=True) / full
        normed[rows] = (value * lax.rsqrt(mean + epsilon) * (1.0 + width[3:4, :])).astype(LOW)

    by_rows(quarter, second_norm)
    keep(middle, middle_out)
    keep(normed, normed_out)
    advance(gate_in)
    for step in range(2, count):
        cots.step(step)
    finish(gate_in, up_in)
    for step in range(count):
        cots.ready(step)
    cots.close()
    for copy in kept:
        copy.wait()


def feed_forward(
    count, normed, cot_all, gate_all, up_own, wdown, biases, normed_all, up_all, hidden_out, gate_out,
    up_out, sums, gate_w, up_w, down_w, piece, gate_v, up_v, grad_v, hidden, grad_gate, grad_up, normed_here,
    send, recv, local,
):
    place = Place(count)
    links = Links(send, recv, local)
    row, z, col = place.row, place.dp, place.col
    quarter, full = normed.shape
    narrow, pair = full // 4, 2 * quarter
    units = wdown.shape[0]
    middle = count // 2
    load = links.keep(wdown, down_w)
    kept = [links.keep(gate_all, gate_w), links.keep(up_own, up_w.at[row])]
    greet(place, rows=True, line=True, cores=True)

    def tokens(own, buffer, whole):
        def at(b):
            return whole.at[strip(2 * b + col, quarter)]

        relay = Relay(links, own, buffer, at(z))
        return LineGather(links, place, own, at), relay

    def columns_of(own, whole):
        yield from gather_rows(
            links,
            place,
            lambda h: own.at[pl.ds(middle * h, middle)],
            lambda q, h: whole.at[q, pl.ds(middle * h, middle)],
        )

    def neighbours(step, body):
        if step == 0:
            body(z)
            return

        def lap(i, carry):
            b = z - step + 2 * step * i
            pl.when((b >= 0) & (b < count))(lambda: body(place.turn(b)))
            return carry

        lax.fori_loop(0, 2, lap, 0)

    def with_piece(source, body):
        k, links.kept = links.kept, links.kept + 1

        def inner(b):
            load = pltpu.make_async_copy(source.at[strip(b, pair)], piece, links.local.at[k])
            load.start()
            load.wait()
            body(strip(b, pair))

        return inner

    def inward(whole, i, values):
        def body(rows):
            weight = whole[...].astype(LOW).reshape(full, units)
            values[rows] = (
                jnp.dot(piece[...], weight, preferred_element_type=WIDE) + biases[i : i + 1, :]
            )

        return body

    def backward(rows):
        grad_v[rows] = lax.dot_general(
            piece[...], down_w[...], (((1,), (1,)), ((), ())), preferred_element_type=WIDE
        )

    def outward(rows):
        def body(inner):
            at = pl.ds(pl.multiple_of(rows.start + inner.start, 16), inner.size)
            gate, up, grad = gate_v[at], up_v[at], grad_v[at]
            t = jnp.tanh(ROOT * (gate + CUBE * (gate * gate * gate)))
            side = 0.5 * gate * (1.0 + t)
            slope = 0.5 * (1.0 + t) + 0.5 * gate * (1.0 - t * t) * (
                ROOT * (1.0 + 3.0 * CUBE * (gate * gate))
            )
            hidden[at] = (side * up).astype(LOW)
            gate, up = grad * up * slope, grad * side
            grad_gate[at] = gate.astype(LOW)
            grad_up[at] = up.astype(LOW)
            sums[0:1, :] += jnp.sum(gate, axis=0, keepdims=True)
            sums[1:2, :] += jnp.sum(up, axis=0, keepdims=True)

        by_rows(pair, body)

    ups = columns_of(up_own, up_w)
    norms, norm_relay = tokens(normed, normed_here, normed_all)
    norms.start()
    advance(ups)
    norm_relay.wait()
    sums[...] = jnp.zeros(sums.shape, WIDE)
    load.wait()
    back = with_piece(cot_all, backward)
    into = with_piece(normed_all, inward(gate_w, 0, gate_v))

    def backs(first, last):
        def lap(b, carry):
            back(b)
            return carry

        lax.fori_loop(first, last, lap, 0)

    backs(0, middle)
    norms.step(1)
    backs(middle, count)
    for copy in kept:
        copy.wait()
    kept.clear()
    for step in range(count):
        if step > 1:
            norms.step(step)
        if step == 2:
            advance(ups)
        norms.ready(step)
        neighbours(step, into)
    finish(ups)
    kept.append(links.keep(up_w, up_all))
    into_up = with_piece(normed_all, inward(up_w, 1, up_v))

    def last(b, carry):
        into_up(b)
        outward(strip(b, pair))
        return carry

    lax.fori_loop(0, count, last, 0)
    norms.close()
    kept.append(links.keep(hidden, hidden_out))
    kept.append(links.keep(grad_gate, gate_out))
    kept.append(links.keep(grad_up, up_out))
    for copy in kept:
        copy.wait()


def side_by_side(blocks):
    return jnp.concatenate([blocks[i] for i in range(blocks.shape[0])], axis=1)


def columns(matrix, parts):
    width = matrix.shape[1] // parts
    return jnp.stack([matrix[:, i * width : (i + 1) * width] for i in range(parts)])


def padded_rows(rows, height, width):
    return jnp.pad(rows, ((0, height - rows.shape[0]), (0, width - rows.shape[1])))


def rounded(values):
    return lax.reduce_precision(values, 8, 7)


def round_up(size, step):
    return -(-size // step) * step


def shards(
    inputs,
    positions,
    branch_matrix,
    gelu_matrix,
    output_matrix,
    gate_matrix,
    up_matrix,
    down_matrix,
    input_blocks,
    decay_blocks,
    conv_taps,
    conv_bias,
    branch_bias,
    gelu_bias,
    input_bias,
    decay_bias,
    decay_param,
    output_bias,
    gate_bias,
    up_bias,
    down_bias,
    norm_first,
    norm_second,
    cotangent,
):
    count, rows_count, cores = lax.axis_size("dp"), lax.axis_size("row"), lax.axis_size("col")
    place_dp, place_row = lax.axis_index("dp"), lax.axis_index("row")
    tall, narrow = inputs.shape
    quarter, full, tokens = tall // rows_count, narrow * rows_count, tall * cores
    depth, width = branch_matrix.shape
    part = width // rows_count
    hidden_part = down_matrix.shape[0]
    heads, block_part, block = input_blocks.shape
    taps = conv_taps.shape[0]
    steps = positions.shape[0]
    splits = rows_count if block_part % (16 * rows_count) == 0 else 1
    share = block_part // splits
    back_share = block_part // rows_count
    remote, local = 64 + 24 * count, 40 + 6 * count

    wxy = jnp.concatenate(
        (columns(branch_matrix.astype(LOW), rows_count), columns(gelu_matrix.astype(LOW), rows_count)),
        axis=2,
    )
    if depth % 16:
        wxy = wxy.astype(WIDE)
    blocks_low = jnp.concatenate((input_blocks, decay_blocks), axis=0).astype(LOW)
    blk = lax.dynamic_slice_in_dim(
        blocks_low, place_row * share if splits > 1 else 0, share, 1
    )
    channel_rows = jnp.concatenate(
        (
            conv_taps,
            jnp.stack((conv_bias, branch_bias, gelu_bias, input_bias, decay_bias)),
        ),
        axis=0,
    )
    decay_raw = rounded(decay_param)
    channel_rows = jnp.concatenate(
        (rounded(channel_rows), -8.0 * jax.nn.softplus(decay_raw)[None, :]), axis=0
    )
    channel_size = channel_rows.shape[1]
    cvec = padded_rows(
        channel_rows,
        round_up(taps + 6, 8),
        round_up(channel_size, 128),
    )
    wvec = padded_rows(
        rounded(jnp.stack((norm_first, output_bias, down_bias, norm_second))),
        8,
        round_up(depth, 128),
    )
    spots = positions[:, None]
    heads_all = 2 * heads
    whole_tokens = ((tokens, full), LOW, False)
    wide_tokens = ((steps, width), WIDE, False)
    nf_shape = pltpu.VMEM((16 + tokens, full), LOW)
    wxy_kind = wxy.dtype
    tokens_scratch = pltpu.VMEM((steps, width), WIDE)
    eight_rows = pltpu.VMEM((8, width), WIDE)
    table_rows = pltpu.VMEM((rows_count, 8, width), WIDE)
    blocks_shape = (heads_all, count, splits, share, block)
    hidden_shape = (rows_count, count, depth, hidden_part)
    here_scratch = pltpu.VMEM((tall, narrow), WIDE)
    (
        normed_first, x_own, cot_all, wxy_all, wout_all, gate_all, up_own, down_all, blocks, vectors,
        width_all, branch, gelu_in, side, conv, input_gate, decay_gate, state, entering, mixed_all,
        middle, normed_own,
    ) = call(
        functools.partial(forward, count, taps),
        "forward",
        1,
        [
            (inputs, False),
            (cotangent, False),
            (wxy, False),
            (output_matrix.astype(LOW), False),
            (columns(gate_matrix.astype(LOW), count).astype(wxy_kind), False),
            (columns(up_matrix.astype(LOW), count).astype(wxy_kind), False),
            (down_matrix.astype(LOW), False),
            (blk, False),
            (cvec, False),
            (wvec, False),
            (spots, True),
        ],
        [
            whole_tokens,
            ((quarter, full), LOW, False),
            ((cores * count * quarter, full), LOW, False),
            ((rows_count, count * depth, 2 * part), wxy_kind, False),
            ((width, narrow), LOW, False),
            (hidden_shape, wxy_kind, False),
            (hidden_shape[1:], wxy_kind, False),
            ((hidden_part, full), LOW, False),
            (blocks_shape, LOW, False),
            ((cvec.shape[0], width), WIDE, False),
            ((8, full), WIDE, False),
            ((steps + 8, width), WIDE, False),
            wide_tokens,
            wide_tokens,
            wide_tokens,
            wide_tokens,
            wide_tokens,
            wide_tokens,
            ((8, width), WIDE, False),
            ((tokens, width), LOW, False),
            ((quarter, full), WIDE, False),
            ((quarter, full), LOW, False),
        ],
        [
            pltpu.VMEM((tokens, full), LOW),
            nf_shape,
            pltpu.VMEM((rows_count, count * depth, 2 * part), wxy_kind),
            pltpu.VMEM((width, narrow), LOW),
            pltpu.VMEM(blocks_shape, LOW),
            pltpu.VMEM((count,) + cvec.shape, WIDE),
            pltpu.VMEM((rows_count, count) + wvec.shape, WIDE),
            pltpu.VMEM((cvec.shape[0], width), WIDE),
            pltpu.VMEM((8, full), WIDE),
            pltpu.VMEM((rows_count, steps + 16, 2 * part), WIDE),
            pltpu.VMEM((rows_count, steps + 8, 2 * part), WIDE),
            pltpu.VMEM((steps + 8, width), WIDE),
            tokens_scratch,
            tokens_scratch,
            tokens_scratch,
            tokens_scratch,
            tokens_scratch,
            tokens_scratch,
            tokens_scratch,
            tokens_scratch,
            eight_rows,
            table_rows,
            eight_rows,
            pltpu.VMEM((steps, width), LOW),
            pltpu.VMEM((tokens, width), LOW),
            pltpu.VMEM((tokens, narrow), WIDE),
            here_scratch,
            here_scratch,
            pltpu.VMEM((quarter, full), WIDE),
            pltpu.VMEM((quarter, full), WIDE),
            pltpu.VMEM((quarter, full), LOW),
            pltpu.VMEM((depth, hidden_part), wxy_kind),
            pltpu.VMEM((depth, hidden_part), wxy_kind),
            pltpu.VMEM((hidden_part, narrow), LOW),
            pltpu.VMEM((quarter, narrow), LOW),
        ],
        remote,
        local,
    )
    wxy_all = wxy_all.reshape(full, 2 * part).astype(LOW)
    blocks = blocks.reshape(heads_all, block, block)
    gelu_pull = jax.vjp(jax.nn.gelu, gelu_in)[1]

    hidden_tokens = cores * count * quarter
    units_rows = ((hidden_tokens, hidden_part), LOW, False)
    biases = padded_rows(rounded(jnp.stack((gate_bias, up_bias))), 8, hidden_part)
    weight_scratch = pltpu.VMEM(hidden_shape, wxy_kind)
    units_wide = pltpu.VMEM((hidden_tokens, hidden_part), WIDE)
    units_low = pltpu.VMEM((hidden_tokens, hidden_part), LOW)
    (
        normed_second, up_all, hidden, grad_gate_low, grad_up_low, hidden_part_sums,
    ) = call(
        functools.partial(feed_forward, count),
        "feed_forward",
        2,
        [
            (normed_own, False),
            (cot_all, False),
            (gate_all, False),
            (up_own, False),
            (down_all, False),
            (biases, True),
        ],
        [
            ((hidden_tokens, full), LOW, False),
            (hidden_shape, wxy_kind, False),
            units_rows,
            units_rows,
            units_rows,
            ((8, hidden_part), WIDE, True),
        ],
        [
            weight_scratch,
            weight_scratch,
            pltpu.VMEM((hidden_part, full), LOW),
            pltpu.VMEM((cores * quarter, full), LOW),
            units_wide,
            units_wide,
            units_wide,
            units_low,
            units_low,
            units_low,
            pltpu.VMEM((quarter, full), LOW),
        ],
        remote,
        local,
    )
    by_device = (count, cores, quarter, full)
    token_scratch = [
        pltpu.VMEM((count, quarter, full), LOW),
        pltpu.VMEM((count, quarter, full), LOW),
        *line_buffers(count, 2, quarter // 2, full),
    ]
    token_low = pltpu.VMEM((quarter, full), LOW)
    back_outs = [
        ((quarter, full), WIDE, True),
        ((tokens, narrow), LOW, False),
        ((8, full), WIDE, True),
        ((2, narrow // 2, hidden_part), LOW, True),
    ]
    back_scratch = token_scratch + [token_low, token_low, row_buffers(narrow, hidden_part)]
    inside = count <= 4
    if inside:
        grad_middle, grad_middle_all, width_sums, gate_own, forward_partial = call(
            functools.partial(second_norm_back_inside, count),
            "second_norm_back",
            5,
            [
                (grad_gate_low, False),
                (grad_up_low, False),
                (gate_all, False),
                (up_all, False),
                (normed_second, False),
                (hidden, False),
                (down_all, False),
                (cot_all, False),
                (middle, True),
                (width_all, True),
            ],
            back_outs + [((hidden_tokens, full), LOW, False)],
            back_scratch
            + [
                units_low,
                units_low,
                weight_scratch,
                weight_scratch,
                pltpu.VMEM((hidden_tokens, narrow), LOW),
                pltpu.VMEM(by_device, LOW),
                pltpu.VMEM((full, hidden_part), LOW),
                units_low,
                pltpu.VMEM((hidden_part, narrow), LOW),
                pltpu.VMEM((hidden_tokens, narrow), LOW),
            ],
            remote,
            local,
        )
    else:
        forward_partial = times(hidden, down_all).astype(LOW)
        gate_all = gate_all.reshape(full, hidden_part).astype(LOW)
        up_all = up_all.reshape(full, hidden_part).astype(LOW)
        grad_normed_second = (
            (times_flipped(grad_gate_low, gate_all) + times_flipped(grad_up_low, up_all))
            .astype(LOW)
            .reshape(by_device)
        )
        grad_middle, grad_middle_all, width_sums, gate_own = call(
            functools.partial(second_norm_back, count),
            "second_norm_back",
            5,
            [
                (grad_normed_second, False),
                (cot_all, False),
                (middle, True),
                (width_all, True),
                (left_product(normed_second, grad_gate_low).astype(LOW), False),
            ],
            back_outs,
            back_scratch,
            remote,
            local,
        )
    forward_partial = forward_partial.reshape(by_device)

    mixed_outs = [
        ((2, steps // 2, width), WIDE, True),
        ((rows_count, quarter, narrow), LOW, False),
        ((2, narrow // 2, hidden_part), LOW, True),
        ((count, depth, hidden_part), LOW, False),
    ]
    mixed_scratch = (
        [row_buffers(steps, width)]
        + token_scratch
        + [token_low, row_buffers(narrow, hidden_part), pltpu.VMEM((depth, hidden_part), LOW)]
    )
    gate_own = gate_own.reshape(count, depth, hidden_part)
    if inside:
        grad_mixed, layer_out, up_own, gate_blocks, output_partial, down_partial = call(
            functools.partial(mixed_and_output_inside, count),
            "mixed_and_output",
            6,
            [
                (grad_middle_all, False),
                (wout_all, False),
                (mixed_all, False),
                (normed_second, False),
                (cot_all, False),
                (grad_up_low, False),
                (hidden, False),
                (forward_partial, False),
                (middle, True),
                (width_all, True),
                (gate_own, False),
            ],
            mixed_outs + [((width, narrow), LOW, False), ((hidden_part, full), LOW, False)],
            mixed_scratch
            + [
                pltpu.VMEM((tokens, narrow), LOW),
                pltpu.VMEM((width, narrow), LOW),
                pltpu.VMEM((tokens, width), LOW),
                pltpu.VMEM((hidden_tokens, narrow), LOW),
                units_low,
                units_low,
                pltpu.VMEM((tokens, width), LOW),
                pltpu.VMEM((full, hidden_part), LOW),
                pltpu.VMEM((width, narrow), LOW),
                pltpu.VMEM((hidden_part, full), LOW),
            ],
            remote,
            local,
        )
    else:
        down_partial = left_product(hidden, cot_all).astype(LOW)
        output_partial = left_product(mixed_all, grad_middle_all).astype(LOW)
        grad_mixed, layer_out, up_own, gate_blocks = call(
            functools.partial(mixed_and_output, count),
            "mixed_and_output",
            6,
            [
                (times_flipped(grad_middle_all, wout_all).astype(LOW), False),
                (forward_partial, False),
                (middle, True),
                (width_all, True),
                (left_product(normed_second, grad_up_low).astype(LOW), False),
                (gate_own, False),
            ],
            mixed_outs,
            mixed_scratch,
            remote,
            local,
        )
    up_own = up_own.reshape(count, depth, hidden_part)
    grad_mixed = grad_mixed.reshape(steps, width)

    sums_rows = round_up(taps + 6, 8)
    output_parts = 2 if output_matrix.shape[0] % 32 == 0 else 1
    if inside:
        channel_part, block_sums, grad_projected, output_grad, up_blocks = call(
            functools.partial(recurrence_back_inside, count, taps),
            "recurrence_backward",
            7,
            [
                (branch, False),
                (side, False),
                (gelu_in, False),
                (spots, True),
                (vectors, True),
                (blocks, False),
                (conv, False),
                (input_gate, False),
                (decay_gate, False),
                (state, False),
                (entering, True),
                (grad_mixed, False),
            ]
            + [
                (output_partial.reshape((count,) + output_matrix.shape), False),
                (up_own, False),
            ],
            [
                ((sums_rows, width), WIDE, True),
                ((2 * heads, block, block), WIDE, True),
                ((rows_count, steps, 2 * part), LOW, False),
                (output_matrix.shape, WIDE, True),
                ((count, depth, hidden_part), LOW, False),
            ],
            [
                pltpu.VMEM((steps, width), LOW),
                pltpu.VMEM((steps, width), LOW),
                pltpu.VMEM((rows_count, steps, 2 * part), LOW),
                tokens_scratch,
                tokens_scratch,
                tokens_scratch,
                eight_rows,
                table_rows,
                pltpu.VMEM((2, 8, width), WIDE),
                eight_rows,
                pltpu.VMEM((steps + 8, block), WIDE),
                pltpu.VMEM((steps + 8, block), WIDE),
                *line_buffers(count, output_parts, output_matrix.shape[0] // output_parts, narrow),
                pltpu.VMEM((count,) + output_matrix.shape, LOW),
                pltpu.VMEM((depth, hidden_part), LOW),
                pltpu.VMEM((steps + 8, width), WIDE),
                tokens_scratch,
                tokens_scratch,
                pltpu.VMEM((2 * heads, block, block), LOW),
                tokens_scratch,
                tokens_scratch,
                tokens_scratch,
                tokens_scratch,
                tokens_scratch,
            ],
            remote,
            local,
        )
        grad_projected = grad_projected.reshape(tokens, 2 * part)
    else:
        grad_gelu = gelu_pull(grad_mixed * state)[0]
        grad_branch_low, channel_part, block_sums = call(
            functools.partial(recurrence_backward, count, taps),
            "recurrence_backward",
            7,
            [
                (array, True)
                for array in (
                    branch,
                    side,
                    spots,
                    vectors,
                    blocks,
                    conv,
                    input_gate,
                    decay_gate,
                    state,
                    entering,
                    grad_mixed,
                )
            ],
            [
                ((steps, width), LOW, True),
                ((round_up(taps + 6, 8), width), WIDE, True),
                ((2 * heads, block, block), WIDE, True),
            ],
            [
                tokens_scratch,
                tokens_scratch,
                tokens_scratch,
                eight_rows,
                table_rows,
                pltpu.VMEM((2, 8, width), WIDE),
                eight_rows,
                pltpu.VMEM((steps + 8, block), WIDE),
                pltpu.VMEM((steps + 8, block), WIDE),
            ],
            remote,
            local,
        )
        grad_gelu_low = grad_gelu.astype(LOW)
        projected_grads = jnp.concatenate(
            (columns(grad_branch_low, rows_count), columns(grad_gelu_low, rows_count)), axis=2
        )
        grad_projected, output_grad, up_blocks = call(
            functools.partial(spread_gradients, count),
            "spread_gradients",
            8,
            [
                (projected_grads, False),
                (output_partial.reshape((count,) + output_matrix.shape), False),
                (up_own, False),
            ],
            [
                ((rows_count, steps, 2 * part), LOW, False),
                (output_matrix.shape, WIDE, True),
                ((count, depth, hidden_part), LOW, False),
            ],
            [
                *line_buffers(count, output_parts, output_matrix.shape[0] // output_parts, narrow),
                pltpu.VMEM((count,) + output_matrix.shape, LOW),
            ],
            remote,
            local,
        )
        grad_projected = grad_projected.reshape(tokens, 2 * part)
        channel_part = channel_part.at[taps + 5].set(jnp.sum(grad_gelu, axis=0))
    hidden_part_sums = padded_rows(hidden_part_sums, 8, round_up(hidden_part, 128))
    block_in = (
        block_sums.astype(LOW)
        .reshape(2 * heads, count, rows_count, back_share, block)
        .transpose(2, 1, 0, 3, 4)
        .reshape(rows_count, count, 2 * heads * back_share, block)
    )
    channel_shape, sums_shape = channel_part.shape, hidden_part_sums.shape
    block_rows = 2 * heads * back_share
    first_outs = [
        ((rows_count, quarter, narrow), LOW, False),
        ((rows_count, depth, 2 * part), LOW, False),
        ((hidden_part, narrow), WIDE, True),
        ((2, 8, narrow), WIDE, True),
        (channel_shape, WIDE, True),
        ((rows_count, block_rows, block), LOW, False),
        (sums_shape, WIDE, True),
    ]
    first_scratch = [
        pltpu.VMEM((rows_count, quarter, full), LOW),
        pltpu.VMEM((rows_count, quarter, full), LOW),
        pltpu.VMEM((rows_count, quarter, full), LOW),
        row_buffers(quarter, full),
        token_low,
        pltpu.VMEM((rows_count, quarter, narrow), LOW),
        pltpu.VMEM((8, full), WIDE),
        pltpu.VMEM((count, rows_count, depth, 2 * part), LOW),
        *line_buffers(count, rows_count, depth, 2 * part),
        pltpu.VMEM((rows_count, depth, 2 * part), LOW),
        pltpu.VMEM((rows_count, 8, narrow), WIDE),
        pltpu.VMEM((count, 8, narrow), WIDE),
        pltpu.VMEM((rows_count, 8, narrow), WIDE),
        pltpu.VMEM((rows_count,) + channel_shape, WIDE),
        pltpu.VMEM((count,) + channel_shape, WIDE),
        pltpu.VMEM((rows_count,) + sums_shape, WIDE),
        pltpu.VMEM(block_in.shape, LOW),
        pltpu.VMEM(block_in.shape[1:], LOW),
        pltpu.VMEM(block_in.shape[1:], LOW),
        pltpu.VMEM((block_rows, block), LOW),
        row_buffers(hidden_part, narrow),
    ]
    sums_in = [
        (width_sums, True),
        (channel_part, True),
        (hidden_part_sums, True),
        (block_in, False),
    ]
    if inside:
        first_kernel, first_ins = first_norm_back_inside, [
            (grad_projected, False),
            (wxy_all, False),
            (normed_first, False),
            (x_own, False),
            (grad_middle, True),
            (width_all, True),
            (down_partial, False),
        ]
        first_scratch += [
            pltpu.VMEM((tokens, 2 * part), LOW),
            pltpu.VMEM((full, 2 * part), LOW),
            pltpu.VMEM((tokens, full), LOW),
            pltpu.VMEM((cores, rows_count, quarter, full), LOW),
        ]
    else:
        first_kernel, first_ins = first_norm_back, [
            (
                times_flipped(grad_projected, wxy_all)
                .astype(LOW)
                .reshape(cores, rows_count, quarter, full),
                False,
            ),
            (x_own, False),
            (grad_middle, True),
            (width_all, True),
            (
                left_product(normed_first, grad_projected)
                .astype(LOW)
                .reshape(rows_count, count, depth, 2 * part),
                False,
            ),
            (down_partial, False),
        ]
    input_grad, proj_grad, down_grad, width_sums, channel_sums, block_grads, hidden_sums = call(
        functools.partial(first_kernel, count),
        "first_norm_back",
        9,
        first_ins + sums_in,
        first_outs,
        first_scratch,
        remote,
        local,
    )
    branch_grad = side_by_side(proj_grad[:, :, :part].astype(WIDE))
    gelu_grad = side_by_side(proj_grad[:, :, part:].astype(WIDE))
    block_grads = (
        block_grads.reshape(rows_count, 2 * heads, back_share, block)
        .transpose(1, 0, 2, 3)
        .reshape(2 * heads, block_part, block)
        .astype(WIDE)
    )
    channel_sums = lax.dynamic_slice_in_dim(channel_sums, place_dp * channel_size, channel_size, 1)
    width_sums = lax.dynamic_slice_in_dim(
        width_sums[0] + width_sums[1], place_dp * depth, depth, 1
    )
    decay_param_grad = -8.0 * channel_sums[taps + 4] * jax.nn.sigmoid(decay_raw)

    return (
        layer_out.reshape(tall, narrow),
        input_grad.reshape(tall, narrow).astype(WIDE),
        branch_grad,
        gelu_grad,
        output_grad,
        side_by_side(gate_blocks.astype(WIDE)),
        side_by_side(up_blocks.astype(WIDE)),
        down_grad,
        block_grads[:heads],
        block_grads[heads:],
        channel_sums[:taps],
        channel_sums[taps],
        channel_sums[taps + 1],
        channel_sums[taps + 5],
        channel_sums[taps + 2],
        channel_sums[taps + 3],
        decay_param_grad,
        width_sums[1],
        hidden_sums[0, :hidden_part],
        hidden_sums[1, :hidden_part],
        width_sums[2],
        width_sums[3],
        width_sums[0],
    )


def solution(mesh):
    in_specs = (
        P(("dp", "col"), "row"),
        P(("dp", "row")),
        P(("row", "dp"), "col"),
        P(("row", "dp"), "col"),
        P(("col", "dp"), "row"),
        P(("row", "dp"), "col"),
        P(("row", "dp"), "col"),
        P(("col", "dp"), "row"),
        P("col", "dp", None),
        P("col", "dp", None),
        P(None, ("col", "dp")),
        P(("col", "dp")),
        P(("col", "dp")),
        P(("col", "dp")),
        P(("col", "dp")),
        P(("col", "dp")),
        P(("col", "dp")),
        P(("row", "dp")),
        P(("col", "dp")),
        P(("col", "dp")),
        P(("row", "dp")),
        P(("row", "dp")),
        P(("row", "dp")),
        P(("dp", "col"), "row"),
    )
    out_specs = (
        P(("dp", "col"), "row"),
        P(("dp", "col"), "row"),
        P(("row", "dp"), "col"),
        P(("row", "dp"), "col"),
        P(("col", "dp"), "row"),
        P(("row", "dp"), "col"),
        P(("row", "dp"), "col"),
        P(("col", "dp"), "row"),
        P("col", "dp", None),
        P("col", "dp", None),
        P(None, ("col", "dp")),
        P(("col", "dp")),
        P(("col", "dp")),
        P(("col", "dp")),
        P(("col", "dp")),
        P(("col", "dp")),
        P(("col", "dp")),
        P(("row", "dp")),
        P(("col", "dp")),
        P(("col", "dp")),
        P(("row", "dp")),
        P(("row", "dp")),
        P(("row", "dp")),
    )
    return jax.shard_map(shards, mesh=mesh, in_specs=in_specs, out_specs=out_specs, check_vma=False)
```

```python
import functools

import jax
import jax.numpy as jnp
from jax import lax
from jax.experimental import pallas as pl
from jax.experimental.pallas import tpu as pltpu
from jax.sharding import PartitionSpec as P

epsilon = 1e-06
ROOT = (2.0 / 3.141592653589793) ** 0.5
CUBE = 0.044715
LOW = jnp.bfloat16
WIDE = jnp.float32
MESH = pl.DeviceIdType.MESH
VMEM = pl.BlockSpec(memory_space=pltpu.VMEM)
ANY = pl.BlockSpec(memory_space=pl.ANY)


def times(piece, matrix):
    return jnp.dot(piece, matrix, preferred_element_type=WIDE)


def times_flipped(piece, matrix):
    return lax.dot_general(piece, matrix, (((1,), (1,)), ((), ())), preferred_element_type=WIDE)


def left_product(left, right):
    return lax.dot_general(left, right, (((0,), (0,)), ((), ())), preferred_element_type=WIDE)


class Links:
    def __init__(self, send, recv, local):
        self.send, self.recv, self.local = send, recv, local
        self.sent = self.kept = 0

    def copy(self, src, dst, **where):
        k, self.sent = self.sent, self.sent + 1
        return pltpu.make_async_remote_copy(
            src_ref=src,
            dst_ref=dst,
            send_sem=self.send.at[k],
            recv_sem=self.recv.at[k],
            device_id=where,
            device_id_type=MESH,
        )

    def keep(self, src, dst):
        k, self.kept = self.kept, self.kept + 1
        copy = pltpu.make_async_copy(src, dst, self.local.at[k])
        copy.start()
        return copy


class Relay:
    def __init__(self, links, src, buffer, dst):
        self.links, self.buffer, self.dst, self.store = links, buffer, dst, None
        self.load = links.keep(src, buffer)

    def pass_on(self):
        if self.store is None:
            self.load.wait()
            self.store = self.links.keep(self.buffer, self.dst)

    def wait(self):
        self.pass_on()
        self.store.wait()


class Place:
    def __init__(self, count_dp):
        self.row, self.dp, self.col = (lax.axis_index(name) for name in ("row", "dp", "col"))
        self.count = count_dp
        first, second = lax.rem(self.row, 2), lax.div(self.row, 2)
        self.near = [self.row, self.row + 1 - 2 * first, self.row + 2 - 4 * second, 3 - self.row]
        self.other = 1 - self.col

    def turn(self, index):
        return lax.rem(index + self.count, self.count)


def greet(place, rows=False, line=False, cores=False):
    barrier = pltpu.get_barrier_semaphore()
    partners = []
    if rows:
        partners += [{"row": place.near[k]} for k in range(1, 4)]
    if line:
        partners += [{"dp": place.turn(place.dp + k)} for k in range(1, place.count)]
    if cores:
        partners += [{"col": place.other}]
    for where in partners:
        pl.semaphore_signal(barrier, inc=1, device_id=where, device_id_type=MESH)
    pl.semaphore_wait(barrier, len(partners))


def run(tasks):
    live = list(tasks)
    while live:
        live = [task for task in live if next(task, None) is not None]


def advance(*tasks):
    for task in tasks:
        next(task, None)


def finish(*tasks):
    run(tasks)


def chain(*tasks):
    for task in tasks:
        yield from task


def when(condition, action):
    pl.when(condition)(lambda: action() and None)


def halves(size):
    first = -(-size // 32) * 16
    return (pl.ds(0, first), pl.ds(first, size - first))


def by_rows(count, body):
    step = 16 if count % 16 == 0 else count

    def lap(i, carry):
        body(pl.ds(pl.multiple_of(i * step, step), step))
        return carry

    lax.fori_loop(0, count // step, lap, 0)


def by_pieces(pieces, height, body):
    def lap(i, carry):
        by_rows(height, lambda rows: body(i, rows))
        return carry

    if pieces == 1:
        by_rows(height, lambda rows: body(0, rows))
    else:
        lax.fori_loop(0, pieces, lap, 0)


def gather_rows(links, place, own, piece):
    row, near, side, _ = place.near
    out = [
        links.copy(own(0), piece(row, 0), row=near),
        links.copy(own(1), piece(row, 1), row=side),
        links.copy(own(1), piece(row, 1), row=near),
        links.copy(own(0), piece(row, 0), row=side),
    ]
    for copy in out:
        copy.start()
    yield 1
    out[0].wait_recv()
    out.append(links.copy(piece(near, 0), piece(near, 0), row=side))
    out[4].start()
    out[1].wait_recv()
    out.append(links.copy(piece(side, 1), piece(side, 1), row=near))
    out[5].start()
    yield 1
    for copy in out[2:]:
        copy.wait_recv()
    for copy in out:
        copy.wait_send()


def exchange_rows(links, place, source, target):
    out = [
        links.copy(source(place.near[k]), target(place.row), row=place.near[k])
        for k in range(1, 4)
    ]
    for copy in out:
        copy.start()
    yield 1
    for copy in out:
        copy.wait_recv()
    for copy in out:
        copy.wait_send()


def exchange_line(links, place, source, target):
    out = []
    for k in range(1, place.count):
        far = place.turn(place.dp + k)
        out.append(links.copy(source(far), target(place.dp), dp=far))
    for copy in out:
        copy.start()
    yield 1
    for copy in out:
        copy.wait_recv()
    for copy in out:
        copy.wait_send()


def gather_line(links, place, own, piece, share=False):
    z, count, turn = place.dp, place.count, place.turn
    ups, downs, shared = [], [], []

    def pass_on(block, valid):
        copy = links.copy(piece(block), piece(block), col=place.other)
        when(valid, copy.start)
        shared.append((copy, valid))

    if share:
        copy = links.copy(own, piece(z), col=place.other)
        copy.start()
        shared.append((copy, z >= 0))
    for step in range(1, count + 1):
        if step > 1:
            yield 1
            below, above = z >= step - 1, z <= count - step
            when(below, ups[-1].wait_recv)
            when(above, downs[-1].wait_recv)
        if step < count:
            low, high = turn(z - step + 1), turn(z + step - 1)
            ups.append(
                links.copy(own if step == 1 else piece(low), piece(low), dp=turn(z + 1))
            )
            downs.append(
                links.copy(own if step == 1 else piece(high), piece(high), dp=turn(z - 1))
            )
            when((z >= step - 1) & (z < count - 1), ups[-1].start)
            when((z <= count - step) & (z > 0), downs[-1].start)
        if step > 1 and share:
            pass_on(turn(z - step + 1), below)
            pass_on(turn(z + step - 1), above)
    yield 1
    for copy, valid in shared:
        when(valid, copy.wait_recv)
    for step in range(1, count):
        when((z >= step - 1) & (z < count - 1), ups[step - 1].wait_send)
        when((z <= count - step) & (z > 0), downs[step - 1].wait_send)
    for copy, valid in shared:
        when(valid, copy.wait_send)


class LineGather:
    def __init__(self, links, place, own, piece):
        self.links, self.place, self.own, self.piece = links, place, own, piece
        self.ups, self.downs, self.shared = [None], [None], []

    def send(self, step):
        z, count, turn = self.place.dp, self.place.count, self.place.turn
        low, high = turn(z - step + 1), turn(z + step - 1)
        for copies, block, target, valid in (
            (self.ups, low, turn(z + 1), (z >= step - 1) & (z < count - 1)),
            (self.downs, high, turn(z - 1), (z <= count - step) & (z > 0)),
        ):
            source = self.own if step == 1 else self.piece(block)
            copy = self.links.copy(source, self.piece(block), dp=target)
            copies.append((copy, valid))
            when(valid, copy.start)

    def share(self, blocks, own=None):
        out = []
        for block, valid in blocks:
            source = self.piece(block) if own is None else own
            copy = self.links.copy(source, self.piece(block), col=self.place.other)
            when(valid, copy.start)
            out.append((copy, valid))
        self.shared.append(out)

    def start(self):
        self.send(1)
        self.share([(self.place.dp, self.place.dp >= 0)], self.own)

    def step(self, step):
        z, count, turn = self.place.dp, self.place.count, self.place.turn
        below, above = z >= step, z <= count - 1 - step
        when(below, self.ups[step][0].wait_recv)
        when(above, self.downs[step][0].wait_recv)
        if step < count - 1:
            self.send(step + 1)
        self.share([(turn(z - step), below), (turn(z + step), above)])

    def ready(self, step):
        for copy, valid in self.shared[step]:
            when(valid, copy.wait_recv)

    def close(self):
        for copy, valid in self.ups[1:] + self.downs[1:] + sum(self.shared, []):
            when(valid, copy.wait_send)


def scatter_rows(links, place, part, buffers, result, prepare=None, gentle=False):
    row, near, side, far = place.near
    if prepare is not None:
        prepare(far)
    heights = [part(row, h).shape[0] for h in range(2)]

    def buffer(i, h):
        return buffers.at[i, pl.ds(0, heights[h])]

    out = [
        links.copy(part(far, 0), buffer(5, 0), row=side),
        links.copy(part(far, 1), buffer(7, 1), row=near),
        links.copy(part(side, 0), buffer(4, 0), row=side),
        links.copy(part(near, 1), buffer(6, 1), row=near),
    ]
    for i, copy in enumerate(out):
        if i == 2 and gentle:
            yield 1
        if i > 1 and prepare is not None:
            prepare(near if i == 3 else side)
        copy.start()
    if prepare is not None:
        prepare(row)
    loads = [
        links.keep(part(near, 0), buffer(0, 0)),
        links.keep(part(side, 1), buffer(1, 1)),
        links.keep(part(row, 0), buffer(2, 0)),
        links.keep(part(row, 1), buffer(3, 1)),
    ]
    yield 1
    for h, target in ((0, near), (1, side)):
        loads[h].wait()
        out[h].wait_recv()

        def add(rows, h=h):
            total = buffers[h, rows].astype(WIDE) + buffers[5 + 2 * h, rows].astype(WIDE)
            buffers[h, rows] = total.astype(LOW)

        by_rows(heights[h], add)
        out.append(links.copy(buffer(h, h), buffer(8 + h, h), row=target))
        out[-1].start()
        yield 1
    for h in range(2):
        loads[2 + h].wait()
        out[2 + h].wait_recv()
        out[4 + h].wait_recv()

        def finish(rows, h=h):
            result(
                h,
                rows,
                buffers[2 + h, rows].astype(WIDE)
                + buffers[4 + 2 * h, rows].astype(WIDE)
                + buffers[8 + h, rows].astype(WIDE),
            )

        by_rows(heights[h], finish)
    for copy in out:
        copy.wait_send()


def row_buffers(size, width):
    return pltpu.VMEM((10, halves(size)[0].size, width), LOW)


def scatter_line(links, place, ready, term, ups_in, downs_in, staging, result):
    z, count, turn = place.dp, place.count, place.turn
    pieces, height = ups_in.shape[1:3]
    ups, downs = [None], [None]

    def sends_up(t):
        return (z <= t - 1) & (z < count - 1)

    def sends_down(t):
        return (z >= count - t) & (z > 0)

    def fill(slot, block, arrived):
        def body(i, rows):
            value = term(block, i, rows)
            if arrived is not None:
                value = value + arrived[i, rows].astype(WIDE)
            staging[slot, i, rows] = value.astype(LOW)

        by_pieces(pieces, height, body)

    for t in range(1, count):
        ready(t)
        ready(count - t)
        for which in range(2):
            copies, into = ((ups, ups_in), (downs, downs_in))[which]
            sends = (sends_up, sends_down)[which]
            first = (z == 0, z == count - 1)[which]
            block = (turn(z - t), turn(z + t))[which]
            target = (turn(z + 1), turn(z - 1))[which]
            slot = 2 * which + t % 2
            if t > 2:
                when(sends(t - 2), copies[t - 2].wait_send)
            copy = links.copy(staging.at[slot], into.at[t - 1], dp=target)
            copies.append(copy)

            def begin(copy=copy, slot=slot, block=block):
                fill(slot, block, None)
                copy.start()

            when(sends(t) & first, begin)
            if t > 1:

                def go_on(copy=copy, slot=slot, block=block, before=copies[t - 1], into=into, t=t):
                    before.wait_recv()
                    fill(slot, block, into.at[t - 2])
                    copy.start()

                when(sends(t) & jnp.logical_not(first), go_on)
        yield 1
    ready(0)
    last = count - 1
    from_below, from_above = ups_in.at[last - 1], downs_in.at[last - 1]
    when(z > 0, ups[last].wait_recv)
    when(z < last, downs[last].wait_recv)

    def finish(below, above):
        def body(i, rows):
            value = term(z, i, rows)
            if below:
                value = value + from_below[i, rows].astype(WIDE)
            if above:
                value = value + from_above[i, rows].astype(WIDE)
            result(i, rows, value)

        by_pieces(pieces, height, body)

    when(z == 0, lambda: finish(False, True))
    when((z > 0) & (z < last), lambda: finish(True, True))
    when(z == last, lambda: finish(True, False))
    for t in range(max(1, count - 2), count):
        when(sends_up(t), ups[t].wait_send)
        when(sends_down(t), downs[t].wait_send)


def scatter_line_in_parts(links, place, ready, term, ups_in, downs_in, staging, result):
    def part(i):
        return scatter_line(
            links,
            place,
            ready,
            lambda b, _, rows: term(b, i, rows),
            ups_in.at[:, pl.ds(i, 1)],
            downs_in.at[:, pl.ds(i, 1)],
            staging.at[:, pl.ds(i, 1)],
            lambda _, rows, value: result(i, rows, value),
        )

    live = [part(i) for i in range(ups_in.shape[1])]
    while live:
        live = [task for task in live if next(task, None) is not None]
        yield 1


def line_buffers(count, pieces, height, width):
    return [pltpu.VMEM((slots, pieces, height, width), LOW) for slots in (count - 1, count - 1, 4)]


def token_scatter(links, place, partial, ours, theirs, buffers, result, prepare=None):
    out, loads = [], []
    for s in list(range(1, place.count)) + [0]:
        block = place.turn(place.dp - s)
        if prepare is not None:
            prepare(block)
        out.append(
            links.copy(partial.at[block, place.other], theirs.at[block], col=place.other)
        )
        out[-1].start()
        loads.append(links.keep(partial.at[block, place.col], ours.at[block]))
    waited = set()

    def ready(s):
        if s not in waited:
            waited.add(s)
            at = s - 1 if s else place.count - 1
            out[at].wait_recv()
            loads[at].wait()

    height = buffers[0].shape[2]

    def at(i, rows):
        return pl.ds(pl.multiple_of(rows.start + i * height, 16), rows.size)

    def term(block, i, rows):
        here = at(i, rows)
        return ours[block, here].astype(WIDE) + theirs[block, here].astype(WIDE)

    yield 1
    yield from scatter_line_in_parts(
        links, place, ready, term, *buffers, lambda i, rows, value: result(at(i, rows), value)
    )
    for copy in out:
        copy.wait_send()


def call(kernel, name, number, ins, outs, scratch, remote, local):
    return pl.pallas_call(
        kernel,
        in_specs=[VMEM if inside else ANY for _, inside in ins],
        out_specs=[VMEM if inside else ANY for _, _, inside in outs],
        out_shape=[jax.ShapeDtypeStruct(shape, kind) for shape, kind, _ in outs],
        scratch_shapes=list(scratch)
        + [
            pltpu.SemaphoreType.DMA((remote,)),
            pltpu.SemaphoreType.DMA((remote,)),
            pltpu.SemaphoreType.DMA((local,)),
        ],
        compiler_params=pltpu.CompilerParams(
            collective_id=number, has_side_effects=True, vmem_limit_bytes=58 * 1024 * 1024
        ),
        name=name,
    )(*[array for array, _ in ins])


def lanes(index, width):
    return pl.ds(pl.multiple_of(index * width, 128), width)


def strip(index, height, step=16):
    return pl.ds(pl.multiple_of(index * height, step), height)


def combine(earlier, later):
    return (earlier[0] * later[0], later[0] * earlier[1] + later[1])


def scan_rows(decay, value, reverse):
    count = decay.shape[0]
    rows = lax.broadcasted_iota(jnp.int32, decay.shape, 0)
    reach = 1
    while reach < count:
        turn = count - reach if reverse else reach
        inside = rows < count - reach if reverse else rows >= reach
        decay_far = jnp.where(inside, pltpu.roll(decay, turn, 0), 1.0)
        value_far = jnp.where(inside, pltpu.roll(value, turn, 0), 0.0)
        value = decay * value_far + value
        decay = decay * decay_far
        reach *= 2
    return decay, value


def minus_expm1(v):
    series = 1.0 + v / 9.0
    for k in range(8, 1, -1):
        series = 1.0 + (v / k) * series
    return jnp.where(v > -0.5, -v * series, 1.0 - jnp.exp(v))


def each_head(heads, width, body):
    def lap(h, carry):
        body(h, pl.ds(pl.multiple_of(h * width, 128), width))
        return carry

    lax.fori_loop(0, heads, lap, 0)


def carry_over(links, place, ends, table, reverse):
    run([exchange_rows(links, place, lambda q: ends, lambda q: table.at[q])])
    row = place.row
    state = jnp.zeros((1, ends.shape[1]), WIDE)
    for k in range(4):
        q = 3 - k if reverse else k

        def entry(i):
            return table[q, i : i + 1, :]

        reached = q > row if reverse else q < row
        state = jnp.where(reached, entry(0) * state + entry(1), state)
    return state


def recurrence_backward(
    count, taps, proj, side, spots, vectors, blocks, conv_in, in_gate, dec_gate, state_in, entering,
    grad_mixed, branch_out, sums_out, blocks_out, reach, local_grad, branch, ends, table, heads_in,
    heads_here, padded, spread, send, recv, local, links=None, between=lambda: None,
):
    place = Place(count)
    if links is None:
        links = Links(send, recv, local)
        greet(place, rows=True)
    tokens, width = side.shape
    heads, block = blocks.shape[0] // 2, blocks.shape[1]
    spot = spots[...]
    starting = spot == 0
    ends[...] = jnp.zeros(ends.shape, WIDE)

    def backwards(h, at):
        rate = vectors[taps + 5 : taps + 6, at]
        decay = jnp.where(starting, 0.0, jnp.exp(rate * dec_gate[:, at]))
        padded[0:tokens, :] = decay
        padded[tokens:, :] = jnp.ones((8, block), WIDE)
        far, grad = scan_rows(padded[1 : tokens + 1, :], grad_mixed[:, at] * side[:, at], True)
        reach[:, at] = far
        local_grad[:, at] = grad
        ends[0:1, at] = decay[0:1, :] * far[0:1, :]
        ends[1:2, at] = decay[0:1, :] * grad[0:1, :]

    each_head(heads, block, backwards)
    own = links.keep(ends, table.at[place.row])
    own.wait()
    heads_here[0:1, :] = carry_over(links, place, ends, table, True)
    between()

    def one_head(h, at):
        def vector(i):
            return vectors[i : i + 1, at]

        grad_state = local_grad[:, at] + reach[:, at] * heads_here[0:1, at]
        padded[8:, :] = state_in[:, at]
        padded[7:8, :] = entering[0:1, at]
        grad_decay = grad_state * padded[7 : 7 + tokens, :]
        input_gate, decay_gate, conv = in_gate[:, at], dec_gate[:, at], conv_in[:, at]
        rate = vector(taps + 5)
        log_decay = rate * decay_gate
        decay = jnp.exp(log_decay)
        multiplier = jnp.where(starting, 1.0, jnp.sqrt(minus_expm1(2.0 * log_decay)))
        grad_gated = grad_state * conv
        grad_log = jnp.where(
            starting, 0.0, decay * (grad_decay - grad_gated * input_gate * (decay / multiplier))
        )
        grad_in = grad_gated * multiplier * (input_gate * (1.0 - input_gate))
        grad_gate = grad_log * decay_gate
        grad_dec = grad_gate * rate * (1.0 - decay_gate)
        low = conv.astype(LOW)
        low_in, low_dec = grad_in.astype(LOW), grad_dec.astype(LOW)
        across = (((1,), (1,)), ((), ()))
        along = (((0,), (0,)), ((), ()))
        grad_conv = (
            grad_state * multiplier * input_gate
            + lax.dot_general(low_in, blocks[h], across, preferred_element_type=WIDE)
            + lax.dot_general(low_dec, blocks[heads + h], across, preferred_element_type=WIDE)
        )
        blocks_out[h] = lax.dot_general(low, low_in, along, preferred_element_type=WIDE)
        blocks_out[heads + h] = lax.dot_general(low, low_dec, along, preferred_element_type=WIDE)
        spread[0:8, :] = jnp.zeros((8, block), WIDE)
        spread[8:, :] = vector(0) * grad_conv
        shift = vector(taps + 1)

        def total(values):
            return jnp.sum(values, axis=0, keepdims=True)

        sums_out[0:1, at] = total(grad_conv * (proj[8:, at] + shift))
        for k in range(1, taps):
            kept = jnp.where(spot >= k, grad_conv, 0.0)
            sums_out[k : k + 1, at] = total(kept * (proj[8 - k : 8 - k + tokens, at] + shift))
            spread[8 - k : 8 - k + tokens, :] += vector(k) * kept
        branch[:, at] = spread[8:, :]
        heads_in[0, :, at] = spread[0:8, :]
        sums_out[taps : taps + 1, at] = total(grad_conv)
        sums_out[taps + 1 : taps + 2, at] = total(spread[...])
        sums_out[taps + 2 : taps + 3, at] = total(grad_in)
        sums_out[taps + 3 : taps + 4, at] = total(grad_dec)
        sums_out[taps + 4 : taps + 5, at] = total(grad_gate)
        sums_out[taps + 5 :, at] = jnp.zeros((sums_out.shape[0] - taps - 5, block), WIDE)

    each_head(heads, block, one_head)
    row = place.row
    before = lax.rem(row + 3, 4)
    owed = links.copy(heads_in.at[0], heads_in.at[1], row=before)
    owed.start()
    owed.wait_recv()
    owed.wait_send()
    between()

    def finish(h, at):
        last = jnp.where(row < 3, heads_in[1, :, at], 0.0)
        branch[tokens - 8 :, at] += last
        branch_out[:, at] = branch[:, at].astype(LOW)

    each_head(heads, block, finish)


def recurrence_back_inside(
    count, taps, proj_hbm, side_hbm, gelu_hbm, spots, vectors, blocks_hbm, conv_hbm, in_hbm, dec_hbm,
    state_hbm, entering, mixed_hbm, output_partial, up_own, sums_out, blocks_out, all_out, output_out, up_out, branch_low, gelu_low, stage, reach, local_grad, branch, ends, table, heads_in,
    heads_here, padded, spread, ups, downs, staging, own, up_here, proj, side, gelu_in, blocks, conv_in,
    in_gate, dec_gate, state_in, grad_mixed, send, recv, local,
):
    place = Place(count)
    links = Links(send, recv, local)
    load = links.keep(output_partial, own)
    arrays = [
        links.keep(source, target)
        for source, target in (
            (dec_hbm, dec_gate), (mixed_hbm, grad_mixed), (side_hbm, side), (state_hbm, state_in),
            (blocks_hbm, blocks), (conv_hbm, conv_in), (in_hbm, in_gate), (proj_hbm, proj),
            (gelu_hbm, gelu_in),
        )
    ]
    greet(place, rows=True, line=True)
    row, z = place.row, place.dp
    part = stage.shape[2] // 2
    kept = Relay(links, up_own.at[z], up_here, up_out.at[z])

    output_half = ups.shape[2]

    def output_rows(i, rows):
        return pl.ds(pl.multiple_of(rows.start + i * output_half, 16), rows.size)

    def keep_output(i, rows, value):
        output_out[output_rows(i, rows)] = value

    output_sum = scatter_line_in_parts(
        links,
        place,
        lambda s: None,
        lambda b, i, rows: own[b, output_rows(i, rows)].astype(WIDE),
        ups,
        downs,
        staging,
        keep_output,
    )
    up_line = exchange_line(links, place, lambda b: up_own.at[b], lambda b: up_out.at[b])
    load.wait()
    advance(output_sum, up_line)
    kept.pass_on()
    for array in arrays:
        array.wait()

    def gelu_back(h, at):
        grad = grad_mixed[:, at] * state_in[:, at] * gelu_slope(gelu_in[:, at])
        gelu_low[:, at] = grad.astype(LOW)
        spread[0:1, :] = jnp.sum(grad, axis=0, keepdims=True)
        sums_out[taps + 5 : taps + 6, at] = spread[0:1, :]

    recurrence_backward(
        count, taps, proj, side, spots, vectors, blocks, conv_in, in_gate, dec_gate, state_in, entering,
        grad_mixed, branch_low, sums_out, blocks_out, reach, local_grad, branch, ends, table, heads_in,
        heads_here, padded, spread, None, None, None, links, lambda: advance(output_sum),
    )
    each_head(blocks.shape[0] // 2, blocks.shape[1], gelu_back)
    for q in range(4):
        at = slice(q * part, (q + 1) * part)
        stage[q, :, :part] = branch_low[:, at]
        stage[q, :, part:] = gelu_low[:, at]
    mine = links.keep(stage.at[row], all_out.at[row])
    spread_out = exchange_rows(links, place, lambda q: stage.at[q], lambda q: all_out.at[q])
    run([spread_out, output_sum, up_line])
    mine.wait()
    kept.wait()


def norm_rule(rows, grad, value, gain, sums, at):
    full = value.shape[1]
    inverse = lax.rsqrt(jnp.sum(value * value, axis=1, keepdims=True) / full + epsilon)
    scaled = grad * (1.0 + gain)
    inner = jnp.sum(scaled * value, axis=1, keepdims=True)
    sums[at : at + 1, :] += jnp.sum(grad * value * inverse, axis=0, keepdims=True)
    return inverse * scaled - value * (inverse * inverse * inverse) * (inner / full)


def second_norm_back_inside(
    count, grad_gate, grad_up, gate_all, up_all, normed, hidden, down_all, cot_all, middle, vectors,
    grad_middle, grad_all, sums, gate_out, forward_out, ours, theirs, ups, downs, staging, cot, low, buffers,
    gate_v, up_v, gate_w, up_w, tile, partial, gate_partial, hidden_v, down_tile, forward_tile, send, recv,
    local,
):
    place = Place(count)
    links = Links(send, recv, local)
    loads = [links.keep(grad_gate, gate_v), links.keep(grad_up, up_v)]
    pieces = [
        (links.keep(gate_all.at[q], gate_w.at[q]), links.keep(up_all.at[q], up_w.at[q]))
        for q in range(4)
    ]
    greet(place, rows=True, line=True, cores=True)
    quarter, full = middle.shape
    narrow, units = full // 4, gate_v.shape[1]
    for load in loads:
        load.wait()
    first = [True]

    def tokens(block):
        rows = strip(block, 2 * quarter)

        def lap(q, carry):
            total = sum(
                times_flipped(values[rows, :], weight[q].astype(LOW).reshape(narrow, units))
                for values, weight in ((gate_v, gate_w), (up_v, up_w))
            ).astype(LOW)
            for core in range(2):
                partial[block, core, :, lanes(q, narrow)] = total[
                    core * quarter : (core + 1) * quarter
                ]
            return carry

        if first:
            first.clear()
            for q in range(4):
                for load in pieces[q]:
                    load.wait()
                lap(q, 0)
        else:
            lax.fori_loop(0, 4, lap, 0)

    k, links.kept = links.kept, links.kept + 1

    def gate(q):
        load = pltpu.make_async_copy(normed.at[:, lanes(q, narrow)], tile, links.local.at[k])
        load.start()
        load.wait()
        gate_partial[strip(q, narrow)] = left_product(tile[...], gate_v[...]).astype(LOW)

    k_down, links.kept = links.kept, links.kept + 1
    load_hidden = links.keep(hidden, hidden_v)

    def forward_sum():
        load_hidden.wait()
        store = None
        for q in range(4):
            load = pltpu.make_async_copy(
                down_all.at[:, lanes(q, narrow)], down_tile, links.local.at[k_down]
            )
            load.start()
            load.wait()
            if store is not None:
                store.wait()
            forward_tile[...] = times(hidden_v[...], down_tile[...]).astype(LOW)
            store = links.keep(forward_tile, forward_out.at[:, lanes(q, narrow)])
            yield 1
        store.wait()

    second_norm_back(
        count, partial, cot_all, middle, vectors, gate_partial, grad_middle, grad_all, sums, gate_out,
        ours, theirs, ups, downs, staging, cot, low, buffers, None, None, None, links, tokens, gate,
        [forward_sum()],
    )


def second_norm_back(
    count, grad_partial, cot_all, middle, vectors, gate_partial, grad_middle, grad_all, sums, gate_out,
    ours, theirs, ups, downs, staging, cot, low, buffers, send, recv, local, links=None,
    prepare_tokens=None, prepare_gate=None, others=(),
):
    place = Place(count)
    if links is None:
        links = Links(send, recv, local)
        greet(place, rows=True, line=True, cores=True)
    row, z, col = place.row, place.dp, place.col
    quarter, full = middle.shape
    narrow = full // 4
    tall = 4 * quarter
    half = gate_partial.shape[0] // 8
    sums[...] = jnp.zeros(sums.shape, WIDE)
    gain = vectors[3:4, :]
    load = links.keep(cot_all.at[strip(2 * z + col, quarter)], cot)

    def back(rows, grad):
        own = cot[rows].astype(WIDE)
        total = own + norm_rule(rows, grad, middle[rows], gain, sums, 0)
        sums[1:2, :] += jnp.sum(total, axis=0, keepdims=True)
        sums[2:3, :] += jnp.sum(own, axis=0, keepdims=True)
        grad_middle[rows] = total
        low[rows] = total.astype(LOW)

    def tokens():
        load.wait()
        yield from token_scatter(
            links, place, grad_partial, ours, theirs, (ups, downs, staging), back, prepare_tokens
        )

        def block(q):
            return grad_all.at[strip(4 * col + q, quarter)]

        mine = links.keep(low.at[:, lanes(row, narrow)], block(row))
        yield from exchange_rows(
            links, place, lambda q: low.at[:, lanes(q, narrow)], block
        )
        mine.wait()
        both = grad_all.at[strip(col, tall)]
        share = links.copy(both, both, col=place.other)
        share.start()
        yield 1
        share.wait_recv()
        share.wait_send()

    def keep_gate(h, rows, value):
        gate_out[h, rows] = value.astype(LOW)

    tokens_back = tokens()
    gate_back = scatter_rows(
        links,
        place,
        lambda q, h: gate_partial.at[strip(2 * q + h, half)],
        buffers,
        keep_gate,
        prepare_gate,
    )
    advance(tokens_back)
    advance(tokens_back)
    run([gate_back, tokens_back, *others])


def mixed_and_output_inside(
    count, grad_all, wout, mixed_all, normed, cot_all, grad_up, hidden, out_partial, middle, vectors, gate_own,
    mixed_out, layer_out, up_out, gate_out, output_out, down_out, mixed_buffers, ours, theirs, ups, downs,
    staging, low, up_buffers, gate_here, grad_v, wout_v, mixed_v, tile, up_v, hidden_v, mixed_partial,
    up_partial, output_v, down_v, send, recv, local,
):
    place = Place(count)
    links = Links(send, recv, local)
    loads = [
        links.keep(source, target)
        for source, target in (
            (grad_all, grad_v), (wout, wout_v), (grad_up, up_v), (mixed_all, mixed_v),
            (hidden, hidden_v),
        )
    ]
    greet(place, rows=True, line=True, cores=True)
    steps = mixed_partial.shape[0] // 4
    narrow = grad_v.shape[1]
    for load in loads[:2]:
        load.wait()

    def mixed(q):
        rows = strip(q, steps)
        mixed_partial[rows] = times_flipped(grad_v[rows, :], wout_v[...]).astype(LOW)

    k, links.kept = links.kept, links.kept + 1

    def fetch(source, q):
        load = pltpu.make_async_copy(source.at[:, lanes(q, narrow)], tile, links.local.at[k])
        load.start()
        load.wait()

    def up(q):
        fetch(normed, q)
        up_partial[strip(q, narrow)] = left_product(tile[...], up_v[...]).astype(LOW)

    def ready():
        for load in loads[2:]:
            load.wait()

    def others():
        output_v[...] = left_product(mixed_v[...], grad_v[...]).astype(LOW)
        stores = [links.keep(output_v, output_out)]

        def lap(q, carry):
            fetch(cot_all, q)
            down_v[:, lanes(q, narrow)] = left_product(hidden_v[...], tile[...]).astype(LOW)
            return carry

        lax.fori_loop(0, 4, lap, 0)
        stores.append(links.keep(down_v, down_out))
        yield 1
        for store in stores:
            store.wait()

    mixed_and_output(
        count, mixed_partial, out_partial, middle, vectors, up_partial, gate_own, mixed_out, layer_out,
        up_out, gate_out, mixed_buffers, ours, theirs, ups, downs, staging, low, up_buffers, gate_here, None,
        None, None, links, ready, mixed, up, others(),
    )


def mixed_and_output(
    count, mixed_partial, out_partial, middle, vectors, up_partial, gate_own, mixed_out, layer_out, up_out,
    gate_out, mixed_buffers, ours, theirs, ups, downs, staging, low, up_buffers, gate_here, send, recv,
    local, links=None, ready=None, prepare_mixed=None, prepare_up=None, others=None,
):
    place = Place(count)
    if links is None:
        links = Links(send, recv, local)
        greet(place, rows=True, line=True, cores=True)
    row = place.row
    quarter, full = middle.shape
    narrow = full // 4
    shift = vectors[2:3, :]
    half = mixed_partial.shape[0] // 8
    up_half = up_partial.shape[0] // 8
    kept = Relay(links, gate_own.at[place.dp], gate_here, gate_out.at[place.dp])

    def keep_mixed(h, rows, value):
        mixed_out[h, rows] = value

    def keep_up(h, rows, value):
        up_out[h, rows] = value.astype(LOW)

    def finish(rows, value):
        low[rows] = (middle[rows] + value + shift).astype(LOW)

    def tokens():
        yield from token_scatter(
            links, place, out_partial, ours, theirs, (ups, downs, staging), finish
        )
        mine = links.keep(low.at[:, lanes(row, narrow)], layer_out.at[row])
        yield from exchange_rows(
            links, place, lambda q: low.at[:, lanes(q, narrow)], lambda q: layer_out.at[q]
        )
        mine.wait()

    outs = tokens()
    mixes = scatter_rows(
        links,
        place,
        lambda q, h: mixed_partial.at[strip(2 * q + h, half)],
        mixed_buffers,
        keep_mixed,
        prepare_mixed,
    )
    sums_up = scatter_rows(
        links,
        place,
        lambda q, h: up_partial.at[strip(2 * q + h, up_half)],
        up_buffers,
        keep_up,
        prepare_up,
    )
    gates = exchange_line(links, place, lambda b: gate_own.at[b], lambda b: gate_out.at[b])
    advance(gates, outs, mixes, outs)
    kept.pass_on()
    if ready is not None:
        ready()
    advance(sums_up, mixes, outs)
    if others is not None:
        advance(others)
    advance(mixes)
    run([outs, sums_up, mixes, gates] + ([others] if others is not None else []))
    kept.wait()


def spread_gradients(
    count, blocks, output_partial, up_own, all_out, output_out, up_out, ups, downs, staging, own, send, recv, local,
):
    place = Place(count)
    links = Links(send, recv, local)
    greet(place, rows=True, line=True)
    row, z = place.row, place.dp
    mine = links.keep(blocks.at[row], all_out.at[row])
    kept = links.keep(up_own.at[z], up_out.at[z])
    load = links.keep(output_partial, own)

    output_half = ups.shape[2]

    def output_rows(i, rows):
        return pl.ds(pl.multiple_of(rows.start + i * output_half, 16), rows.size)

    def keep_output(i, rows, value):
        output_out[output_rows(i, rows)] = value

    def outputs():
        load.wait()
        yield from scatter_line_in_parts(
            links,
            place,
            lambda s: None,
            lambda b, i, rows: own[b, output_rows(i, rows)].astype(WIDE),
            ups,
            downs,
            staging,
            keep_output,
        )

    run(
        [
            exchange_rows(links, place, lambda q: blocks.at[q], lambda q: all_out.at[q]),
            outputs(),
            exchange_line(links, place, lambda b: up_own.at[b], lambda b: up_out.at[b]),
        ]
    )
    mine.wait()
    kept.wait()


def first_norm_back(
    count, grad_partial, x_own, grad_middle, vectors, proj_partial, down_partial, sums_in,
    channel_in, hidden_in, block_in, grad_out, proj_out, down_out, width_sums, channel_sums, block_out, hidden_sums,
    theirs, ours, added,
    row_buffer, x, result, sums, proj_own, proj_ups, proj_downs, proj_staging, proj_low, width_table,
    width_line, width_part, channel_table, channel_line, hidden_table, block_table, block_part, block_line, block_low,
    down_buffers, send, recv, local, links=None, prepare_tokens=None, prepare_proj=None,
):
    place = Place(count)
    if links is None:
        links = Links(send, recv, local)
        greet(place, rows=True, line=True, cores=True)
    row, z, col = place.row, place.dp, place.col
    quarter, full = grad_middle.shape
    narrow = full // 4
    gain = vectors[0:1, :]
    load_x = links.keep(x_own, x)
    if prepare_proj is None:
        load_proj = [links.keep(proj_partial.at[:, b], proj_own.at[b]) for b in range(count)]

    parts = halves(down_partial.shape[0])

    def keep_down(h, rows, value):
        down_out[pl.ds(pl.multiple_of(parts[h].start + rows.start, 16), rows.size)] = value

    down_sum = scatter_rows(
        links,
        place,
        lambda q, h: down_partial.at[parts[h], lanes(q, narrow)],
        down_buffers,
        keep_down,
    )

    def tokens():
        if prepare_tokens is not None:
            prepare_tokens(place.other)
        share = links.copy(grad_partial.at[place.other], theirs, col=place.other)
        share.start()
        if prepare_tokens is not None:
            prepare_tokens(col)
        load = links.keep(grad_partial.at[col], ours)
        yield 1
        share.wait_recv()
        load.wait()

        def add(rows):
            for q in range(4):
                total = ours[q, rows].astype(WIDE) + theirs[q, rows].astype(WIDE)
                added[q, rows] = total.astype(LOW)

        by_rows(quarter, add)
        load_x.wait()
        sums[0:3, :] = sums_in[0:3, :]
        sums[3:, :] = jnp.zeros((sums.shape[0] - 3, full), WIDE)
        half = quarter // 2

        def back(h, rows, grad):
            here = pl.ds(pl.multiple_of(rows.start + half * h, 16), rows.size)
            value = x[here].astype(WIDE)
            total = grad_middle[here] + norm_rule(rows, grad, value, gain, sums, 3)
            for q in range(4):
                result[q, here] = total[:, q * narrow : (q + 1) * narrow].astype(LOW)

        yield from scatter_rows(
            links,
            place,
            lambda q, h: added.at[q, pl.ds(half * h, half)],
            row_buffer,
            back,
        )
        share.wait_send()
        mine = links.keep(result.at[row], grad_out.at[row])
        for q in range(4):
            width_part[q] = sums[:, q * narrow : (q + 1) * narrow]
        own = links.keep(width_part.at[row], width_table.at[row])
        vectors_out = exchange_rows(
            links, place, lambda q: width_part.at[q], lambda q: width_table.at[q]
        )
        results_out = exchange_rows(
            links, place, lambda q: result.at[q], lambda q: grad_out.at[q]
        )
        advance(vectors_out, results_out)
        yield 1
        finish(vectors_out)
        own.wait()
        width_line[z] = width_table[0] + width_table[1] + width_table[2] + width_table[3]
        yield from exchange_line(
            links, place, lambda b: width_line.at[z], lambda b: width_line.at[b]
        )
        total = width_line[0]
        for b in range(1, count):
            total = total + width_line[b]
        width_sums[0] = total
        yield 1
        last = links.copy(width_sums.at[0], width_sums.at[1], col=place.other)
        last.start()
        yield 1
        last.wait_recv()
        last.wait_send()
        finish(results_out)
        mine.wait()

    def projections():
        if prepare_proj is None:
            for load in load_proj:
                load.wait()
        else:
            prepare_proj()

        def keep_proj(i, rows, value):
            proj_low[i, rows] = value.astype(LOW)

        yield from scatter_line_in_parts(
            links,
            place,
            lambda s: None,
            lambda b, i, rows: proj_own[b, i, rows].astype(WIDE),
            proj_ups,
            proj_downs,
            proj_staging,
            keep_proj,
        )
        mine = links.keep(proj_low.at[row], proj_out.at[row])
        yield from exchange_rows(
            links, place, lambda q: proj_low.at[q], lambda q: proj_out.at[q]
        )
        mine.wait()

    def hidden():
        own = links.keep(hidden_in, hidden_table.at[row])
        yield from exchange_rows(
            links, place, lambda q: hidden_in, lambda q: hidden_table.at[q]
        )
        own.wait()
        hidden_sums[...] = hidden_table[0] + hidden_table[1] + hidden_table[2] + hidden_table[3]

    def channels():
        own = links.keep(channel_in, channel_table.at[row])
        yield from exchange_rows(
            links, place, lambda q: channel_in, lambda q: channel_table.at[q]
        )
        own.wait()
        channel_line[z] = (
            channel_table[0] + channel_table[1] + channel_table[2] + channel_table[3]
        )
        yield from exchange_line(
            links, place, lambda b: channel_line.at[z], lambda b: channel_line.at[b]
        )
        total = channel_line[0]
        for b in range(1, count):
            total = total + channel_line[b]
        channel_sums[...] = total

    def blocks():
        own = links.keep(block_in.at[row], block_table.at[row])
        yield from exchange_rows(
            links, place, lambda q: block_in.at[q], lambda q: block_table.at[q]
        )
        own.wait()

        for b in range(count):
            block_part[b] = sum(block_table[q, b].astype(WIDE) for q in range(4)).astype(LOW)
        own = links.keep(block_part.at[z], block_line.at[z])
        yield from exchange_line(
            links, place, lambda b: block_part.at[b], lambda b: block_line.at[b]
        )
        own.wait()
        block_low[...] = sum(block_line[b].astype(WIDE) for b in range(count)).astype(LOW)
        own = links.keep(block_low, block_out.at[row])
        yield from exchange_rows(links, place, lambda q: block_low, lambda q: block_out.at[q])
        own.wait()

    proj_sum, token_sum = projections(), tokens()
    small = [channels(), hidden(), blocks()]
    advance(down_sum, proj_sum, token_sum, *small)
    advance(token_sum)
    run([proj_sum, token_sum, down_sum] + small)


def first_norm_back_inside(
    count, grad_proj, wxy, nf, x_own, grad_middle, vectors, down_partial, *refs
):
    rest, (grad_v, wxy_v, nf_v, partial, send, recv, local) = refs[:-7], refs[-7:]
    proj_own = rest[18]
    place = Place(count)
    links = Links(send, recv, local)
    loads = [
        links.keep(source, target)
        for source, target in ((grad_proj, grad_v), (nf, nf_v), (wxy, wxy_v))
    ]
    greet(place, rows=True, line=True, cores=True)
    quarter, full = grad_middle.shape
    narrow, tall = full // 4, 4 * quarter
    depth = proj_own.shape[2]

    def tokens(core):
        def lap(q, carry):
            total = times_flipped(
                grad_v[strip(core, tall), :], wxy_v[strip(q, narrow), :]
            ).astype(LOW)
            for r in range(4):
                partial[core, r, :, lanes(q, narrow)] = total[r * quarter : (r + 1) * quarter]
            return carry

        lax.fori_loop(0, 4, lap, 0)

    def proj():
        for load in loads:
            load.wait()

        def lap(q, carry):
            total = left_product(nf_v[:, lanes(q, narrow)], grad_v[...]).astype(LOW)
            for b in range(count):
                proj_own[b, q] = total[b * depth : (b + 1) * depth]
            return carry

        lax.fori_loop(0, 4, lap, 0)

    first_norm_back(
        count, partial, x_own, grad_middle, vectors, None, down_partial, *rest, None, None, None, links,
        tokens, proj,
    )


def gelu(v):
    return 0.5 * v * (1.0 + jnp.tanh(ROOT * (v + CUBE * (v * v * v))))


def gelu_slope(v):
    t = jnp.tanh(ROOT * (v + CUBE * (v * v * v)))
    return 0.5 * (1.0 + t) + 0.5 * v * (1.0 - t * t) * (ROOT * (1.0 + 3.0 * CUBE * (v * v)))


def block_of(blocks, h):
    width = blocks.shape[-1]
    return blocks[h].reshape(width, width)


def forward(
    count, taps, x, cot, wxy, wout, wgate, wup, wdown, blk, cvec, wvec, spots,
    nf_out, x_out, cot_all, wxy_out, wout_out, gate_all, up_own, down_all, blocks_out, vectors_out,
    width_out, branch_out, gelu_out, side_out, conv_out, in_out, dec_out, state_out, entering_out,
    mixed_out, middle_out, normed_out,
    x_all, nf, wxy_all, wout_all, blocks, cvec_all, wvec_all, vectors, width, stage, arrived, branch,
    gelu_in, side, conv, in_gate, dec_gate, state, running, local_state, ends, table, entering, mixed,
    mixed_all, partial, theirs, here, wide, middle, normed, gate_here, up_here, down_here, cot_here,
    send, recv, local,
):
    place = Place(count)
    links = Links(send, recv, local)
    row, z, col = place.row, place.dp, place.col
    greet(place, rows=True, line=True, cores=True)
    tall, narrow = x.shape
    full = 4 * narrow
    half, quarter = tall // 2, tall // 4
    depth, part = wxy.shape[1], wxy.shape[2] // 2
    tokens, steps = 2 * tall, tall // 2
    heads, block = blocks.shape[0] // 2, blocks.shape[-1]
    share = blocks.shape[3]
    kept = []

    def keep(src, dst):
        kept.append(links.keep(src, dst))
        return kept[-1]

    def projections():
        def at(q, b):
            return wxy_all.at[q, strip(b, depth, 8)]

        mine = links.keep(wxy.at[row], at(row, z))
        yield from exchange_rows(links, place, lambda q: wxy.at[q], lambda q: at(q, z))
        mine.wait()

        def piece(b):
            return wxy_all.at[:, strip(b, depth, 8)]

        yield from gather_line(links, place, piece(z), piece)

    def inputs():
        def at(q, core):
            return x_all.at[strip(core, tall), lanes(q, narrow)]

        mine = links.keep(x, at(row, col))
        shared = [links.copy(x, at(row, col), col=place.other)]
        shared[0].start()
        yield from gather_rows(
            links,
            place,
            lambda h: x.at[pl.ds(half * h, half)],
            lambda q, h: x_all.at[strip(2 * col + h, half), lanes(q, narrow)],
        )
        for k in range(1, 4):
            q = place.near[k]
            shared.append(links.copy(at(q, col), at(q, col), col=place.other))
            shared[-1].start()
        yield 1
        mine.wait()
        for copy in shared:
            copy.wait_recv()
        for copy in shared:
            copy.wait_send()

    def channel_vectors():
        keep(cvec, cvec_all.at[z])
        yield from exchange_line(links, place, lambda b: cvec, lambda b: cvec_all.at[b])

    def width_vectors():
        mine = links.keep(wvec, wvec_all.at[row, z])
        yield from exchange_line(links, place, lambda b: wvec, lambda b: wvec_all.at[row, b])
        mine.wait()
        yield from exchange_rows(
            links, place, lambda q: wvec_all.at[row], lambda q: wvec_all.at[q]
        )

    def gate_blocks():
        split = blocks.shape[2] > 1
        own = row if split else 0
        mine = links.keep(blk, blocks.at[:, z, own])
        yield from exchange_line(links, place, lambda b: blk, lambda b: blocks.at[:, b, own])
        mine.wait()
        middle = count // 2
        if split:

            def at(q, h):
                return blocks.at[:, pl.ds(middle * h, middle), q]

            yield from gather_rows(links, place, lambda h: at(row, h), at)

    def hidden_rows():
        parts = halves(wdown.shape[0])
        mine = Relay(links, wdown, down_here, down_all.at[:, lanes(row, narrow)])
        kept.append(mine)
        yield from gather_rows(
            links,
            place,
            lambda h: wdown.at[parts[h]],
            lambda q, h: down_all.at[parts[h], lanes(q, narrow)],
        )

    def cotangent_rows():
        def spot(q):
            return cot_all.at[strip(2 * z + col, quarter), lanes(q, narrow)]

        mine = Relay(links, cot.at[strip(row, quarter)], cot_here, spot(row))
        yield from exchange_rows(links, place, lambda q: cot.at[strip(q, quarter)], spot)
        mine.wait()

    def hidden_columns(matrix, buffer, own):
        mine = Relay(links, matrix.at[z], buffer, own.at[z])
        yield from exchange_line(links, place, lambda b: matrix.at[b], lambda b: own.at[b])
        mine.wait()

    def all_hidden_columns(matrix, buffer, whole):
        yield from hidden_columns(matrix, buffer, whole.at[row])
        middle = count // 2

        def at(q, h):
            return whole.at[q, pl.ds(middle * h, middle)]

        yield from gather_rows(links, place, lambda h: at(row, h), at)

    def cot_block(b):
        return cot_all.at[strip(2 * b + col, quarter)]

    def output_rows():
        at = wout.shape[0]
        mine = links.keep(wout, wout_all.at[strip(z, at)])
        yield from gather_line(links, place, wout, lambda b: wout_all.at[strip(b, at)])
        mine.wait()

    weights, rows_in = projections(), inputs()
    vectors_in, widths_in, blocks_in = channel_vectors(), width_vectors(), gate_blocks()
    cot_in, output_in, down_in = cotangent_rows(), output_rows(), hidden_rows()
    gate_in = all_hidden_columns(wgate, gate_here, gate_all)
    cots = LineGather(links, place, cot_block(z), cot_block)
    up_in = hidden_columns(wup, up_here, up_own)
    advance(weights, rows_in, widths_in, vectors_in, blocks_in, cot_in)
    advance(weights, widths_in, vectors_in, blocks_in)
    finish(widths_in, vectors_in)
    for copy in kept:
        copy.wait()
    kept.clear()

    for b in range(count):
        size = vectors.shape[1] // count
        vectors[:, b * size : (b + 1) * size] = cvec_all[b, :, :size]
        for q in range(4):
            at = q * narrow + b * depth
            width[:, at : at + depth] = wvec_all[q, b, :, :depth]
    keep(vectors, vectors_out)
    keep(width, width_out)
    advance(rows_in)
    advance(weights)
    finish(rows_in)
    advance(down_in)
    keep(x_all.at[strip(4 * col + row, quarter)], x_out)

    nf[0:16, :] = jnp.zeros((16, full), LOW)

    def first_norm(rows):
        value = x_all[rows].astype(WIDE)
        mean = jnp.sum(value * value, axis=1, keepdims=True) / full
        value = value * lax.rsqrt(mean + epsilon) * (1.0 + width[0:1, :])
        nf[pl.ds(pl.multiple_of(rows.start + 16, 16), rows.size)] = value.astype(LOW)

    by_rows(tokens, first_norm)
    keep(nf.at[pl.ds(16, tokens)], nf_out)
    advance(weights, blocks_in, cot_in)
    finish(blocks_in)
    keep(blocks, blocks_out)
    finish(weights, cot_in)
    keep(wxy_all, wxy_out)

    advance(output_in)
    advance(down_in)
    out = []
    for k in (3, 2, 1, 0):
        q = place.near[k]

        def product(k=k, q=q):
            stage[k] = jnp.dot(
                nf[pl.ds(pl.multiple_of(q * steps, 16), steps + 16), :],
                wxy_all[...].astype(LOW).reshape(full, 2 * part),
                preferred_element_type=WIDE,
            )

        product()
        source = stage.at[k, pl.ds(8, steps + 8)]
        if k:
            out.append(links.copy(source, arrived.at[row], row=q))
            out[-1].start()
        else:
            mine = links.keep(source, arrived.at[row])
    advance(output_in, gate_in)
    cots.start()
    mine.wait()
    for copy in out:
        copy.wait_recv()
    finish(down_in)
    for copy in out:
        copy.wait_send()

    spot = spots[...]
    starting = spot == 0
    for q in range(4):
        at = slice(q * part, (q + 1) * part)
        branch[:, at] = arrived[q, :, :part]
        gelu_in[:, at] = arrived[q, 8:, part:] + vectors[taps + 2 : taps + 3, at]
    keep(branch, branch_out)
    keep(gelu_in, gelu_out)
    ends[...] = jnp.zeros(ends.shape, WIDE)
    entering[...] = jnp.zeros(ends.shape, WIDE)

    def one_head(h, at):
        def vector(i):
            return vectors[i : i + 1, at]

        conv_here = vector(taps) + vector(0) * (branch[8:, at] + vector(taps + 1))
        for k in range(1, taps):
            earlier = branch[8 - k : 8 - k + steps, at] + vector(taps + 1)
            conv_here = conv_here + vector(k) * jnp.where(spot >= k, earlier, 0.0)
        conv[:, at] = conv_here
        low = conv_here.astype(LOW)
        input_gate = jax.nn.sigmoid(
            jnp.dot(low, block_of(blocks, h), preferred_element_type=WIDE) + vector(taps + 3)
        )
        decay_gate = jax.nn.sigmoid(
            jnp.dot(low, block_of(blocks, heads + h), preferred_element_type=WIDE)
            + vector(taps + 4)
        )
        in_gate[:, at] = input_gate
        dec_gate[:, at] = decay_gate
        log_decay = vector(taps + 5) * decay_gate
        decay = jnp.where(starting, 0.0, jnp.exp(log_decay))
        multiplier = jnp.where(starting, 1.0, jnp.sqrt(minus_expm1(2.0 * log_decay)))
        reach, value = scan_rows(decay, multiplier * input_gate * conv_here, False)
        running[:, at] = reach
        local_state[:, at] = value
        ends[0:1, at] = reach[steps - 1 :, :]
        ends[1:2, at] = value[steps - 1 :, :]
        side[:, at] = gelu(gelu_in[:, at])

    each_head(heads, block, one_head)
    for scratch, output in (
        (conv, conv_out), (in_gate, in_out), (dec_gate, dec_out), (side, side_out),
    ):
        keep(scratch, output)
    own = links.keep(ends, table.at[row])
    advance(output_in)
    own.wait()
    entering[0:1, :] = carry_over(links, place, ends, table, False)

    def mix(h, at):
        value = local_state[:, at] + running[:, at] * entering[0:1, at]
        state[:, at] = value
        mixed[:, at] = (value * side[:, at]).astype(LOW)

    each_head(heads, block, mix)
    mine = links.keep(mixed, mixed_all.at[strip(row, steps)])
    mixes = gather_rows(
        links,
        place,
        lambda h: mixed.at[pl.ds(steps // 2 * h, steps // 2)],
        lambda q, h: mixed_all.at[strip(2 * q + h, steps // 2)],
    )
    advance(mixes)
    keep(state, state_out)
    keep(entering, entering_out)
    finish(output_in)
    keep(wout_all, wout_out)
    advance(mixes, up_in)
    finish(mixes)
    mine.wait()
    cots.step(1)
    advance(gate_in)
    keep(mixed_all, mixed_out)

    def product_rows(first):
        def body(i, carry):
            rows = pl.ds(pl.multiple_of(first * tall + i * steps, 16), steps)
            partial[rows] = jnp.dot(mixed_all[rows], wout_all[...], preferred_element_type=WIDE)
            return carry

        lax.fori_loop(0, tall // steps, body, 0)

    product_rows(place.other)
    swap = links.copy(partial.at[strip(place.other, tall)], theirs, col=place.other)
    swap.start()
    product_rows(col)
    swap.wait_recv()

    def add(rows):
        at = pl.ds(pl.multiple_of(col * tall + rows.start, 16), rows.size)
        here[rows] = partial[at] + theirs[rows] + x_all[at, lanes(row, narrow)].astype(WIDE)

    by_rows(tall, add)

    def quarter_of(q):
        return here.at[strip(q, quarter)]

    mine = links.keep(quarter_of(row), wide.at[:, lanes(row, narrow)])
    middles = exchange_rows(links, place, quarter_of, lambda q: wide.at[:, lanes(q, narrow)])
    advance(middles)
    mine.wait()
    finish(middles)
    swap.wait_send()

    def second_norm(rows):
        value = wide[rows] + width[1:2, :]
        middle[rows] = value
        mean = jnp.sum(value * value, axis=1, keepdims=True) / full
        normed[rows] = (value * lax.rsqrt(mean + epsilon) * (1.0 + width[3:4, :])).astype(LOW)

    by_rows(quarter, second_norm)
    keep(middle, middle_out)
    keep(normed, normed_out)
    advance(gate_in)
    for step in range(2, count):
        cots.step(step)
    finish(gate_in, up_in)
    for step in range(count):
        cots.ready(step)
    cots.close()
    for copy in kept:
        copy.wait()


def feed_forward(
    count, normed, cot_all, gate_all, up_own, wdown, biases, normed_all, up_all, hidden_out, gate_out,
    up_out, sums, gate_w, up_w, down_w, piece, gate_v, up_v, grad_v, hidden, grad_gate, grad_up, normed_here,
    send, recv, local,
):
    place = Place(count)
    links = Links(send, recv, local)
    row, z, col = place.row, place.dp, place.col
    quarter, full = normed.shape
    narrow, pair = full // 4, 2 * quarter
    units = wdown.shape[0]
    middle = count // 2
    load = links.keep(wdown, down_w)
    kept = [links.keep(gate_all, gate_w), links.keep(up_own, up_w.at[row])]
    greet(place, rows=True, line=True, cores=True)

    def tokens(own, buffer, whole):
        def at(b):
            return whole.at[strip(2 * b + col, quarter)]

        relay = Relay(links, own, buffer, at(z))
        return LineGather(links, place, own, at), relay

    def columns_of(own, whole):
        yield from gather_rows(
            links,
            place,
            lambda h: own.at[pl.ds(middle * h, middle)],
            lambda q, h: whole.at[q, pl.ds(middle * h, middle)],
        )

    def neighbours(step, body):
        if step == 0:
            body(z)
            return

        def lap(i, carry):
            b = z - step + 2 * step * i
            pl.when((b >= 0) & (b < count))(lambda: body(place.turn(b)))
            return carry

        lax.fori_loop(0, 2, lap, 0)

    def with_piece(source, body):
        k, links.kept = links.kept, links.kept + 1

        def inner(b):
            load = pltpu.make_async_copy(source.at[strip(b, pair)], piece, links.local.at[k])
            load.start()
            load.wait()
            body(strip(b, pair))

        return inner

    def inward(whole, i, values):
        def body(rows):
            weight = whole[...].astype(LOW).reshape(full, units)
            values[rows] = (
                jnp.dot(piece[...], weight, preferred_element_type=WIDE) + biases[i : i + 1, :]
            )

        return body

    def backward(rows):
        grad_v[rows] = lax.dot_general(
            piece[...], down_w[...], (((1,), (1,)), ((), ())), preferred_element_type=WIDE
        )

    def outward(rows):
        def body(inner):
            at = pl.ds(pl.multiple_of(rows.start + inner.start, 16), inner.size)
            gate, up, grad = gate_v[at], up_v[at], grad_v[at]
            t = jnp.tanh(ROOT * (gate + CUBE * (gate * gate * gate)))
            side = 0.5 * gate * (1.0 + t)
            slope = 0.5 * (1.0 + t) + 0.5 * gate * (1.0 - t * t) * (
                ROOT * (1.0 + 3.0 * CUBE * (gate * gate))
            )
            hidden[at] = (side * up).astype(LOW)
            gate, up = grad * up * slope, grad * side
            grad_gate[at] = gate.astype(LOW)
            grad_up[at] = up.astype(LOW)
            sums[0:1, :] += jnp.sum(gate, axis=0, keepdims=True)
            sums[1:2, :] += jnp.sum(up, axis=0, keepdims=True)

        by_rows(pair, body)

    ups = columns_of(up_own, up_w)
    norms, norm_relay = tokens(normed, normed_here, normed_all)
    norms.start()
    advance(ups)
    norm_relay.wait()
    sums[...] = jnp.zeros(sums.shape, WIDE)
    load.wait()
    back = with_piece(cot_all, backward)
    into = with_piece(normed_all, inward(gate_w, 0, gate_v))

    def backs(first, last):
        def lap(b, carry):
            back(b)
            return carry

        lax.fori_loop(first, last, lap, 0)

    backs(0, middle)
    norms.step(1)
    backs(middle, count)
    for copy in kept:
        copy.wait()
    kept.clear()
    for step in range(count):
        if step > 1:
            norms.step(step)
        if step == 2:
            advance(ups)
        norms.ready(step)
        neighbours(step, into)
    finish(ups)
    kept.append(links.keep(up_w, up_all))
    into_up = with_piece(normed_all, inward(up_w, 1, up_v))

    def last(b, carry):
        into_up(b)
        outward(strip(b, pair))
        return carry

    lax.fori_loop(0, count, last, 0)
    norms.close()
    kept.append(links.keep(hidden, hidden_out))
    kept.append(links.keep(grad_gate, gate_out))
    kept.append(links.keep(grad_up, up_out))
    for copy in kept:
        copy.wait()


def side_by_side(blocks):
    return jnp.concatenate([blocks[i] for i in range(blocks.shape[0])], axis=1)


def columns(matrix, parts):
    width = matrix.shape[1] // parts
    return jnp.stack([matrix[:, i * width : (i + 1) * width] for i in range(parts)])


def padded_rows(rows, height, width):
    return jnp.pad(rows, ((0, height - rows.shape[0]), (0, width - rows.shape[1])))


def rounded(values):
    return lax.reduce_precision(values, 8, 7)


def round_up(size, step):
    return -(-size // step) * step


def shards(
    inputs,
    positions,
    branch_matrix,
    gelu_matrix,
    output_matrix,
    gate_matrix,
    up_matrix,
    down_matrix,
    input_blocks,
    decay_blocks,
    conv_taps,
    conv_bias,
    branch_bias,
    gelu_bias,
    input_bias,
    decay_bias,
    decay_param,
    output_bias,
    gate_bias,
    up_bias,
    down_bias,
    norm_first,
    norm_second,
    cotangent,
):
    count, rows_count, cores = lax.axis_size("dp"), lax.axis_size("row"), lax.axis_size("col")
    place_dp, place_row = lax.axis_index("dp"), lax.axis_index("row")
    tall, narrow = inputs.shape
    quarter, full, tokens = tall // rows_count, narrow * rows_count, tall * cores
    depth, width = branch_matrix.shape
    part = width // rows_count
    hidden_part = down_matrix.shape[0]
    heads, block_part, block = input_blocks.shape
    taps = conv_taps.shape[0]
    steps = positions.shape[0]
    splits = rows_count if block_part % (16 * rows_count) == 0 else 1
    share = block_part // splits
    back_share = block_part // rows_count
    remote, local = 64 + 24 * count, 40 + 6 * count

    wxy = jnp.concatenate(
        (columns(branch_matrix.astype(LOW), rows_count), columns(gelu_matrix.astype(LOW), rows_count)),
        axis=2,
    )
    if depth % 16:
        wxy = wxy.astype(WIDE)
    blocks_low = jnp.concatenate((input_blocks, decay_blocks), axis=0).astype(LOW)
    blk = lax.dynamic_slice_in_dim(
        blocks_low, place_row * share if splits > 1 else 0, share, 1
    )
    channel_rows = jnp.concatenate(
        (
            conv_taps,
            jnp.stack((conv_bias, branch_bias, gelu_bias, input_bias, decay_bias)),
        ),
        axis=0,
    )
    decay_raw = rounded(decay_param)
    channel_rows = jnp.concatenate(
        (rounded(channel_rows), -8.0 * jax.nn.softplus(decay_raw)[None, :]), axis=0
    )
    channel_size = channel_rows.shape[1]
    cvec = padded_rows(
        channel_rows,
        round_up(taps + 6, 8),
        round_up(channel_size, 128),
    )
    wvec = padded_rows(
        rounded(jnp.stack((norm_first, output_bias, down_bias, norm_second))),
        8,
        round_up(depth, 128),
    )
    spots = positions[:, None]
    heads_all = 2 * heads
    whole_tokens = ((tokens, full), LOW, False)
    wide_tokens = ((steps, width), WIDE, False)
    nf_shape = pltpu.VMEM((16 + tokens, full), LOW)
    wxy_kind = wxy.dtype
    tokens_scratch = pltpu.VMEM((steps, width), WIDE)
    eight_rows = pltpu.VMEM((8, width), WIDE)
    table_rows = pltpu.VMEM((rows_count, 8, width), WIDE)
    blocks_shape = (heads_all, count, splits, share, block)
    hidden_shape = (rows_count, count, depth, hidden_part)
    here_scratch = pltpu.VMEM((tall, narrow), WIDE)
    (
        normed_first, x_own, cot_all, wxy_all, wout_all, gate_all, up_own, down_all, blocks, vectors,
        width_all, branch, gelu_in, side, conv, input_gate, decay_gate, state, entering, mixed_all,
        middle, normed_own,
    ) = call(
        functools.partial(forward, count, taps),
        "forward",
        1,
        [
            (inputs, False),
            (cotangent, False),
            (wxy, False),
            (output_matrix.astype(LOW), False),
            (columns(gate_matrix.astype(LOW), count).astype(wxy_kind), False),
            (columns(up_matrix.astype(LOW), count).astype(wxy_kind), False),
            (down_matrix.astype(LOW), False),
            (blk, False),
            (cvec, False),
            (wvec, False),
            (spots, True),
        ],
        [
            whole_tokens,
            ((quarter, full), LOW, False),
            ((cores * count * quarter, full), LOW, False),
            ((rows_count, count * depth, 2 * part), wxy_kind, False),
            ((width, narrow), LOW, False),
            (hidden_shape, wxy_kind, False),
            (hidden_shape[1:], wxy_kind, False),
            ((hidden_part, full), LOW, False),
            (blocks_shape, LOW, False),
            ((cvec.shape[0], width), WIDE, False),
            ((8, full), WIDE, False),
            ((steps + 8, width), WIDE, False),
            wide_tokens,
            wide_tokens,
            wide_tokens,
            wide_tokens,
            wide_tokens,
            wide_tokens,
            ((8, width), WIDE, False),
            ((tokens, width), LOW, False),
            ((quarter, full), WIDE, False),
            ((quarter, full), LOW, False),
        ],
        [
            pltpu.VMEM((tokens, full), LOW),
            nf_shape,
            pltpu.VMEM((rows_count, count * depth, 2 * part), wxy_kind),
            pltpu.VMEM((width, narrow), LOW),
            pltpu.VMEM(blocks_shape, LOW),
            pltpu.VMEM((count,) + cvec.shape, WIDE),
            pltpu.VMEM((rows_count, count) + wvec.shape, WIDE),
            pltpu.VMEM((cvec.shape[0], width), WIDE),
            pltpu.VMEM((8, full), WIDE),
            pltpu.VMEM((rows_count, steps + 16, 2 * part), WIDE),
            pltpu.VMEM((rows_count, steps + 8, 2 * part), WIDE),
            pltpu.VMEM((steps + 8, width), WIDE),
            tokens_scratch,
            tokens_scratch,
            tokens_scratch,
            tokens_scratch,
            tokens_scratch,
            tokens_scratch,
            tokens_scratch,
            tokens_scratch,
            eight_rows,
            table_rows,
            eight_rows,
            pltpu.VMEM((steps, width), LOW),
            pltpu.VMEM((tokens, width), LOW),
            pltpu.VMEM((tokens, narrow), WIDE),
            here_scratch,
            here_scratch,
            pltpu.VMEM((quarter, full), WIDE),
            pltpu.VMEM((quarter, full), WIDE),
            pltpu.VMEM((quarter, full), LOW),
            pltpu.VMEM((depth, hidden_part), wxy_kind),
            pltpu.VMEM((depth, hidden_part), wxy_kind),
            pltpu.VMEM((hidden_part, narrow), LOW),
            pltpu.VMEM((quarter, narrow), LOW),
        ],
        remote,
        local,
    )
    wxy_all = wxy_all.reshape(full, 2 * part).astype(LOW)
    blocks = blocks.reshape(heads_all, block, block)
    gelu_pull = jax.vjp(jax.nn.gelu, gelu_in)[1]

    hidden_tokens = cores * count * quarter
    units_rows = ((hidden_tokens, hidden_part), LOW, False)
    biases = padded_rows(rounded(jnp.stack((gate_bias, up_bias))), 8, hidden_part)
    weight_scratch = pltpu.VMEM(hidden_shape, wxy_kind)
    units_wide = pltpu.VMEM((hidden_tokens, hidden_part), WIDE)
    units_low = pltpu.VMEM((hidden_tokens, hidden_part), LOW)
    (
        normed_second, up_all, hidden, grad_gate_low, grad_up_low, hidden_part_sums,
    ) = call(
        functools.partial(feed_forward, count),
        "feed_forward",
        2,
        [
            (normed_own, False),
            (cot_all, False),
            (gate_all, False),
            (up_own, False),
            (down_all, False),
            (biases, True),
        ],
        [
            ((hidden_tokens, full), LOW, False),
            (hidden_shape, wxy_kind, False),
            units_rows,
            units_rows,
            units_rows,
            ((8, hidden_part), WIDE, True),
        ],
        [
            weight_scratch,
            weight_scratch,
            pltpu.VMEM((hidden_part, full), LOW),
            pltpu.VMEM((cores * quarter, full), LOW),
            units_wide,
            units_wide,
            units_wide,
            units_low,
            units_low,
            units_low,
            pltpu.VMEM((quarter, full), LOW),
        ],
        remote,
        local,
    )
    by_device = (count, cores, quarter, full)
    token_scratch = [
        pltpu.VMEM((count, quarter, full), LOW),
        pltpu.VMEM((count, quarter, full), LOW),
        *line_buffers(count, 2, quarter // 2, full),
    ]
    token_low = pltpu.VMEM((quarter, full), LOW)
    back_outs = [
        ((quarter, full), WIDE, True),
        ((tokens, narrow), LOW, False),
        ((8, full), WIDE, True),
        ((2, narrow // 2, hidden_part), LOW, True),
    ]
    back_scratch = token_scratch + [token_low, token_low, row_buffers(narrow, hidden_part)]
    inside = count <= 4
    if inside:
        grad_middle, grad_middle_all, width_sums, gate_own, forward_partial = call(
            functools.partial(second_norm_back_inside, count),
            "second_norm_back",
            5,
            [
                (grad_gate_low, False),
                (grad_up_low, False),
                (gate_all, False),
                (up_all, False),
                (normed_second, False),
                (hidden, False),
                (down_all, False),
                (cot_all, False),
                (middle, True),
                (width_all, True),
            ],
            back_outs + [((hidden_tokens, full), LOW, False)],
            back_scratch
            + [
                units_low,
                units_low,
                weight_scratch,
                weight_scratch,
                pltpu.VMEM((hidden_tokens, narrow), LOW),
                pltpu.VMEM(by_device, LOW),
                pltpu.VMEM((full, hidden_part), LOW),
                units_low,
                pltpu.VMEM((hidden_part, narrow), LOW),
                pltpu.VMEM((hidden_tokens, narrow), LOW),
            ],
            remote,
            local,
        )
    else:
        forward_partial = times(hidden, down_all).astype(LOW)
        gate_all = gate_all.reshape(full, hidden_part).astype(LOW)
        up_all = up_all.reshape(full, hidden_part).astype(LOW)
        grad_normed_second = (
            (times_flipped(grad_gate_low, gate_all) + times_flipped(grad_up_low, up_all))
            .astype(LOW)
            .reshape(by_device)
        )
        grad_middle, grad_middle_all, width_sums, gate_own = call(
            functools.partial(second_norm_back, count),
            "second_norm_back",
            5,
            [
                (grad_normed_second, False),
                (cot_all, False),
                (middle, True),
                (width_all, True),
                (left_product(normed_second, grad_gate_low).astype(LOW), False),
            ],
            back_outs,
            back_scratch,
            remote,
            local,
        )
    forward_partial = forward_partial.reshape(by_device)

    mixed_outs = [
        ((2, steps // 2, width), WIDE, True),
        ((rows_count, quarter, narrow), LOW, False),
        ((2, narrow // 2, hidden_part), LOW, True),
        ((count, depth, hidden_part), LOW, False),
    ]
    mixed_scratch = (
        [row_buffers(steps, width)]
        + token_scratch
        + [token_low, row_buffers(narrow, hidden_part), pltpu.VMEM((depth, hidden_part), LOW)]
    )
    gate_own = gate_own.reshape(count, depth, hidden_part)
    if inside:
        grad_mixed, layer_out, up_own, gate_blocks, output_partial, down_partial = call(
            functools.partial(mixed_and_output_inside, count),
            "mixed_and_output",
            6,
            [
                (grad_middle_all, False),
                (wout_all, False),
                (mixed_all, False),
                (normed_second, False),
                (cot_all, False),
                (grad_up_low, False),
                (hidden, False),
                (forward_partial, False),
                (middle, True),
                (width_all, True),
                (gate_own, False),
            ],
            mixed_outs + [((width, narrow), LOW, False), ((hidden_part, full), LOW, False)],
            mixed_scratch
            + [
                pltpu.VMEM((tokens, narrow), LOW),
                pltpu.VMEM((width, narrow), LOW),
                pltpu.VMEM((tokens, width), LOW),
                pltpu.VMEM((hidden_tokens, narrow), LOW),
                units_low,
                units_low,
                pltpu.VMEM((tokens, width), LOW),
                pltpu.VMEM((full, hidden_part), LOW),
                pltpu.VMEM((width, narrow), LOW),
                pltpu.VMEM((hidden_part, full), LOW),
            ],
            remote,
            local,
        )
    else:
        down_partial = left_product(hidden, cot_all).astype(LOW)
        output_partial = left_product(mixed_all, grad_middle_all).astype(LOW)
        grad_mixed, layer_out, up_own, gate_blocks = call(
            functools.partial(mixed_and_output, count),
            "mixed_and_output",
            6,
            [
                (times_flipped(grad_middle_all, wout_all).astype(LOW), False),
                (forward_partial, False),
                (middle, True),
                (width_all, True),
                (left_product(normed_second, grad_up_low).astype(LOW), False),
                (gate_own, False),
            ],
            mixed_outs,
            mixed_scratch,
            remote,
            local,
        )
    up_own = up_own.reshape(count, depth, hidden_part)
    grad_mixed = grad_mixed.reshape(steps, width)

    sums_rows = round_up(taps + 6, 8)
    output_parts = 2 if output_matrix.shape[0] % 32 == 0 else 1
    if inside:
        channel_part, block_sums, grad_projected, output_grad, up_blocks = call(
            functools.partial(recurrence_back_inside, count, taps),
            "recurrence_backward",
            7,
            [
                (branch, False),
                (side, False),
                (gelu_in, False),
                (spots, True),
                (vectors, True),
                (blocks, False),
                (conv, False),
                (input_gate, False),
                (decay_gate, False),
                (state, False),
                (entering, True),
                (grad_mixed, False),
            ]
            + [
                (output_partial.reshape((count,) + output_matrix.shape), False),
                (up_own, False),
            ],
            [
                ((sums_rows, width), WIDE, True),
                ((2 * heads, block, block), WIDE, True),
                ((rows_count, steps, 2 * part), LOW, False),
                (output_matrix.shape, WIDE, True),
                ((count, depth, hidden_part), LOW, False),
            ],
            [
                pltpu.VMEM((steps, width), LOW),
                pltpu.VMEM((steps, width), LOW),
                pltpu.VMEM((rows_count, steps, 2 * part), LOW),
                tokens_scratch,
                tokens_scratch,
                tokens_scratch,
                eight_rows,
                table_rows,
                pltpu.VMEM((2, 8, width), WIDE),
                eight_rows,
                pltpu.VMEM((steps + 8, block), WIDE),
                pltpu.VMEM((steps + 8, block), WIDE),
                *line_buffers(count, output_parts, output_matrix.shape[0] // output_parts, narrow),
                pltpu.VMEM((count,) + output_matrix.shape, LOW),
                pltpu.VMEM((depth, hidden_part), LOW),
                pltpu.VMEM((steps + 8, width), WIDE),
                tokens_scratch,
                tokens_scratch,
                pltpu.VMEM((2 * heads, block, block), LOW),
                tokens_scratch,
                tokens_scratch,
                tokens_scratch,
                tokens_scratch,
                tokens_scratch,
            ],
            remote,
            local,
        )
        grad_projected = grad_projected.reshape(tokens, 2 * part)
    else:
        grad_gelu = gelu_pull(grad_mixed * state)[0]
        grad_branch_low, channel_part, block_sums = call(
            functools.partial(recurrence_backward, count, taps),
            "recurrence_backward",
            7,
            [
                (array, True)
                for array in (
                    branch,
                    side,
                    spots,
                    vectors,
                    blocks,
                    conv,
                    input_gate,
                    decay_gate,
                    state,
                    entering,
                    grad_mixed,
                )
            ],
            [
                ((steps, width), LOW, True),
                ((round_up(taps + 6, 8), width), WIDE, True),
                ((2 * heads, block, block), WIDE, True),
            ],
            [
                tokens_scratch,
                tokens_scratch,
                tokens_scratch,
                eight_rows,
                table_rows,
                pltpu.VMEM((2, 8, width), WIDE),
                eight_rows,
                pltpu.VMEM((steps + 8, block), WIDE),
                pltpu.VMEM((steps + 8, block), WIDE),
            ],
            remote,
            local,
        )
        grad_gelu_low = grad_gelu.astype(LOW)
        projected_grads = jnp.concatenate(
            (columns(grad_branch_low, rows_count), columns(grad_gelu_low, rows_count)), axis=2
        )
        grad_projected, output_grad, up_blocks = call(
            functools.partial(spread_gradients, count),
            "spread_gradients",
            8,
            [
                (projected_grads, False),
                (output_partial.reshape((count,) + output_matrix.shape), False),
                (up_own, False),
            ],
            [
                ((rows_count, steps, 2 * part), LOW, False),
                (output_matrix.shape, WIDE, True),
                ((count, depth, hidden_part), LOW, False),
            ],
            [
                *line_buffers(count, output_parts, output_matrix.shape[0] // output_parts, narrow),
                pltpu.VMEM((count,) + output_matrix.shape, LOW),
            ],
            remote,
            local,
        )
        grad_projected = grad_projected.reshape(tokens, 2 * part)
        channel_part = channel_part.at[taps + 5].set(jnp.sum(grad_gelu, axis=0))
    hidden_part_sums = padded_rows(hidden_part_sums, 8, round_up(hidden_part, 128))
    block_in = (
        block_sums.astype(LOW)
        .reshape(2 * heads, count, rows_count, back_share, block)
        .transpose(2, 1, 0, 3, 4)
        .reshape(rows_count, count, 2 * heads * back_share, block)
    )
    channel_shape, sums_shape = channel_part.shape, hidden_part_sums.shape
    block_rows = 2 * heads * back_share
    first_outs = [
        ((rows_count, quarter, narrow), LOW, False),
        ((rows_count, depth, 2 * part), LOW, False),
        ((hidden_part, narrow), WIDE, True),
        ((2, 8, narrow), WIDE, True),
        (channel_shape, WIDE, True),
        ((rows_count, block_rows, block), LOW, False),
        (sums_shape, WIDE, True),
    ]
    first_scratch = [
        pltpu.VMEM((rows_count, quarter, full), LOW),
        pltpu.VMEM((rows_count, quarter, full), LOW),
        pltpu.VMEM((rows_count, quarter, full), LOW),
        row_buffers(quarter, full),
        token_low,
        pltpu.VMEM((rows_count, quarter, narrow), LOW),
        pltpu.VMEM((8, full), WIDE),
        pltpu.VMEM((count, rows_count, depth, 2 * part), LOW),
        *line_buffers(count, rows_count, depth, 2 * part),
        pltpu.VMEM((rows_count, depth, 2 * part), LOW),
        pltpu.VMEM((rows_count, 8, narrow), WIDE),
        pltpu.VMEM((count, 8, narrow), WIDE),
        pltpu.VMEM((rows_count, 8, narrow), WIDE),
        pltpu.VMEM((rows_count,) + channel_shape, WIDE),
        pltpu.VMEM((count,) + channel_shape, WIDE),
        pltpu.VMEM((rows_count,) + sums_shape, WIDE),
        pltpu.VMEM(block_in.shape, LOW),
        pltpu.VMEM(block_in.shape[1:], LOW),
        pltpu.VMEM(block_in.shape[1:], LOW),
        pltpu.VMEM((block_rows, block), LOW),
        row_buffers(hidden_part, narrow),
    ]
    sums_in = [
        (width_sums, True),
        (channel_part, True),
        (hidden_part_sums, True),
        (block_in, False),
    ]
    if inside:
        first_kernel, first_ins = first_norm_back_inside, [
            (grad_projected, False),
            (wxy_all, False),
            (normed_first, False),
            (x_own, False),
            (grad_middle, True),
            (width_all, True),
            (down_partial, False),
        ]
        first_scratch += [
            pltpu.VMEM((tokens, 2 * part), LOW),
            pltpu.VMEM((full, 2 * part), LOW),
            pltpu.VMEM((tokens, full), LOW),
            pltpu.VMEM((cores, rows_count, quarter, full), LOW),
        ]
    else:
        first_kernel, first_ins = first_norm_back, [
            (
                times_flipped(grad_projected, wxy_all)
                .astype(LOW)
                .reshape(cores, rows_count, quarter, full),
                False,
            ),
            (x_own, False),
            (grad_middle, True),
            (width_all, True),
            (
                left_product(normed_first, grad_projected)
                .astype(LOW)
                .reshape(rows_count, count, depth, 2 * part),
                False,
            ),
            (down_partial, False),
        ]
    input_grad, proj_grad, down_grad, width_sums, channel_sums, block_grads, hidden_sums = call(
        functools.partial(first_kernel, count),
        "first_norm_back",
        9,
        first_ins + sums_in,
        first_outs,
        first_scratch,
        remote,
        local,
    )
    branch_grad = side_by_side(proj_grad[:, :, :part].astype(WIDE))
    gelu_grad = side_by_side(proj_grad[:, :, part:].astype(WIDE))
    block_grads = (
        block_grads.reshape(rows_count, 2 * heads, back_share, block)
        .transpose(1, 0, 2, 3)
        .reshape(2 * heads, block_part, block)
        .astype(WIDE)
    )
    channel_sums = lax.dynamic_slice_in_dim(channel_sums, place_dp * channel_size, channel_size, 1)
    width_sums = lax.dynamic_slice_in_dim(
        width_sums[0] + width_sums[1], place_dp * depth, depth, 1
    )
    decay_param_grad = -8.0 * channel_sums[taps + 4] * jax.nn.sigmoid(decay_raw)

    return (
        layer_out.reshape(tall, narrow),
        input_grad.reshape(tall, narrow).astype(WIDE),
        branch_grad,
        gelu_grad,
        output_grad,
        side_by_side(gate_blocks.astype(WIDE)),
        side_by_side(up_blocks.astype(WIDE)),
        down_grad,
        block_grads[:heads],
        block_grads[heads:],
        channel_sums[:taps],
        channel_sums[taps],
        channel_sums[taps + 1],
        channel_sums[taps + 5],
        channel_sums[taps + 2],
        channel_sums[taps + 3],
        decay_param_grad,
        width_sums[1],
        hidden_sums[0, :hidden_part],
        hidden_sums[1, :hidden_part],
        width_sums[2],
        width_sums[3],
        width_sums[0],
    )


def solution(mesh):
    in_specs = (
        P(("dp", "col"), "row"),
        P(("dp", "row")),
        P(("row", "dp"), "col"),
        P(("row", "dp"), "col"),
        P(("col", "dp"), "row"),
        P(("row", "dp"), "col"),
        P(("row", "dp"), "col"),
        P(("col", "dp"), "row"),
        P("col", "dp", None),
        P("col", "dp", None),
        P(None, ("col", "dp")),
        P(("col", "dp")),
        P(("col", "dp")),
        P(("col", "dp")),
        P(("col", "dp")),
        P(("col", "dp")),
        P(("col", "dp")),
        P(("row", "dp")),
        P(("col", "dp")),
        P(("col", "dp")),
        P(("row", "dp")),
        P(("row", "dp")),
        P(("row", "dp")),
        P(("dp", "col"), "row"),
    )
    out_specs = (
        P(("dp", "col"), "row"),
        P(("dp", "col"), "row"),
        P(("row", "dp"), "col"),
        P(("row", "dp"), "col"),
        P(("col", "dp"), "row"),
        P(("row", "dp"), "col"),
        P(("row", "dp"), "col"),
        P(("col", "dp"), "row"),
        P("col", "dp", None),
        P("col", "dp", None),
        P(None, ("col", "dp")),
        P(("col", "dp")),
        P(("col", "dp")),
        P(("col", "dp")),
        P(("col", "dp")),
        P(("col", "dp")),
        P(("col", "dp")),
        P(("row", "dp")),
        P(("col", "dp")),
        P(("col", "dp")),
        P(("row", "dp")),
        P(("row", "dp")),
        P(("row", "dp")),
    )
    return jax.shard_map(shards, mesh=mesh, in_specs=in_specs, out_specs=out_specs, check_vma=False)
```
